32 devices in a mesh: dp: 4 (over z), fsdp: 8 (over y, x, core).
Axes of the slice: x: 2, y: 2, z: 4, core: 2. Of those that a mesh axis runs over, the one named last changes fastest.
Arguments:
- word_table: float32 [30720, 128], P(('dp', 'fsdp')), may hold values from -0.875 to 0.875
- position_table: float32 [512, 128], P(('dp', 'fsdp')), may hold values from -0.875 to 0.875
- head_weights: float32 [768, 1024], P(None, ('dp', 'fsdp'))
- decoder_bias: float32 [30720], P(('dp', 'fsdp')), may hold values from -1.25 to 1.25
- layer_wide: float32 [768, 6144], P(None, ('dp', 'fsdp'))
- layer_tall: float32 [3072, 768], P(('dp', 'fsdp')), may hold values from -0.109375 to 0.109375
- vectors: float32 [13184], replicated
- word_first: float32 [30720, 128], P(('dp', 'fsdp')), may hold values from -4.7683716e-07 to 4.7683716e-07
- word_second: float32 [30720, 128], P(('dp', 'fsdp')), may hold values from 5.2494893e-16 to 2.0997957e-15
- position_first: float32 [512, 128], P(('dp', 'fsdp')), may hold values from -4.7683716e-07 to 4.7683716e-07
- position_second: float32 [512, 128], P(('dp', 'fsdp')), may hold values from 5.2494893e-16 to 2.0997957e-15
- head_first: float32 [768, 1024], P(None, ('dp', 'fsdp')), may hold values from -9.536743e-07 to 9.536743e-07
- head_second: float32 [768, 1024], P(None, ('dp', 'fsdp')), may hold values from 2.0997957e-15 to 8.399183e-15
- decoder_first: float32 [30720], P(('dp', 'fsdp')), may hold values from -4.7683716e-07 to 4.7683716e-07
- decoder_second: float32 [30720], P(('dp', 'fsdp')), may hold values from 5.2494893e-16 to 2.0997957e-15
- wide_first: float32 [768, 6144], P(None, ('dp', 'fsdp')), may hold values from -9.536743e-07 to 9.536743e-07
- wide_second: float32 [768, 6144], P(None, ('dp', 'fsdp')), may hold values from 2.0997957e-15 to 8.399183e-15
- tall_first: float32 [3072, 768], P(('dp', 'fsdp')), may hold values from -9.536743e-07 to 9.536743e-07
- tall_second: float32 [3072, 768], P(('dp', 'fsdp')), may hold values from 2.0997957e-15 to 8.399183e-15
- vector_first: float32 [13184], replicated, may hold values from -3.8146973e-06 to 3.8146973e-06
- vector_second: float32 [13184], replicated, may hold values from 3.3596732e-14 to 1.3438693e-13
- token_ids: int32 [8192], P(('dp', 'fsdp')), may hold values from 0 to 30719
- seq_lengths: int32 [64], P(('dp', 'fsdp')), may hold values from 0 to 256, as said below
- mlm_rows: int32 [1280], P(('dp', 'fsdp')), may hold values from 0 to 255, as said below
- mlm_labels: int32 [1280], P(('dp', 'fsdp')), may hold values from -1 to 30719, as said below
- sop_labels: int32 [64], P(('dp', 'fsdp')), may hold values from 0 to 1
Outputs:
- word_new: float32 [30720, 128], P(('dp', 'fsdp'))
- word_first_new: float32 [30720, 128], P(('dp', 'fsdp'))
- word_second_new: float32 [30720, 128], P(('dp', 'fsdp'))
- position_new: float32 [512, 128], P(('dp', 'fsdp'))
- position_first_new: float32 [512, 128], P(('dp', 'fsdp'))
- position_second_new: float32 [512, 128], P(('dp', 'fsdp'))
- head_new: float32 [768, 1024], P(None, ('dp', 'fsdp'))
- head_first_new: float32 [768, 1024], P(None, ('dp', 'fsdp'))
- head_second_new: float32 [768, 1024], P(None, ('dp', 'fsdp'))
- decoder_new: float32 [30720], P(('dp', 'fsdp'))
- decoder_first_new: float32 [30720], P(('dp', 'fsdp'))
- decoder_second_new: float32 [30720], P(('dp', 'fsdp'))
- wide_new: float32 [768, 6144], P(None, ('dp', 'fsdp'))
- wide_first_new: float32 [768, 6144], P(None, ('dp', 'fsdp'))
- wide_second_new: float32 [768, 6144], P(None, ('dp', 'fsdp'))
- tall_new: float32 [3072, 768], P(('dp', 'fsdp'))
- tall_first_new: float32 [3072, 768], P(('dp', 'fsdp'))
- tall_second_new: float32 [3072, 768], P(('dp', 'fsdp'))
- vectors_new: float32 [13184], replicated
- vector_first_new: float32 [13184], replicated
- vector_second_new: float32 [13184], replicated
- mlm_sum: float32 [], replicated
- mlm_count: float32 [], replicated
- sop_sum: float32 [], replicated
- sop_count: float32 [], replicated
- grad_norm: float32 [], replicated
The draws below stay inside these ranges and needn't reach their ends.
Inputs may be any that keep to these rules, and one draw needn't show every extreme that they name: `seq_lengths`: per device either one sequence of length l0 in (128, 256] with l1 = 0, or two sequences of lengths in [64, 128], the second starting at row 128. Some device holds a sequence of 256. `mlm_rows`: each slot names a live row of its own device's block. `mlm_labels`: -1 marks an unused slot; the others are word ids. Used slots come first on each device.
All inputs are finite; a program needn't handle non-finite values.
Results may differ from the reference program's by a relative error of at most 0.0085.
The reference program's roundings to bfloat16 on the way count: a program that leaves them out, or rounds other values in their place, can miss the bound.
Values may be sent and summed in bfloat16 or wider, within the bound.
A program may use at most 192 MiB of HBM per device.

```python
import math
import jax
import jax.numpy as jnp
import numpy as np
from jax import lax

D = 768
HEADS = 12
HEAD_DIM = 64
FF = 3072
E = 128
VOCAB = 30720
POS = 512
LAYERS = 4
STEP = 10
BUCKET = 128
MLM_DEV = 40
TOKENS = 8192
SEQ_SLOTS = 64
NPARAM = 11905920
N_DP = 4
N_FSDP = 8


def vector_layout():
    return [('proj_b', D), ('q_b', D), ('v_b', D), ('o_b', D), ('ln1_g', D), ('ln1_b', D), ('ffo_b', D), ('ln2_g', D), ('ln2_b', D), ('pool_b', D), ('cls', 2 * D), ('ff_b', FF), ('emb_g', E), ('emb_b', E), ('mlm_b', E), ('mlm_g', E), ('mlm_lb', E), ('types', 2 * E)]


def lengths_of(key):
    key = jax.random.fold_in(key, 101)
    devices = N_DP * N_FSDP
    subkeys = jax.random.split(key, 4)
    device_index = jnp.arange(devices)
    longer = jax.random.randint(subkeys[0], (devices,), 0, 2)
    forced = jax.random.randint(subkeys[1], (), 0, devices)
    longer = jnp.where(device_index == forced, 1, longer)
    long_len = jax.random.randint(subkeys[2], (devices,), BUCKET + 1, 2 * BUCKET + 1)
    long_len = jnp.where(device_index == forced, 2 * BUCKET, long_len)
    shorter = jax.random.randint(subkeys[3], (devices, 2), BUCKET // 2, BUCKET + 1)
    leading = jnp.where(longer == 1, long_len, shorter[:, 0])
    second = jnp.where(longer == 1, 0, shorter[:, 1])
    return jnp.stack([leading, second], 1)


def mlm_plan(key):
    lengths = lengths_of(key)
    key = jax.random.fold_in(key, 202)
    subkeys = jax.random.split(key, 3)
    devices = N_DP * N_FSDP
    device_index = jnp.arange(devices)
    shard_index = device_index % N_FSDP
    group_index = device_index // N_FSDP
    lowest = max(MLM_DEV // 3, 1)
    rising = shard_index * max(N_DP - 1, 1) + group_index * max(N_FSDP - 1, 1)
    divisor = 2 * max(N_FSDP - 1, 1) * max(N_DP - 1, 1)
    filled = lowest + (MLM_DEV - lowest) * rising // divisor - jax.random.randint(subkeys[0], (devices,), 0, 3)
    filled = jnp.clip(filled, 1, MLM_DEV)
    slot_index = jnp.arange(MLM_DEV)
    live_total = lengths[:, 0] + lengths[:, 1]
    picked = jax.random.randint(subkeys[1], (devices, MLM_DEV), 0, live_total[:, None])
    picked = jnp.where(slot_index[None, :] == 0, 0, picked)
    picked = jnp.where(slot_index[None, :] == 1, live_total[:, None] - 1, picked)
    row_ids = jnp.where(picked < lengths[:, :1], picked, BUCKET + picked - lengths[:, :1])
    words = jax.random.randint(subkeys[2], (devices, MLM_DEV), 0, VOCAB)
    words = words.at[0, 0].set(VOCAB - 1)
    labels = jnp.where(slot_index[None, :] < filled[:, None], words, -1)
    return (row_ids.reshape(-1).astype(jnp.int32), labels.reshape(-1).astype(jnp.int32))


def draw_seq_lengths(key, part):
    shared = lengths_of(key)
    return shared.reshape(-1).astype(jnp.int32)


def draw_mlm_rows(key, part):
    shared = mlm_plan(key)
    return shared[0]


def draw_mlm_labels(key, part):
    shared = mlm_plan(key)
    return shared[1]


def draw_layer_wide(key, part):
    key = jax.random.fold_in(key, 4)
    column = jnp.arange(4 * D + FF)
    scaling = jnp.where((column >= 3 * D) & (column < 4 * D), 4.0, 1.0) * D ** (-0.5)
    values = jax.random.normal(key, (D, 4 * D + FF), jnp.float32)
    return values * scaling[None, :]


def draw_head_weights(key, part):
    key = jax.random.fold_in(key, 5)
    column = jnp.arange(2 * E + D)
    scaling = jnp.where(column >= E + D, E ** (-0.5), D ** (-0.5))
    values = jax.random.normal(key, (D, 2 * E + D), jnp.float32)
    return values * scaling[None, :]


def draw_vectors(key, part):
    key = jax.random.fold_in(key, 6)
    segments = []
    number = 0
    for member, length in vector_layout():
        subkey = jax.random.fold_in(key, number)
        number += 1
        base = jax.random.normal(subkey, (length,), jnp.float32)
        if member in ('ln1_g', 'ln2_g', 'emb_g', 'mlm_g'):
            rising = 0.5 + jnp.arange(length).astype(jnp.float32) / (length - 1)
            jitter = jax.random.uniform(jax.random.fold_in(subkey, 7), (length,), jnp.float32, 0.8, 1.2)
            segments.append(rising * jitter)
        elif member == 'cls':
            segments.append(base * 3.0 * D ** (-0.5))
        elif member == 'types':
            segments.append(base * 0.15)
        else:
            segments.append(base * 0.1)
    return jnp.concatenate(segments)


def plant(entries, own_key, smallest, top_value):
    longest = entries.shape.index(max(entries.shape))
    spots = []
    for shift in (0, 1):
        where = [jax.random.randint(jax.random.fold_in(own_key, axis), (), 0, length) for axis, length in enumerate(entries.shape)]
        where[longest] = (where[longest] + shift) % entries.shape[longest]
        spots.append(tuple(where))
    return entries.at[spots[0]].set(smallest).at[spots[1]].set(top_value)


def level_of(rng, extent, cuts, smallest, high):
    factor_of, own = 1.0, jax.random.fold_in(rng, 6)
    for axis_at, shards_of in cuts:
        steps = jnp.exp(jax.random.uniform(jax.random.fold_in(own, axis_at), (shards_of,), jnp.float32, smallest / len(cuts), high / len(cuts)))
        factor_of = factor_of * jnp.repeat(steps, extent[axis_at] // shards_of).reshape([-1 if axis == axis_at else 1 for axis in range(len(extent))])
    return factor_of


def rank_table(number_of, lean):
    loads = [(1 << 20) // math.isqrt(grade ** lean) + 1 for grade in range(1, number_of + 1)]
    width = 1 + sum(loads) // (1 << 30)
    return np.cumsum(np.array([max(1, weight // width) for weight in loads]))


def ranked_ids(rng, extent, count, slope):
    listing = rank_table(count, slope)
    ticket = jax.random.randint(jax.random.fold_in(rng, 1), extent, 0, int(listing[count - 1]))
    standing = jnp.searchsorted(jnp.asarray(listing, jnp.int32), ticket, side="right")
    return jax.random.permutation(jax.random.fold_in(rng, 2), count)[standing].astype(jnp.int32)


def normal_values(own_key, dims, scale, limit, cuts=(), held_as=jnp.bfloat16):
    result = scale * jax.random.normal(own_key, dims, jnp.float32)
    if cuts:
        result = result * level_of(own_key, dims, cuts, -0.22, 0.18)
    return jnp.clip(result, -limit, limit).astype(held_as)


def setup_inputs(seed: int = 0) -> dict:
    key_of = jax.random.split(jax.random.key(seed), 27)
    return {
        "word_table": normal_values(key_of[0], (VOCAB, E), 0.15, 0.875, ((0, 32),), jnp.float32),
        "position_table": normal_values(key_of[1], (POS, E), 0.15, 0.875, ((0, 32),), jnp.float32),
        "head_weights": draw_head_weights(jax.random.fold_in(key_of[26], 71), 0),
        "decoder_bias": normal_values(key_of[3], (VOCAB,), 0.2, 1.25, ((0, 32),), jnp.float32),
        "layer_wide": draw_layer_wide(jax.random.fold_in(key_of[26], 71), 0),
        "layer_tall": normal_values(key_of[5], (FF, D), FF ** -0.5, 0.109375, ((0, 32),), jnp.float32),
        "vectors": draw_vectors(jax.random.fold_in(key_of[26], 71), 0),
        "word_first": normal_values(key_of[7], (VOCAB, E), (0.000278 * NPARAM ** -0.5), 4.76837158203125e-07, ((0, 32),), jnp.float32),
        "word_second": jnp.clip(jnp.exp(math.log(2.0997957350345946e-15) - 1.3862944 * jax.random.uniform(key_of[8], (VOCAB, E), jnp.float32) ** level_of(key_of[8], (VOCAB, E), ((0, 32),), -0.2, 0.2)), 5.249489337586487e-16, 2.0997957350345946e-15),
        "position_first": normal_values(key_of[9], (POS, E), (0.000278 * NPARAM ** -0.5), 4.76837158203125e-07, ((0, 32),), jnp.float32),
        "position_second": jnp.clip(jnp.exp(math.log(2.0997957350345946e-15) - 1.3862944 * jax.random.uniform(key_of[10], (POS, E), jnp.float32) ** level_of(key_of[10], (POS, E), ((0, 32),), -0.2, 0.2)), 5.249489337586487e-16, 2.0997957350345946e-15),
        "head_first": normal_values(key_of[11], (D, 2 * E + D), (0.000555 * NPARAM ** -0.5), 9.5367431640625e-07, ((1, 32),), jnp.float32),
        "head_second": jnp.clip(jnp.exp(math.log(8.399182940138378e-15) - 1.3862944 * jax.random.uniform(key_of[12], (D, 2 * E + D), jnp.float32) ** level_of(key_of[12], (D, 2 * E + D), ((1, 32),), -0.2, 0.2)), 2.0997957350345946e-15, 8.399182940138378e-15),
        "decoder_first": normal_values(key_of[13], (VOCAB,), (0.000278 * NPARAM ** -0.5), 4.76837158203125e-07, ((0, 32),), jnp.float32),
        "decoder_second": jnp.clip(jnp.exp(math.log(2.0997957350345946e-15) - 1.3862944 * jax.random.uniform(key_of[14], (VOCAB,), jnp.float32) ** level_of(key_of[14], (VOCAB,), ((0, 32),), -0.2, 0.2)), 5.249489337586487e-16, 2.0997957350345946e-15),
        "wide_first": normal_values(key_of[15], (D, 4 * D + FF), (0.000555 * NPARAM ** -0.5), 9.5367431640625e-07, ((1, 32),), jnp.float32),
        "wide_second": jnp.clip(jnp.exp(math.log(8.399182940138378e-15) - 1.3862944 * jax.random.uniform(key_of[16], (D, 4 * D + FF), jnp.float32) ** level_of(key_of[16], (D, 4 * D + FF), ((1, 32),), -0.2, 0.2)), 2.0997957350345946e-15, 8.399182940138378e-15),
        "tall_first": normal_values(key_of[17], (FF, D), (0.000555 * NPARAM ** -0.5), 9.5367431640625e-07, ((0, 32),), jnp.float32),
        "tall_second": jnp.clip(jnp.exp(math.log(8.399182940138378e-15) - 1.3862944 * jax.random.uniform(key_of[18], (FF, D), jnp.float32) ** level_of(key_of[18], (FF, D), ((0, 32),), -0.2, 0.2)), 2.0997957350345946e-15, 8.399182940138378e-15),
        "vector_first": normal_values(key_of[19], (12 * D + FF + 7 * E,), (0.00222 * NPARAM ** -0.5), 3.814697265625e-06, (), jnp.float32),
        "vector_second": jnp.clip(jnp.exp(jax.random.uniform(key_of[20], (12 * D + FF + 7 * E,), jnp.float32, math.log(3.3596731760553514e-14), math.log(1.3438692704221405e-13))), 3.3596731760553514e-14, 1.3438692704221405e-13),
        "token_ids": plant(ranked_ids(key_of[21], (TOKENS,), VOCAB, 2), jax.random.fold_in(key_of[21], 3), 0, VOCAB - 1).astype(jnp.int32),
        "seq_lengths": draw_seq_lengths(jax.random.fold_in(key_of[26], 71), 0),
        "mlm_rows": draw_mlm_rows(jax.random.fold_in(key_of[26], 71), 0),
        "mlm_labels": draw_mlm_labels(jax.random.fold_in(key_of[26], 71), 0),
        "sop_labels": plant(jax.random.randint(key_of[25], (SEQ_SLOTS,), 0, 2), jax.random.fold_in(key_of[25], 1), 0, 1).astype(jnp.int32),
    }


PRECISE = lax.Precision.HIGHEST
EPSILON = 1e-06
LEARN_RATE = 0.1
SMALL_RATE = 0.5
BETA_ONE = 0.9
BETA_TWO = 0.999
ADAM_EPSILON = 1e-08
WEIGHT_DECAY = 0.01
CLIP_NORM = 0.005
NORM_EPSILON = 1e-06
MASKED = -1e+30

@jax.custom_vjp
def low(v):
    return lax.optimization_barrier(v.astype(jnp.bfloat16)).astype(jnp.float32)

@jax.custom_vjp
def low_back(v):
    return v

def low_keep(v):
    return (low(v), None)

def low_pass(kept, grad):
    return (grad,)

def back_keep(v):
    return (v, None)

def back_low(kept, grad):
    return (low(grad),)
low.defvjp(low_keep, low_pass)
low_back.defvjp(back_keep, back_low)

def layout():
    return [('proj_b', D), ('q_b', D), ('v_b', D), ('o_b', D), ('ln1_g', D), ('ln1_b', D), ('ffo_b', D), ('ln2_g', D), ('ln2_b', D), ('pool_b', D), ('cls', 2 * D), ('ff_b', FF), ('emb_g', E), ('emb_b', E), ('mlm_b', E), ('mlm_g', E), ('mlm_lb', E), ('types', 2 * E)]

def split_vectors(vectors):
    pieces = {}
    offset = 0
    for member, length in layout():
        pieces[member] = vectors[offset:offset + length]
        offset += length
    return pieces

def layer_norm(x, factor, offset):
    centre = x - lax.optimization_barrier(jnp.mean(x, -1, keepdims=True))
    spread = lax.optimization_barrier(jnp.mean(centre * centre, -1, keepdims=True))
    return centre * lax.rsqrt(spread + EPSILON) * factor + offset

def gelu_tanh(x):
    return jax.nn.gelu(x, approximate=True)

def highest(a, b):
    return jnp.dot(a, b, precision=PRECISE, preferred_element_type=jnp.float32)

def row_layout(lengths):
    row_index = jnp.arange(2 * BUCKET, dtype=jnp.int32)
    second = (row_index >= BUCKET) & (lengths[1] > 0)
    seq_id = second.astype(jnp.int32)
    position = row_index - BUCKET * seq_id
    own_length = jnp.where(second, lengths[1], lengths[0])
    is_live = position < own_length
    token_kind = (position >= own_length // 2).astype(jnp.int32)
    allowed = (seq_id[:, None] == seq_id[None, :]) & is_live[None, :]
    return (position, token_kind, allowed)

def attention(projected, allowed):
    total_rows = projected.shape[0]
    heads = projected.reshape(total_rows, 3, HEADS, HEAD_DIM)
    queries, key_rows, values = (heads[:, 0], heads[:, 1], heads[:, 2])
    scores = low_back(jnp.einsum('qhd,khd->hqk', queries, key_rows, precision=PRECISE) * HEAD_DIM ** (-0.5))
    scores = jnp.where(allowed[None], scores, MASKED)
    powers = jnp.exp(scores - lax.optimization_barrier(jnp.max(scores, -1, keepdims=True)))
    weighting = low(powers / lax.optimization_barrier(jnp.sum(powers, -1, keepdims=True)))
    mixed = jnp.einsum('hqk,khd->qhd', weighting, values, precision=PRECISE)
    return low_back(low(mixed.reshape(total_rows, D)))

def layer(hidden, wide, tall, pieces, allowed):
    joint_bias = jnp.concatenate([pieces['q_b'], jnp.zeros_like(pieces['q_b']), pieces['v_b']])
    projected = low_back(low(highest(low(hidden), wide[:, :3 * D]) + joint_bias))
    mixed = attention(projected, allowed)
    branch = low_back(highest(mixed, wide[:, 3 * D:4 * D]) + pieces['o_b'])
    middle = layer_norm(hidden + branch, pieces['ln1_g'], pieces['ln1_b'])
    inner = low_back(highest(low(middle), wide[:, 4 * D:]) + pieces['ff_b'])
    outer = low_back(highest(low(gelu_tanh(inner)), tall) + pieces['ffo_b'])
    return layer_norm(middle + outer, pieces['ln2_g'], pieces['ln2_b'])

def device_loss(weights, token_ids, lengths, mlm_rows, mlm_labels, sop_labels, scales):
    word, place, head, decoder, wide, tall, vectors = weights
    pieces = split_vectors(vectors)
    position, token_kind, allowed = row_layout(lengths)
    types = pieces['types'].reshape(2, E)
    embedded = word[token_ids] + place[position] + types[token_kind]
    normed = low(layer_norm(embedded, pieces['emb_g'], pieces['emb_b']))
    hidden = low_back(highest(normed, head[:, E + D:].T) + pieces['proj_b'])
    for unused in range(LAYERS):
        hidden = layer(hidden, wide, tall, pieces, allowed)
    picked = low(hidden[mlm_rows])
    dense = low_back(highest(picked, head[:, :E]) + pieces['mlm_b'])
    head_rows = low(layer_norm(gelu_tanh(dense), pieces['mlm_g'], pieces['mlm_lb']))
    logits = low_back(highest(head_rows, word.T) + decoder)
    top = lax.optimization_barrier(jnp.max(logits, -1, keepdims=True))
    log_total = jnp.log(lax.optimization_barrier(jnp.sum(jnp.exp(logits - top), -1))) + top[:, 0]
    target = jnp.take_along_axis(logits, jnp.maximum(mlm_labels, 0)[:, None], 1)[:, 0]
    used = (mlm_labels >= 0).astype(logits.dtype)
    mlm_sum = jnp.sum((log_total - target) * used)
    firsts = low(jnp.concatenate([hidden[0:1], hidden[BUCKET:BUCKET + 1]], 0))
    pooled = jnp.tanh(low_back(highest(firsts, head[:, E:E + D]) + pieces['pool_b']))
    classes = highest(pooled, pieces['cls'].reshape(2, D).T)
    class_top = lax.optimization_barrier(jnp.max(classes, -1, keepdims=True))
    class_total = jnp.log(lax.optimization_barrier(jnp.sum(jnp.exp(classes - class_top), -1))) + class_top[:, 0]
    class_target = jnp.take_along_axis(classes, sop_labels[:, None], 1)[:, 0]
    present = jnp.stack([jnp.ones_like(lengths[0]), (lengths[1] > 0).astype(jnp.int32)]).astype(classes.dtype)
    sop_sum = jnp.sum((class_total - class_target) * present)
    return (mlm_sum * scales[0] + sop_sum * scales[1], (mlm_sum, sop_sum))

def group_loss(weights, batch, scales):

    def single(token_ids, lengths, mlm_rows, mlm_labels, sop_labels):
        return device_loss(weights, token_ids, lengths, mlm_rows, mlm_labels, sop_labels, scales)
    totals, sums = jax.vmap(single)(*batch)
    return (jnp.sum(totals), jnp.sum(sums[0]), jnp.sum(sums[1]))

def forward(weights, batch, scales):
    saved = jax.checkpoint(group_loss)

    def step(carry, group):
        parts = saved(weights, group, scales)
        return ((carry[0] + parts[0], carry[1] + parts[1], carry[2] + parts[2]), None)
    zero = jnp.zeros((), scales.dtype)
    sums, unused = lax.scan(step, (zero, zero, zero), batch)
    return (sums[0], (sums[1], sums[2]))

def adam_update(weight, gradient, first, second, rate):
    first = BETA_ONE * first + (1 - BETA_ONE) * gradient
    second = BETA_TWO * second + (1 - BETA_TWO) * gradient * gradient
    first_hat = first / (1 - BETA_ONE ** STEP)
    second_hat = second / (1 - BETA_TWO ** STEP)
    updated = weight - rate * (first_hat / (jnp.sqrt(second_hat) + ADAM_EPSILON) + WEIGHT_DECAY * weight)
    return (updated, first, second)

def reference(word_table, position_table, head_weights, decoder_bias, layer_wide, layer_tall, vectors, word_first, word_second, position_first, position_second, head_first, head_second, decoder_first, decoder_second, wide_first, wide_second, tall_first, tall_second, vector_first, vector_second, token_ids, seq_lengths, mlm_rows, mlm_labels, sop_labels):
    devices = N_DP * N_FSDP
    group = min(devices, max(1, 4096 // (2 * BUCKET)))
    groups = devices // group
    batch = (token_ids.reshape(groups, group, 2 * BUCKET), seq_lengths.reshape(groups, group, 2), mlm_rows.reshape(groups, group, MLM_DEV), mlm_labels.reshape(groups, group, MLM_DEV), sop_labels.reshape(groups, group, 2))
    mlm_count = jnp.sum((mlm_labels >= 0).astype(jnp.int32)).astype(jnp.float32)
    sop_count = (devices + jnp.sum((seq_lengths.reshape(devices, 2)[:, 1] > 0).astype(jnp.int32))).astype(jnp.float32)
    scales = jnp.stack([1.0 / mlm_count, 1.0 / sop_count])
    masters = (word_table, position_table, head_weights, decoder_bias, layer_wide, layer_tall, vectors)

    def loss_of(weights):
        sent = (low(weights[0]), low(weights[1]), low(weights[2]), low(weights[3]), low(weights[4]), low(weights[5]), weights[6])
        return forward(sent, batch, scales)
    loss, backward, sums = jax.vjp(loss_of, masters, has_aux=True)
    gradients = backward(jnp.ones_like(loss))[0]
    squares = jnp.zeros((), jnp.float32)
    for gradient in gradients:
        squares = squares + jnp.sum(gradient * gradient)
    grad_norm = jnp.sqrt(squares)
    factor = jnp.minimum(1.0, CLIP_NORM / (grad_norm + NORM_EPSILON))
    word_new, word_first_new, word_second_new = adam_update(word_table, factor * gradients[0], word_first, word_second, LEARN_RATE)
    position_new, position_first_new, position_second_new = adam_update(position_table, factor * gradients[1], position_first, position_second, LEARN_RATE)
    head_new, head_first_new, head_second_new = adam_update(head_weights, factor * gradients[2], head_first, head_second, LEARN_RATE)
    decoder_new, decoder_first_new, decoder_second_new = adam_update(decoder_bias, factor * gradients[3], decoder_first, decoder_second, LEARN_RATE)
    wide_new, wide_first_new, wide_second_new = adam_update(layer_wide, factor * gradients[4], wide_first, wide_second, LEARN_RATE)
    tall_new, tall_first_new, tall_second_new = adam_update(layer_tall, factor * gradients[5], tall_first, tall_second, LEARN_RATE)
    vectors_new, vector_first_new, vector_second_new = adam_update(vectors, factor * gradients[6], vector_first, vector_second, SMALL_RATE)
    return (word_new, word_first_new, word_second_new, position_new, position_first_new, position_second_new, head_new, head_first_new, head_second_new, decoder_new, decoder_first_new, decoder_second_new, wide_new, wide_first_new, wide_second_new, tall_new, tall_first_new, tall_second_new, vectors_new, vector_first_new, vector_second_new, sums[0], mlm_count, sums[1], sop_count, grad_norm)
```

```python
import jax
import jax.numpy as jnp
from jax import lax
from jax.sharding import PartitionSpec as P

D = 768
HEADS = 12
HEAD_DIM = 64
FF = 3072
E = 128
LAYERS = 4
STEP = 10
BUCKET = 128
ROWS = 2 * BUCKET

PRECISE = lax.Precision.HIGHEST
EPSILON = 1e-06
LEARN_RATE = 0.1
SMALL_RATE = 0.5
BETA_ONE = 0.9
BETA_TWO = 0.999
ADAM_EPSILON = 1e-08
WEIGHT_DECAY = 0.01
CLIP_NORM = 0.005
NORM_EPSILON = 1e-06
MASKED = -1e30
SCALE = HEAD_DIM ** (-0.5)
AXES = ("dp", "fsdp")


def layout():
    return [
        ("proj_b", D),
        ("q_b", D),
        ("v_b", D),
        ("o_b", D),
        ("ln1_g", D),
        ("ln1_b", D),
        ("ffo_b", D),
        ("ln2_g", D),
        ("ln2_b", D),
        ("pool_b", D),
        ("cls", 2 * D),
        ("ff_b", FF),
        ("emb_g", E),
        ("emb_b", E),
        ("mlm_b", E),
        ("mlm_g", E),
        ("mlm_lb", E),
        ("types", 2 * E),
    ]


def split_vectors(vectors):
    pieces = {}
    offset = 0
    for member, length in layout():
        pieces[member] = vectors[offset : offset + length]
        offset += length
    return pieces


def join_vectors(gradients):
    return jnp.concatenate([gradients[member].reshape(-1) for member, length in layout()])


def to_half(x):
    return x.astype(jnp.bfloat16)


def product(a, b):
    return jnp.dot(a, b, preferred_element_type=jnp.float32)


def times_transpose(a, b):
    return lax.dot_general(a, b, (((1,), (1,)), ((), ())), preferred_element_type=jnp.float32)


def transpose_times(a, b):
    return lax.dot_general(a, b, (((0,), (0,)), ((), ())), preferred_element_type=jnp.float32)


def column_sum(x):
    return jnp.sum(x.astype(jnp.float32), 0)


def norm_forward(x):
    centre = x - jnp.mean(x, -1, keepdims=True)
    inverse = lax.rsqrt(jnp.mean(centre * centre, -1, keepdims=True) + EPSILON)
    return centre * inverse, inverse


def norm_backward(upstream, factor, hat, inverse):
    scaled = upstream * factor
    return inverse * (
        scaled
        - jnp.mean(scaled, -1, keepdims=True)
        - hat * jnp.mean(scaled * hat, -1, keepdims=True)
    )


GELU_A = 0.7978845608028654
GELU_B = 0.044715


def gelu_tanh(x):
    return 0.5 * x * (1.0 + jnp.tanh(GELU_A * (x + GELU_B * x * x * x)))


def gelu_slope(x):
    bend = jnp.tanh(GELU_A * (x + GELU_B * x * x * x))
    return 0.5 * (1.0 + bend) + 0.5 * x * (1.0 - bend * bend) * GELU_A * (
        1.0 + 3.0 * GELU_B * x * x
    )


def row_layout(lengths):
    row_index = jnp.arange(ROWS, dtype=jnp.int32)
    second = (row_index >= BUCKET) & (lengths[1] > 0)
    seq_id = second.astype(jnp.int32)
    position = row_index - BUCKET * seq_id
    own_length = jnp.where(second, lengths[1], lengths[0])
    is_live = position < own_length
    token_kind = (position >= own_length // 2).astype(jnp.int32)
    allowed = (seq_id[:, None] == seq_id[None, :]) & is_live[None, :]
    return (token_kind, allowed)


def gather_rows(shards):
    return [lax.all_gather(s, AXES, axis=0, tiled=True) for s in shards]


def scatter_rows(partials):
    return [lax.psum_scatter(s, AXES, scatter_dimension=0, tiled=True) for s in partials]


def layer_forward(hidden, wide, tall, pieces, allowed):
    hidden_half = to_half(hidden)
    joint_bias = jnp.concatenate([pieces["q_b"], jnp.zeros_like(pieces["q_b"]), pieces["v_b"]])
    projected = to_half(times_transpose(hidden_half, wide[: 3 * D]) + joint_bias)
    heads = projected.reshape(ROWS, 3, HEADS, HEAD_DIM)
    queries, key_rows, values = (heads[:, 0], heads[:, 1], heads[:, 2])
    scores = (
        jnp.einsum("qhd,khd->hqk", queries, key_rows, preferred_element_type=jnp.float32) * SCALE
    )
    scores = jnp.where(allowed[None], scores, MASKED)
    powers = jnp.exp(scores - jnp.max(scores, -1, keepdims=True))
    weighting = powers / jnp.sum(powers, -1, keepdims=True)
    mixed = jnp.einsum(
        "hqk,khd->qhd", to_half(weighting), values, preferred_element_type=jnp.float32
    )
    mixed = to_half(mixed.reshape(ROWS, D))
    first_sum = hidden + times_transpose(mixed, wide[3 * D : 4 * D]) + pieces["o_b"]
    hat_one, inverse_one = norm_forward(first_sum)
    middle = hat_one * pieces["ln1_g"] + pieces["ln1_b"]
    middle_half = to_half(middle)
    inner = times_transpose(middle_half, wide[4 * D :]) + pieces["ff_b"]
    active = to_half(gelu_tanh(inner))
    second_sum = middle + product(active, tall) + pieces["ffo_b"]
    hat_two, inverse_two = norm_forward(second_sum)
    output = hat_two * pieces["ln2_g"] + pieces["ln2_b"]
    kept = {
        "hidden_half": hidden_half,
        "projected": projected,
        "weighting": weighting,
        "mixed": mixed,
        "hat_one": hat_one,
        "inverse_one": inverse_one,
        "middle_half": middle_half,
        "inner": inner,
        "active": active,
        "hat_two": hat_two,
        "inverse_two": inverse_two,
    }
    return (output, kept)


def layer_backward(upstream, kept, wide, tall, pieces):
    gain_two = jnp.sum(upstream * kept["hat_two"], 0)
    shift_two = jnp.sum(upstream, 0)
    back_second = norm_backward(upstream, pieces["ln2_g"], kept["hat_two"], kept["inverse_two"])
    outer_half = to_half(back_second)
    inner_half = to_half(times_transpose(outer_half, tall) * gelu_slope(kept["inner"]))
    back_middle = back_second + product(inner_half, wide[4 * D :])
    gain_one = jnp.sum(back_middle * kept["hat_one"], 0)
    shift_one = jnp.sum(back_middle, 0)
    back_first = norm_backward(back_middle, pieces["ln1_g"], kept["hat_one"], kept["inverse_one"])
    branch_half = to_half(back_first)
    back_mixed = to_half(product(branch_half, wide[3 * D : 4 * D])).reshape(ROWS, HEADS, HEAD_DIM)
    heads = kept["projected"].reshape(ROWS, 3, HEADS, HEAD_DIM)
    queries, key_rows, values = (heads[:, 0], heads[:, 1], heads[:, 2])
    weighting = kept["weighting"]
    back_soft = jnp.einsum("qhd,khd->hqk", back_mixed, values, preferred_element_type=jnp.float32)
    scores_half = to_half(
        weighting * (back_soft - jnp.sum(weighting * back_soft, -1, keepdims=True))
    )
    back_queries = (
        jnp.einsum("hqk,khd->qhd", scores_half, key_rows, preferred_element_type=jnp.float32)
        * SCALE
    )
    back_key_rows = (
        jnp.einsum("hqk,qhd->khd", scores_half, queries, preferred_element_type=jnp.float32) * SCALE
    )
    back_values = jnp.einsum(
        "hqk,qhd->khd", to_half(weighting), back_mixed, preferred_element_type=jnp.float32
    )
    joint_half = to_half(
        jnp.stack([back_queries, back_key_rows, back_values], 1).reshape(ROWS, 3 * D)
    )
    back_hidden = back_first + product(joint_half, wide[: 3 * D])
    out = {
        "joint_half": joint_half,
        "branch_half": branch_half,
        "inner_half": inner_half,
        "outer_half": outer_half,
        "norms": jnp.stack([gain_one, shift_one, gain_two, shift_two]),
    }
    return (back_hidden, out)


def adam_update(weight, gradient, first, second, rate):
    first = BETA_ONE * first + (1 - BETA_ONE) * gradient
    second = BETA_TWO * second + (1 - BETA_TWO) * gradient * gradient
    first_hat = first / (1 - BETA_ONE**STEP)
    second_hat = second / (1 - BETA_TWO**STEP)
    updated = weight - rate * (
        first_hat / (jnp.sqrt(second_hat) + ADAM_EPSILON) + WEIGHT_DECAY * weight
    )
    return (updated, first, second)


def local(
    word_table,
    position_table,
    head_weights,
    decoder_bias,
    layer_wide,
    layer_tall,
    vectors,
    word_first,
    word_second,
    position_first,
    position_second,
    head_first,
    head_second,
    decoder_first,
    decoder_second,
    wide_first,
    wide_second,
    tall_first,
    tall_second,
    vector_first,
    vector_second,
    token_ids,
    seq_lengths,
    mlm_rows,
    mlm_labels,
    sop_labels,
):
    own = lax.axis_index(AXES)
    words = word_table.shape[0]
    slots = mlm_labels.shape[0]
    pieces = split_vectors(vectors)
    token_kind, allowed = row_layout(seq_lengths)

    facts = jnp.concatenate([token_ids, mlm_labels, seq_lengths])
    padded = -(-facts.shape[0] // 1024) * 1024
    facts = jnp.pad(facts, (0, padded - facts.shape[0])).reshape(-1, 128)
    (all_facts,) = gather_rows([facts])
    all_facts = all_facts.reshape(-1, padded)
    devices = all_facts.shape[0]
    all_ids = all_facts[:, :ROWS].reshape(-1)
    all_labels = all_facts[:, ROWS : ROWS + slots].reshape(-1)
    all_seconds = all_facts[:, ROWS + slots + 1] > 0
    all_used = (all_labels >= 0).astype(jnp.float32)
    mlm_count = jnp.sum(all_used)
    sop_count = devices + jnp.sum(all_seconds.astype(jnp.float32))
    scales = (1.0 / mlm_count, 1.0 / sop_count)

    word_half = to_half(word_table)
    wide, tall, head, place = gather_rows(
        [
            to_half(layer_wide).T,
            to_half(layer_tall),
            to_half(head_weights).T,
            to_half(position_table),
        ]
    )

    offset = own * words
    column = jnp.arange(words, dtype=jnp.int32)
    select = to_half((all_ids - offset)[:, None] == column[None, :])
    (found,) = scatter_rows([to_half(product(select, word_half))])
    two = seq_lengths[1] > 0
    place = place[:ROWS].astype(jnp.float32)
    placed = jnp.concatenate([place[:BUCKET], jnp.where(two, place[:BUCKET], place[BUCKET:])], 0)
    types = pieces["types"].reshape(2, E)
    embedded = (
        found.astype(jnp.float32)
        + placed
        + jnp.where(token_kind[:, None] == 0, types[0:1], types[1:2])
    )
    embed_hat, embed_inverse = norm_forward(embedded)
    normed_half = to_half(embed_hat * pieces["emb_g"] + pieces["emb_b"])
    hidden = product(normed_half, head[E + D :]) + pieces["proj_b"]

    final, kept = lax.scan(
        lambda h, unused: layer_forward(h, wide, tall, pieces, allowed),
        hidden,
        None,
        length=LAYERS,
    )

    final_half = to_half(final)
    pick = to_half(mlm_rows[:, None] == jnp.arange(ROWS, dtype=jnp.int32)[None, :])
    picked = to_half(product(pick, final_half))
    dense = times_transpose(picked, head[:E]) + pieces["mlm_b"]
    mlm_hat, mlm_inverse = norm_forward(gelu_tanh(dense))
    rows_half = to_half(mlm_hat * pieces["mlm_g"] + pieces["mlm_lb"])
    (all_rows,) = gather_rows([rows_half])
    logits = times_transpose(all_rows, word_half) + to_half(decoder_bias).astype(jnp.float32)
    onehot = ((all_labels - offset)[:, None] == column[None, :]).astype(jnp.float32)
    own_top = jnp.max(logits, -1)
    own_total = jnp.sum(jnp.exp(logits - own_top[:, None]), -1)
    own_target = jnp.sum(logits * onehot, -1)
    stats = lax.all_gather(jnp.stack([own_top, own_total, own_target]), AXES)
    top = jnp.max(stats[:, 0], 0)
    total = jnp.sum(stats[:, 1] * jnp.exp(stats[:, 0] - top[None]), 0)
    log_total = jnp.log(total) + top
    mlm_sum = jnp.sum((log_total - jnp.sum(stats[:, 2], 0)) * all_used)
    logits_half = to_half(
        (jnp.exp(logits - top[:, None]) / total[:, None] - onehot) * (all_used * scales[0])[:, None]
    )
    back_decoder = column_sum(logits_half)
    back_word_head = transpose_times(logits_half, all_rows)
    (back_rows,) = scatter_rows([product(logits_half, word_half)])
    back_mlm_g = jnp.sum(back_rows * mlm_hat, 0)
    back_mlm_lb = jnp.sum(back_rows, 0)
    dense_half = to_half(
        norm_backward(back_rows, pieces["mlm_g"], mlm_hat, mlm_inverse) * gelu_slope(dense)
    )
    back_mlm = transpose_times(dense_half, picked)
    back_picked = product(dense_half, head[:E])
    back_final = lax.dot_general(
        pick.astype(jnp.float32), back_picked, (((0,), (0,)), ((), ())), precision=PRECISE
    )

    firsts = jnp.concatenate([final_half[0:1], final_half[BUCKET : BUCKET + 1]], 0)
    pooled = jnp.tanh(times_transpose(firsts, head[E : E + D]) + pieces["pool_b"])
    classifier = pieces["cls"].reshape(2, D)
    classes = jnp.sum(pooled[:, None] * classifier[None], -1)
    class_top = jnp.max(classes, -1, keepdims=True)
    class_powers = jnp.exp(classes - class_top)
    class_totals = jnp.sum(class_powers, -1, keepdims=True)
    class_onehot = (jnp.arange(2, dtype=jnp.int32)[None, :] == sop_labels[:, None]).astype(
        jnp.float32
    )
    present = jnp.stack([jnp.float32(1.0), two.astype(jnp.float32)])
    sop_sum = jnp.sum(
        (jnp.log(class_totals[:, 0]) + class_top[:, 0] - jnp.sum(classes * class_onehot, -1))
        * present
    )
    back_classes = (class_powers / class_totals - class_onehot) * (present * scales[1])[:, None]
    back_cls = jnp.sum(back_classes[:, :, None] * pooled[:, None], 0)
    back_pooled = jnp.sum(back_classes[:, :, None] * classifier[None], 1)
    pre_half = to_half(back_pooled * (1.0 - pooled * pooled))
    back_pool = transpose_times(pre_half, firsts)
    back_firsts = product(pre_half, head[E : E + D])
    row_index = jnp.arange(ROWS, dtype=jnp.int32)[:, None]
    back_final = (
        back_final
        + jnp.where(row_index == 0, back_firsts[0:1], 0.0)
        + jnp.where(row_index == BUCKET, back_firsts[1:2], 0.0)
    )

    back_hidden, back = lax.scan(
        lambda up, k: layer_backward(up, k, wide, tall, pieces), back_final, kept, reverse=True
    )

    upstream_half = to_half(back_hidden)
    back_normed = times_transpose(upstream_half, head[E + D :])
    back_proj = transpose_times(normed_half, upstream_half)
    back_embedded = norm_backward(back_normed, pieces["emb_g"], embed_hat, embed_inverse)
    (all_back,) = gather_rows([to_half(back_embedded)])
    back_word = back_word_head + transpose_times(select, all_back)
    places = position_table.shape[0]
    by_device = all_back.reshape(devices, ROWS, E)
    folded = by_device[:, :BUCKET].astype(jnp.float32) + jnp.where(
        all_seconds[:, None, None], by_device[:, BUCKET:].astype(jnp.float32), 0.0
    )
    rest = jnp.where(all_seconds[:, None, None], 0.0, by_device[:, BUCKET:].astype(jnp.float32))
    all_place = jnp.concatenate([jnp.sum(folded, 0), jnp.sum(rest, 0)], 0)
    all_place = jnp.pad(all_place, ((0, places * devices - ROWS), (0, 0)))
    back_place = lax.dynamic_slice(all_place, (own * places, 0), (places, E))

    def long(x):
        return x.reshape(-1, x.shape[-1])

    joint_all, branch_all = long(back["joint_half"]), long(back["branch_half"])
    inner_all, outer_all = long(back["inner_half"]), long(back["outer_half"])
    back_wide = jnp.concatenate(
        [
            transpose_times(joint_all, long(kept["hidden_half"])),
            transpose_times(branch_all, long(kept["mixed"])),
            transpose_times(inner_all, long(kept["middle_half"])),
        ],
        0,
    )
    back_tall = transpose_times(long(kept["active"]), outer_all)
    back_head = jnp.concatenate([back_mlm, back_pool, back_proj], 0)
    sum_wide, sum_tall, sum_head = scatter_rows([back_wide, back_tall, back_head])

    joint_sum = column_sum(joint_all)
    norms = jnp.sum(back["norms"], 0)
    kind_one = jnp.sum(jnp.where(token_kind[:, None] == 1, back_embedded, 0.0), 0)
    kind_zero = jnp.sum(jnp.where(token_kind[:, None] == 0, back_embedded, 0.0), 0)
    vector_grad = join_vectors(
        {
            "proj_b": column_sum(upstream_half),
            "q_b": joint_sum[:D],
            "v_b": joint_sum[2 * D :],
            "o_b": column_sum(branch_all),
            "ln1_g": norms[0],
            "ln1_b": norms[1],
            "ffo_b": column_sum(outer_all),
            "ln2_g": norms[2],
            "ln2_b": norms[3],
            "pool_b": column_sum(pre_half),
            "cls": back_cls,
            "ff_b": column_sum(inner_all),
            "emb_g": jnp.sum(back_normed * embed_hat, 0),
            "emb_b": jnp.sum(back_normed, 0),
            "mlm_b": column_sum(dense_half),
            "mlm_g": back_mlm_g,
            "mlm_lb": back_mlm_lb,
            "types": jnp.concatenate([kind_zero, kind_one]),
        }
    )
    shards = (back_word, back_place, sum_head.T, back_decoder, sum_wide.T, sum_tall)
    local_squares = jnp.sum(jnp.stack([jnp.sum(s * s) for s in shards]))
    reduced, sop_total, squares = lax.psum((vector_grad, sop_sum, local_squares), AXES)
    grad_norm = jnp.sqrt(squares + jnp.sum(reduced * reduced))
    factor = jnp.minimum(1.0, CLIP_NORM / (grad_norm + NORM_EPSILON))
    updates = []
    for weight, gradient, first, second, rate in (
        (word_table, shards[0], word_first, word_second, LEARN_RATE),
        (position_table, shards[1], position_first, position_second, LEARN_RATE),
        (head_weights, shards[2], head_first, head_second, LEARN_RATE),
        (decoder_bias, shards[3], decoder_first, decoder_second, LEARN_RATE),
        (layer_wide, shards[4], wide_first, wide_second, LEARN_RATE),
        (layer_tall, shards[5], tall_first, tall_second, LEARN_RATE),
        (vectors, reduced, vector_first, vector_second, SMALL_RATE),
    ):
        updates.extend(adam_update(weight, factor * gradient, first, second, rate))
    return (*updates, mlm_sum, mlm_count, sop_total, sop_count, grad_norm)


def solution(mesh):
    rows = P(AXES, None)
    columns = P(None, AXES)
    flat = P(AXES)
    whole = P()
    return jax.shard_map(
        local,
        mesh=mesh,
        in_specs=(rows, rows, columns, flat, columns, rows, whole)
        + (rows, rows) * 2
        + (columns, columns, flat, flat, columns, columns, rows, rows, whole, whole)
        + (flat,) * 5,
        out_specs=(rows,) * 6
        + (columns,) * 3
        + (flat,) * 3
        + (columns,) * 3
        + (rows,) * 3
        + (whole,) * 8,
        check_vma=False,
    )
```

```python
import functools

import jax
import jax.numpy as jnp
from jax import lax
from jax.experimental import pallas as pl
from jax.experimental.pallas import tpu as pltpu
from jax.sharding import PartitionSpec as P

D = 768
HEADS = 12
HEAD_DIM = 64
FF = 3072
E = 128
LAYERS = 4
STEP = 10
BUCKET = 128
ROWS = 2 * BUCKET

PRECISE = lax.Precision.HIGHEST
EPSILON = 1e-06
LEARN_RATE = 0.1
SMALL_RATE = 0.5
BETA_ONE = 0.9
BETA_TWO = 0.999
ADAM_EPSILON = 1e-08
WEIGHT_DECAY = 0.01
CLIP_NORM = 0.005
NORM_EPSILON = 1e-06
MASKED = -1e30
SCALE = HEAD_DIM ** (-0.5)
AXES = ("dp", "fsdp")


def layout():
    return [
        ("proj_b", D),
        ("q_b", D),
        ("v_b", D),
        ("o_b", D),
        ("ln1_g", D),
        ("ln1_b", D),
        ("ffo_b", D),
        ("ln2_g", D),
        ("ln2_b", D),
        ("pool_b", D),
        ("cls", 2 * D),
        ("ff_b", FF),
        ("emb_g", E),
        ("emb_b", E),
        ("mlm_b", E),
        ("mlm_g", E),
        ("mlm_lb", E),
        ("types", 2 * E),
    ]


def split_vectors(vectors):
    pieces = {}
    offset = 0
    for member, length in layout():
        pieces[member] = vectors[offset : offset + length]
        offset += length
    return pieces


def join_vectors(gradients):
    return jnp.concatenate([gradients[member].reshape(-1) for member, length in layout()])


def to_half(x):
    return x.astype(jnp.bfloat16)


def product(a, b):
    return jnp.dot(a, b, preferred_element_type=jnp.float32)


def times_transpose(a, b):
    return lax.dot_general(a, b, (((1,), (1,)), ((), ())), preferred_element_type=jnp.float32)


def transpose_times(a, b):
    return lax.dot_general(a, b, (((0,), (0,)), ((), ())), preferred_element_type=jnp.float32)


def column_sum(x):
    return jnp.sum(x.astype(jnp.float32), 0)


def norm_forward(x):
    centre = x - jnp.mean(x, -1, keepdims=True)
    inverse = lax.rsqrt(jnp.mean(centre * centre, -1, keepdims=True) + EPSILON)
    return centre * inverse, inverse


def norm_backward(upstream, factor, hat, inverse):
    scaled = upstream * factor
    return inverse * (
        scaled
        - jnp.mean(scaled, -1, keepdims=True)
        - hat * jnp.mean(scaled * hat, -1, keepdims=True)
    )


GELU_A = 0.7978845608028654
GELU_B = 0.044715


def gelu_tanh(x):
    return 0.5 * x * (1.0 + jnp.tanh(GELU_A * (x + GELU_B * x * x * x)))


def gelu_slope(x):
    bend = jnp.tanh(GELU_A * (x + GELU_B * x * x * x))
    return 0.5 * (1.0 + bend) + 0.5 * x * (1.0 - bend * bend) * GELU_A * (
        1.0 + 3.0 * GELU_B * x * x
    )


def row_layout(lengths):
    row_index = jnp.arange(ROWS, dtype=jnp.int32)
    second = (row_index >= BUCKET) & (lengths[1] > 0)
    seq_id = second.astype(jnp.int32)
    position = row_index - BUCKET * seq_id
    own_length = jnp.where(second, lengths[1], lengths[0])
    is_live = position < own_length
    token_kind = (position >= own_length // 2).astype(jnp.int32)
    allowed = (seq_id[:, None] == seq_id[None, :]) & is_live[None, :]
    return (token_kind, allowed)


MESH_ID = pl.DeviceIdType.MESH
VMEM_SPACE = pltpu.VMEM
VMEM_ASK = 60 * 1024 * 1024


def greet(peers):
    barrier = pltpu.get_barrier_semaphore()
    count = 0
    for present, who in peers:
        if present is None:
            pl.semaphore_signal(barrier, inc=1, device_id=who, device_id_type=MESH_ID)
            count = count + 1
        else:

            @pl.when(present)
            def _(who=who):
                pl.semaphore_signal(barrier, inc=1, device_id=who, device_id_type=MESH_ID)

            count = count + present.astype(jnp.int32)
    pl.semaphore_wait(barrier, count)


def maybe(condition, action):
    if condition is None:
        action()
    else:
        pl.when(condition)(action)


def remote(source, target, send, receive, who):
    return pltpu.make_async_remote_copy(
        src_ref=source,
        dst_ref=target,
        send_sem=send,
        recv_sem=receive,
        device_id=who,
        device_id_type=MESH_ID,
    )


def small_gather_kernel(count, planes, width, *refs):
    ins, outs = refs[:count], refs[count : 2 * count]
    send_z, recv_z, send_f, recv_f = refs[2 * count :]
    z, f = lax.axis_index("dp"), lax.axis_index("fsdp")
    line = [(lax.rem(z + d, planes), f) for d in range(1, planes)]
    plane = [(z, lax.rem(f + d, width)) for d in range(1, width)]
    greet([(None, who) for who in line + plane])
    first = [
        remote(ins[i], outs[i].at[z, f], send_z.at[i, d], recv_z.at[i, d], who)
        for d, who in enumerate(line)
        for i in range(count)
    ]
    for copy in first:
        copy.start()
    for i in range(count):
        outs[i][z, f] = ins[i][...]
    for copy in first:
        copy.wait_recv()
    second = [
        remote(outs[i].at[:, f], outs[i].at[:, f], send_f.at[i, d], recv_f.at[i, d], who)
        for d, who in enumerate(plane)
        for i in range(count)
    ]
    for copy in second:
        copy.start()
    for d in range(1, width):
        other = lax.rem(f - d + width, width)
        for i in range(count):
            remote(
                outs[i].at[:, other],
                outs[i].at[:, other],
                send_f.at[i, d - 1],
                recv_f.at[i, d - 1],
                (z, f),
            ).wait_recv()
    for copy in first + second:
        copy.wait_send()


def small_gather(arrays, mesh_shape, identity):
    planes, width = mesh_shape
    count = len(arrays)
    return pl.pallas_call(
        functools.partial(small_gather_kernel, count, planes, width),
        out_shape=[
            jax.ShapeDtypeStruct((planes, width, *a.shape), a.dtype) for a in arrays
        ],
        in_specs=[pl.BlockSpec(memory_space=VMEM_SPACE)] * count,
        out_specs=[pl.BlockSpec(memory_space=VMEM_SPACE)] * count,
        scratch_shapes=[
            pltpu.SemaphoreType.DMA((count, planes)),
            pltpu.SemaphoreType.DMA((count, planes)),
            pltpu.SemaphoreType.DMA((count, width)),
            pltpu.SemaphoreType.DMA((count, width)),
        ],
        compiler_params=pltpu.CompilerParams(
            collective_id=identity, has_side_effects=True, vmem_limit_bytes=VMEM_ASK
        ),
    )(*arrays)


def small_scatter_kernel(planes, width, x, out, first_in, middle, second_in, *sems):
    send_f, recv_f, send_z, recv_z = sems
    z, f = lax.axis_index("dp"), lax.axis_index("fsdp")
    line = [(lax.rem(z + d, planes), f) for d in range(1, planes)]
    plane = [(z, lax.rem(f + d, width)) for d in range(1, width)]
    greet([(None, who) for who in line + plane])
    first = [
        remote(x.at[:, who[1]], first_in.at[d], send_f.at[d], recv_f.at[d], who)
        for d, who in enumerate(plane)
    ]
    for copy in first:
        copy.start()
    total = x[:, f]
    for d, copy in enumerate(first):
        copy.wait_recv()
        total = total + first_in[d]
    middle[...] = total
    second = [
        remote(middle.at[who[0]], second_in.at[d], send_z.at[d], recv_z.at[d], who)
        for d, who in enumerate(line)
    ]
    for copy in second:
        copy.start()
    total = middle[z]
    for d, copy in enumerate(second):
        copy.wait_recv()
        total = total + second_in[d]
    out[...] = total
    for copy in first + second:
        copy.wait_send()


def small_scatter(x, mesh_shape, identity):
    planes, width = mesh_shape
    block = x.shape[2:]
    return pl.pallas_call(
        functools.partial(small_scatter_kernel, planes, width),
        out_shape=jax.ShapeDtypeStruct(block, x.dtype),
        in_specs=[pl.BlockSpec(memory_space=VMEM_SPACE)],
        out_specs=pl.BlockSpec(memory_space=VMEM_SPACE),
        scratch_shapes=[
            VMEM_SPACE((width - 1, planes, *block), x.dtype),
            VMEM_SPACE((planes, *block), x.dtype),
            VMEM_SPACE((planes - 1, *block), x.dtype),
            pltpu.SemaphoreType.DMA((width - 1,)),
            pltpu.SemaphoreType.DMA((width - 1,)),
            pltpu.SemaphoreType.DMA((planes - 1,)),
            pltpu.SemaphoreType.DMA((planes - 1,)),
        ],
        compiler_params=pltpu.CompilerParams(
            collective_id=identity, has_side_effects=True, vmem_limit_bytes=VMEM_ASK
        ),
    )(x)


OWN, ACROSS_X, ACROSS_Y, DIAGONAL = 0, 1, 2, 3


def cuts_of(rows):
    tail = max(32, round(rows * 0.22 / 32) * 32)
    head = rows - tail
    return ((0, head), (head, rows))


def half_of(span, which):
    low, high = span
    middle = (low + high) // 2
    return (low, middle) if which == 0 else (middle, high)


def places():
    z, f = lax.axis_index("dp"), lax.axis_index("fsdp")
    q, c = f // 2, lax.rem(f, 2)
    qx = q + 1 - 2 * lax.rem(q, 2)
    qy = lax.rem(q + 2, 4)
    qd = qx + qy - q
    return z, c, (q, qx, qy, qd)


def big_gather_kernel(planes, rows, members, x, *refs):
    outs = refs[: len(members)]
    buf, out_sem, send, recv, side_send, side_recv = refs[len(members) :]
    z, c, cols = places()
    cuts = cuts_of(rows)
    at_x, at_y, mate = (z, cols[1] * 2 + c), (z, cols[2] * 2 + c), (z, cols[0] * 2 + 1 - c)
    above, below = z < planes - 1, z > 0
    up, down = (z + 1, cols[0] * 2 + c), (z - 1, cols[0] * 2 + c)
    greet([(None, at_x), (None, at_y), (None, mate), (above, up), (below, down)])
    sent = []

    def block(zs, col, core, span):
        return buf.at[zs, cols[col], core, pl.ds(span[0], span[1] - span[0])]

    def push(condition, zs, col, span, who, slot, receive, mine=False):
        def make():
            here = block(zs, col, c, span)
            source = x.at[pl.ds(span[0], span[1] - span[0])] if mine else here
            return remote(source, here, send.at[slot[0], zs, slot[1]], receive, who)

        maybe(condition, lambda: make().start())
        sent.append((condition, make))

    def await_block(zs, col, span, receive, core=None):
        here = block(zs, col, c if core is None else core, span)
        remote(here, here, send.at[0, 0, 0], receive, mate).wait_recv()

    def deliver(zs, col, core, span):
        for index, (out, (low, high)) in enumerate(zip(outs, members)):
            first, last = max(low, span[0]), min(high, span[1])
            if first < last:
                pltpu.make_async_copy(
                    buf.at[zs, cols[col], core, pl.ds(first, last - first)],
                    out.at[zs, cols[col], core, pl.ds(first - low, last - first)],
                    out_sem.at[index],
                ).start()

    def share(condition, part, zs, col, span, kind, mine=False):
        def make():
            here = block(zs, col, c, span)
            source = x.at[pl.ds(span[0], span[1] - span[0])] if mine else here
            return remote(
                source, here, side_send.at[part, zs, kind], side_recv.at[part, zs, kind], mate
            )

        def action():
            make().start()
            if not mine:
                deliver(zs, col, c, span)

        maybe(condition, action)
        sent.append((condition, make))
        shared.append((condition, part, zs, col, span, kind))

    shared = []
    whole = [cuts[0], cuts[1]]
    for part in (1, 0):
        push(None, z, OWN, whole[part], at_x, (part, 0), recv.at[part, z, ACROSS_X], True)
        push(None, z, OWN, whole[part], at_y, (part, 1), recv.at[part, z, ACROSS_Y], True)
    for part in (0, 1):
        push(above, z, OWN, whole[part], up, (part, 2), recv.at[part, z, OWN], True)
        push(below, z, OWN, whole[part], down, (part, 3), recv.at[part, z, OWN], True)
    for part in (0, 1):
        share(None, part, z, OWN, whole[part], 0, True)
    own_copy = pltpu.make_async_copy(x, buf.at[z, cols[0], c], out_sem.at[len(members)])
    own_copy.start()

    def turn(condition, part, zs):
        span = whole[part]
        for col, which, who, slot in ((ACROSS_X, 1, at_y, 4), (ACROSS_Y, 0, at_x, 5)):
            maybe(
                condition,
                lambda col=col: await_block(zs, col, span, recv.at[part, zs, col]),
            )
            push(condition, zs, col, half_of(span, which), who, (part, slot), recv.at[part, zs, 4 + which])
            if part == 1:
                push(above, zs, col, span, up, (1, 4 + 2 * col), recv.at[1, zs, col])
                push(below, zs, col, span, down, (1, 5 + 2 * col), recv.at[1, zs, col])
            share(condition, part, zs, col, span, col)

    turn(None, 1, z)
    turn(None, 0, z)
    for which in (0, 1):
        await_block(z, DIAGONAL, half_of(whole[1], which), recv.at[1, z, 4 + which])
    push(above, z, DIAGONAL, whole[1], up, (1, 10), recv.at[1, z, DIAGONAL])
    push(below, z, DIAGONAL, whole[1], down, (1, 11), recv.at[1, z, DIAGONAL])
    share(None, 1, z, DIAGONAL, whole[1], 3)

    def settle(upto):
        while len(shared) > upto:
            condition, part, zs, col, span, kind = shared.pop(0)

            def action():
                await_block(zs, col, span, side_recv.at[part, zs, kind], 1 - c)
                deliver(zs, col, 1 - c, span)

            maybe(condition, action)

    for step in range(1, planes):
        ways = ((z - step >= 0, z - step, above, up), (z + step < planes, z + step, below, down))
        for valid, zs, further, onward in ways:
            go = jnp.logical_and(valid, further)
            pl.when(valid)(
                lambda zs=zs: await_block(zs, OWN, whole[0], recv.at[0, zs, OWN])
            )
            push(go, zs, OWN, whole[0], onward, (0, 2), recv.at[0, zs, OWN])
            push(valid, zs, OWN, whole[0], at_x, (0, 0), recv.at[0, zs, ACROSS_X])
            push(valid, zs, OWN, whole[0], at_y, (0, 1), recv.at[0, zs, ACROSS_Y])
            share(valid, 0, zs, OWN, whole[0], 0)
        waiting = len(shared)
        for valid, zs, further, onward in ways:
            go = jnp.logical_and(valid, further)
            for col in (OWN, ACROSS_X, ACROSS_Y, DIAGONAL):
                pl.when(valid)(
                    lambda zs=zs, col=col: await_block(zs, col, whole[1], recv.at[1, zs, col])
                )
                push(go, zs, col, whole[1], onward, (1, col), recv.at[1, zs, col])
                share(valid, 1, zs, col, whole[1], col)
        for valid, zs, further, onward in ways:
            turn(valid, 0, zs)
        settle(8)
    own_copy.wait()
    deliver(z, OWN, c, (0, rows))
    everywhere = [(None, z)] + [
        (valid, zs)
        for step in range(1, planes)
        for valid, zs in ((z - step >= 0, z - step), (z + step < planes, z + step))
    ]
    for condition, zs in everywhere:
        for which in (0, 1):
            span = half_of(whole[0], which)
            maybe(
                condition,
                lambda zs=zs, which=which, span=span: await_block(
                    zs, DIAGONAL, span, recv.at[0, zs, 4 + which]
                ),
            )
            share(condition, 0, zs, DIAGONAL, span, 3 + which)
    settle(0)
    for condition, make in sent:
        maybe(condition, lambda make=make: make().wait_send())
    for index, (out, (low, high)) in enumerate(zip(outs, members)):
        pltpu.make_async_copy(
            buf.at[:, :, :, pl.ds(low, high - low)], out, out_sem.at[index]
        ).wait()


def big_gather(x, heights, mesh_shape, identity):
    planes, width = mesh_shape
    rows, columns = x.shape
    members, low = [], 0
    for height in heights:
        members.append((low, low + height))
        low += height
    outs = pl.pallas_call(
        functools.partial(big_gather_kernel, planes, rows, tuple(members)),
        out_shape=[
            jax.ShapeDtypeStruct((planes, width // 2, 2, height, columns), x.dtype)
            for height in heights
        ],
        in_specs=[pl.BlockSpec(memory_space=VMEM_SPACE)],
        out_specs=[pl.BlockSpec(memory_space=pl.ANY)] * len(heights),
        scratch_shapes=[
            VMEM_SPACE((planes, width // 2, 2, rows, columns), x.dtype),
            pltpu.SemaphoreType.DMA((len(heights) + 1,)),
            pltpu.SemaphoreType.DMA((2, planes, 12)),
            pltpu.SemaphoreType.DMA((2, planes, 6)),
            pltpu.SemaphoreType.DMA((2, planes, 5)),
            pltpu.SemaphoreType.DMA((2, planes, 5)),
        ],
        compiler_params=pltpu.CompilerParams(
            collective_id=identity, has_side_effects=True, vmem_limit_bytes=VMEM_ASK
        ),
    )(x)
    return [out.reshape(-1, columns) for out in outs]


def accumulate(target, sources, height):
    step = 32

    def body(i, unused):
        rows = pl.ds(pl.multiple_of(i * step, step), step)
        total = sources[0][rows].astype(jnp.float32)
        for source in sources[1:]:
            total = total + source[rows].astype(jnp.float32)
        target[rows] = total.astype(target.dtype)
        return unused

    lax.fori_loop(0, height // step, body, 0)


def big_scatter_kernel(planes, rows, members, *refs):
    count = len(members)
    grads, out = refs[:count], refs[count]
    own, side, half_in, full_in, line_in, tail_line, tail_half, tail_full = refs[
        count + 1 : count + 9
    ]
    load, side_send, side_recv, send, recv, tail_send, tail_recv = refs[count + 9 :]
    z, c, cols = places()
    cuts = cuts_of(rows)
    at_x, at_y, mate = (z, cols[1] * 2 + c), (z, cols[2] * 2 + c), (z, cols[0] * 2 + 1 - c)
    above, below = z < planes - 1, z > 0
    up, down = (z + 1, cols[0] * 2 + c), (z - 1, cols[0] * 2 + c)
    greet([(None, at_x), (None, at_y), (None, mate), (above, up), (below, down)])
    sent = []

    def push(condition, make):
        maybe(condition, lambda: make().start())
        sent.append((condition, make))

    def piece(ref, span):
        return ref.at[pl.ds(span[0], span[1] - span[0])]

    order = (DIAGONAL, ACROSS_X, ACROSS_Y, OWN)
    loads = {}
    for col in order:
        for a, (low, high) in enumerate(members):
            copy = pltpu.make_async_copy(
                grads[a].at[:, cols[col], c],
                own.at[:, col, pl.ds(low, high - low)],
                load.at[col, a],
            )
            copy.start()

            def make(col=col, a=a, low=low, high=high):
                return remote(
                    grads[a].at[:, cols[col], 1 - c],
                    side.at[:, col, pl.ds(low, high - low)],
                    side_send.at[col, a],
                    side_recv.at[col, a],
                    mate,
                )

            push(None, make)
            loads[col, a] = (copy, make)

    def merge(col):
        for a in range(count):
            copy, make = loads[col, a]
            copy.wait()
            make().wait_recv()

        def body(zt, unused):
            accumulate(own.at[zt, col], [own.at[zt, col], side.at[zt, col]], rows)
            return unused

        lax.fori_loop(0, planes, body, 0)

    targets = []
    for distance in range(planes - 1, 0, -1):
        targets.append((z + distance < planes, z + distance, 0))
        targets.append((z - distance >= 0, z - distance, 1))
    targets.append((None, z, 2))
    head, tail = cuts
    height, tail_height = head[1] - head[0], tail[1] - tail[0]

    def half_message(zt, which):
        return remote(
            piece(own.at[zt, DIAGONAL], half_of(head, which)),
            half_in.at[which, zt],
            send.at[0, which, zt],
            recv.at[0, which, zt],
            (at_x, at_y)[which],
        )

    def full_message(zt, which):
        return remote(
            piece(own.at[zt, (ACROSS_X, ACROSS_Y)[which]], head),
            full_in.at[which, zt],
            send.at[1, which, zt],
            recv.at[1, which, zt],
            (at_x, at_y)[which],
        )

    def line_message(zt, way):
        return remote(
            piece(own.at[zt, OWN], head),
            line_in.at[way, zt],
            send.at[2, way, zt],
            recv.at[2, way, zt],
            (up, down)[way],
        )

    def tail_message(zt, way):
        return remote(
            own.at[zt, :, pl.ds(tail[0], tail_height)],
            tail_line.at[way, zt],
            tail_send.at[way, zt],
            tail_recv.at[way, zt],
            (up, down)[way],
        )

    merge(DIAGONAL)
    for valid, zt, unused in targets:
        for which in (0, 1):
            push(valid, functools.partial(half_message, zt, which))
    merge(ACROSS_X)
    merge(ACROSS_Y)

    def second(valid, zt):
        def add():
            for which, col in ((1, ACROSS_X), (0, ACROSS_Y)):
                half_message(zt, which).wait_recv()
                span = half_of(head, which)
                target = piece(own.at[zt, col], span)
                accumulate(target, [target, half_in.at[which, zt]], height // 2)

        maybe(valid, add)
        for which in (0, 1):
            push(valid, functools.partial(full_message, zt, which))

    def tail_add(zt, way):
        tail_message(zt, way).wait_recv()
        for col in range(4):
            target = piece(own.at[zt, col], tail)
            accumulate(target, [target, tail_line.at[way, zt, col]], tail_height)

    def tail_step(valid, zt, way):
        behind = (below, above)[way]
        pl.when(jnp.logical_and(valid, behind))(lambda: tail_add(zt, way))
        push(valid, functools.partial(tail_message, zt, way))

    second(*targets[0][:2])
    second(*targets[1][:2])
    merge(OWN)
    for number in range(2, len(targets)):
        if number - 2 < len(targets) - 1:
            tail_step(*targets[number - 2])
        second(*targets[number][:2])
    for number in range(len(targets) - 2, len(targets) - 1):
        tail_step(*targets[number])

    def third(valid, zt, way):
        def add():
            for which in (0, 1):
                full_message(zt, which).wait_recv()
            base = [piece(own.at[zt, OWN], head), full_in.at[0, zt], full_in.at[1, zt]]
            behind = (below, above)[way]

            @pl.when(behind)
            def _():
                line_message(zt, way).wait_recv()
                accumulate(base[0], base + [line_in.at[way, zt]], height)

            @pl.when(jnp.logical_not(behind))
            def _():
                accumulate(base[0], base, height)

        pl.when(valid)(add)
        push(valid, functools.partial(line_message, zt, way))

    half_tail = tail_height // 2

    def tail_half_message(which):
        return remote(
            piece(own.at[z, DIAGONAL], half_of(tail, which)),
            tail_half.at[which],
            tail_send.at[2, which],
            tail_recv.at[2, which],
            (at_x, at_y)[which],
        )

    def tail_full_message(which):
        return remote(
            piece(own.at[z, (ACROSS_X, ACROSS_Y)[which]], tail),
            tail_full.at[which],
            tail_send.at[3, which],
            tail_recv.at[3, which],
            (at_x, at_y)[which],
        )

    for number, target in enumerate(targets[:-1]):
        third(*target)
        if number == len(targets) - 3:
            pl.when(below)(lambda: tail_add(z, 0))
            pl.when(above)(lambda: tail_add(z, 1))
            for which in (0, 1):
                push(None, functools.partial(tail_half_message, which))
    for which, col in ((1, ACROSS_X), (0, ACROSS_Y)):
        tail_half_message(which).wait_recv()
        target = piece(own.at[z, col], half_of(tail, which))
        accumulate(target, [target, tail_half.at[which]], half_tail)
    for which in (0, 1):
        push(None, functools.partial(tail_full_message, which))
    for which in (0, 1):
        full_message(z, which).wait_recv()
    goal = piece(out, head)
    accumulate(goal, [piece(own.at[z, OWN], head), full_in.at[0, z], full_in.at[1, z]], height)
    for present, way in ((below, 0), (above, 1)):

        def add(way=way):
            line_message(z, way).wait_recv()
            accumulate(goal, [goal, line_in.at[way, z]], height)

        pl.when(present)(add)
    for which in (0, 1):
        tail_full_message(which).wait_recv()
    accumulate(
        piece(out, tail),
        [piece(own.at[z, OWN], tail), tail_full.at[0], tail_full.at[1]],
        tail_height,
    )
    for condition, make in sent:
        maybe(condition, lambda make=make: make().wait_send())


def big_scatter(arrays, mesh_shape, identity):
    planes, width = mesh_shape
    columns = arrays[0].shape[1]
    members, low, views = [], 0, []
    for a in arrays:
        height = a.shape[0] // (planes * width)
        members.append((low, low + height))
        low += height
        views.append(a.reshape(planes, width // 2, 2, height, columns))
    rows = low
    head, tail = (high - low for low, high in cuts_of(rows))
    half = arrays[0].dtype
    return pl.pallas_call(
        functools.partial(big_scatter_kernel, planes, rows, tuple(members)),
        out_shape=jax.ShapeDtypeStruct((rows, columns), jnp.float32),
        in_specs=[pl.BlockSpec(memory_space=pl.ANY)] * len(arrays),
        out_specs=pl.BlockSpec(memory_space=VMEM_SPACE),
        scratch_shapes=[
            VMEM_SPACE((planes, 4, rows, columns), half),
            VMEM_SPACE((planes, 4, rows, columns), half),
            VMEM_SPACE((2, planes, head // 2, columns), half),
            VMEM_SPACE((2, planes, head, columns), half),
            VMEM_SPACE((2, planes, head, columns), half),
            VMEM_SPACE((2, planes, 4, tail, columns), half),
            VMEM_SPACE((2, tail // 2, columns), half),
            VMEM_SPACE((2, tail, columns), half),
            pltpu.SemaphoreType.DMA((4, len(arrays))),
            pltpu.SemaphoreType.DMA((4, len(arrays))),
            pltpu.SemaphoreType.DMA((4, len(arrays))),
            pltpu.SemaphoreType.DMA((3, 2, planes)),
            pltpu.SemaphoreType.DMA((3, 2, planes)),
            pltpu.SemaphoreType.DMA((4, planes)),
            pltpu.SemaphoreType.DMA((4, planes)),
        ],
        compiler_params=pltpu.CompilerParams(
            collective_id=identity, has_side_effects=True, vmem_limit_bytes=VMEM_ASK
        ),
    )(*views)


class Network:
    def __init__(self, mesh):
        self.shape = (mesh.shape["dp"], mesh.shape["fsdp"])
        self.devices = self.shape[0] * self.shape[1]
        self.kernels = self.shape[1] == 8
        self.calls = 0

    def identity(self):
        self.calls += 1
        return self.calls

    def gather_small(self, blocks):
        if not self.kernels:
            return [lax.all_gather(b, AXES) for b in blocks]
        gathered = small_gather(blocks, self.shape, self.identity())
        return [g.reshape(self.devices, *g.shape[2:]) for g in gathered]

    def scatter_small(self, blocks):
        if not self.kernels:
            return lax.psum_scatter(blocks, AXES, scatter_dimension=0)
        return small_scatter(
            blocks.reshape(*self.shape, *blocks.shape[1:]), self.shape, self.identity()
        )

    def gather(self, shards):
        if not self.kernels:
            return [lax.all_gather(s, AXES, axis=0, tiled=True) for s in shards]
        heights = tuple(s.shape[0] for s in shards)
        packed = jnp.concatenate(shards, 0) if len(shards) > 1 else shards[0]
        return big_gather(packed, heights, self.shape, self.identity())

    def scatter(self, partials):
        if not self.kernels:
            return [
                lax.psum_scatter(
                    p.astype(jnp.float32), AXES, scatter_dimension=0, tiled=True
                )
                for p in partials
            ]
        total = big_scatter(partials, self.shape, self.identity())
        out, low = [], 0
        for p in partials:
            height = p.shape[0] // self.devices
            out.append(total[low : low + height])
            low += height
        return out


def layer_forward(hidden, wide, tall, pieces, allowed):
    hidden_half = to_half(hidden)
    joint_bias = jnp.concatenate([pieces["q_b"], jnp.zeros_like(pieces["q_b"]), pieces["v_b"]])
    projected = to_half(times_transpose(hidden_half, wide[: 3 * D]) + joint_bias)
    heads = projected.reshape(ROWS, 3, HEADS, HEAD_DIM)
    queries, key_rows, values = (heads[:, 0], heads[:, 1], heads[:, 2])
    scores = (
        jnp.einsum("qhd,khd->hqk", queries, key_rows, preferred_element_type=jnp.float32) * SCALE
    )
    scores = jnp.where(allowed[None], scores, MASKED)
    powers = jnp.exp(scores - jnp.max(scores, -1, keepdims=True))
    weighting = powers / jnp.sum(powers, -1, keepdims=True)
    mixed = jnp.einsum(
        "hqk,khd->qhd", to_half(weighting), values, preferred_element_type=jnp.float32
    )
    mixed = to_half(mixed.reshape(ROWS, D))
    first_sum = hidden + times_transpose(mixed, wide[3 * D : 4 * D]) + pieces["o_b"]
    hat_one, inverse_one = norm_forward(first_sum)
    middle = hat_one * pieces["ln1_g"] + pieces["ln1_b"]
    middle_half = to_half(middle)
    inner = times_transpose(middle_half, wide[4 * D :]) + pieces["ff_b"]
    active = to_half(gelu_tanh(inner))
    second_sum = middle + product(active, tall) + pieces["ffo_b"]
    hat_two, inverse_two = norm_forward(second_sum)
    output = hat_two * pieces["ln2_g"] + pieces["ln2_b"]
    kept = {
        "hidden_half": hidden_half,
        "projected": projected,
        "weighting": weighting,
        "mixed": mixed,
        "hat_one": hat_one,
        "inverse_one": inverse_one,
        "middle_half": middle_half,
        "inner": inner,
        "active": active,
        "hat_two": hat_two,
        "inverse_two": inverse_two,
    }
    return (output, kept)


def layer_backward(upstream, kept, wide, tall, pieces):
    gain_two = jnp.sum(upstream * kept["hat_two"], 0)
    shift_two = jnp.sum(upstream, 0)
    back_second = norm_backward(upstream, pieces["ln2_g"], kept["hat_two"], kept["inverse_two"])
    outer_half = to_half(back_second)
    inner_half = to_half(times_transpose(outer_half, tall) * gelu_slope(kept["inner"]))
    back_middle = back_second + product(inner_half, wide[4 * D :])
    gain_one = jnp.sum(back_middle * kept["hat_one"], 0)
    shift_one = jnp.sum(back_middle, 0)
    back_first = norm_backward(back_middle, pieces["ln1_g"], kept["hat_one"], kept["inverse_one"])
    branch_half = to_half(back_first)
    back_mixed = to_half(product(branch_half, wide[3 * D : 4 * D])).reshape(ROWS, HEADS, HEAD_DIM)
    heads = kept["projected"].reshape(ROWS, 3, HEADS, HEAD_DIM)
    queries, key_rows, values = (heads[:, 0], heads[:, 1], heads[:, 2])
    weighting = kept["weighting"]
    back_soft = jnp.einsum("qhd,khd->hqk", back_mixed, values, preferred_element_type=jnp.float32)
    scores_half = to_half(
        weighting * (back_soft - jnp.sum(weighting * back_soft, -1, keepdims=True))
    )
    back_queries = (
        jnp.einsum("hqk,khd->qhd", scores_half, key_rows, preferred_element_type=jnp.float32)
        * SCALE
    )
    back_key_rows = (
        jnp.einsum("hqk,qhd->khd", scores_half, queries, preferred_element_type=jnp.float32) * SCALE
    )
    back_values = jnp.einsum(
        "hqk,qhd->khd", to_half(weighting), back_mixed, preferred_element_type=jnp.float32
    )
    joint_half = to_half(
        jnp.stack([back_queries, back_key_rows, back_values], 1).reshape(ROWS, 3 * D)
    )
    back_hidden = back_first + product(joint_half, wide[: 3 * D])
    out = {
        "joint_half": joint_half,
        "branch_half": branch_half,
        "inner_half": inner_half,
        "outer_half": outer_half,
        "norms": jnp.stack([gain_one, shift_one, gain_two, shift_two]),
    }
    return (back_hidden, out)


def adam_update(weight, gradient, first, second, rate):
    first = BETA_ONE * first + (1 - BETA_ONE) * gradient
    second = BETA_TWO * second + (1 - BETA_TWO) * gradient * gradient
    first_hat = first / (1 - BETA_ONE**STEP)
    second_hat = second / (1 - BETA_TWO**STEP)
    updated = weight - rate * (
        first_hat / (jnp.sqrt(second_hat) + ADAM_EPSILON) + WEIGHT_DECAY * weight
    )
    return (updated, first, second)


def local(
    mesh,
    word_table,
    position_table,
    head_weights,
    decoder_bias,
    layer_wide,
    layer_tall,
    vectors,
    word_first,
    word_second,
    position_first,
    position_second,
    head_first,
    head_second,
    decoder_first,
    decoder_second,
    wide_first,
    wide_second,
    tall_first,
    tall_second,
    vector_first,
    vector_second,
    token_ids,
    seq_lengths,
    mlm_rows,
    mlm_labels,
    sop_labels,
):
    network = Network(mesh)
    own = lax.axis_index(AXES)
    words = word_table.shape[0]
    slots = mlm_labels.shape[0]
    pieces = split_vectors(vectors)
    token_kind, allowed = row_layout(seq_lengths)

    facts = jnp.concatenate([token_ids, mlm_labels, seq_lengths])
    padded = -(-facts.shape[0] // 1024) * 1024
    facts = jnp.pad(facts, (0, padded - facts.shape[0])).reshape(-1, 128)
    places_own = to_half(position_table).astype(jnp.float32)
    all_facts, place = network.gather_small([facts, places_own])
    all_facts = all_facts.reshape(-1, padded)
    place = place.reshape(-1, E)
    devices = all_facts.shape[0]
    all_ids = all_facts[:, :ROWS].reshape(-1)
    all_labels = all_facts[:, ROWS : ROWS + slots].reshape(-1)
    all_seconds = all_facts[:, ROWS + slots + 1] > 0
    all_used = (all_labels >= 0).astype(jnp.float32)
    mlm_count = jnp.sum(all_used)
    sop_count = devices + jnp.sum(all_seconds.astype(jnp.float32))
    scales = (1.0 / mlm_count, 1.0 / sop_count)

    word_half = to_half(word_table)
    wide, tall, head = network.gather(
        [to_half(layer_wide).T, to_half(layer_tall), to_half(head_weights).T]
    )

    offset = own * words
    column = jnp.arange(words, dtype=jnp.int32)
    select = to_half((all_ids - offset)[:, None] == column[None, :])
    (found,) = network.scatter([to_half(product(select, word_half))])
    two = seq_lengths[1] > 0
    place = place[:ROWS]
    placed = jnp.concatenate([place[:BUCKET], jnp.where(two, place[:BUCKET], place[BUCKET:])], 0)
    types = pieces["types"].reshape(2, E)
    embedded = (
        found
        + placed
        + jnp.where(token_kind[:, None] == 0, types[0:1], types[1:2])
    )
    embed_hat, embed_inverse = norm_forward(embedded)
    normed_half = to_half(embed_hat * pieces["emb_g"] + pieces["emb_b"])
    hidden = product(normed_half, head[E + D :]) + pieces["proj_b"]

    final, kept = lax.scan(
        lambda h, unused: layer_forward(h, wide, tall, pieces, allowed),
        hidden,
        None,
        length=LAYERS,
    )

    final_half = to_half(final)
    pick = to_half(mlm_rows[:, None] == jnp.arange(ROWS, dtype=jnp.int32)[None, :])
    picked = to_half(product(pick, final_half))
    dense = times_transpose(picked, head[:E]) + pieces["mlm_b"]
    mlm_hat, mlm_inverse = norm_forward(gelu_tanh(dense))
    rows_half = to_half(mlm_hat * pieces["mlm_g"] + pieces["mlm_lb"])
    lifted = -(-slots // 16) * 16
    (all_rows,) = network.gather_small([jnp.pad(rows_half, ((0, lifted - slots), (0, 0)))])
    all_rows = all_rows[:, :slots].reshape(-1, E)
    logits = times_transpose(all_rows, word_half) + to_half(decoder_bias).astype(jnp.float32)
    onehot = ((all_labels - offset)[:, None] == column[None, :]).astype(jnp.float32)
    own_top = jnp.max(logits, -1)
    own_total = jnp.sum(jnp.exp(logits - own_top[:, None]), -1)
    own_target = jnp.sum(logits * onehot, -1)
    stats = jnp.concatenate([own_top, own_total, own_target])
    lifted = -(-stats.shape[0] // 1024) * 1024
    (stats,) = network.gather_small(
        [jnp.pad(stats, (0, lifted - stats.shape[0])).reshape(-1, 128)]
    )
    stats = stats.reshape(devices, lifted)[:, : 3 * devices * slots]
    stats = stats.reshape(devices, 3, devices * slots)
    top = jnp.max(stats[:, 0], 0)
    total = jnp.sum(stats[:, 1] * jnp.exp(stats[:, 0] - top[None]), 0)
    log_total = jnp.log(total) + top
    mlm_sum = jnp.sum((log_total - jnp.sum(stats[:, 2], 0)) * all_used)
    logits_half = to_half(
        (jnp.exp(logits - top[:, None]) / total[:, None] - onehot) * (all_used * scales[0])[:, None]
    )
    back_decoder = column_sum(logits_half)
    back_word_head = transpose_times(logits_half, all_rows)
    back_rows = network.scatter_small(
        product(logits_half, word_half).reshape(devices, slots, E)
    )
    back_mlm_g = jnp.sum(back_rows * mlm_hat, 0)
    back_mlm_lb = jnp.sum(back_rows, 0)
    dense_half = to_half(
        norm_backward(back_rows, pieces["mlm_g"], mlm_hat, mlm_inverse) * gelu_slope(dense)
    )
    back_mlm = transpose_times(dense_half, picked)
    back_picked = product(dense_half, head[:E])
    back_final = lax.dot_general(
        pick.astype(jnp.float32), back_picked, (((0,), (0,)), ((), ())), precision=PRECISE
    )

    firsts = jnp.concatenate([final_half[0:1], final_half[BUCKET : BUCKET + 1]], 0)
    pooled = jnp.tanh(times_transpose(firsts, head[E : E + D]) + pieces["pool_b"])
    classifier = pieces["cls"].reshape(2, D)
    classes = jnp.sum(pooled[:, None] * classifier[None], -1)
    class_top = jnp.max(classes, -1, keepdims=True)
    class_powers = jnp.exp(classes - class_top)
    class_totals = jnp.sum(class_powers, -1, keepdims=True)
    class_onehot = (jnp.arange(2, dtype=jnp.int32)[None, :] == sop_labels[:, None]).astype(
        jnp.float32
    )
    present = jnp.stack([jnp.float32(1.0), two.astype(jnp.float32)])
    sop_sum = jnp.sum(
        (jnp.log(class_totals[:, 0]) + class_top[:, 0] - jnp.sum(classes * class_onehot, -1))
        * present
    )
    back_classes = (class_powers / class_totals - class_onehot) * (present * scales[1])[:, None]
    back_cls = jnp.sum(back_classes[:, :, None] * pooled[:, None], 0)
    back_pooled = jnp.sum(back_classes[:, :, None] * classifier[None], 1)
    pre_half = to_half(back_pooled * (1.0 - pooled * pooled))
    back_pool = transpose_times(pre_half, firsts)
    back_firsts = product(pre_half, head[E : E + D])
    row_index = jnp.arange(ROWS, dtype=jnp.int32)[:, None]
    back_final = (
        back_final
        + jnp.where(row_index == 0, back_firsts[0:1], 0.0)
        + jnp.where(row_index == BUCKET, back_firsts[1:2], 0.0)
    )

    back_hidden, back = lax.scan(
        lambda up, k: layer_backward(up, k, wide, tall, pieces), back_final, kept, reverse=True
    )

    upstream_half = to_half(back_hidden)
    back_normed = times_transpose(upstream_half, head[E + D :])
    back_proj = transpose_times(normed_half, upstream_half)
    back_embedded = norm_backward(back_normed, pieces["emb_g"], embed_hat, embed_inverse)
    (all_back,) = network.gather([to_half(back_embedded)])
    back_word = back_word_head + transpose_times(select, all_back)
    places = position_table.shape[0]
    by_device = all_back.reshape(devices, ROWS, E)
    folded = by_device[:, :BUCKET].astype(jnp.float32) + jnp.where(
        all_seconds[:, None, None], by_device[:, BUCKET:].astype(jnp.float32), 0.0
    )
    rest = jnp.where(all_seconds[:, None, None], 0.0, by_device[:, BUCKET:].astype(jnp.float32))
    all_place = jnp.concatenate([jnp.sum(folded, 0), jnp.sum(rest, 0)], 0)
    all_place = jnp.pad(all_place, ((0, places * devices - ROWS), (0, 0)))
    back_place = lax.dynamic_slice(all_place, (own * places, 0), (places, E))

    def long(x):
        return x.reshape(-1, x.shape[-1])

    joint_all, branch_all = long(back["joint_half"]), long(back["branch_half"])
    inner_all, outer_all = long(back["inner_half"]), long(back["outer_half"])
    back_wide = jnp.concatenate(
        [
            to_half(transpose_times(joint_all, long(kept["hidden_half"]))),
            to_half(transpose_times(branch_all, long(kept["mixed"]))),
            to_half(transpose_times(inner_all, long(kept["middle_half"]))),
        ],
        0,
    )
    back_tall = to_half(transpose_times(long(kept["active"]), outer_all))
    back_head = to_half(jnp.concatenate([back_mlm, back_pool, back_proj], 0))
    sum_wide, sum_tall, sum_head = network.scatter([back_wide, back_tall, back_head])

    joint_sum = column_sum(joint_all)
    norms = jnp.sum(back["norms"], 0)
    kind_one = jnp.sum(jnp.where(token_kind[:, None] == 1, back_embedded, 0.0), 0)
    kind_zero = jnp.sum(jnp.where(token_kind[:, None] == 0, back_embedded, 0.0), 0)
    vector_grad = join_vectors(
        {
            "proj_b": column_sum(upstream_half),
            "q_b": joint_sum[:D],
            "v_b": joint_sum[2 * D :],
            "o_b": column_sum(branch_all),
            "ln1_g": norms[0],
            "ln1_b": norms[1],
            "ffo_b": column_sum(outer_all),
            "ln2_g": norms[2],
            "ln2_b": norms[3],
            "pool_b": column_sum(pre_half),
            "cls": back_cls,
            "ff_b": column_sum(inner_all),
            "emb_g": jnp.sum(back_normed * embed_hat, 0),
            "emb_b": jnp.sum(back_normed, 0),
            "mlm_b": column_sum(dense_half),
            "mlm_g": back_mlm_g,
            "mlm_lb": back_mlm_lb,
            "types": jnp.concatenate([kind_zero, kind_one]),
        }
    )
    shards = (back_word, back_place, sum_head.T, back_decoder, sum_wide.T, sum_tall)
    local_squares = jnp.sum(jnp.stack([jnp.sum(s * s) for s in shards]))
    total = vector_grad.shape[0]
    share = -(-total // (devices * 1024)) * 1024
    own_vector = network.scatter_small(
        jnp.pad(vector_grad, (0, devices * share - total)).reshape(devices, -1, 128)
    )
    scalars = jnp.stack([sop_sum, local_squares])
    scalars = jnp.pad(scalars, (0, 1024 - scalars.shape[0])).reshape(8, 128)
    (last,) = network.gather_small([jnp.concatenate([own_vector, scalars], 0)])
    reduced = last[:, : share // 128].reshape(-1)[:total]
    sop_total = jnp.sum(last[:, share // 128, 0])
    grad_norm = jnp.sqrt(jnp.sum(last[:, share // 128, 1]) + jnp.sum(reduced * reduced))
    factor = jnp.minimum(1.0, CLIP_NORM / (grad_norm + NORM_EPSILON))
    updates = []
    for weight, gradient, first, second, rate in (
        (word_table, shards[0], word_first, word_second, LEARN_RATE),
        (position_table, shards[1], position_first, position_second, LEARN_RATE),
        (head_weights, shards[2], head_first, head_second, LEARN_RATE),
        (decoder_bias, shards[3], decoder_first, decoder_second, LEARN_RATE),
        (layer_wide, shards[4], wide_first, wide_second, LEARN_RATE),
        (layer_tall, shards[5], tall_first, tall_second, LEARN_RATE),
        (vectors, reduced, vector_first, vector_second, SMALL_RATE),
    ):
        updates.extend(adam_update(weight, factor * gradient, first, second, rate))
    return (*updates, mlm_sum, mlm_count, sop_total, sop_count, grad_norm)


def solution(mesh):
    rows = P(AXES, None)
    columns = P(None, AXES)
    flat = P(AXES)
    whole = P()
    return jax.shard_map(
        functools.partial(local, mesh),
        mesh=mesh,
        in_specs=(rows, rows, columns, flat, columns, rows, whole)
        + (rows, rows) * 2
        + (columns, columns, flat, flat, columns, columns, rows, rows, whole, whole)
        + (flat,) * 5,
        out_specs=(rows,) * 6
        + (columns,) * 3
        + (flat,) * 3
        + (columns,) * 3
        + (rows,) * 3
        + (whole,) * 8,
        check_vma=False,
    )
```

```python
import functools

import jax
import jax.numpy as jnp
from jax import lax
from jax.experimental import pallas as pl
from jax.experimental.pallas import tpu as pltpu
from jax.sharding import PartitionSpec as P

D = 768
HEADS = 12
HEAD_DIM = 64
FF = 3072
E = 128
LAYERS = 4
STEP = 10
BUCKET = 128
ROWS = 2 * BUCKET

PRECISE = lax.Precision.HIGHEST
EPSILON = 1e-06
LEARN_RATE = 0.1
SMALL_RATE = 0.5
BETA_ONE = 0.9
BETA_TWO = 0.999
ADAM_EPSILON = 1e-08
WEIGHT_DECAY = 0.01
CLIP_NORM = 0.005
NORM_EPSILON = 1e-06
MASKED = -1e30
SCALE = HEAD_DIM ** (-0.5)
AXES = ("dp", "fsdp")


def layout():
    return [
        ("proj_b", D),
        ("q_b", D),
        ("v_b", D),
        ("o_b", D),
        ("ln1_g", D),
        ("ln1_b", D),
        ("ffo_b", D),
        ("ln2_g", D),
        ("ln2_b", D),
        ("pool_b", D),
        ("cls", 2 * D),
        ("ff_b", FF),
        ("emb_g", E),
        ("emb_b", E),
        ("mlm_b", E),
        ("mlm_g", E),
        ("mlm_lb", E),
        ("types", 2 * E),
    ]


def split_vectors(vectors):
    pieces = {}
    offset = 0
    for member, length in layout():
        pieces[member] = vectors[offset : offset + length]
        offset += length
    return pieces


def join_vectors(gradients):
    order = ("proj_b", "layer", "pool_b", "cls", "ff_b", "emb_g", "emb_b")
    order = order + ("mlm_b", "mlm_g", "mlm_lb", "types")
    return jnp.concatenate([gradients[member].reshape(-1) for member in order])


def to_half(x):
    return x.astype(jnp.bfloat16)


def product(a, b):
    return jnp.dot(a, b, preferred_element_type=jnp.float32)


def times_transpose(a, b):
    return lax.dot_general(a, b, (((1,), (1,)), ((), ())), preferred_element_type=jnp.float32)


def transpose_times(a, b):
    return lax.dot_general(a, b, (((0,), (0,)), ((), ())), preferred_element_type=jnp.float32)


def column_sum(x):
    return jnp.sum(x.astype(jnp.float32), 0)


def norm_forward(x):
    centre = x - jnp.mean(x, -1, keepdims=True)
    inverse = lax.rsqrt(jnp.mean(centre * centre, -1, keepdims=True) + EPSILON)
    return centre * inverse, inverse


def norm_backward(upstream, factor, hat, inverse):
    scaled = upstream * factor
    return inverse * (
        scaled
        - jnp.mean(scaled, -1, keepdims=True)
        - hat * jnp.mean(scaled * hat, -1, keepdims=True)
    )


GELU_A = 0.7978845608028654
GELU_B = 0.044715


def gelu_tanh(x):
    return 0.5 * x * (1.0 + jnp.tanh(GELU_A * (x + GELU_B * x * x * x)))


def gelu_slope(x):
    bend = jnp.tanh(GELU_A * (x + GELU_B * x * x * x))
    return 0.5 * (1.0 + bend) + 0.5 * x * (1.0 - bend * bend) * GELU_A * (
        1.0 + 3.0 * GELU_B * x * x
    )


def row_kind(lengths):
    row_index = jnp.arange(ROWS, dtype=jnp.int32)
    second = (row_index >= BUCKET) & (lengths[1] > 0)
    seq_id = second.astype(jnp.int32)
    position = row_index - BUCKET * seq_id
    own_length = jnp.where(second, lengths[1], lengths[0])
    token_kind = (position >= own_length // 2).astype(jnp.int32)
    return token_kind


MESH_ID = pl.DeviceIdType.MESH
VMEM_SPACE = pltpu.VMEM
VMEM_ASK = 60 * 1024 * 1024


def greet(peers):
    barrier = pltpu.get_barrier_semaphore()
    count = 0
    for present, who in peers:
        if present is None:
            pl.semaphore_signal(barrier, inc=1, device_id=who, device_id_type=MESH_ID)
            count = count + 1
        else:

            @pl.when(present)
            def _(who=who):
                pl.semaphore_signal(barrier, inc=1, device_id=who, device_id_type=MESH_ID)

            count = count + present.astype(jnp.int32)
    pl.semaphore_wait(barrier, count)


def maybe(condition, action):
    if condition is None:
        action()
    else:
        pl.when(condition)(action)


def remote(source, target, send, receive, who):
    return pltpu.make_async_remote_copy(
        src_ref=source,
        dst_ref=target,
        send_sem=send,
        recv_sem=receive,
        device_id=who,
        device_id_type=MESH_ID,
    )


def small_gather_kernel(count, planes, width, *refs):
    ins, outs = refs[:count], refs[count : 2 * count]
    send_z, recv_z, send_f, recv_f = refs[2 * count :]
    z, f = lax.axis_index("dp"), lax.axis_index("fsdp")
    line = [(lax.rem(z + d, planes), f) for d in range(1, planes)]
    plane = [(z, lax.rem(f + d, width)) for d in range(1, width)]
    greet([(None, who) for who in line + plane])
    first = [
        remote(ins[i], outs[i].at[z, f], send_z.at[i, d], recv_z.at[i, d], who)
        for d, who in enumerate(line)
        for i in range(count)
    ]
    for copy in first:
        copy.start()
    for i in range(count):
        outs[i][z, f] = ins[i][...]
    for copy in first:
        copy.wait_recv()
    second = [
        remote(outs[i].at[:, f], outs[i].at[:, f], send_f.at[i, d], recv_f.at[i, d], who)
        for d, who in enumerate(plane)
        for i in range(count)
    ]
    for copy in second:
        copy.start()
    for d in range(1, width):
        other = lax.rem(f - d + width, width)
        for i in range(count):
            remote(
                outs[i].at[:, other],
                outs[i].at[:, other],
                send_f.at[i, d - 1],
                recv_f.at[i, d - 1],
                (z, f),
            ).wait_recv()
    for copy in first + second:
        copy.wait_send()


def small_gather(arrays, mesh_shape, identity):
    planes, width = mesh_shape
    count = len(arrays)
    return pl.pallas_call(
        functools.partial(small_gather_kernel, count, planes, width),
        out_shape=[
            jax.ShapeDtypeStruct((planes, width, *a.shape), a.dtype) for a in arrays
        ],
        in_specs=[pl.BlockSpec(memory_space=VMEM_SPACE)] * count,
        out_specs=[pl.BlockSpec(memory_space=VMEM_SPACE)] * count,
        scratch_shapes=[
            pltpu.SemaphoreType.DMA((count, planes)),
            pltpu.SemaphoreType.DMA((count, planes)),
            pltpu.SemaphoreType.DMA((count, width)),
            pltpu.SemaphoreType.DMA((count, width)),
        ],
        compiler_params=pltpu.CompilerParams(
            collective_id=identity, has_side_effects=True, vmem_limit_bytes=VMEM_ASK
        ),
    )(*arrays)


def small_scatter_kernel(planes, width, x, out, first_in, middle, second_in, *sems):
    send_f, recv_f, send_z, recv_z = sems
    z, f = lax.axis_index("dp"), lax.axis_index("fsdp")
    line = [(lax.rem(z + d, planes), f) for d in range(1, planes)]
    plane = [(z, lax.rem(f + d, width)) for d in range(1, width)]
    greet([(None, who) for who in line + plane])
    first = [
        remote(x.at[:, who[1]], first_in.at[d], send_f.at[d], recv_f.at[d], who)
        for d, who in enumerate(plane)
    ]
    for copy in first:
        copy.start()
    total = x[:, f]
    for d, copy in enumerate(first):
        copy.wait_recv()
        total = total + first_in[d]
    middle[...] = total
    second = [
        remote(middle.at[who[0]], second_in.at[d], send_z.at[d], recv_z.at[d], who)
        for d, who in enumerate(line)
    ]
    for copy in second:
        copy.start()
    total = middle[z]
    for d, copy in enumerate(second):
        copy.wait_recv()
        total = total + second_in[d]
    out[...] = total
    for copy in first + second:
        copy.wait_send()


def small_scatter(x, mesh_shape, identity):
    planes, width = mesh_shape
    block = x.shape[2:]
    return pl.pallas_call(
        functools.partial(small_scatter_kernel, planes, width),
        out_shape=jax.ShapeDtypeStruct(block, x.dtype),
        in_specs=[pl.BlockSpec(memory_space=VMEM_SPACE)],
        out_specs=pl.BlockSpec(memory_space=VMEM_SPACE),
        scratch_shapes=[
            VMEM_SPACE((width - 1, planes, *block), x.dtype),
            VMEM_SPACE((planes, *block), x.dtype),
            VMEM_SPACE((planes - 1, *block), x.dtype),
            pltpu.SemaphoreType.DMA((width - 1,)),
            pltpu.SemaphoreType.DMA((width - 1,)),
            pltpu.SemaphoreType.DMA((planes - 1,)),
            pltpu.SemaphoreType.DMA((planes - 1,)),
        ],
        compiler_params=pltpu.CompilerParams(
            collective_id=identity, has_side_effects=True, vmem_limit_bytes=VMEM_ASK
        ),
    )(x)


OWN, ACROSS_X, ACROSS_Y, DIAGONAL = 0, 1, 2, 3


def cuts_of(rows):
    tail = max(32, round(rows * 0.22 / 32) * 32)
    head = rows - tail
    return ((0, head), (head, rows))


def half_of(span, which):
    low, high = span
    middle = (low + high) // 2
    return (low, middle) if which == 0 else (middle, high)


def places():
    z, f = lax.axis_index("dp"), lax.axis_index("fsdp")
    q, c = f // 2, lax.rem(f, 2)
    qx = q + 1 - 2 * lax.rem(q, 2)
    qy = lax.rem(q + 2, 4)
    qd = qx + qy - q
    return z, c, (q, qx, qy, qd)


def big_gather_kernel(planes, rows, members, x, *refs):
    outs = refs[: len(members)]
    buf, out_sem, send, recv, side_send, side_recv = refs[len(members) :]
    z, c, cols = places()
    cuts = cuts_of(rows)
    at_x, at_y, mate = (z, cols[1] * 2 + c), (z, cols[2] * 2 + c), (z, cols[0] * 2 + 1 - c)
    above, below = z < planes - 1, z > 0
    up, down = (z + 1, cols[0] * 2 + c), (z - 1, cols[0] * 2 + c)
    greet([(None, at_x), (None, at_y), (None, mate), (above, up), (below, down)])
    sent = []

    def block(zs, col, core, span):
        return buf.at[zs, cols[col], core, pl.ds(span[0], span[1] - span[0])]

    def push(condition, zs, col, span, who, slot, receive, mine=False):
        def make():
            here = block(zs, col, c, span)
            source = x.at[pl.ds(span[0], span[1] - span[0])] if mine else here
            return remote(source, here, send.at[slot[0], zs, slot[1]], receive, who)

        maybe(condition, lambda: make().start())
        sent.append((condition, make))

    def await_block(zs, col, span, receive, core=None):
        here = block(zs, col, c if core is None else core, span)
        remote(here, here, send.at[0, 0, 0], receive, mate).wait_recv()

    def deliver(zs, col, core, span):
        for index, (out, (low, high)) in enumerate(zip(outs, members)):
            first, last = max(low, span[0]), min(high, span[1])
            if first < last:
                pltpu.make_async_copy(
                    buf.at[zs, cols[col], core, pl.ds(first, last - first)],
                    out.at[zs, cols[col], core, pl.ds(first - low, last - first)],
                    out_sem.at[index],
                ).start()

    def share(condition, part, zs, col, span, kind, mine=False):
        def make():
            here = block(zs, col, c, span)
            source = x.at[pl.ds(span[0], span[1] - span[0])] if mine else here
            return remote(
                source, here, side_send.at[part, zs, kind], side_recv.at[part, zs, kind], mate
            )

        def action():
            make().start()
            if not mine:
                deliver(zs, col, c, span)

        maybe(condition, action)
        sent.append((condition, make))
        shared.append((condition, part, zs, col, span, kind))

    shared = []
    whole = [cuts[0], cuts[1]]
    for part in (1, 0):
        push(None, z, OWN, whole[part], at_x, (part, 0), recv.at[part, z, ACROSS_X], True)
        push(None, z, OWN, whole[part], at_y, (part, 1), recv.at[part, z, ACROSS_Y], True)
    for part in (0, 1):
        push(above, z, OWN, whole[part], up, (part, 2), recv.at[part, z, OWN], True)
        push(below, z, OWN, whole[part], down, (part, 3), recv.at[part, z, OWN], True)
    for part in (0, 1):
        share(None, part, z, OWN, whole[part], 0, True)
    own_copy = pltpu.make_async_copy(x, buf.at[z, cols[0], c], out_sem.at[len(members)])
    own_copy.start()

    def turn(condition, part, zs):
        span = whole[part]
        for col, which, who, slot in ((ACROSS_X, 1, at_y, 4), (ACROSS_Y, 0, at_x, 5)):
            maybe(
                condition,
                lambda col=col: await_block(zs, col, span, recv.at[part, zs, col]),
            )
            push(condition, zs, col, half_of(span, which), who, (part, slot), recv.at[part, zs, 4 + which])
            if part == 1:
                push(above, zs, col, span, up, (1, 4 + 2 * col), recv.at[1, zs, col])
                push(below, zs, col, span, down, (1, 5 + 2 * col), recv.at[1, zs, col])
            share(condition, part, zs, col, span, col)

    turn(None, 1, z)
    turn(None, 0, z)
    for which in (0, 1):
        await_block(z, DIAGONAL, half_of(whole[1], which), recv.at[1, z, 4 + which])
    push(above, z, DIAGONAL, whole[1], up, (1, 10), recv.at[1, z, DIAGONAL])
    push(below, z, DIAGONAL, whole[1], down, (1, 11), recv.at[1, z, DIAGONAL])
    share(None, 1, z, DIAGONAL, whole[1], 3)

    def settle(upto):
        while len(shared) > upto:
            condition, part, zs, col, span, kind = shared.pop(0)

            def action():
                await_block(zs, col, span, side_recv.at[part, zs, kind], 1 - c)
                deliver(zs, col, 1 - c, span)

            maybe(condition, action)

    for step in range(1, planes):
        ways = ((z - step >= 0, z - step, above, up), (z + step < planes, z + step, below, down))
        for valid, zs, further, onward in ways:
            go = jnp.logical_and(valid, further)
            pl.when(valid)(
                lambda zs=zs: await_block(zs, OWN, whole[0], recv.at[0, zs, OWN])
            )
            push(go, zs, OWN, whole[0], onward, (0, 2), recv.at[0, zs, OWN])
            push(valid, zs, OWN, whole[0], at_x, (0, 0), recv.at[0, zs, ACROSS_X])
            push(valid, zs, OWN, whole[0], at_y, (0, 1), recv.at[0, zs, ACROSS_Y])
            share(valid, 0, zs, OWN, whole[0], 0)
        waiting = len(shared)
        for valid, zs, further, onward in ways:
            go = jnp.logical_and(valid, further)
            for col in (OWN, ACROSS_X, ACROSS_Y, DIAGONAL):
                pl.when(valid)(
                    lambda zs=zs, col=col: await_block(zs, col, whole[1], recv.at[1, zs, col])
                )
                push(go, zs, col, whole[1], onward, (1, col), recv.at[1, zs, col])
                share(valid, 1, zs, col, whole[1], col)
        for valid, zs, further, onward in ways:
            turn(valid, 0, zs)
        settle(8)
    own_copy.wait()
    deliver(z, OWN, c, (0, rows))
    everywhere = [(None, z)] + [
        (valid, zs)
        for step in range(1, planes)
        for valid, zs in ((z - step >= 0, z - step), (z + step < planes, z + step))
    ]
    for condition, zs in everywhere:
        for which in (0, 1):
            span = half_of(whole[0], which)
            maybe(
                condition,
                lambda zs=zs, which=which, span=span: await_block(
                    zs, DIAGONAL, span, recv.at[0, zs, 4 + which]
                ),
            )
            share(condition, 0, zs, DIAGONAL, span, 3 + which)
    settle(0)
    for condition, make in sent:
        maybe(condition, lambda make=make: make().wait_send())
    for index, (out, (low, high)) in enumerate(zip(outs, members)):
        pltpu.make_async_copy(
            buf.at[:, :, :, pl.ds(low, high - low)], out, out_sem.at[index]
        ).wait()


def big_gather(x, heights, mesh_shape, identity):
    planes, width = mesh_shape
    rows, columns = x.shape
    members, low = [], 0
    for height in heights:
        members.append((low, low + height))
        low += height
    outs = pl.pallas_call(
        functools.partial(big_gather_kernel, planes, rows, tuple(members)),
        out_shape=[
            jax.ShapeDtypeStruct((planes, width // 2, 2, height, columns), x.dtype)
            for height in heights
        ],
        in_specs=[pl.BlockSpec(memory_space=VMEM_SPACE)],
        out_specs=[pl.BlockSpec(memory_space=pl.ANY)] * len(heights),
        scratch_shapes=[
            VMEM_SPACE((planes, width // 2, 2, rows, columns), x.dtype),
            pltpu.SemaphoreType.DMA((len(heights) + 1,)),
            pltpu.SemaphoreType.DMA((2, planes, 12)),
            pltpu.SemaphoreType.DMA((2, planes, 6)),
            pltpu.SemaphoreType.DMA((2, planes, 5)),
            pltpu.SemaphoreType.DMA((2, planes, 5)),
        ],
        compiler_params=pltpu.CompilerParams(
            collective_id=identity, has_side_effects=True, vmem_limit_bytes=VMEM_ASK
        ),
    )(x)
    return [out.reshape(-1, columns) for out in outs]


def accumulate(target, sources, height):
    step = 32

    def body(i, unused):
        rows = pl.ds(pl.multiple_of(i * step, step), step)
        total = sources[0][rows].astype(jnp.float32)
        for source in sources[1:]:
            total = total + source[rows].astype(jnp.float32)
        target[rows] = total.astype(target.dtype)
        return unused

    lax.fori_loop(0, height // step, body, 0)


def big_scatter_kernel(planes, rows, members, *refs):
    count = len(members)
    grads, out = refs[:count], refs[count]
    own, side, half_in, full_in, line_in, tail_line, tail_half, tail_full = refs[
        count + 1 : count + 9
    ]
    load, side_send, side_recv, send, recv, tail_send, tail_recv = refs[count + 9 :]
    z, c, cols = places()
    cuts = cuts_of(rows)
    at_x, at_y, mate = (z, cols[1] * 2 + c), (z, cols[2] * 2 + c), (z, cols[0] * 2 + 1 - c)
    above, below = z < planes - 1, z > 0
    up, down = (z + 1, cols[0] * 2 + c), (z - 1, cols[0] * 2 + c)
    greet([(None, at_x), (None, at_y), (None, mate), (above, up), (below, down)])
    sent = []

    def push(condition, make):
        maybe(condition, lambda: make().start())
        sent.append((condition, make))

    def piece(ref, span):
        return ref.at[pl.ds(span[0], span[1] - span[0])]

    order = (DIAGONAL, ACROSS_X, ACROSS_Y, OWN)
    loads = {}
    for col in order:
        for a, (low, high) in enumerate(members):
            copy = pltpu.make_async_copy(
                grads[a].at[:, cols[col], c],
                own.at[:, col, pl.ds(low, high - low)],
                load.at[col, a],
            )
            copy.start()

            def make(col=col, a=a, low=low, high=high):
                return remote(
                    grads[a].at[:, cols[col], 1 - c],
                    side.at[:, col, pl.ds(low, high - low)],
                    side_send.at[col, a],
                    side_recv.at[col, a],
                    mate,
                )

            push(None, make)
            loads[col, a] = (copy, make)

    def merge(col):
        for a in range(count):
            copy, make = loads[col, a]
            copy.wait()
            make().wait_recv()

        def body(zt, unused):
            accumulate(own.at[zt, col], [own.at[zt, col], side.at[zt, col]], rows)
            return unused

        lax.fori_loop(0, planes, body, 0)

    targets = []
    for distance in range(planes - 1, 0, -1):
        targets.append((z + distance < planes, z + distance, 0))
        targets.append((z - distance >= 0, z - distance, 1))
    targets.append((None, z, 2))
    head, tail = cuts
    height, tail_height = head[1] - head[0], tail[1] - tail[0]

    def half_message(zt, which):
        return remote(
            piece(own.at[zt, DIAGONAL], half_of(head, which)),
            half_in.at[which, zt],
            send.at[0, which, zt],
            recv.at[0, which, zt],
            (at_x, at_y)[which],
        )

    def full_message(zt, which):
        return remote(
            piece(own.at[zt, (ACROSS_X, ACROSS_Y)[which]], head),
            full_in.at[which, zt],
            send.at[1, which, zt],
            recv.at[1, which, zt],
            (at_x, at_y)[which],
        )

    def line_message(zt, way):
        return remote(
            piece(own.at[zt, OWN], head),
            line_in.at[way, zt],
            send.at[2, way, zt],
            recv.at[2, way, zt],
            (up, down)[way],
        )

    def tail_message(zt, way):
        return remote(
            own.at[zt, :, pl.ds(tail[0], tail_height)],
            tail_line.at[way, zt],
            tail_send.at[way, zt],
            tail_recv.at[way, zt],
            (up, down)[way],
        )

    merge(DIAGONAL)
    for valid, zt, unused in targets:
        for which in (0, 1):
            push(valid, functools.partial(half_message, zt, which))
    merge(ACROSS_X)
    merge(ACROSS_Y)

    def second(valid, zt):
        def add():
            for which, col in ((1, ACROSS_X), (0, ACROSS_Y)):
                half_message(zt, which).wait_recv()
                span = half_of(head, which)
                target = piece(own.at[zt, col], span)
                accumulate(target, [target, half_in.at[which, zt]], height // 2)

        maybe(valid, add)
        for which in (0, 1):
            push(valid, functools.partial(full_message, zt, which))

    def tail_add(zt, way):
        tail_message(zt, way).wait_recv()
        for col in range(4):
            target = piece(own.at[zt, col], tail)
            accumulate(target, [target, tail_line.at[way, zt, col]], tail_height)

    def tail_step(valid, zt, way):
        behind = (below, above)[way]
        pl.when(jnp.logical_and(valid, behind))(lambda: tail_add(zt, way))
        push(valid, functools.partial(tail_message, zt, way))

    second(*targets[0][:2])
    second(*targets[1][:2])
    merge(OWN)
    for number in range(2, len(targets)):
        if number - 2 < len(targets) - 1:
            tail_step(*targets[number - 2])
        second(*targets[number][:2])
    for number in range(len(targets) - 2, len(targets) - 1):
        tail_step(*targets[number])

    def third(valid, zt, way):
        def add():
            for which in (0, 1):
                full_message(zt, which).wait_recv()
            base = [piece(own.at[zt, OWN], head), full_in.at[0, zt], full_in.at[1, zt]]
            behind = (below, above)[way]

            @pl.when(behind)
            def _():
                line_message(zt, way).wait_recv()
                accumulate(base[0], base + [line_in.at[way, zt]], height)

            @pl.when(jnp.logical_not(behind))
            def _():
                accumulate(base[0], base, height)

        pl.when(valid)(add)
        push(valid, functools.partial(line_message, zt, way))

    half_tail = tail_height // 2

    def tail_half_message(which):
        return remote(
            piece(own.at[z, DIAGONAL], half_of(tail, which)),
            tail_half.at[which],
            tail_send.at[2, which],
            tail_recv.at[2, which],
            (at_x, at_y)[which],
        )

    def tail_full_message(which):
        return remote(
            piece(own.at[z, (ACROSS_X, ACROSS_Y)[which]], tail),
            tail_full.at[which],
            tail_send.at[3, which],
            tail_recv.at[3, which],
            (at_x, at_y)[which],
        )

    for number, target in enumerate(targets[:-1]):
        third(*target)
        if number == len(targets) - 3:
            pl.when(below)(lambda: tail_add(z, 0))
            pl.when(above)(lambda: tail_add(z, 1))
            for which in (0, 1):
                push(None, functools.partial(tail_half_message, which))
    for which, col in ((1, ACROSS_X), (0, ACROSS_Y)):
        tail_half_message(which).wait_recv()
        target = piece(own.at[z, col], half_of(tail, which))
        accumulate(target, [target, tail_half.at[which]], half_tail)
    for which in (0, 1):
        push(None, functools.partial(tail_full_message, which))
    for which in (0, 1):
        full_message(z, which).wait_recv()
    goal = piece(out, head)
    accumulate(goal, [piece(own.at[z, OWN], head), full_in.at[0, z], full_in.at[1, z]], height)
    for present, way in ((below, 0), (above, 1)):

        def add(way=way):
            line_message(z, way).wait_recv()
            accumulate(goal, [goal, line_in.at[way, z]], height)

        pl.when(present)(add)
    for which in (0, 1):
        tail_full_message(which).wait_recv()
    accumulate(
        piece(out, tail),
        [piece(own.at[z, OWN], tail), tail_full.at[0], tail_full.at[1]],
        tail_height,
    )
    for condition, make in sent:
        maybe(condition, lambda make=make: make().wait_send())


def big_scatter(arrays, mesh_shape, identity):
    planes, width = mesh_shape
    columns = arrays[0].shape[1]
    members, low, views = [], 0, []
    for a in arrays:
        height = a.shape[0] // (planes * width)
        members.append((low, low + height))
        low += height
        views.append(a.reshape(planes, width // 2, 2, height, columns))
    rows = low
    head, tail = (high - low for low, high in cuts_of(rows))
    half = arrays[0].dtype
    return pl.pallas_call(
        functools.partial(big_scatter_kernel, planes, rows, tuple(members)),
        out_shape=jax.ShapeDtypeStruct((rows, columns), jnp.float32),
        in_specs=[pl.BlockSpec(memory_space=pl.ANY)] * len(arrays),
        out_specs=pl.BlockSpec(memory_space=VMEM_SPACE),
        scratch_shapes=[
            VMEM_SPACE((planes, 4, rows, columns), half),
            VMEM_SPACE((planes, 4, rows, columns), half),
            VMEM_SPACE((2, planes, head // 2, columns), half),
            VMEM_SPACE((2, planes, head, columns), half),
            VMEM_SPACE((2, planes, head, columns), half),
            VMEM_SPACE((2, planes, 4, tail, columns), half),
            VMEM_SPACE((2, tail // 2, columns), half),
            VMEM_SPACE((2, tail, columns), half),
            pltpu.SemaphoreType.DMA((4, len(arrays))),
            pltpu.SemaphoreType.DMA((4, len(arrays))),
            pltpu.SemaphoreType.DMA((4, len(arrays))),
            pltpu.SemaphoreType.DMA((3, 2, planes)),
            pltpu.SemaphoreType.DMA((3, 2, planes)),
            pltpu.SemaphoreType.DMA((4, planes)),
            pltpu.SemaphoreType.DMA((4, planes)),
        ],
        compiler_params=pltpu.CompilerParams(
            collective_id=identity, has_side_effects=True, vmem_limit_bytes=VMEM_ASK
        ),
    )(*views)


def far_first(i, z, planes):
    low = (2 * z < planes).astype(jnp.int32)
    falling = planes - 1 - i - (i >= planes - 1 - z).astype(jnp.int32)
    rising = i + (i >= z).astype(jnp.int32)
    last = (jnp.int32(i) == planes - 1).astype(jnp.int32)
    return last * z + (1 - last) * (low * falling + (1 - low) * rising)


def finish_kernel(
    planes,
    heights,
    split,
    left_wide,
    left_tall,
    rights,
    outer,
    head_grad,
    own_rows,
    vector_terms,
    out,
    all_rows,
    own_vector,
    both,
    side,
    half_in,
    full_in,
    line_in,
    tail_line,
    tail_half,
    tail_full,
    wide_buf,
    tall_buf,
    vector_in,
    vector_mid,
    vector_last,
    fetch,
    head_load,
    side_send,
    side_recv,
    send,
    recv,
    tail_send,
    tail_recv,
    row_send,
    row_recv,
    vec_send,
    vec_recv,
):
    width = 8
    wide_height, tall_height, head_height = heights
    rows = wide_height + tall_height + head_height
    z, c, cols = places()
    q = cols[0]
    f = q * 2 + c
    x, y = lax.rem(q, 2), q // 2
    cuts = cuts_of(rows)
    head, tail = cuts
    head_rows, tail_rows = head[1] - head[0], tail[1] - tail[0]
    at_x, at_y, mate = (z, cols[1] * 2 + c), (z, cols[2] * 2 + c), (z, q * 2 + 1 - c)
    above, below = z < planes - 1, z > 0
    up, down = (z + 1, f), (z - 1, f)
    line = [(lax.rem(z + d, planes), f) for d in range(1, planes)]
    plane = [(z, lax.rem(f + d, width)) for d in range(1, width)]
    greet([(None, who) for who in line + plane])
    order = (DIAGONAL, ACROSS_X, ACROSS_Y, OWN)
    sent = []

    def push(condition, make):
        maybe(condition, lambda: make().start())
        sent.append((condition, make))

    def piece(ref, span):
        return ref.at[pl.ds(span[0], span[1] - span[0])]

    def plane_at(i):
        return far_first(i, z, planes)

    def chip_of(n):
        place, i = n // planes, lax.rem(n, planes)
        flip_x, flip_y = 1 - place // 2, 1 - lax.rem(place, 2)
        return plane_at(i) * 4 + 2 * lax.rem(y + flip_y, 2) + lax.rem(x + flip_x, 2)

    def fetches(n):
        k, slot = chip_of(n), lax.rem(n, 2)
        wide_rows = pl.ds(pl.multiple_of(k * 2 * wide_height, 16), 2 * wide_height)
        tall_rows = pl.ds(pl.multiple_of(k * 2 * tall_height, 16), 2 * tall_height)
        return (
            pltpu.make_async_copy(
                left_wide.at[wide_rows], wide_buf.at[slot], fetch.at[0, slot]
            ),
            pltpu.make_async_copy(
                left_tall.at[tall_rows], tall_buf.at[slot], fetch.at[1, slot]
            ),
        )

    for copy in fetches(jnp.int32(0)):
        copy.start()

    def vector_first(d, who):
        return remote(
            vector_terms.at[:, who[1]], vector_in.at[d], vec_send.at[0, d], vec_recv.at[0, d], who
        )

    def vector_second(d, who):
        return remote(
            vector_mid.at[who[0]], vector_last.at[d], vec_send.at[1, d], vec_recv.at[1, d], who
        )

    def row_line(d, who):
        return remote(
            own_rows, all_rows.at[z, q, c], row_send.at[0, d], row_recv.at[0, d], who
        )

    def row_plane(col):
        return remote(
            all_rows.at[:, q, c],
            all_rows.at[:, q, c],
            row_send.at[1, col],
            row_recv.at[1, col],
            (z, cols[col] * 2 + c),
        )

    def row_mate():
        return remote(
            all_rows.at[:, :, c], all_rows.at[:, :, c], row_send.at[2, 0], row_recv.at[2, 0], mate
        )

    for d, who in enumerate(line):
        push(None, functools.partial(row_line, d, who))
    for d, who in enumerate(plane):
        push(None, functools.partial(vector_first, d, who))
    all_rows[z, q, c] = own_rows[...]
    head_copies = []
    for col in order:
        copy = pltpu.make_async_copy(
            head_grad.at[:, cols[col]],
            both.at[:, col, :, pl.ds(wide_height + tall_height, head_height)],
            head_load.at[col],
        )
        copy.start()
        head_copies.append(copy)

    def side_message(zt, col):
        return remote(
            both.at[zt, col, 1 - c],
            side.at[zt, col],
            side_send.at[col, zt],
            side_recv.at[col, zt],
            mate,
        )

    def half_message(zt, which):
        return remote(
            piece(both.at[zt, DIAGONAL, c], half_of(head, which)),
            half_in.at[which, zt],
            send.at[0, which, zt],
            recv.at[0, which, zt],
            (at_x, at_y)[which],
        )

    def full_message(zt, which):
        return remote(
            piece(both.at[zt, (ACROSS_X, ACROSS_Y)[which], c], head),
            full_in.at[which, zt],
            send.at[1, which, zt],
            recv.at[1, which, zt],
            (at_x, at_y)[which],
        )

    def line_message(zt, way):
        return remote(
            piece(both.at[zt, OWN, c], head),
            line_in.at[way, zt],
            send.at[2, way, zt],
            recv.at[2, way, zt],
            (up, down)[way],
        )

    def tail_message(zt, way):
        return remote(
            both.at[zt, :, c, pl.ds(tail[0], tail_rows)],
            tail_line.at[way, zt],
            tail_send.at[way, zt],
            tail_recv.at[way, zt],
            (up, down)[way],
        )

    def merged(zt, col):
        side_message(zt, col).wait_recv()
        mine = both.at[zt, col, c]
        accumulate(mine, [mine, side.at[zt, col]], rows)
        if col == DIAGONAL:
            half_message(zt, 0).start()
            half_message(zt, 1).start()
        elif col != OWN:
            which = 0 if col == ACROSS_X else 1
            half_message(zt, 1 - which).wait_recv()
            target = piece(mine, half_of(head, 1 - which))
            accumulate(target, [target, half_in.at[1 - which, zt]], head_rows // 2)
            full_message(zt, which).start()

    for place, col in enumerate(order):
        head_copies[place].wait()

        def body(i, unused, place=place, col=col):
            n = place * planes + i
            for copy in fetches(n):
                copy.wait()

            @pl.when(n + 1 < 4 * planes)
            def _():
                for copy in fetches(n + 1):
                    copy.start()

            zt, k, slot = plane_at(i), chip_of(n), lax.rem(n, 2)
            region = (k >= split[0]).astype(jnp.int32) + (k >= split[1]).astype(jnp.int32)
            product_wide = to_half(nn(wide_buf[slot], rights[region]))
            both[zt, col, 0, :wide_height] = product_wide[:wide_height]
            both[zt, col, 1, :wide_height] = product_wide[wide_height:]
            product_tall = to_half(nn(tall_buf[slot], outer[...]))
            here = slice(wide_height, wide_height + tall_height)
            both[zt, col, 0, here] = product_tall[:tall_height]
            both[zt, col, 1, here] = product_tall[tall_height:]
            side_message(zt, col).start()

            @pl.when(i > 0)
            def _():
                merged(plane_at(i - 1), col)

            return unused

        lax.fori_loop(0, planes, body, 0)
        merged(z, col)
        if place == 0:
            for d, who in enumerate(line):
                row_line(d, who).wait_recv()
            for step in (ACROSS_X, ACROSS_Y, DIAGONAL):
                push(None, functools.partial(row_plane, step))
            total = vector_terms[:, f]
            for d, who in enumerate(plane):
                vector_first(d, who).wait_recv()
                total = total + vector_in[d]
            vector_mid[...] = total
            for d, who in enumerate(line):
                push(None, functools.partial(vector_second, d, who))
        elif place == 2:
            for step in (ACROSS_X, ACROSS_Y, DIAGONAL):
                remote(
                    all_rows.at[:, cols[step], c],
                    all_rows.at[:, cols[step], c],
                    row_send.at[1, step],
                    row_recv.at[1, step],
                    mate,
                ).wait_recv()
            push(None, row_mate)

    targets = [plane_at(i) for i in range(planes)]

    def tail_add(zt, way):
        tail_message(zt, way).wait_recv()
        for col in range(4):
            target = piece(both.at[zt, col, c], tail)
            accumulate(target, [target, tail_line.at[way, zt, col]], tail_rows)

    def tail_step(zt):
        for way, valid in ((0, zt > z), (1, zt < z)):
            behind = (below, above)[way]
            pl.when(jnp.logical_and(valid, behind))(lambda way=way: tail_add(zt, way))
            push(valid, functools.partial(tail_message, zt, way))

    def third(zt):
        for which in (0, 1):
            full_message(zt, which).wait_recv()
        base = [piece(both.at[zt, OWN, c], head), full_in.at[0, zt], full_in.at[1, zt]]
        accumulate(base[0], base, head_rows)
        for way, valid in ((0, zt > z), (1, zt < z)):
            behind = (below, above)[way]

            def add(way=way):
                line_message(zt, way).wait_recv()
                accumulate(base[0], [base[0], line_in.at[way, zt]], head_rows)

            pl.when(jnp.logical_and(valid, behind))(add)
            push(valid, functools.partial(line_message, zt, way))

    def tail_half_message(which):
        return remote(
            piece(both.at[z, DIAGONAL, c], half_of(tail, which)),
            tail_half.at[which],
            tail_send.at[2, which],
            tail_recv.at[2, which],
            (at_x, at_y)[which],
        )

    def tail_full_message(which):
        return remote(
            piece(both.at[z, (ACROSS_X, ACROSS_Y)[which], c], tail),
            tail_full.at[which],
            tail_send.at[3, which],
            tail_recv.at[3, which],
            (at_x, at_y)[which],
        )

    tail_step(targets[0])
    for number in range(planes - 1):
        third(targets[number])
        if number + 1 < planes - 1:
            tail_step(targets[number + 1])
    pl.when(below)(lambda: tail_add(z, 0))
    pl.when(above)(lambda: tail_add(z, 1))
    for which in (0, 1):
        push(None, functools.partial(tail_half_message, which))
    for which, col in ((1, ACROSS_X), (0, ACROSS_Y)):
        tail_half_message(which).wait_recv()
        target = piece(both.at[z, col, c], half_of(tail, which))
        accumulate(target, [target, tail_half.at[which]], tail_rows // 2)
    for which in (0, 1):
        push(None, functools.partial(tail_full_message, which))
    for which in (0, 1):
        full_message(z, which).wait_recv()
    goal = piece(out, head)
    accumulate(
        goal, [piece(both.at[z, OWN, c], head), full_in.at[0, z], full_in.at[1, z]], head_rows
    )
    for present, way in ((below, 0), (above, 1)):

        def add(way=way):
            line_message(z, way).wait_recv()
            accumulate(goal, [goal, line_in.at[way, z]], head_rows)

        pl.when(present)(add)
    for which in (0, 1):
        tail_full_message(which).wait_recv()
    accumulate(
        piece(out, tail),
        [piece(both.at[z, OWN, c], tail), tail_full.at[0], tail_full.at[1]],
        tail_rows,
    )
    total = vector_mid[z]
    for d, who in enumerate(line):
        vector_second(d, who).wait_recv()
        total = total + vector_last[d]
    own_vector[...] = total
    remote(
        all_rows.at[:, :, 1 - c],
        all_rows.at[:, :, 1 - c],
        row_send.at[2, 0],
        row_recv.at[2, 0],
        mate,
    ).wait_recv()
    for condition, make in sent:
        maybe(condition, lambda make=make: make().wait_send())
    for zt in targets:
        for col in order:
            side_message(zt, col).wait_send()
        for which in (0, 1):
            half_message(zt, which).wait_send()
            full_message(zt, which).wait_send()


def run_finish(
    left_wide, left_tall, rights, outer, head_grad, own_rows, vector_terms, mesh_shape, identity
):
    planes, width = mesh_shape
    devices = planes * width
    columns = outer.shape[1]
    heights = (
        left_wide.shape[0] // devices,
        left_tall.shape[0] // devices,
        head_grad.shape[0] // devices,
    )
    rows = sum(heights)
    long = left_wide.shape[1]
    split = (3 * D // (2 * heights[0]), 4 * D // (2 * heights[0]))
    head, tail = (high - low for low, high in cuts_of(rows))
    half, single = jnp.bfloat16, jnp.float32
    block = vector_terms.shape[1:]
    vmem = pl.BlockSpec(memory_space=VMEM_SPACE)
    any_space = pl.BlockSpec(memory_space=pl.ANY)
    dma = pltpu.SemaphoreType.DMA
    out, all_rows, own_vector = pl.pallas_call(
        functools.partial(finish_kernel, planes, heights, split),
        out_shape=[
            jax.ShapeDtypeStruct((rows, columns), single),
            jax.ShapeDtypeStruct((planes, width // 2, 2, *own_rows.shape), half),
            jax.ShapeDtypeStruct(block, single),
        ],
        in_specs=[any_space, any_space, vmem, vmem, any_space, vmem, vmem],
        out_specs=[vmem] * 3,
        scratch_shapes=[
            VMEM_SPACE((planes, 4, 2, rows, columns), half),
            VMEM_SPACE((planes, 4, rows, columns), half),
            VMEM_SPACE((2, planes, head // 2, columns), half),
            VMEM_SPACE((2, planes, head, columns), half),
            VMEM_SPACE((2, planes, head, columns), half),
            VMEM_SPACE((2, planes, 4, tail, columns), half),
            VMEM_SPACE((2, tail // 2, columns), half),
            VMEM_SPACE((2, tail, columns), half),
            VMEM_SPACE((2, 2 * heights[0], long), half),
            VMEM_SPACE((2, 2 * heights[1], long), half),
            VMEM_SPACE((width - 1, planes, *block), single),
            VMEM_SPACE((planes, *block), single),
            VMEM_SPACE((planes - 1, *block), single),
            dma((2, 2)),
            dma((4,)),
            dma((4, planes)),
            dma((4, planes)),
            dma((3, 2, planes)),
            dma((3, 2, planes)),
            dma((4, planes)),
            dma((4, planes)),
            dma((3, 4)),
            dma((3, 4)),
            dma((2, width)),
            dma((2, width)),
        ],
        compiler_params=pltpu.CompilerParams(
            collective_id=identity, has_side_effects=True, vmem_limit_bytes=VMEM_ASK
        ),
    )(
        left_wide,
        left_tall,
        rights,
        outer,
        head_grad.reshape(planes, width // 2, 2, heights[2], columns),
        own_rows,
        vector_terms.reshape(planes, width, *block),
    )
    return out, heights, all_rows.reshape(-1, own_rows.shape[1]), own_vector


class Network:
    def __init__(self, mesh):
        self.shape = (mesh.shape["dp"], mesh.shape["fsdp"])
        self.devices = self.shape[0] * self.shape[1]
        self.kernels = self.shape[1] == 8
        self.calls = 0

    def identity(self):
        self.calls += 1
        return self.calls

    def gather_small(self, blocks):
        if not self.kernels:
            return [lax.all_gather(b, AXES) for b in blocks]
        gathered = small_gather(blocks, self.shape, self.identity())
        return [g.reshape(self.devices, *g.shape[2:]) for g in gathered]

    def scatter_small(self, blocks):
        if not self.kernels:
            return lax.psum_scatter(blocks, AXES, scatter_dimension=0)
        return small_scatter(
            blocks.reshape(*self.shape, *blocks.shape[1:]), self.shape, self.identity()
        )

    def gather(self, shards):
        if not self.kernels:
            return [lax.all_gather(s, AXES, axis=0, tiled=True) for s in shards]
        heights = tuple(s.shape[0] for s in shards)
        packed = jnp.concatenate(shards, 0) if len(shards) > 1 else shards[0]
        return big_gather(packed, heights, self.shape, self.identity())

    def scatter(self, partials):
        if not self.kernels:
            return [
                lax.psum_scatter(
                    p.astype(jnp.float32), AXES, scatter_dimension=0, tiled=True
                )
                for p in partials
            ]
        total = big_scatter(partials, self.shape, self.identity())
        out, low = [], 0
        for p in partials:
            height = p.shape[0] // self.devices
            out.append(total[low : low + height])
            low += height
        return out

    def finish(self, left_wide, left_tall, rights, outer, head_grad, own_rows, vector):
        total = vector.shape[0]
        share = -(-total // (self.devices * 1024)) * 1024
        vector = jnp.pad(vector, (0, self.devices * share - total))
        vector = vector.reshape(self.devices, -1, 128)
        if self.kernels:
            out, heights, all_rows, own_vector = run_finish(
                left_wide,
                left_tall,
                rights,
                outer,
                to_half(head_grad),
                own_rows,
                vector,
                self.shape,
                self.identity(),
            )
            first, second = heights[0], heights[0] + heights[1]
            return out[:first], out[first:second], out[second:], all_rows, own_vector
        back_wide = jnp.concatenate(
            [
                product(left_wide[: 3 * D], rights[0]),
                product(left_wide[3 * D : 4 * D], rights[1]),
                product(left_wide[4 * D :], rights[2]),
            ],
            0,
        )
        sums = self.scatter([back_wide, product(left_tall, outer), head_grad])
        return (*sums, self.gather([own_rows])[0], self.scatter_small(vector))


def nt(a, b):
    return lax.dot_general(a, b, (((1,), (1,)), ((), ())), preferred_element_type=jnp.float32)


def nn(a, b):
    return jnp.dot(a, b, preferred_element_type=jnp.float32)


def tn(a, b):
    return lax.dot_general(a, b, (((0,), (0,)), ((), ())), preferred_element_type=jnp.float32)


CHUNK = 512
PAIR = 2 * HEAD_DIM
PROJ_B, Q_B, V_B, O_B, LN1_G, LN1_B, FFO_B, LN2_G, LN2_B, POOL_B = range(10)


def allowed_block(lengths):
    shape = (ROWS, ROWS)
    row = lax.broadcasted_iota(jnp.int32, shape, 0)
    col = lax.broadcasted_iota(jnp.int32, shape, 1)
    two = lengths[1] > 0
    row_second = jnp.logical_and(row >= BUCKET, two).astype(jnp.int32)
    col_second = jnp.logical_and(col >= BUCKET, two).astype(jnp.int32)
    length = jnp.where(col_second == 1, lengths[1], lengths[0])
    live = col - BUCKET * col_second < length
    return jnp.logical_and(row_second == col_second, live)


def halves(x):
    lane = lax.broadcasted_iota(jnp.int32, x.shape, 1)
    zero = jnp.zeros_like(x)
    return jnp.where(lane < HEAD_DIM, x, zero), jnp.where(lane < HEAD_DIM, zero, x)


def forward_kernel(
    lengths,
    start,
    wide,
    tall,
    vec,
    ff_b,
    final,
    rights,
    projected,
    weighting,
    hat_one,
    inverse_one,
    slope,
    active,
    hat_two,
    inverse_two,
    hidden,
):
    layer = pl.program_id(0)

    @pl.when(layer == 0)
    def _():
        hidden[...] = start[...]

    def row(index):
        return vec[pl.ds(index, 1), :]

    half = to_half(hidden[...])
    rights[0] = half
    for part, bias in ((0, Q_B), (1, None), (2, V_B)):
        for low in range(0, D, 256):
            here = part * D + low
            value = nt(half, wide[pl.ds(here, 256), :])
            if bias is not None:
                value = value + vec[pl.ds(bias, 1), pl.ds(low, 256)]
            projected[:, pl.ds(here, 256)] = to_half(value)
    allowed = allowed_block(lengths)
    for pair in range(HEADS // 2):
        lanes = pair * PAIR
        queries = halves(projected[:, pl.ds(lanes, PAIR)])
        keys = projected[:, pl.ds(D + lanes, PAIR)]
        values = halves(projected[:, pl.ds(2 * D + lanes, PAIR)])
        total = jnp.zeros((ROWS, PAIR), jnp.float32)
        for side in (0, 1):
            scores = jnp.where(allowed, nt(queries[side], keys) * SCALE, MASKED)
            powers = jnp.exp(scores - jnp.max(scores, -1, keepdims=True))
            weights = powers * (1.0 / jnp.sum(powers, -1, keepdims=True))
            weighting[2 * pair + side] = weights
            total = total + nn(to_half(weights), values[side])
        rights[1, :, pl.ds(lanes, PAIR)] = to_half(total)
    first_sum = hidden[...] + nt(rights[1], wide[pl.ds(3 * D, D), :]) + row(O_B)
    hat, inverse = norm_forward(first_sum)
    hat_one[...] = hat
    inverse_one[...] = inverse
    middle = hat * row(LN1_G) + row(LN1_B)
    half = to_half(middle)
    rights[2] = half
    total = middle + row(FFO_B)
    for low in range(0, FF, CHUNK):
        inner = nt(half, wide[pl.ds(4 * D + low, CHUNK), :]) + ff_b[:, pl.ds(low, CHUNK)]
        square = inner * inner
        bend = jnp.tanh(GELU_A * inner * (1.0 + GELU_B * square))
        act = to_half(0.5 * inner * (1.0 + bend))
        slope[:, pl.ds(low, CHUNK)] = 0.5 * (1.0 + bend) + (0.5 * GELU_A) * inner * (
            1.0 - bend * bend
        ) * (1.0 + 3.0 * GELU_B * square)
        active[pl.ds(low, CHUNK), :] = act.T
        total = total + nn(act, tall[pl.ds(low, CHUNK), :])
    hat, inverse = norm_forward(total)
    hat_two[...] = hat
    inverse_two[...] = inverse
    output = hat * row(LN2_G) + row(LN2_B)
    hidden[...] = output
    final[...] = output


def whole_spec():
    return pl.BlockSpec(memory_space=VMEM_SPACE, pipeline_mode=pl.Buffered(1))


def by_layer(*shape, order=lambda i: i):
    return pl.BlockSpec(
        (None, *shape), lambda i: (order(i),) + (0,) * len(shape), memory_space=VMEM_SPACE
    )


def run_forward(lengths, start, wide, tall, vec, ff_b):
    def kept(*shape, dtype=jnp.bfloat16):
        return jax.ShapeDtypeStruct((LAYERS, *shape), dtype)

    single = jnp.float32
    names = (
        "final",
        "rights",
        "projected",
        "weighting",
        "hat_one",
        "inverse_one",
        "slope",
        "active",
        "hat_two",
        "inverse_two",
    )
    outs = pl.pallas_call(
        forward_kernel,
        grid=(LAYERS,),
        out_shape=[
            jax.ShapeDtypeStruct((ROWS, D), single),
            jax.ShapeDtypeStruct((3, LAYERS, ROWS, D), jnp.bfloat16),
            kept(ROWS, 3 * D),
            kept(HEADS, ROWS, ROWS, dtype=single),
            kept(ROWS, D, dtype=single),
            kept(ROWS, 1, dtype=single),
            kept(ROWS, FF, dtype=single),
            jax.ShapeDtypeStruct((FF, LAYERS * ROWS), jnp.bfloat16),
            kept(ROWS, D, dtype=single),
            kept(ROWS, 1, dtype=single),
        ],
        in_specs=[pl.BlockSpec(memory_space=pltpu.SMEM)] + [whole_spec()] * 5,
        out_specs=[
            pl.BlockSpec((ROWS, D), lambda i: (0, 0)),
            pl.BlockSpec((3, None, ROWS, D), lambda i: (0, i, 0, 0)),
            by_layer(ROWS, 3 * D),
            by_layer(HEADS, ROWS, ROWS),
            by_layer(ROWS, D),
            by_layer(ROWS, 1),
            by_layer(ROWS, FF),
            pl.BlockSpec((FF, ROWS), lambda i: (0, i)),
            by_layer(ROWS, D),
            by_layer(ROWS, 1),
        ],
        scratch_shapes=[VMEM_SPACE((ROWS, D), single)],
        compiler_params=pltpu.CompilerParams(
            dimension_semantics=("arbitrary",), vmem_limit_bytes=VMEM_ASK
        ),
    )(lengths, start, wide, tall, vec, ff_b)
    return dict(zip(names, outs))


def backward_kernel(
    start,
    wide,
    tall,
    vec,
    projected,
    weighting,
    hat_one,
    inverse_one,
    slope,
    hat_two,
    inverse_two,
    result,
    turned,
    outer,
    sums,
    ff_sum,
    upstream,
    back_mixed,
    joint,
):
    step = pl.program_id(0)

    @pl.when(step == 0)
    def _():
        upstream[...] = start[...]
        sums[...] = jnp.zeros_like(sums)
        ff_sum[...] = jnp.zeros_like(ff_sum)

    def row(index):
        return vec[pl.ds(index, 1), :]

    def add_sum(index, value):
        here = pl.ds(index - Q_B, 1)
        sums[here, :] = sums[here, :] + jnp.sum(value, 0, keepdims=True)

    up = upstream[...]
    hat = hat_two[...]
    add_sum(LN2_G, up * hat)
    add_sum(LN2_B, up)
    back_second = norm_backward(up, row(LN2_G), hat, inverse_two[...])
    half = to_half(back_second)
    outer[...] = half
    add_sum(FFO_B, half.astype(jnp.float32))
    total = back_second
    for low in range(0, FF, CHUNK):
        lanes = pl.ds(low, CHUNK)
        inner = to_half(nt(half, tall[lanes, :]) * slope[:, lanes])
        ff_sum[:, lanes] = ff_sum[:, lanes] + jnp.sum(
            inner.astype(jnp.float32), 0, keepdims=True
        )
        turned[pl.ds(4 * D + low, CHUNK), :] = inner.T
        total = total + nn(inner, wide[pl.ds(4 * D + low, CHUNK), :])
    hat = hat_one[...]
    add_sum(LN1_G, total * hat)
    add_sum(LN1_B, total)
    back_first = norm_backward(total, row(LN1_G), hat, inverse_one[...])
    upstream[...] = back_first
    half = to_half(back_first)
    add_sum(O_B, half.astype(jnp.float32))
    turned[pl.ds(3 * D, D), :] = half.T
    back_mixed[...] = to_half(nn(half, wide[pl.ds(3 * D, D), :]))
    for pair in range(HEADS // 2):
        lanes = pair * PAIR
        queries = halves(projected[:, pl.ds(lanes, PAIR)])
        keys = halves(projected[:, pl.ds(D + lanes, PAIR)])
        values = projected[:, pl.ds(2 * D + lanes, PAIR)]
        grads = halves(back_mixed[:, pl.ds(lanes, PAIR)])
        zero = jnp.zeros((ROWS, PAIR), jnp.float32)
        back_query, back_key, back_value = zero, zero, zero
        for side in (0, 1):
            weights = weighting[2 * pair + side]
            soft = nt(grads[side], values)
            scores = to_half(
                weights * (soft - jnp.sum(weights * soft, -1, keepdims=True))
            )
            back_query = back_query + nn(scores, keys[side])
            back_key = back_key + tn(scores, queries[side])
            back_value = back_value + tn(to_half(weights), grads[side])
        joint[:, pl.ds(lanes, PAIR)] = to_half(back_query * SCALE)
        joint[:, pl.ds(D + lanes, PAIR)] = to_half(back_key * SCALE)
        joint[:, pl.ds(2 * D + lanes, PAIR)] = to_half(back_value)
    total = upstream[...]
    for part, bias in ((0, Q_B), (1, None), (2, V_B)):
        here = pl.ds(part * D, D)
        value = joint[:, here]
        if bias is not None:
            add_sum(bias, value.astype(jnp.float32))
        turned[here, :] = value.T
        total = total + nn(value, wide[here, :])
    upstream[...] = total
    result[...] = total


def run_backward(start, wide, tall, vec, kept):
    single, half = jnp.float32, jnp.bfloat16
    last = LAYERS - 1

    def order(i):
        return last - i

    return pl.pallas_call(
        backward_kernel,
        grid=(LAYERS,),
        out_shape=[
            jax.ShapeDtypeStruct((ROWS, D), single),
            jax.ShapeDtypeStruct((4 * D + FF, LAYERS * ROWS), half),
            jax.ShapeDtypeStruct((LAYERS, ROWS, D), half),
            jax.ShapeDtypeStruct((8, D), single),
            jax.ShapeDtypeStruct((1, FF), single),
        ],
        in_specs=[whole_spec()] * 4
        + [
            by_layer(ROWS, 3 * D, order=order),
            by_layer(HEADS, ROWS, ROWS, order=order),
            by_layer(ROWS, D, order=order),
            by_layer(ROWS, 1, order=order),
            by_layer(ROWS, FF, order=order),
            by_layer(ROWS, D, order=order),
            by_layer(ROWS, 1, order=order),
        ],
        out_specs=[
            pl.BlockSpec((ROWS, D), lambda i: (0, 0)),
            pl.BlockSpec((4 * D + FF, ROWS), lambda i: (0, order(i))),
            by_layer(ROWS, D, order=order),
            pl.BlockSpec((8, D), lambda i: (0, 0)),
            pl.BlockSpec((1, FF), lambda i: (0, 0)),
        ],
        scratch_shapes=[
            VMEM_SPACE((ROWS, D), single),
            VMEM_SPACE((ROWS, D), half),
            VMEM_SPACE((ROWS, 3 * D), half),
        ],
        compiler_params=pltpu.CompilerParams(
            dimension_semantics=("arbitrary",), vmem_limit_bytes=VMEM_ASK
        ),
    )(
        start,
        wide,
        tall,
        vec,
        kept["projected"],
        kept["weighting"],
        kept["hat_one"],
        kept["inverse_one"],
        kept["slope"],
        kept["hat_two"],
        kept["inverse_two"],
    )


def adam_update(weight, gradient, first, second, rate):
    first = BETA_ONE * first + (1 - BETA_ONE) * gradient
    second = BETA_TWO * second + (1 - BETA_TWO) * gradient * gradient
    first_hat = first / (1 - BETA_ONE**STEP)
    second_hat = second / (1 - BETA_TWO**STEP)
    updated = weight - rate * (
        first_hat / (jnp.sqrt(second_hat) + ADAM_EPSILON) + WEIGHT_DECAY * weight
    )
    return (updated, first, second)


def local(
    mesh,
    word_table,
    position_table,
    head_weights,
    decoder_bias,
    layer_wide,
    layer_tall,
    vectors,
    word_first,
    word_second,
    position_first,
    position_second,
    head_first,
    head_second,
    decoder_first,
    decoder_second,
    wide_first,
    wide_second,
    tall_first,
    tall_second,
    vector_first,
    vector_second,
    token_ids,
    seq_lengths,
    mlm_rows,
    mlm_labels,
    sop_labels,
):
    network = Network(mesh)
    own = lax.axis_index(AXES)
    words = word_table.shape[0]
    slots = mlm_labels.shape[0]
    pieces = split_vectors(vectors)
    token_kind = row_kind(seq_lengths)

    facts = jnp.concatenate([token_ids, mlm_labels, seq_lengths])
    padded = -(-facts.shape[0] // 1024) * 1024
    facts = jnp.pad(facts, (0, padded - facts.shape[0])).reshape(-1, 128)
    places_own = to_half(position_table).astype(jnp.float32)
    all_facts, place = network.gather_small([facts, places_own])
    all_facts = all_facts.reshape(-1, padded)
    place = place.reshape(-1, E)
    devices = all_facts.shape[0]
    all_ids = all_facts[:, :ROWS].reshape(-1)
    all_labels = all_facts[:, ROWS : ROWS + slots].reshape(-1)
    all_seconds = all_facts[:, ROWS + slots + 1] > 0
    all_used = (all_labels >= 0).astype(jnp.float32)
    mlm_count = jnp.sum(all_used)
    sop_count = devices + jnp.sum(all_seconds.astype(jnp.float32))
    scales = (1.0 / mlm_count, 1.0 / sop_count)

    word_half = to_half(word_table)
    wide, tall, head = network.gather(
        [to_half(layer_wide).T, to_half(layer_tall), to_half(head_weights).T]
    )

    offset = own * words
    column = jnp.arange(words, dtype=jnp.int32)
    select = to_half((all_ids - offset)[:, None] == column[None, :])
    (found,) = network.scatter([to_half(product(select, word_half))])
    two = seq_lengths[1] > 0
    place = place[:ROWS]
    placed = jnp.concatenate([place[:BUCKET], jnp.where(two, place[:BUCKET], place[BUCKET:])], 0)
    types = pieces["types"].reshape(2, E)
    embedded = (
        found
        + placed
        + jnp.where(token_kind[:, None] == 0, types[0:1], types[1:2])
    )
    embed_hat, embed_inverse = norm_forward(embedded)
    normed_half = to_half(embed_hat * pieces["emb_g"] + pieces["emb_b"])
    hidden = product(normed_half, head[E + D :]) + pieces["proj_b"]

    vec = vectors[: 10 * D].reshape(10, D)
    kept = run_forward(seq_lengths, hidden, wide, tall, vec, pieces["ff_b"][None])
    final = kept["final"]

    final_half = to_half(final)
    pick = to_half(mlm_rows[:, None] == jnp.arange(ROWS, dtype=jnp.int32)[None, :])
    picked = to_half(product(pick, final_half))
    dense = times_transpose(picked, head[:E]) + pieces["mlm_b"]
    mlm_hat, mlm_inverse = norm_forward(gelu_tanh(dense))
    rows_half = to_half(mlm_hat * pieces["mlm_g"] + pieces["mlm_lb"])
    lifted = -(-slots // 16) * 16
    (all_rows,) = network.gather_small([jnp.pad(rows_half, ((0, lifted - slots), (0, 0)))])
    all_rows = all_rows[:, :slots].reshape(-1, E)
    logits = times_transpose(all_rows, word_half) + to_half(decoder_bias).astype(jnp.float32)
    onehot = ((all_labels - offset)[:, None] == column[None, :]).astype(jnp.float32)
    own_top = jnp.max(logits, -1)
    own_total = jnp.sum(jnp.exp(logits - own_top[:, None]), -1)
    own_target = jnp.sum(logits * onehot, -1)
    stats = jnp.concatenate([own_top, own_total, own_target])
    lifted = -(-stats.shape[0] // 1024) * 1024
    (stats,) = network.gather_small(
        [jnp.pad(stats, (0, lifted - stats.shape[0])).reshape(-1, 128)]
    )
    stats = stats.reshape(devices, lifted)[:, : 3 * devices * slots]
    stats = stats.reshape(devices, 3, devices * slots)
    top = jnp.max(stats[:, 0], 0)
    total = jnp.sum(stats[:, 1] * jnp.exp(stats[:, 0] - top[None]), 0)
    log_total = jnp.log(total) + top
    mlm_sum = jnp.sum((log_total - jnp.sum(stats[:, 2], 0)) * all_used)
    logits_half = to_half(
        (jnp.exp(logits - top[:, None]) / total[:, None] - onehot) * (all_used * scales[0])[:, None]
    )
    back_decoder = column_sum(logits_half)
    back_word_head = transpose_times(logits_half, all_rows)
    back_rows = network.scatter_small(
        product(logits_half, word_half).reshape(devices, slots, E)
    )
    back_mlm_g = jnp.sum(back_rows * mlm_hat, 0)
    back_mlm_lb = jnp.sum(back_rows, 0)
    dense_half = to_half(
        norm_backward(back_rows, pieces["mlm_g"], mlm_hat, mlm_inverse) * gelu_slope(dense)
    )
    back_mlm = transpose_times(dense_half, picked)
    back_picked = product(dense_half, head[:E])
    back_final = lax.dot_general(
        pick.astype(jnp.float32), back_picked, (((0,), (0,)), ((), ())), precision=PRECISE
    )

    firsts = jnp.concatenate([final_half[0:1], final_half[BUCKET : BUCKET + 1]], 0)
    pooled = jnp.tanh(times_transpose(firsts, head[E : E + D]) + pieces["pool_b"])
    classifier = pieces["cls"].reshape(2, D)
    classes = jnp.sum(pooled[:, None] * classifier[None], -1)
    class_top = jnp.max(classes, -1, keepdims=True)
    class_powers = jnp.exp(classes - class_top)
    class_totals = jnp.sum(class_powers, -1, keepdims=True)
    class_onehot = (jnp.arange(2, dtype=jnp.int32)[None, :] == sop_labels[:, None]).astype(
        jnp.float32
    )
    present = jnp.stack([jnp.float32(1.0), two.astype(jnp.float32)])
    sop_sum = jnp.sum(
        (jnp.log(class_totals[:, 0]) + class_top[:, 0] - jnp.sum(classes * class_onehot, -1))
        * present
    )
    back_classes = (class_powers / class_totals - class_onehot) * (present * scales[1])[:, None]
    back_cls = jnp.sum(back_classes[:, :, None] * pooled[:, None], 0)
    back_pooled = jnp.sum(back_classes[:, :, None] * classifier[None], 1)
    pre_half = to_half(back_pooled * (1.0 - pooled * pooled))
    back_pool = transpose_times(pre_half, firsts)
    back_firsts = product(pre_half, head[E : E + D])
    row_index = jnp.arange(ROWS, dtype=jnp.int32)[:, None]
    back_final = (
        back_final
        + jnp.where(row_index == 0, back_firsts[0:1], 0.0)
        + jnp.where(row_index == BUCKET, back_firsts[1:2], 0.0)
    )

    back_hidden, turned, outer, layer_sums, ff_sum = run_backward(
        back_final, wide, tall, vec, kept
    )

    upstream_half = to_half(back_hidden)
    back_normed = times_transpose(upstream_half, head[E + D :])
    back_proj = transpose_times(normed_half, upstream_half)
    back_embedded = norm_backward(back_normed, pieces["emb_g"], embed_hat, embed_inverse)
    back_head = jnp.concatenate([back_mlm, back_pool, back_proj], 0)
    kind_one = jnp.sum(jnp.where(token_kind[:, None] == 1, back_embedded, 0.0), 0)
    kind_zero = jnp.sum(jnp.where(token_kind[:, None] == 0, back_embedded, 0.0), 0)
    vector_grad = join_vectors(
        {
            "proj_b": column_sum(upstream_half),
            "layer": layer_sums,
            "pool_b": column_sum(pre_half),
            "cls": back_cls,
            "ff_b": ff_sum,
            "emb_g": jnp.sum(back_normed * embed_hat, 0),
            "emb_b": jnp.sum(back_normed, 0),
            "mlm_b": column_sum(dense_half),
            "mlm_g": back_mlm_g,
            "mlm_lb": back_mlm_lb,
            "types": jnp.concatenate([kind_zero, kind_one]),
        }
    )
    sum_wide, sum_tall, sum_head, all_back, own_vector = network.finish(
        turned,
        kept["active"],
        kept["rights"].reshape(3, -1, D),
        outer.reshape(-1, D),
        back_head,
        to_half(back_embedded),
        vector_grad,
    )
    back_word = back_word_head + transpose_times(select, all_back)
    places = position_table.shape[0]
    by_device = all_back.reshape(devices, ROWS, E)
    folded = by_device[:, :BUCKET].astype(jnp.float32) + jnp.where(
        all_seconds[:, None, None], by_device[:, BUCKET:].astype(jnp.float32), 0.0
    )
    rest = jnp.where(all_seconds[:, None, None], 0.0, by_device[:, BUCKET:].astype(jnp.float32))
    all_place = jnp.concatenate([jnp.sum(folded, 0), jnp.sum(rest, 0)], 0)
    all_place = jnp.pad(all_place, ((0, places * devices - ROWS), (0, 0)))
    back_place = lax.dynamic_slice(all_place, (own * places, 0), (places, E))
    shards = (back_word, back_place, sum_head.T, back_decoder, sum_wide.T, sum_tall)
    local_squares = jnp.sum(jnp.stack([jnp.sum(s * s) for s in shards]))
    total = vector_grad.shape[0]
    share = -(-total // (devices * 1024)) * 1024
    scalars = jnp.stack([sop_sum, local_squares])
    scalars = jnp.pad(scalars, (0, 1024 - scalars.shape[0])).reshape(8, 128)
    (last,) = network.gather_small([jnp.concatenate([own_vector, scalars], 0)])
    reduced = last[:, : share // 128].reshape(-1)[:total]
    sop_total = jnp.sum(last[:, share // 128, 0])
    grad_norm = jnp.sqrt(jnp.sum(last[:, share // 128, 1]) + jnp.sum(reduced * reduced))
    factor = jnp.minimum(1.0, CLIP_NORM / (grad_norm + NORM_EPSILON))
    updates = []
    for weight, gradient, first, second, rate in (
        (word_table, shards[0], word_first, word_second, LEARN_RATE),
        (position_table, shards[1], position_first, position_second, LEARN_RATE),
        (head_weights, shards[2], head_first, head_second, LEARN_RATE),
        (decoder_bias, shards[3], decoder_first, decoder_second, LEARN_RATE),
        (layer_wide, shards[4], wide_first, wide_second, LEARN_RATE),
        (layer_tall, shards[5], tall_first, tall_second, LEARN_RATE),
        (vectors, reduced, vector_first, vector_second, SMALL_RATE),
    ):
        updates.extend(adam_update(weight, factor * gradient, first, second, rate))
    return (*updates, mlm_sum, mlm_count, sop_total, sop_count, grad_norm)


def solution(mesh):
    rows = P(AXES, None)
    columns = P(None, AXES)
    flat = P(AXES)
    whole = P()
    return jax.shard_map(
        functools.partial(local, mesh),
        mesh=mesh,
        in_specs=(rows, rows, columns, flat, columns, rows, whole)
        + (rows, rows) * 2
        + (columns, columns, flat, flat, columns, columns, rows, rows, whole, whole)
        + (flat,) * 5,
        out_specs=(rows,) * 6
        + (columns,) * 3
        + (flat,) * 3
        + (columns,) * 3
        + (rows,) * 3
        + (whole,) * 8,
        check_vma=False,
    )
```

```python
import functools

import jax
import jax.numpy as jnp
from jax import lax
from jax.experimental import pallas as pl
from jax.experimental.pallas import tpu as pltpu
from jax.sharding import PartitionSpec as P

D = 768
HEADS = 12
HEAD_DIM = 64
FF = 3072
E = 128
LAYERS = 4
STEP = 10
BUCKET = 128
ROWS = 2 * BUCKET

PRECISE = lax.Precision.HIGHEST
EPSILON = 1e-06
LEARN_RATE = 0.1
SMALL_RATE = 0.5
BETA_ONE = 0.9
BETA_TWO = 0.999
ADAM_EPSILON = 1e-08
WEIGHT_DECAY = 0.01
CLIP_NORM = 0.005
NORM_EPSILON = 1e-06
MASKED = -1e30
SCALE = HEAD_DIM ** (-0.5)
AXES = ("dp", "fsdp")


def to_half(x):
    return x.astype(jnp.bfloat16)


def product(a, b):
    return jnp.dot(a, b, preferred_element_type=jnp.float32)


def times_transpose(a, b):
    return lax.dot_general(a, b, (((1,), (1,)), ((), ())), preferred_element_type=jnp.float32)


def transpose_times(a, b):
    return lax.dot_general(a, b, (((0,), (0,)), ((), ())), preferred_element_type=jnp.float32)


def column_sum(x):
    return jnp.sum(x.astype(jnp.float32), 0)


def norm_forward(x):
    centre = x - jnp.mean(x, -1, keepdims=True)
    inverse = lax.rsqrt(jnp.mean(centre * centre, -1, keepdims=True) + EPSILON)
    return centre * inverse, inverse


def norm_backward(upstream, factor, hat, inverse):
    scaled = upstream * factor
    return inverse * (
        scaled
        - jnp.mean(scaled, -1, keepdims=True)
        - hat * jnp.mean(scaled * hat, -1, keepdims=True)
    )


GELU_A = 0.7978845608028654
GELU_B = 0.044715


MESH_ID = pl.DeviceIdType.MESH
VMEM_SPACE = pltpu.VMEM
VMEM_ASK = 60 * 1024 * 1024


def greet(peers):
    barrier = pltpu.get_barrier_semaphore()
    count = 0
    for present, who in peers:
        if present is None:
            pl.semaphore_signal(barrier, inc=1, device_id=who, device_id_type=MESH_ID)
            count = count + 1
        else:

            @pl.when(present)
            def _(who=who):
                pl.semaphore_signal(barrier, inc=1, device_id=who, device_id_type=MESH_ID)

            count = count + present.astype(jnp.int32)
    pl.semaphore_wait(barrier, count)


def maybe(condition, action):
    if condition is None:
        action()
    else:
        pl.when(condition)(action)


def remote(source, target, send, receive, who):
    return pltpu.make_async_remote_copy(
        src_ref=source,
        dst_ref=target,
        send_sem=send,
        recv_sem=receive,
        device_id=who,
        device_id_type=MESH_ID,
    )


def small_gather_kernel(count, planes, width, *refs):
    ins, outs = refs[:count], refs[count : 2 * count]
    send_z, recv_z, send_f, recv_f = refs[2 * count :]
    z, f = lax.axis_index("dp"), lax.axis_index("fsdp")
    line = [(lax.rem(z + d, planes), f) for d in range(1, planes)]
    plane = [(z, lax.rem(f + d, width)) for d in range(1, width)]
    greet([(None, who) for who in line + plane])
    first = [
        remote(ins[i], outs[i].at[z, f], send_z.at[i, d], recv_z.at[i, d], who)
        for d, who in enumerate(line)
        for i in range(count)
    ]
    for copy in first:
        copy.start()
    for i in range(count):
        outs[i][z, f] = ins[i][...]
    for copy in first:
        copy.wait_recv()
    second = [
        remote(outs[i].at[:, f], outs[i].at[:, f], send_f.at[i, d], recv_f.at[i, d], who)
        for d, who in enumerate(plane)
        for i in range(count)
    ]
    for copy in second:
        copy.start()
    for d in range(1, width):
        other = lax.rem(f - d + width, width)
        for i in range(count):
            remote(
                outs[i].at[:, other],
                outs[i].at[:, other],
                send_f.at[i, d - 1],
                recv_f.at[i, d - 1],
                (z, f),
            ).wait_recv()
    for copy in first + second:
        copy.wait_send()


def small_gather(arrays, mesh_shape, identity):
    planes, width = mesh_shape
    count = len(arrays)
    return pl.pallas_call(
        functools.partial(small_gather_kernel, count, planes, width),
        out_shape=[
            jax.ShapeDtypeStruct((planes, width, *a.shape), a.dtype) for a in arrays
        ],
        in_specs=[pl.BlockSpec(memory_space=VMEM_SPACE)] * count,
        out_specs=[pl.BlockSpec(memory_space=VMEM_SPACE)] * count,
        scratch_shapes=[
            pltpu.SemaphoreType.DMA((count, planes)),
            pltpu.SemaphoreType.DMA((count, planes)),
            pltpu.SemaphoreType.DMA((count, width)),
            pltpu.SemaphoreType.DMA((count, width)),
        ],
        compiler_params=pltpu.CompilerParams(
            collective_id=identity, has_side_effects=True, vmem_limit_bytes=VMEM_ASK
        ),
    )(*arrays)


def small_scatter_kernel(planes, width, x, out, first_in, middle, second_in, *sems):
    send_f, recv_f, send_z, recv_z = sems
    z, f = lax.axis_index("dp"), lax.axis_index("fsdp")
    line = [(lax.rem(z + d, planes), f) for d in range(1, planes)]
    plane = [(z, lax.rem(f + d, width)) for d in range(1, width)]
    greet([(None, who) for who in line + plane])
    first = [
        remote(x.at[:, who[1]], first_in.at[d], send_f.at[d], recv_f.at[d], who)
        for d, who in enumerate(plane)
    ]
    for copy in first:
        copy.start()
    total = x[:, f]
    for d, copy in enumerate(first):
        copy.wait_recv()
        total = total + first_in[d]
    middle[...] = total
    second = [
        remote(middle.at[who[0]], second_in.at[d], send_z.at[d], recv_z.at[d], who)
        for d, who in enumerate(line)
    ]
    for copy in second:
        copy.start()
    total = middle[z]
    for d, copy in enumerate(second):
        copy.wait_recv()
        total = total + second_in[d]
    out[...] = total
    for copy in first + second:
        copy.wait_send()


def small_scatter(x, mesh_shape, identity):
    planes, width = mesh_shape
    block = x.shape[2:]
    return pl.pallas_call(
        functools.partial(small_scatter_kernel, planes, width),
        out_shape=jax.ShapeDtypeStruct(block, x.dtype),
        in_specs=[pl.BlockSpec(memory_space=VMEM_SPACE)],
        out_specs=pl.BlockSpec(memory_space=VMEM_SPACE),
        scratch_shapes=[
            VMEM_SPACE((width - 1, planes, *block), x.dtype),
            VMEM_SPACE((planes, *block), x.dtype),
            VMEM_SPACE((planes - 1, *block), x.dtype),
            pltpu.SemaphoreType.DMA((width - 1,)),
            pltpu.SemaphoreType.DMA((width - 1,)),
            pltpu.SemaphoreType.DMA((planes - 1,)),
            pltpu.SemaphoreType.DMA((planes - 1,)),
        ],
        compiler_params=pltpu.CompilerParams(
            collective_id=identity, has_side_effects=True, vmem_limit_bytes=VMEM_ASK
        ),
    )(x)


OWN, ACROSS_X, ACROSS_Y, DIAGONAL = 0, 1, 2, 3


def cuts_of(rows):
    tail = max(32, round(rows * 0.22 / 32) * 32)
    head = rows - tail
    return ((0, head), (head, rows))


def half_of(span, which):
    low, high = span
    middle = (low + high) // 2
    return (low, middle) if which == 0 else (middle, high)


def places():
    z, f = lax.axis_index("dp"), lax.axis_index("fsdp")
    q, c = f // 2, lax.rem(f, 2)
    qx = q + 1 - 2 * lax.rem(q, 2)
    qy = lax.rem(q + 2, 4)
    qd = qx + qy - q
    return z, c, (q, qx, qy, qd)


def gather_stages(planes, rows, members, x, outs, buf, sems, where, opening):
    out_sem, send, recv, side_send, side_recv = sems
    z, c, cols = where
    cuts = cuts_of(rows)
    at_x, at_y, mate = (z, cols[1] * 2 + c), (z, cols[2] * 2 + c), (z, cols[0] * 2 + 1 - c)
    above, below = z < planes - 1, z > 0
    up, down = (z + 1, cols[0] * 2 + c), (z - 1, cols[0] * 2 + c)
    sent = []

    def block(zs, col, core, span):
        return buf.at[zs, cols[col], core, pl.ds(span[0], span[1] - span[0])]

    def push(condition, zs, col, span, who, slot, receive, mine=False):
        def make():
            here = block(zs, col, c, span)
            source = x.at[pl.ds(span[0], span[1] - span[0])] if mine else here
            return remote(source, here, send.at[slot[0], zs, slot[1]], receive, who)

        maybe(condition, lambda: make().start())
        sent.append((condition, make))

    def await_block(zs, col, span, receive, core=None):
        here = block(zs, col, c if core is None else core, span)
        remote(here, here, send.at[0, 0, 0], receive, mate).wait_recv()

    def deliver(zs, col, core, span):
        for index, (out, (low, high)) in enumerate(zip(outs, members)):
            first, last = max(low, span[0]), min(high, span[1])
            if first < last:
                pltpu.make_async_copy(
                    buf.at[zs, cols[col], core, pl.ds(first, last - first)],
                    out.at[zs, cols[col], core, pl.ds(first - low, last - first)],
                    out_sem.at[index],
                ).start()

    def share(condition, part, zs, col, span, kind, mine=False):
        def make():
            here = block(zs, col, c, span)
            source = x.at[pl.ds(span[0], span[1] - span[0])] if mine else here
            return remote(
                source, here, side_send.at[part, zs, kind], side_recv.at[part, zs, kind], mate
            )

        def action():
            make().start()
            if not mine:
                deliver(zs, col, c, span)

        maybe(condition, action)
        sent.append((condition, make))
        shared.append((condition, part, zs, col, span, kind))

    shared = []
    whole = [cuts[0], cuts[1]]
    for part in (0, 1):
        push(above, z, OWN, whole[part], up, (part, 2), recv.at[part, z, OWN], True)
        push(below, z, OWN, whole[part], down, (part, 3), recv.at[part, z, OWN], True)
    for part in (1, 0):
        if part == 0:
            opening()
        push(None, z, OWN, whole[part], at_x, (part, 0), recv.at[part, z, ACROSS_X], True)
        push(None, z, OWN, whole[part], at_y, (part, 1), recv.at[part, z, ACROSS_Y], True)
    for part in (0, 1):
        share(None, part, z, OWN, whole[part], 0, True)
    own_copy = pltpu.make_async_copy(x, buf.at[z, cols[0], c], out_sem.at[len(members)])
    own_copy.start()

    def turn(condition, part, zs):
        span = whole[part]
        for col, which, who, slot in ((ACROSS_X, 1, at_y, 4), (ACROSS_Y, 0, at_x, 5)):
            maybe(
                condition,
                lambda col=col: await_block(zs, col, span, recv.at[part, zs, col]),
            )
            push(condition, zs, col, half_of(span, which), who, (part, slot), recv.at[part, zs, 4 + which])
            if part == 1:
                push(above, zs, col, span, up, (1, 4 + 2 * col), recv.at[1, zs, col])
                push(below, zs, col, span, down, (1, 5 + 2 * col), recv.at[1, zs, col])
            share(condition, part, zs, col, span, col)

    yield
    turn(None, 1, z)
    yield
    for which in (0, 1):
        await_block(z, DIAGONAL, half_of(whole[1], which), recv.at[1, z, 4 + which])
    push(above, z, DIAGONAL, whole[1], up, (1, 10), recv.at[1, z, DIAGONAL])
    push(below, z, DIAGONAL, whole[1], down, (1, 11), recv.at[1, z, DIAGONAL])
    share(None, 1, z, DIAGONAL, whole[1], 3)
    yield
    turn(None, 0, z)

    def settle(upto):
        while len(shared) > upto:
            condition, part, zs, col, span, kind = shared.pop(0)

            def action():
                await_block(zs, col, span, side_recv.at[part, zs, kind], 1 - c)
                deliver(zs, col, 1 - c, span)

            maybe(condition, action)

    for step in range(1, planes):
        yield
        ways = ((z - step >= 0, z - step, above, up), (z + step < planes, z + step, below, down))
        for valid, zs, further, onward in ways:
            go = jnp.logical_and(valid, further)
            pl.when(valid)(
                lambda zs=zs: await_block(zs, OWN, whole[0], recv.at[0, zs, OWN])
            )
            push(go, zs, OWN, whole[0], onward, (0, 2), recv.at[0, zs, OWN])
            push(valid, zs, OWN, whole[0], at_x, (0, 0), recv.at[0, zs, ACROSS_X])
            push(valid, zs, OWN, whole[0], at_y, (0, 1), recv.at[0, zs, ACROSS_Y])
            share(valid, 0, zs, OWN, whole[0], 0)
        yield
        for valid, zs, further, onward in ways:
            go = jnp.logical_and(valid, further)
            for col in (OWN, ACROSS_X, ACROSS_Y, DIAGONAL):
                pl.when(valid)(
                    lambda zs=zs, col=col: await_block(zs, col, whole[1], recv.at[1, zs, col])
                )
                push(go, zs, col, whole[1], onward, (1, col), recv.at[1, zs, col])
                share(valid, 1, zs, col, whole[1], col)
        yield
        for valid, zs, further, onward in ways:
            turn(valid, 0, zs)
        settle(8)
    yield
    own_copy.wait()
    deliver(z, OWN, c, (0, rows))
    everywhere = [(None, z)] + [
        (valid, zs)
        for step in range(1, planes)
        for valid, zs in ((z - step >= 0, z - step), (z + step < planes, z + step))
    ]
    for condition, zs in everywhere:
        for which in (0, 1):
            span = half_of(whole[0], which)
            maybe(
                condition,
                lambda zs=zs, which=which, span=span: await_block(
                    zs, DIAGONAL, span, recv.at[0, zs, 4 + which]
                ),
            )
            share(condition, 0, zs, DIAGONAL, span, 3 + which)
    settle(0)
    for condition, make in sent:
        maybe(condition, lambda make=make: make().wait_send())
    for index, (out, (low, high)) in enumerate(zip(outs, members)):
        pltpu.make_async_copy(
            buf.at[:, :, :, pl.ds(low, high - low)], out, out_sem.at[index]
        ).wait()


def select_stages(planes, facts, own_word, found, refs, where, offset):
    part, side, plane_in, middle, line_in, turned, sems_send, sems_recv = refs
    z, c, cols = where
    q = cols[0]
    f = q * 2 + c
    mate = (z, q * 2 + 1 - c)
    words = own_word.shape[0]
    line = [(lax.rem(z + d, planes), f) for d in range(1, planes)]
    turned[...] = to_half(own_word[...].T)
    yield

    def mate_message(col):
        return remote(
            part.at[:, col, 1 - c], side.at[:, col], sems_send.at[0, col], sems_recv.at[0, col], mate
        )

    def plane_message(col):
        return remote(
            part.at[:, col, c],
            plane_in.at[col],
            sems_send.at[1, col],
            sems_recv.at[1, col],
            (z, cols[col] * 2 + c),
        )

    def line_message(d, who):
        return remote(
            middle.at[who[0]], line_in.at[d], sems_send.at[2, d], sems_recv.at[2, d], who
        )

    def merge(col):
        mate_message(col).wait_recv()
        for zt in range(planes):
            part[zt, col, c] = part[zt, col, c] + side[zt, col]
        if col != OWN:
            plane_message(col).start()

    order = (DIAGONAL, ACROSS_X, ACROSS_Y, OWN)
    for place, col in enumerate(order):

        def body(n, unused, col=col):
            zt, core = n // 2, lax.rem(n, 2)
            ids = facts[zt, cols[col] * 2 + core]
            row = lax.broadcasted_iota(jnp.int32, (words, BUCKET), 0) + offset
            picks = jnp.concatenate(
                [to_half((row == ids[i : i + 1, :]).astype(jnp.float32)) for i in (0, 1)], 1
            )
            part[zt, col, core] = to_half(nn(turned[...], picks))
            return unused

        lax.fori_loop(0, 2 * planes, body, 0)
        mate_message(col).start()
        if place > 0:
            merge(order[place - 1])
        yield
    merge(OWN)
    total = part[:, OWN, c]
    yield
    for col in order[:3]:
        plane_message(col).wait_recv()
        total = total + plane_in[col]
    middle[...] = total
    for d, who in enumerate(line):
        line_message(d, who).start()
    yield
    total = middle[z]
    for d, who in enumerate(line):
        line_message(d, who).wait_recv()
        total = total + line_in[d]
    found[...] = total.astype(jnp.float32).T
    for col in order:
        mate_message(col).wait_send()
    for col in order[:3]:
        plane_message(col).wait_send()
    for d, who in enumerate(line):
        line_message(d, who).wait_send()


PLAN = (1, 1, 1, 1, 1, 1, 1, 1, 1, 1, 1, 1, 1, 1)


def start_kernel(
    planes,
    rows,
    members,
    x,
    own_word,
    own_facts,
    own_place,
    *refs,
):
    width = 8
    count = len(members)
    outs, (facts, place, found) = refs[:count], refs[count : count + 3]
    buf = refs[count + 3]
    gather_sems = refs[count + 4 : count + 9]
    select_refs = refs[count + 9 : count + 17]
    line_send, line_recv, plane_send, plane_recv = refs[count + 17 :]
    where = places()
    z, c, cols = where
    f = cols[0] * 2 + c
    line = [(lax.rem(z + d, planes), f) for d in range(1, planes)]
    plane = [(z, lax.rem(f + d, width)) for d in range(1, width)]
    greet([(None, who) for who in line + plane])
    pairs = ((own_facts, facts), (own_place, place))

    def along(i, d, who):
        return remote(
            pairs[i][0], pairs[i][1].at[z, f], line_send.at[i, d], line_recv.at[i, d], who
        )

    def around(i, d, who, source):
        here = pairs[i][1].at[:, source]
        return remote(here, here, plane_send.at[i, d], plane_recv.at[i, d], who)

    for d, who in enumerate(line):
        for i in (0, 1):
            along(i, d, who).start()
    for own, everyone in pairs:
        everyone[z, f] = own[...]

    def opening():
        for d, who in enumerate(line):
            for i in (0, 1):
                along(i, d, who).wait_recv()
        for d, who in enumerate(plane):
            for i in (0, 1):
                around(i, d, who, f).start()

    gather = gather_stages(planes, rows, members, x, outs, buf, gather_sems, where, opening)
    offset = (z * width + f) * own_word.shape[0]
    select = select_stages(planes, facts, own_word, found, select_refs, where, offset)
    done = object()
    next(gather)
    next(select)
    for d in range(1, width):
        source = lax.rem(f - d + width, width)
        for i in (0, 1):
            around(i, d - 1, mate_of(where), source).wait_recv()
    for number in range(64):
        for unused in range(PLAN[number] if number < len(PLAN) else 1):
            next(select, done)
        if next(gather, done) is done:
            break
    for unused in select:
        pass
    for d, who in enumerate(line):
        for i in (0, 1):
            along(i, d, who).wait_send()
    for d, who in enumerate(plane):
        for i in (0, 1):
            around(i, d, who, f).wait_send()


def mate_of(where):
    z, c, cols = where
    return (z, cols[0] * 2 + 1 - c)


def run_start(x, heights, own_word, own_facts, own_place, mesh_shape, identity):
    planes, width = mesh_shape
    rows, columns = x.shape
    members, low = [], 0
    for height in heights:
        members.append((low, low + height))
        low += height
    half, single = jnp.bfloat16, jnp.float32
    vmem = pl.BlockSpec(memory_space=VMEM_SPACE)
    dma = pltpu.SemaphoreType.DMA
    words, features = own_word.shape
    block = (features, ROWS)
    *outs, facts, place, found = pl.pallas_call(
        functools.partial(start_kernel, planes, rows, tuple(members)),
        out_shape=[
            jax.ShapeDtypeStruct((planes, width // 2, 2, height, columns), half)
            for height in heights
        ]
        + [
            jax.ShapeDtypeStruct((planes, width, *own_facts.shape), own_facts.dtype),
            jax.ShapeDtypeStruct((planes, width, *own_place.shape), own_place.dtype),
            jax.ShapeDtypeStruct((ROWS, features), single),
        ],
        in_specs=[vmem] * 4,
        out_specs=[pl.BlockSpec(memory_space=pl.ANY)] * len(heights) + [vmem] * 3,
        scratch_shapes=[
            VMEM_SPACE((planes, width // 2, 2, rows, columns), half),
            dma((len(heights) + 1,)),
            dma((2, planes, 12)),
            dma((2, planes, 6)),
            dma((2, planes, 5)),
            dma((2, planes, 5)),
            VMEM_SPACE((planes, 4, 2, *block), half),
            VMEM_SPACE((planes, 4, *block), half),
            VMEM_SPACE((4, planes, *block), half),
            VMEM_SPACE((planes, *block), half),
            VMEM_SPACE((planes - 1, *block), half),
            VMEM_SPACE((features, words), half),
            dma((3, 4)),
            dma((3, 4)),
            dma((2, planes)),
            dma((2, planes)),
            dma((2, width)),
            dma((2, width)),
        ],
        compiler_params=pltpu.CompilerParams(
            collective_id=identity, has_side_effects=True, vmem_limit_bytes=VMEM_ASK
        ),
    )(x, own_word, own_facts, own_place)
    weights = [out.reshape(-1, columns) for out in outs]
    devices = planes * width
    return (
        weights,
        facts.reshape(devices, *own_facts.shape),
        place.reshape(devices, *own_place.shape),
        found,
    )


def accumulate(target, sources, height):
    step = 32

    def body(i, unused):
        rows = pl.ds(pl.multiple_of(i * step, step), step)
        total = sources[0][rows].astype(jnp.float32)
        for source in sources[1:]:
            total = total + source[rows].astype(jnp.float32)
        target[rows] = total.astype(target.dtype)
        return unused

    lax.fori_loop(0, height // step, body, 0)


ROWS_AT = 1


def far_first(i, z, planes):
    low = (2 * z < planes).astype(jnp.int32)
    falling = planes - 1 - i - (i >= planes - 1 - z).astype(jnp.int32)
    rising = i + (i >= z).astype(jnp.int32)
    last = (jnp.int32(i) == planes - 1).astype(jnp.int32)
    return last * z + (1 - last) * (low * falling + (1 - low) * rising)


def finish_kernel(
    planes,
    heights,
    split,
    left_wide,
    left_tall,
    rights,
    outer,
    head_grad,
    own_rows,
    vector_terms,
    out,
    all_rows,
    own_vector,
    both,
    side,
    half_in,
    full_in,
    line_in,
    tail_line,
    tail_half,
    tail_full,
    wide_buf,
    tall_buf,
    vector_in,
    vector_mid,
    vector_last,
    fetch,
    head_load,
    side_send,
    side_recv,
    send,
    recv,
    tail_send,
    tail_recv,
    row_send,
    row_recv,
    vec_send,
    vec_recv,
):
    width = 8
    wide_height, tall_height, head_height = heights
    rows = wide_height + tall_height + head_height
    z, c, cols = places()
    q = cols[0]
    f = q * 2 + c
    x, y = lax.rem(q, 2), q // 2
    cuts = cuts_of(rows)
    head, tail = cuts
    head_rows, tail_rows = head[1] - head[0], tail[1] - tail[0]
    at_x, at_y, mate = (z, cols[1] * 2 + c), (z, cols[2] * 2 + c), (z, q * 2 + 1 - c)
    above, below = z < planes - 1, z > 0
    up, down = (z + 1, f), (z - 1, f)
    line = [(lax.rem(z + d, planes), f) for d in range(1, planes)]
    plane = [(z, lax.rem(f + d, width)) for d in range(1, width)]
    greet([(None, who) for who in line + plane])
    order = (DIAGONAL, ACROSS_X, ACROSS_Y, OWN)
    sent = []

    def push(condition, make):
        maybe(condition, lambda: make().start())
        sent.append((condition, make))

    def piece(ref, span):
        return ref.at[pl.ds(span[0], span[1] - span[0])]

    def plane_at(i):
        return far_first(i, z, planes)

    def turn_of(n):
        m = n - 1 - 3 * (n == 0).astype(jnp.int32) + (n > 4 * planes - 4).astype(jnp.int32)
        group, j = (m + 4) // 4 - 1, lax.rem(m + 4, 4)
        ahead = (j == 0).astype(jnp.int32)
        return group + ahead, DIAGONAL * ahead + j * (j < 3).astype(jnp.int32)

    def chip_of(n):
        i, col = turn_of(n)
        flip_x, flip_y = lax.rem(col, 2), col // 2
        return plane_at(i) * 4 + 2 * lax.rem(y + flip_y, 2) + lax.rem(x + flip_x, 2)

    def fetches(n):
        k, slot = chip_of(n), lax.rem(n, 2)
        wide_rows = pl.ds(pl.multiple_of(k * 2 * wide_height, 16), 2 * wide_height)
        tall_rows = pl.ds(pl.multiple_of(k * 2 * tall_height, 16), 2 * tall_height)
        return (
            pltpu.make_async_copy(
                left_wide.at[wide_rows], wide_buf.at[slot], fetch.at[0, slot]
            ),
            pltpu.make_async_copy(
                left_tall.at[tall_rows], tall_buf.at[slot], fetch.at[1, slot]
            ),
        )

    for copy in fetches(jnp.int32(0)):
        copy.start()

    def vector_first(d, who):
        return remote(
            vector_terms.at[:, who[1]], vector_in.at[d], vec_send.at[0, d], vec_recv.at[0, d], who
        )

    def vector_second(d, who):
        return remote(
            vector_mid.at[who[0]], vector_last.at[d], vec_send.at[1, d], vec_recv.at[1, d], who
        )

    def row_line(d, who):
        return remote(
            own_rows, all_rows.at[z, q, c], row_send.at[0, d], row_recv.at[0, d], who
        )

    def row_plane(col):
        return remote(
            all_rows.at[:, q, c],
            all_rows.at[:, q, c],
            row_send.at[1, col],
            row_recv.at[1, col],
            (z, cols[col] * 2 + c),
        )

    def row_mate():
        return remote(
            all_rows.at[:, :, c], all_rows.at[:, :, c], row_send.at[2, 0], row_recv.at[2, 0], mate
        )

    for d, who in enumerate(line):
        push(None, functools.partial(row_line, d, who))
    for d, who in enumerate(plane):
        push(None, functools.partial(vector_first, d, who))
    all_rows[z, q, c] = own_rows[...]
    head_copies = []
    for col in order:
        copy = pltpu.make_async_copy(
            head_grad.at[:, cols[col]],
            both.at[:, col, :, pl.ds(wide_height + tall_height, head_height)],
            head_load.at[col],
        )
        copy.start()
        head_copies.append(copy)

    def side_message(zt, col):
        return remote(
            both.at[zt, col, 1 - c],
            side.at[zt, col],
            side_send.at[col, zt],
            side_recv.at[col, zt],
            mate,
        )

    def half_message(zt, which):
        return remote(
            piece(both.at[zt, DIAGONAL, c], half_of(head, which)),
            half_in.at[which, zt],
            send.at[0, which, zt],
            recv.at[0, which, zt],
            (at_x, at_y)[which],
        )

    def full_message(zt, which):
        return remote(
            piece(both.at[zt, (ACROSS_X, ACROSS_Y)[which], c], head),
            full_in.at[which, zt],
            send.at[1, which, zt],
            recv.at[1, which, zt],
            (at_x, at_y)[which],
        )

    def line_message(zt, way):
        return remote(
            piece(both.at[zt, OWN, c], head),
            line_in.at[way, zt],
            send.at[2, way, zt],
            recv.at[2, way, zt],
            (up, down)[way],
        )

    def tail_message(zt, way):
        return remote(
            both.at[zt, :, c, pl.ds(tail[0], tail_rows)],
            tail_line.at[way, zt],
            tail_send.at[way, zt],
            tail_recv.at[way, zt],
            (up, down)[way],
        )

    def merged(zt, col):
        side_message(zt, col).wait_recv()
        mine = both.at[zt, col, c]
        accumulate(mine, [mine, side.at[zt, col]], rows)

    def second(zt):
        for which, col in ((0, ACROSS_X), (1, ACROSS_Y)):
            half_message(zt, 1 - which).wait_recv()
            target = piece(both.at[zt, col, c], half_of(head, 1 - which))
            accumulate(target, [target, half_in.at[1 - which, zt]], head_rows // 2)
            full_message(zt, which).start()

    def tail_add(zt, way):
        tail_message(zt, way).wait_recv()
        for col in range(4):
            target = piece(both.at[zt, col, c], tail)
            accumulate(target, [target, tail_line.at[way, zt, col]], tail_rows)

    def onward(zt, add, message):
        for way, valid in ((0, zt > z), (1, zt < z)):
            behind = (below, above)[way]
            pl.when(jnp.logical_and(valid, behind))(functools.partial(add, zt, way))
            pl.when(valid)(lambda way=way: message(zt, way).start())

    def tail_step(zt):
        onward(zt, tail_add, tail_message)

    def line_add(zt, way):
        line_message(zt, way).wait_recv()
        mine = piece(both.at[zt, OWN, c], head)
        accumulate(mine, [mine, line_in.at[way, zt]], head_rows)

    def third(zt):
        for which in (0, 1):
            full_message(zt, which).wait_recv()
        base = [piece(both.at[zt, OWN, c], head), full_in.at[0, zt], full_in.at[1, zt]]
        accumulate(base[0], base, head_rows)
        onward(zt, line_add, line_message)

    def after(n):
        i, col = turn_of(n)
        zt = plane_at(i)
        merged(zt, col)

        @pl.when(col == DIAGONAL)
        def _():
            half_message(zt, 0).start()
            half_message(zt, 1).start()

        @pl.when(col == OWN)
        def _():
            second(zt)
            pl.when(i < planes - 1)(lambda: tail_step(zt))
            pl.when(i > 0)(lambda: third(plane_at(i - 1)))

    for copy in head_copies:
        copy.wait()

    def body(n, unused):
        for copy in fetches(n):
            copy.wait()

        @pl.when(n + 1 < 4 * planes)
        def _():
            for copy in fetches(n + 1):
                copy.start()

        (i, col), k, slot = turn_of(n), chip_of(n), lax.rem(n, 2)
        zt = plane_at(i)
        region = (k >= split[0]).astype(jnp.int32) + (k >= split[1]).astype(jnp.int32)
        product_wide = to_half(nn(wide_buf[slot], rights[region]))
        both[zt, col, 0, :wide_height] = product_wide[:wide_height]
        both[zt, col, 1, :wide_height] = product_wide[wide_height:]
        product_tall = to_half(nn(tall_buf[slot], outer[...]))
        here = slice(wide_height, wide_height + tall_height)
        both[zt, col, 0, here] = product_tall[:tall_height]
        both[zt, col, 1, here] = product_tall[tall_height:]
        side_message(zt, col).start()
        pl.when(n > 0)(lambda: after(n - 1))

        @pl.when(n == ROWS_AT)
        def _():
            for d, who in enumerate(line):
                row_line(d, who).wait_recv()
            for step in (ACROSS_X, ACROSS_Y, DIAGONAL):
                row_plane(step).start()
            total = vector_terms[:, f]
            for d, who in enumerate(plane):
                vector_first(d, who).wait_recv()
                total = total + vector_in[d]
            vector_mid[...] = total
            for d, who in enumerate(line):
                vector_second(d, who).start()

        return unused

    lax.fori_loop(0, 4 * planes, body, 0)
    after(jnp.int32(4 * planes - 1))
    for step in (ACROSS_X, ACROSS_Y, DIAGONAL):
        remote(
            all_rows.at[:, cols[step], c],
            all_rows.at[:, cols[step], c],
            row_send.at[1, step],
            row_recv.at[1, step],
            mate,
        ).wait_recv()
    push(None, row_mate)
    targets = [plane_at(i) for i in range(planes)]

    def tail_half_message(which):
        return remote(
            piece(both.at[z, DIAGONAL, c], half_of(tail, which)),
            tail_half.at[which],
            tail_send.at[2, which],
            tail_recv.at[2, which],
            (at_x, at_y)[which],
        )

    def tail_full_message(which):
        return remote(
            piece(both.at[z, (ACROSS_X, ACROSS_Y)[which], c], tail),
            tail_full.at[which],
            tail_send.at[3, which],
            tail_recv.at[3, which],
            (at_x, at_y)[which],
        )

    pl.when(below)(lambda: tail_add(z, 0))
    pl.when(above)(lambda: tail_add(z, 1))
    for which in (0, 1):
        push(None, functools.partial(tail_half_message, which))
    for which, col in ((1, ACROSS_X), (0, ACROSS_Y)):
        tail_half_message(which).wait_recv()
        target = piece(both.at[z, col, c], half_of(tail, which))
        accumulate(target, [target, tail_half.at[which]], tail_rows // 2)
    for which in (0, 1):
        push(None, functools.partial(tail_full_message, which))
    for which in (0, 1):
        full_message(z, which).wait_recv()
    goal = piece(out, head)
    accumulate(
        goal, [piece(both.at[z, OWN, c], head), full_in.at[0, z], full_in.at[1, z]], head_rows
    )
    for present, way in ((below, 0), (above, 1)):

        def add(way=way):
            line_message(z, way).wait_recv()
            accumulate(goal, [goal, line_in.at[way, z]], head_rows)

        pl.when(present)(add)
    for which in (0, 1):
        tail_full_message(which).wait_recv()
    accumulate(
        piece(out, tail),
        [piece(both.at[z, OWN, c], tail), tail_full.at[0], tail_full.at[1]],
        tail_rows,
    )
    total = vector_mid[z]
    for d, who in enumerate(line):
        vector_second(d, who).wait_recv()
        total = total + vector_last[d]
    own_vector[...] = total
    remote(
        all_rows.at[:, :, 1 - c],
        all_rows.at[:, :, 1 - c],
        row_send.at[2, 0],
        row_recv.at[2, 0],
        mate,
    ).wait_recv()
    for condition, make in sent:
        maybe(condition, lambda make=make: make().wait_send())
    for zt in targets:
        for col in order:
            side_message(zt, col).wait_send()
        for which in (0, 1):
            half_message(zt, which).wait_send()
            full_message(zt, which).wait_send()
        for way, valid in ((0, zt > z), (1, zt < z)):

            def done(zt=zt, way=way):
                tail_message(zt, way).wait_send()
                line_message(zt, way).wait_send()

            pl.when(valid)(done)
    for step in (ACROSS_X, ACROSS_Y, DIAGONAL):
        row_plane(step).wait_send()
    for d, who in enumerate(line):
        vector_second(d, who).wait_send()


def run_finish(
    left_wide, left_tall, rights, outer, head_grad, own_rows, vector_terms, mesh_shape, identity
):
    planes, width = mesh_shape
    devices = planes * width
    columns = outer.shape[1]
    heights = (
        left_wide.shape[0] // devices,
        left_tall.shape[0] // devices,
        head_grad.shape[0] // devices,
    )
    rows = sum(heights)
    long = left_wide.shape[1]
    split = (3 * D // (2 * heights[0]), 4 * D // (2 * heights[0]))
    head, tail = (high - low for low, high in cuts_of(rows))
    half, single = jnp.bfloat16, jnp.float32
    block = vector_terms.shape[1:]
    vmem = pl.BlockSpec(memory_space=VMEM_SPACE)
    any_space = pl.BlockSpec(memory_space=pl.ANY)
    dma = pltpu.SemaphoreType.DMA
    out, all_rows, own_vector = pl.pallas_call(
        functools.partial(finish_kernel, planes, heights, split),
        out_shape=[
            jax.ShapeDtypeStruct((rows, columns), single),
            jax.ShapeDtypeStruct((planes, width // 2, 2, *own_rows.shape), half),
            jax.ShapeDtypeStruct(block, single),
        ],
        in_specs=[any_space, any_space, vmem, vmem, any_space, vmem, vmem],
        out_specs=[vmem] * 3,
        scratch_shapes=[
            VMEM_SPACE((planes, 4, 2, rows, columns), half),
            VMEM_SPACE((planes, 4, rows, columns), half),
            VMEM_SPACE((2, planes, head // 2, columns), half),
            VMEM_SPACE((2, planes, head, columns), half),
            VMEM_SPACE((2, planes, head, columns), half),
            VMEM_SPACE((2, planes, 4, tail, columns), half),
            VMEM_SPACE((2, tail // 2, columns), half),
            VMEM_SPACE((2, tail, columns), half),
            VMEM_SPACE((2, 2 * heights[0], long), half),
            VMEM_SPACE((2, 2 * heights[1], long), half),
            VMEM_SPACE((width - 1, planes, *block), single),
            VMEM_SPACE((planes, *block), single),
            VMEM_SPACE((planes - 1, *block), single),
            dma((2, 2)),
            dma((4,)),
            dma((4, planes)),
            dma((4, planes)),
            dma((3, 2, planes)),
            dma((3, 2, planes)),
            dma((4, planes)),
            dma((4, planes)),
            dma((3, 4)),
            dma((3, 4)),
            dma((2, width)),
            dma((2, width)),
        ],
        compiler_params=pltpu.CompilerParams(
            collective_id=identity, has_side_effects=True, vmem_limit_bytes=VMEM_ASK
        ),
    )(
        left_wide,
        left_tall,
        rights,
        outer,
        head_grad.reshape(planes, width // 2, 2, heights[2], columns),
        own_rows,
        vector_terms.reshape(planes, width, *block),
    )
    return out, heights, all_rows.reshape(-1, own_rows.shape[1]), own_vector


LIFT = 128
WIRE = 48


def exact_rows(pick, values):
    first = to_half(values)
    rest = values - first.astype(jnp.float32)
    second = to_half(rest)
    third = to_half(rest - second.astype(jnp.float32))
    return nn(pick, first) + nn(pick, second) + nn(pick, third)


def lanes_to_rows(x):
    return jnp.concatenate([x[:, i : i + 128] for i in range(0, x.shape[1], 128)], 0)


def rows_to_lanes(x):
    return jnp.concatenate([x[i : i + 1] for i in range(x.shape[0])], 1)


def head_kernel(
    planes,
    lengths,
    sop_labels,
    scales,
    final,
    head,
    word,
    decoder,
    labels,
    own_facts,
    vec,
    small,
    cls,
    back_final,
    back_word,
    back_decoder,
    back_head,
    wide_sums,
    small_sums,
    totals,
    all_t,
    stats,
    powers,
    back_t,
    plane_in,
    middle,
    line_in,
    word_half,
    sends,
    recvs,
):
    width = 8
    z, c, cols = places()
    f = cols[0] * 2 + c
    line = [(lax.rem(z + d, planes), f) for d in range(1, planes)]
    plane = [(z, lax.rem(f + d, width)) for d in range(1, width)]
    greet([(None, who) for who in line + plane])
    offset = (z * width + f) * word.shape[0]
    words, slots = word.shape[0], planes * width * WIRE
    single = jnp.float32

    def gather_line(ref, kind):
        here = ref.at[z, f]
        return [
            remote(here, here, sends.at[kind, d], recvs.at[kind, d], who)
            for d, who in enumerate(line)
        ]

    def gather_plane(ref, kind):
        here = ref.at[:, f]
        return [
            remote(here, here, sends.at[kind, d], recvs.at[kind, d], who)
            for d, who in enumerate(plane)
        ]

    def await_line(ref, kind):
        for d in range(planes - 1):
            here = ref.at[lax.rem(z - d - 1 + planes, planes), f]
            remote(here, here, sends.at[kind, d], recvs.at[kind, d], line[d]).wait_recv()

    def await_plane(ref, kind):
        for d in range(width - 1):
            here = ref.at[:, lax.rem(f - d - 1 + width, width)]
            remote(here, here, sends.at[kind, d], recvs.at[kind, d], plane[d]).wait_recv()

    started = []

    def start(copies):
        for copy in copies:
            copy.start()
        started.extend(copies)

    final_half = to_half(final[...])
    place = lax.broadcasted_iota(jnp.int32, (ROWS, LIFT), 0)
    scatter = to_half((place == own_facts[3:4, :]).astype(single))
    pick = scatter.T
    picked = to_half(nn(pick, final_half))
    dense = nt(picked, head[:E, :]) + small[2:3, :]
    bend = jnp.tanh(GELU_A * dense * (1.0 + GELU_B * dense * dense))
    hat, inverse = norm_forward(0.5 * dense * (1.0 + bend))
    slope = 0.5 * (1.0 + bend) + (0.5 * GELU_A) * dense * (1.0 - bend * bend) * (
        1.0 + 3.0 * GELU_B * dense * dense
    )
    rows_half = to_half(hat * small[3:4, :] + small[4:5, :])
    all_t[z, f] = rows_half[:WIRE]
    start(gather_line(all_t, 0))

    word_half[...] = to_half(word[...])
    row16 = lax.broadcasted_iota(jnp.int32, (16, ROWS), 0)
    col16 = lax.broadcasted_iota(jnp.int32, (16, ROWS), 1)
    leads = to_half(
        (jnp.logical_and(row16 < 2, col16 == row16 * BUCKET)).astype(single)
    )
    firsts = to_half(nn(leads, final_half))
    pooled = jnp.tanh(nt(firsts, head[E : E + D, :]) + vec[POOL_B : POOL_B + 1, :])
    await_line(all_t, 0)
    start(gather_plane(all_t, 1))
    zero_class, one_class = cls[0:1, :], cls[1:2, :]
    c0 = jnp.sum(pooled * zero_class, -1, keepdims=True)
    c1 = jnp.sum(pooled * one_class, -1, keepdims=True)
    class_top = jnp.maximum(c0, c1)
    e0, e1 = jnp.exp(c0 - class_top), jnp.exp(c1 - class_top)
    class_total = e0 + e1
    which = lax.broadcasted_iota(jnp.int32, (16, 1), 0)
    label = jnp.where(which == 0, sop_labels[0], sop_labels[1])
    hit = (label == 1).astype(single)
    two = (lengths[1] > 0).astype(single)
    present = jnp.where(which == 0, 1.0, jnp.where(which == 1, two, 0.0))
    losses = (jnp.log(class_total) + class_top - (c0 + hit * (c1 - c0))) * present
    weight = present * scales[1]
    back_c0 = (e0 / class_total - (1.0 - hit)) * weight
    back_c1 = (e1 / class_total - hit) * weight
    wide_sums[1:2, :] = jnp.sum(back_c0 * pooled, 0, keepdims=True)
    wide_sums[2:3, :] = jnp.sum(back_c1 * pooled, 0, keepdims=True)
    pre_half = to_half((back_c0 * zero_class + back_c1 * one_class) * (1.0 - pooled * pooled))
    wide_sums[0:1, :] = jnp.sum(pre_half.astype(single), 0, keepdims=True)
    back_head[E : E + D, :] = to_half(tn(pre_half, firsts))
    back_firsts = nn(pre_half, head[E : E + D, :])
    await_plane(all_t, 1)

    row = lax.broadcasted_iota(jnp.int32, (words, 128), 0) + offset
    tops, sums, targets = [], [], []
    chunk = width * WIRE
    flat_t = all_t[...].reshape(slots, E)
    for low in range(0, slots, chunk):
        logits = nt(word_half[...], flat_t[low : low + chunk]) + decoder[...]
        top = jnp.max(logits, 0, keepdims=True)
        power = jnp.exp(logits - top)
        powers[:, pl.ds(low, chunk)] = power
        tops.append(top)
        sums.append(jnp.sum(power, 0, keepdims=True))
        for at in range(0, chunk, 128):
            mark = row == labels[:, low + at : low + at + 128]
            targets.append(
                jnp.sum(jnp.where(mark, logits[:, at : at + 128], 0.0), 0, keepdims=True)
            )
    own_top = lanes_to_rows(jnp.concatenate(tops, 1))
    groups = slots // 128
    stats[z, f, 0:groups] = own_top
    stats[z, f, groups : 2 * groups] = lanes_to_rows(jnp.concatenate(sums, 1))
    start(gather_line(stats, 2))
    used = (lanes_to_rows(labels[...]) >= 0).astype(single)
    target = jnp.sum(jnp.concatenate(targets, 0) * used)
    await_line(stats, 2)
    start(gather_plane(stats, 3))
    await_plane(stats, 3)
    every = stats[...].reshape(planes * width, 2 * groups, 128)
    top = jnp.max(every[:, :groups], 0)
    total = jnp.sum(every[:, groups:] * jnp.exp(every[:, :groups] - top[None]), 0)
    log_sum = jnp.sum((jnp.log(total) + top) * used)
    weight = used * scales[0]
    factor = rows_to_lanes(weight * jnp.exp(own_top - top) / total)
    weight = rows_to_lanes(weight)

    def slot_terms(zz, d, who):
        return remote(
            back_t.at[zz, who[1]],
            plane_in.at[d, zz],
            sends.at[4 + zz, d],
            recvs.at[4 + zz, d],
            who,
        )

    words_total = jnp.zeros((words, E), single)
    lane_total = jnp.zeros((words, 1), single)
    for low in range(0, slots, chunk):
        parts = []
        for at in range(low, low + chunk, 128):
            mark = row == labels[:, at : at + 128]
            part = powers[:, pl.ds(at, 128)] * factor[:, at : at + 128] - jnp.where(
                mark, weight[:, at : at + 128], 0.0
            )
            parts.append(to_half(part))
        half = jnp.concatenate(parts, 1)
        lane_total = lane_total + jnp.sum(half.astype(single), 1, keepdims=True)
        words_total = words_total + nn(half, flat_t[low : low + chunk])
        zz = low // chunk
        back_t[zz] = tn(half, word_half[...]).reshape(width, WIRE, E)
        start([slot_terms(zz, d, who) for d, who in enumerate(plane)])
    back_word[...] = words_total
    back_decoder[...] = lane_total

    for zz in range(planes):
        total = back_t[zz, f]
        for d in range(width - 1):
            slot_terms(zz, d, plane[d]).wait_recv()
            total = total + plane_in[d, zz]
        middle[zz] = total
    start(
        [
            remote(middle.at[who[0]], line_in.at[d], sends.at[4 + planes, d], recvs.at[4 + planes, d], who)
            for d, who in enumerate(line)
        ]
    )
    total = middle[z]
    for d in range(planes - 1):
        remote(
            line_in.at[d], line_in.at[d], sends.at[4 + planes, d], recvs.at[4 + planes, d], line[d]
        ).wait_recv()
        total = total + line_in[d]
    back_rows = jnp.concatenate([total, jnp.zeros((LIFT - WIRE, E), single)], 0)
    small_sums[1:2, :] = jnp.sum(back_rows * hat, 0, keepdims=True)
    small_sums[2:3, :] = jnp.sum(back_rows, 0, keepdims=True)
    dense_half = to_half(norm_backward(back_rows, small[3:4, :], hat, inverse) * slope)
    small_sums[0:1, :] = jnp.sum(dense_half.astype(single), 0, keepdims=True)
    back_head[:E, :] = to_half(tn(dense_half, picked))
    back_final[...] = exact_rows(scatter, nn(dense_half, head[:E, :]))
    back_final[0:1, :] = back_final[0:1, :] + back_firsts[0:1]
    back_final[BUCKET : BUCKET + 1, :] = back_final[BUCKET : BUCKET + 1, :] + back_firsts[1:2]
    lane = lax.broadcasted_iota(jnp.int32, (1, 128), 1)
    sop_sum = jnp.sum(losses)
    totals[...] = jnp.where(
        lane == 0, log_sum, jnp.where(lane == 1, target, jnp.where(lane == 2, sop_sum, 0.0))
    )
    for copy in started:
        copy.wait_send()


def run_head(
    lengths, sop_labels, scales, final, head, word, decoder, labels, own_facts, vec, small, cls, mesh_shape, identity
):
    planes, width = mesh_shape
    words = word.shape[0]
    slots = planes * width * WIRE
    groups = slots // 128
    single, half = jnp.float32, jnp.bfloat16
    vmem = pl.BlockSpec(memory_space=VMEM_SPACE)
    smem = pl.BlockSpec(memory_space=pltpu.SMEM)
    dma = pltpu.SemaphoreType.DMA
    return pl.pallas_call(
        functools.partial(head_kernel, planes),
        out_shape=[
            jax.ShapeDtypeStruct((ROWS, D), single),
            jax.ShapeDtypeStruct((words, E), single),
            jax.ShapeDtypeStruct((words, 1), single),
            jax.ShapeDtypeStruct((E + D, D), half),
            jax.ShapeDtypeStruct((3, D), single),
            jax.ShapeDtypeStruct((3, E), single),
            jax.ShapeDtypeStruct((1, 128), single),
        ],
        in_specs=[smem] * 3 + [vmem] * 9,
        out_specs=[vmem] * 7,
        scratch_shapes=[
            VMEM_SPACE((planes, width, WIRE, E), half),
            VMEM_SPACE((planes, width, 2 * groups, 128), single),
            VMEM_SPACE((words, slots), single),
            VMEM_SPACE((planes, width, WIRE, E), single),
            VMEM_SPACE((width - 1, planes, WIRE, E), single),
            VMEM_SPACE((planes, WIRE, E), single),
            VMEM_SPACE((planes - 1, WIRE, E), single),
            VMEM_SPACE((words, E), half),
            dma((5 + planes, width)),
            dma((5 + planes, width)),
        ],
        compiler_params=pltpu.CompilerParams(
            collective_id=identity, has_side_effects=True, vmem_limit_bytes=VMEM_ASK
        ),
    )(lengths, sop_labels, scales, final, head, word, decoder, labels, own_facts, vec, small, cls)


class Network:
    def __init__(self, mesh):
        self.shape = (mesh.shape["dp"], mesh.shape["fsdp"])
        self.devices = self.shape[0] * self.shape[1]
        self.kernels = self.shape[1] == 8
        self.calls = 0

    def identity(self):
        self.calls += 1
        return self.calls

    def gather_small(self, blocks):
        if not self.kernels:
            return [lax.all_gather(b, AXES) for b in blocks]
        gathered = small_gather(blocks, self.shape, self.identity())
        return [g.reshape(self.devices, *g.shape[2:]) for g in gathered]

    def scatter_small(self, blocks):
        if not self.kernels:
            return lax.psum_scatter(blocks, AXES, scatter_dimension=0)
        return small_scatter(
            blocks.reshape(*self.shape, *blocks.shape[1:]), self.shape, self.identity()
        )

    def start(self, shards, own_word, own_facts, own_place):
        if self.kernels:
            heights = tuple(shard.shape[0] for shard in shards)
            packed = jnp.concatenate([to_half(shard) for shard in shards], 0)
            return run_start(
                packed, heights, own_word, own_facts, own_place, self.shape, self.identity()
            )
        weights = [lax.all_gather(to_half(w), AXES, axis=0, tiled=True) for w in shards]
        facts, place = self.gather_small([own_facts, own_place])
        words = own_word.shape[0]
        ids = facts[:, : ROWS // 128].reshape(-1) - lax.axis_index(AXES) * words
        column = jnp.arange(words, dtype=jnp.int32)
        select = to_half(ids[:, None] == column[None, :])
        terms = product(select, to_half(own_word))
        found = lax.psum_scatter(terms, AXES, scatter_dimension=0, tiled=True)
        return weights, facts, place, found

    def head(
        self, lengths, sop_labels, scales, final, head, word, decoder, facts, own_facts, vec, small, cls
    ):
        labels = facts[:, 2, :WIRE].reshape(1, -1)
        decoder = to_half(decoder).astype(jnp.float32)[:, None]
        given = (lengths, sop_labels, scales, final, head, word, decoder, labels, own_facts)
        given = (*given, vec, small, cls)
        if self.kernels:
            return run_head(*given, self.shape, self.identity())
        return self.plain_head(*given)

    def plain_head(
        self, lengths, sop_labels, scales, final, head, word, decoder, labels, own_facts, vec, small, cls
    ):
        single = jnp.float32
        offset = lax.axis_index(AXES) * word.shape[0]
        word_half, final_half = to_half(word), to_half(final)
        rows = own_facts[3, :WIRE]
        pick = (rows[:, None] == jnp.arange(ROWS, dtype=jnp.int32)[None]).astype(single)
        picked = to_half(product(to_half(pick), final_half))
        dense = times_transpose(picked, head[:E]) + small[MLM_B]
        bend = jnp.tanh(GELU_A * dense * (1.0 + GELU_B * dense * dense))
        hat, inverse = norm_forward(0.5 * dense * (1.0 + bend))
        slope = 0.5 * (1.0 + bend) + (0.5 * GELU_A) * dense * (1.0 - bend * bend) * (
            1.0 + 3.0 * GELU_B * dense * dense
        )
        rows_half = to_half(hat * small[MLM_G] + small[MLM_LB])
        all_rows = lax.all_gather(rows_half, AXES, axis=0, tiled=True)
        logits = times_transpose(word_half, all_rows) + decoder
        mark = jnp.arange(word.shape[0], dtype=jnp.int32)[:, None] + offset == labels
        own_top = jnp.max(logits, 0)
        own_total = jnp.sum(jnp.exp(logits - own_top), 0)
        used = (labels[0] >= 0).astype(single)
        target = jnp.sum(jnp.sum(jnp.where(mark, logits, 0.0), 0) * used)
        top = lax.pmax(own_top, AXES)
        total = lax.psum(own_total * jnp.exp(own_top - top), AXES)
        log_sum = jnp.sum((jnp.log(total) + top) * used)
        weight = used * scales[0]
        half = to_half((jnp.exp(logits - top) / total - mark.astype(single)) * weight)
        back_rows = lax.psum_scatter(
            transpose_times(half, word_half), AXES, scatter_dimension=0, tiled=True
        )
        dense_half = to_half(norm_backward(back_rows, small[MLM_G], hat, inverse) * slope)
        back_final = lax.dot_general(
            pick, product(dense_half, head[:E]), (((0,), (0,)), ((), ())), precision=PRECISE
        )
        firsts = jnp.stack([final_half[0], final_half[BUCKET]])
        pooled = jnp.tanh(times_transpose(firsts, head[E : E + D]) + vec[POOL_B])
        classes = jnp.sum(pooled[:, None] * cls[None], -1)
        powers = jnp.exp(classes - jnp.max(classes, -1, keepdims=True))
        totals = jnp.sum(powers, -1, keepdims=True)
        onehot = jnp.stack([1 - sop_labels, sop_labels], 1).astype(single)
        present = jnp.stack([jnp.float32(1.0), (lengths[1] > 0).astype(single)])
        losses = jnp.log(totals[:, 0]) + jnp.max(classes, -1) - jnp.sum(classes * onehot, -1)
        back_classes = (powers / totals - onehot) * (present * scales[1])[:, None]
        back_pooled = jnp.sum(back_classes[:, :, None] * cls[None], 1)
        pre_half = to_half(back_pooled * (1.0 - pooled * pooled))
        back_firsts = product(pre_half, head[E : E + D])
        back_final = back_final.at[0].add(back_firsts[0]).at[BUCKET].add(back_firsts[1])
        back_cls = jnp.sum(back_classes[:, :, None] * pooled[:, None], 0)
        small_sums = [column_sum(dense_half), jnp.sum(back_rows * hat, 0), jnp.sum(back_rows, 0)]
        back_head = [transpose_times(dense_half, picked), transpose_times(pre_half, firsts)]
        ends = jnp.stack([log_sum, target, jnp.sum(losses * present)])
        return (
            back_final,
            product(half, all_rows),
            column_sum(half.T)[:, None],
            to_half(jnp.concatenate(back_head, 0)),
            jnp.concatenate([column_sum(pre_half)[None], back_cls], 0),
            jnp.stack(small_sums),
            jnp.pad(ends, (0, 125))[None],
        )

    def finish(self, left_wide, left_tall, rights, outer, head_grad, own_rows, vector):
        if self.kernels:
            out, heights, all_rows, own_vector = run_finish(
                left_wide,
                left_tall,
                rights,
                outer,
                to_half(head_grad),
                own_rows,
                vector,
                self.shape,
                self.identity(),
            )
            first, second = heights[0], heights[0] + heights[1]
            return out[:first], out[first:second], out[second:], all_rows, own_vector
        back_wide = jnp.concatenate(
            [
                product(left_wide[: 3 * D], rights[0]),
                product(left_wide[3 * D : 4 * D], rights[1]),
                product(left_wide[4 * D :], rights[2]),
            ],
            0,
        )
        sums = [
            lax.psum_scatter(p.astype(jnp.float32), AXES, scatter_dimension=0, tiled=True)
            for p in (back_wide, product(left_tall, outer), head_grad)
        ]
        all_rows = lax.all_gather(own_rows, AXES, axis=0, tiled=True)
        return (*sums, all_rows, self.scatter_small(vector))


def nt(a, b):
    return lax.dot_general(a, b, (((1,), (1,)), ((), ())), preferred_element_type=jnp.float32)


def nn(a, b):
    return jnp.dot(a, b, preferred_element_type=jnp.float32)


def tn(a, b):
    return lax.dot_general(a, b, (((0,), (0,)), ((), ())), preferred_element_type=jnp.float32)


CHUNK = 512
PAIR = 2 * HEAD_DIM
PROJ_B, Q_B, V_B, O_B, LN1_G, LN1_B, FFO_B, LN2_G, LN2_B, POOL_B = range(10)


def allowed_block(lengths):
    shape = (ROWS, ROWS)
    row = lax.broadcasted_iota(jnp.int32, shape, 0)
    col = lax.broadcasted_iota(jnp.int32, shape, 1)
    two = lengths[1] > 0
    row_second = jnp.logical_and(row >= BUCKET, two).astype(jnp.int32)
    col_second = jnp.logical_and(col >= BUCKET, two).astype(jnp.int32)
    length = jnp.where(col_second == 1, lengths[1], lengths[0])
    live = col - BUCKET * col_second < length
    return jnp.logical_and(row_second == col_second, live)


def halves(x):
    lane = lax.broadcasted_iota(jnp.int32, x.shape, 1)
    zero = jnp.zeros_like(x)
    return jnp.where(lane < HEAD_DIM, x, zero), jnp.where(lane < HEAD_DIM, zero, x)


def kinds(lengths):
    row = lax.broadcasted_iota(jnp.int32, (ROWS, 1), 0)
    second = jnp.logical_and(row >= BUCKET, lengths[1] > 0).astype(jnp.int32)
    length = jnp.where(second == 1, lengths[1], lengths[0])
    return (row - BUCKET * second >= length // 2).astype(jnp.float32)


EMB_G, EMB_B, MLM_B, MLM_G, MLM_LB, TYPE_ZERO, TYPE_ONE = range(7)


def forward_kernel(
    lengths,
    found,
    place,
    lift,
    wide,
    tall,
    vec,
    small,
    ff_b,
    final,
    embed_hat,
    embed_inverse,
    normed_half,
    rights,
    projected,
    weighting,
    hat_one,
    inverse_one,
    slope,
    active,
    hat_two,
    inverse_two,
    hidden,
):
    layer = pl.program_id(0)

    def row(index):
        return vec[pl.ds(index, 1), :]

    @pl.when(layer == 0)
    def _():
        two = (lengths[1] > 0).astype(jnp.float32)
        kind = kinds(lengths)
        lower = place[pl.ds(BUCKET, BUCKET), :]
        lower = jnp.where(two > 0, place[pl.ds(0, BUCKET), :], lower)
        embedded = found[...] + jnp.concatenate([place[pl.ds(0, BUCKET), :], lower], 0)
        zero, one = small[pl.ds(TYPE_ZERO, 1), :], small[pl.ds(TYPE_ONE, 1), :]
        hat, inverse = norm_forward(embedded + jnp.where(kind > 0, one, zero))
        embed_hat[...] = hat
        embed_inverse[...] = inverse
        normed = to_half(hat * small[pl.ds(EMB_G, 1), :] + small[pl.ds(EMB_B, 1), :])
        normed_half[...] = normed
        hidden[...] = nn(normed, lift[...]) + row(PROJ_B)

    half = to_half(hidden[...])
    rights[0] = half
    for part, bias in ((0, Q_B), (1, None), (2, V_B)):
        for low in range(0, D, 256):
            here = part * D + low
            value = nt(half, wide[pl.ds(here, 256), :])
            if bias is not None:
                value = value + vec[pl.ds(bias, 1), pl.ds(low, 256)]
            projected[:, pl.ds(here, 256)] = to_half(value)
    allowed = allowed_block(lengths)
    for pair in range(HEADS // 2):
        lanes = pair * PAIR
        queries = halves(projected[:, pl.ds(lanes, PAIR)])
        keys = projected[:, pl.ds(D + lanes, PAIR)]
        values = halves(projected[:, pl.ds(2 * D + lanes, PAIR)])
        total = jnp.zeros((ROWS, PAIR), jnp.float32)
        for side in (0, 1):
            scores = jnp.where(allowed, nt(queries[side], keys) * SCALE, MASKED)
            powers = jnp.exp(scores - jnp.max(scores, -1, keepdims=True))
            weights = powers * (1.0 / jnp.sum(powers, -1, keepdims=True))
            weighting[2 * pair + side] = weights
            total = total + nn(to_half(weights), values[side])
        rights[1, :, pl.ds(lanes, PAIR)] = to_half(total)
    first_sum = hidden[...] + nt(rights[1], wide[pl.ds(3 * D, D), :]) + row(O_B)
    hat, inverse = norm_forward(first_sum)
    hat_one[...] = hat
    inverse_one[...] = inverse
    middle = hat * row(LN1_G) + row(LN1_B)
    half = to_half(middle)
    rights[2] = half
    total = middle + row(FFO_B)
    for low in range(0, FF, CHUNK):
        inner = nt(half, wide[pl.ds(4 * D + low, CHUNK), :]) + ff_b[:, pl.ds(low, CHUNK)]
        square = inner * inner
        bend = jnp.tanh(GELU_A * inner * (1.0 + GELU_B * square))
        act = to_half(0.5 * inner * (1.0 + bend))
        slope[:, pl.ds(low, CHUNK)] = 0.5 * (1.0 + bend) + (0.5 * GELU_A) * inner * (
            1.0 - bend * bend
        ) * (1.0 + 3.0 * GELU_B * square)
        active[pl.ds(low, CHUNK), :] = act.T
        total = total + nn(act, tall[pl.ds(low, CHUNK), :])
    hat, inverse = norm_forward(total)
    hat_two[...] = hat
    inverse_two[...] = inverse
    output = hat * row(LN2_G) + row(LN2_B)
    hidden[...] = output
    final[...] = output


def whole_spec():
    return pl.BlockSpec(memory_space=VMEM_SPACE, pipeline_mode=pl.Buffered(1))


def lift_spec():
    return pl.BlockSpec((E, D), lambda i: ((E + D) // E, 0), pipeline_mode=pl.Buffered(1))


def by_layer(*shape, order=lambda i: i):
    return pl.BlockSpec(
        (None, *shape), lambda i: (order(i),) + (0,) * len(shape), memory_space=VMEM_SPACE
    )


def run_forward(lengths, found, place, head, wide, tall, vec, small, ff_b):
    def kept(*shape, dtype=jnp.bfloat16):
        return jax.ShapeDtypeStruct((LAYERS, *shape), dtype)

    single = jnp.float32
    names = (
        "final",
        "embed_hat",
        "embed_inverse",
        "normed_half",
        "rights",
        "projected",
        "weighting",
        "hat_one",
        "inverse_one",
        "slope",
        "active",
        "hat_two",
        "inverse_two",
    )
    outs = pl.pallas_call(
        forward_kernel,
        grid=(LAYERS,),
        out_shape=[
            jax.ShapeDtypeStruct((ROWS, D), single),
            jax.ShapeDtypeStruct((ROWS, E), single),
            jax.ShapeDtypeStruct((ROWS, 1), single),
            jax.ShapeDtypeStruct((ROWS, E), jnp.bfloat16),
            jax.ShapeDtypeStruct((3, LAYERS, ROWS, D), jnp.bfloat16),
            kept(ROWS, 3 * D),
            kept(HEADS, ROWS, ROWS, dtype=single),
            kept(ROWS, D, dtype=single),
            kept(ROWS, 1, dtype=single),
            kept(ROWS, FF, dtype=single),
            jax.ShapeDtypeStruct((FF, LAYERS * ROWS), jnp.bfloat16),
            kept(ROWS, D, dtype=single),
            kept(ROWS, 1, dtype=single),
        ],
        in_specs=[pl.BlockSpec(memory_space=pltpu.SMEM)]
        + [whole_spec()] * 2
        + [lift_spec()]
        + [whole_spec()] * 5,
        out_specs=[
            pl.BlockSpec((ROWS, D), lambda i: (0, 0)),
            pl.BlockSpec((ROWS, E), lambda i: (0, 0)),
            pl.BlockSpec((ROWS, 1), lambda i: (0, 0)),
            pl.BlockSpec((ROWS, E), lambda i: (0, 0)),
            pl.BlockSpec((3, None, ROWS, D), lambda i: (0, i, 0, 0)),
            by_layer(ROWS, 3 * D),
            by_layer(HEADS, ROWS, ROWS),
            by_layer(ROWS, D),
            by_layer(ROWS, 1),
            by_layer(ROWS, FF),
            pl.BlockSpec((FF, ROWS), lambda i: (0, i)),
            by_layer(ROWS, D),
            by_layer(ROWS, 1),
        ],
        scratch_shapes=[VMEM_SPACE((ROWS, D), single)],
        compiler_params=pltpu.CompilerParams(
            dimension_semantics=("arbitrary",), vmem_limit_bytes=VMEM_ASK
        ),
    )(lengths, found, place, head, wide, tall, vec, small, ff_b)
    return dict(zip(names, outs))


def backward_kernel(
    lengths,
    start,
    wide_sums,
    small_sums,
    embed_hat,
    embed_inverse,
    normed_half,
    lift,
    small,
    wide,
    tall,
    vec,
    projected,
    weighting,
    hat_one,
    inverse_one,
    slope,
    hat_two,
    inverse_two,
    rows_out,
    back_lift,
    turned,
    outer,
    vector,
    sums,
    ff_sum,
    upstream,
    back_mixed,
    joint,
):
    step = pl.program_id(0)

    @pl.when(step == 0)
    def _():
        upstream[...] = start[...]
        sums[...] = jnp.zeros_like(sums)
        ff_sum[...] = jnp.zeros_like(ff_sum)

    def row(index):
        return vec[pl.ds(index, 1), :]

    def add_sum(index, value):
        here = pl.ds(index - Q_B, 1)
        sums[here, :] = sums[here, :] + jnp.sum(value, 0, keepdims=True)

    up = upstream[...]
    hat = hat_two[...]
    add_sum(LN2_G, up * hat)
    add_sum(LN2_B, up)
    back_second = norm_backward(up, row(LN2_G), hat, inverse_two[...])
    half = to_half(back_second)
    outer[...] = half
    add_sum(FFO_B, half.astype(jnp.float32))
    total = back_second
    for low in range(0, FF, CHUNK):
        lanes = pl.ds(low, CHUNK)
        inner = to_half(nt(half, tall[lanes, :]) * slope[:, lanes])
        ff_sum[:, lanes] = ff_sum[:, lanes] + jnp.sum(
            inner.astype(jnp.float32), 0, keepdims=True
        )
        turned[pl.ds(4 * D + low, CHUNK), :] = inner.T
        total = total + nn(inner, wide[pl.ds(4 * D + low, CHUNK), :])
    hat = hat_one[...]
    add_sum(LN1_G, total * hat)
    add_sum(LN1_B, total)
    back_first = norm_backward(total, row(LN1_G), hat, inverse_one[...])
    upstream[...] = back_first
    half = to_half(back_first)
    add_sum(O_B, half.astype(jnp.float32))
    turned[pl.ds(3 * D, D), :] = half.T
    back_mixed[...] = to_half(nn(half, wide[pl.ds(3 * D, D), :]))
    for pair in range(HEADS // 2):
        lanes = pair * PAIR
        queries = halves(projected[:, pl.ds(lanes, PAIR)])
        keys = halves(projected[:, pl.ds(D + lanes, PAIR)])
        values = projected[:, pl.ds(2 * D + lanes, PAIR)]
        grads = halves(back_mixed[:, pl.ds(lanes, PAIR)])
        zero = jnp.zeros((ROWS, PAIR), jnp.float32)
        back_query, back_key, back_value = zero, zero, zero
        for side in (0, 1):
            weights = weighting[2 * pair + side]
            soft = nt(grads[side], values)
            scores = to_half(
                weights * (soft - jnp.sum(weights * soft, -1, keepdims=True))
            )
            back_query = back_query + nn(scores, keys[side])
            back_key = back_key + tn(scores, queries[side])
            back_value = back_value + tn(to_half(weights), grads[side])
        joint[:, pl.ds(lanes, PAIR)] = to_half(back_query * SCALE)
        joint[:, pl.ds(D + lanes, PAIR)] = to_half(back_key * SCALE)
        joint[:, pl.ds(2 * D + lanes, PAIR)] = to_half(back_value)
    total = upstream[...]
    for part, bias in ((0, Q_B), (1, None), (2, V_B)):
        here = pl.ds(part * D, D)
        value = joint[:, here]
        if bias is not None:
            add_sum(bias, value.astype(jnp.float32))
        turned[here, :] = value.T
        total = total + nn(value, wide[here, :])
    upstream[...] = total

    @pl.when(step == LAYERS - 1)
    def _():
        half = to_half(upstream[...])
        back_lift[...] = to_half(tn(normed_half[...], half))
        back_normed = nt(half, lift[...])
        hat = embed_hat[...]
        back = norm_backward(back_normed, small[pl.ds(EMB_G, 1), :], hat, embed_inverse[...])
        rows_out[...] = to_half(back)
        kind = kinds(lengths)
        ones = jnp.sum(back * kind, 0, keepdims=True)
        zeros = jnp.sum(back * (1.0 - kind), 0, keepdims=True)
        vector[...] = jnp.zeros_like(vector)
        parts = [jnp.sum(half.astype(jnp.float32), 0, keepdims=True)]
        parts += [sums[pl.ds(i, 1), :] for i in range(8)]
        parts += [wide_sums[pl.ds(i, 1), :] for i in range(3)]
        parts += [ff_sum[...]]
        parts += [
            jnp.sum(back_normed * hat, 0, keepdims=True),
            jnp.sum(back_normed, 0, keepdims=True),
        ]
        parts += [small_sums[pl.ds(i, 1), :] for i in range(3)]
        parts += [zeros, ones]
        at = 0
        for part in parts:
            for low in range(0, part.shape[1], 128):
                vector[pl.ds(at, 1), :] = part[:, low : low + 128]
                at += 1


def run_backward(lengths, start, wide_sums, small_sums, head, wide, tall, vec, small, kept, lines):
    single, half = jnp.float32, jnp.bfloat16
    last = LAYERS - 1

    def order(i):
        return last - i

    return pl.pallas_call(
        backward_kernel,
        grid=(LAYERS,),
        out_shape=[
            jax.ShapeDtypeStruct((ROWS, E), half),
            jax.ShapeDtypeStruct((E, D), half),
            jax.ShapeDtypeStruct((4 * D + FF, LAYERS * ROWS), half),
            jax.ShapeDtypeStruct((LAYERS, ROWS, D), half),
            jax.ShapeDtypeStruct((lines, 128), single),
        ],
        in_specs=[pl.BlockSpec(memory_space=pltpu.SMEM)]
        + [whole_spec()] * 6
        + [lift_spec()]
        + [whole_spec()] * 4
        + [
            by_layer(ROWS, 3 * D, order=order),
            by_layer(HEADS, ROWS, ROWS, order=order),
            by_layer(ROWS, D, order=order),
            by_layer(ROWS, 1, order=order),
            by_layer(ROWS, FF, order=order),
            by_layer(ROWS, D, order=order),
            by_layer(ROWS, 1, order=order),
        ],
        out_specs=[
            pl.BlockSpec((ROWS, E), lambda i: (0, 0)),
            pl.BlockSpec((E, D), lambda i: (0, 0)),
            pl.BlockSpec((4 * D + FF, ROWS), lambda i: (0, order(i))),
            by_layer(ROWS, D, order=order),
            pl.BlockSpec((lines, 128), lambda i: (0, 0)),
        ],
        scratch_shapes=[
            VMEM_SPACE((8, D), single),
            VMEM_SPACE((1, FF), single),
            VMEM_SPACE((ROWS, D), single),
            VMEM_SPACE((ROWS, D), half),
            VMEM_SPACE((ROWS, 3 * D), half),
        ],
        compiler_params=pltpu.CompilerParams(
            dimension_semantics=("arbitrary",), vmem_limit_bytes=VMEM_ASK
        ),
    )(
        lengths,
        start,
        wide_sums,
        small_sums,
        kept["embed_hat"],
        kept["embed_inverse"],
        kept["normed_half"],
        head,
        small,
        wide,
        tall,
        vec,
        kept["projected"],
        kept["weighting"],
        kept["hat_one"],
        kept["inverse_one"],
        kept["slope"],
        kept["hat_two"],
        kept["inverse_two"],
    )


def adam_update(weight, gradient, first, second, rate):
    first = BETA_ONE * first + (1 - BETA_ONE) * gradient
    second = BETA_TWO * second + (1 - BETA_TWO) * gradient * gradient
    first_hat = first / (1 - BETA_ONE**STEP)
    second_hat = second / (1 - BETA_TWO**STEP)
    updated = weight - rate * (
        first_hat / (jnp.sqrt(second_hat) + ADAM_EPSILON) + WEIGHT_DECAY * weight
    )
    return (updated, first, second)


def local(
    mesh,
    word_table,
    position_table,
    head_weights,
    decoder_bias,
    layer_wide,
    layer_tall,
    vectors,
    word_first,
    word_second,
    position_first,
    position_second,
    head_first,
    head_second,
    decoder_first,
    decoder_second,
    wide_first,
    wide_second,
    tall_first,
    tall_second,
    vector_first,
    vector_second,
    token_ids,
    seq_lengths,
    mlm_rows,
    mlm_labels,
    sop_labels,
):
    network = Network(mesh)
    own = lax.axis_index(AXES)
    words = word_table.shape[0]

    def line(x, missing=-1):
        return jnp.pad(x, (0, 128 - x.shape[0]), constant_values=missing)[None]

    facts = jnp.concatenate(
        [
            token_ids.reshape(-1, 128),
            line(mlm_labels),
            line(mlm_rows),
            line(jnp.concatenate([seq_lengths, sop_labels])),
            jnp.zeros((3, 128), jnp.int32),
        ],
        0,
    )
    places_own = to_half(position_table).astype(jnp.float32)
    (wide, tall, head), all_facts, place, found = network.start(
        [layer_wide.T, layer_tall, head_weights.T], word_table, facts, places_own
    )
    devices = all_facts.shape[0]
    all_seconds = all_facts[:, 4, 1] > 0
    mlm_count = jnp.sum((all_facts[:, 2] >= 0).astype(jnp.float32))
    sop_count = devices + jnp.sum(all_seconds.astype(jnp.float32))
    scales = jnp.stack([1.0 / mlm_count, 1.0 / sop_count])
    place = place.reshape(-1, E)
    vec = vectors[: 10 * D].reshape(10, D)
    cls = vectors[10 * D : 12 * D].reshape(2, D)
    ff_b = vectors[12 * D : 12 * D + FF][None]
    small = vectors[12 * D + FF :].reshape(7, E)
    kept = run_forward(seq_lengths, found, place, head, wide, tall, vec, small, ff_b)
    (back_final, back_word_head, back_decoder, back_head, wide_sums, small_sums, totals) = (
        network.head(
            seq_lengths,
            sop_labels,
            scales,
            kept["final"],
            head,
            word_table,
            decoder_bias,
            all_facts,
            facts,
            vec,
            small,
            cls,
        )
    )
    back_decoder = back_decoder[:, 0]
    total = vectors.shape[0]
    share = -(-total // (devices * 1024)) * 1024
    back_rows, back_lift, turned, outer, vector_grad = run_backward(
        seq_lengths,
        back_final,
        wide_sums,
        small_sums,
        head,
        wide,
        tall,
        vec,
        small,
        kept,
        devices * share // 128,
    )
    sum_wide, sum_tall, sum_head, all_back, own_vector = network.finish(
        turned,
        kept["active"],
        kept["rights"].reshape(3, -1, D),
        outer.reshape(-1, D),
        jnp.concatenate([back_head, back_lift], 0),
        back_rows,
        vector_grad.reshape(devices, -1, 128),
    )
    offset = own * words
    ids = all_facts[:, : ROWS // 128].reshape(-1) - offset
    select = to_half(ids[:, None] == jnp.arange(words, dtype=jnp.int32)[None, :])
    back_word = back_word_head + transpose_times(select, all_back)
    places = position_table.shape[0]
    by_device = all_back.reshape(devices, ROWS, E)
    folded = by_device[:, :BUCKET].astype(jnp.float32) + jnp.where(
        all_seconds[:, None, None], by_device[:, BUCKET:].astype(jnp.float32), 0.0
    )
    rest = jnp.where(all_seconds[:, None, None], 0.0, by_device[:, BUCKET:].astype(jnp.float32))
    all_place = jnp.concatenate([jnp.sum(folded, 0), jnp.sum(rest, 0)], 0)
    all_place = jnp.pad(all_place, ((0, places * devices - ROWS), (0, 0)))
    back_place = lax.dynamic_slice(all_place, (own * places, 0), (places, E))
    shards = (back_word, back_place, sum_head.T, back_decoder, sum_wide.T, sum_tall)
    local_squares = jnp.sum(jnp.stack([jnp.sum(g * g) for g in shards]))
    scalars = jnp.concatenate([totals, jnp.broadcast_to(local_squares, (7, 128))], 0)
    (last,) = network.gather_small([jnp.concatenate([own_vector, scalars], 0)])
    tail = share // 128
    reduced = last[:, :tail].reshape(-1)[:total]
    mlm_sum = totals[0, 0] - jnp.sum(last[:, tail, 1])
    sop_total = jnp.sum(last[:, tail, 2])
    grad_norm = jnp.sqrt(jnp.sum(last[:, tail + 1, 0]) + jnp.sum(reduced * reduced))
    factor = jnp.minimum(1.0, CLIP_NORM / (grad_norm + NORM_EPSILON))
    updates = []
    for weight, gradient, first, second, rate in (
        (word_table, shards[0], word_first, word_second, LEARN_RATE),
        (position_table, shards[1], position_first, position_second, LEARN_RATE),
        (head_weights, shards[2], head_first, head_second, LEARN_RATE),
        (decoder_bias, shards[3], decoder_first, decoder_second, LEARN_RATE),
        (layer_wide, shards[4], wide_first, wide_second, LEARN_RATE),
        (layer_tall, shards[5], tall_first, tall_second, LEARN_RATE),
        (vectors, reduced, vector_first, vector_second, SMALL_RATE),
    ):
        updates.extend(adam_update(weight, factor * gradient, first, second, rate))
    return (*updates, mlm_sum, mlm_count, sop_total, sop_count, grad_norm)


def solution(mesh):
    rows = P(AXES, None)
    columns = P(None, AXES)
    flat = P(AXES)
    whole = P()
    return jax.shard_map(
        functools.partial(local, mesh),
        mesh=mesh,
        in_specs=(rows, rows, columns, flat, columns, rows, whole)
        + (rows, rows) * 2
        + (columns, columns, flat, flat, columns, columns, rows, rows, whole, whole)
        + (flat,) * 5,
        out_specs=(rows,) * 6
        + (columns,) * 3
        + (flat,) * 3
        + (columns,) * 3
        + (rows,) * 3
        + (whole,) * 8,
        check_vma=False,
    )
```

```python
import functools

import jax
import jax.numpy as jnp
from jax import lax
from jax.experimental import pallas as pl
from jax.experimental.pallas import tpu as pltpu
from jax.sharding import PartitionSpec as P

D = 768
HEADS = 12
HEAD_DIM = 64
FF = 3072
E = 128
LAYERS = 4
STEP = 10
BUCKET = 128
ROWS = 2 * BUCKET

PRECISE = lax.Precision.HIGHEST
EPSILON = 1e-06
LEARN_RATE = 0.1
SMALL_RATE = 0.5
BETA_ONE = 0.9
BETA_TWO = 0.999
ADAM_EPSILON = 1e-08
WEIGHT_DECAY = 0.01
CLIP_NORM = 0.005
NORM_EPSILON = 1e-06
MASKED = -1e30
SCALE = HEAD_DIM ** (-0.5)
AXES = ("dp", "fsdp")


def to_half(x):
    return x.astype(jnp.bfloat16)


def product(a, b):
    return jnp.dot(a, b, preferred_element_type=jnp.float32)


def times_transpose(a, b):
    return lax.dot_general(a, b, (((1,), (1,)), ((), ())), preferred_element_type=jnp.float32)


def transpose_times(a, b):
    return lax.dot_general(a, b, (((0,), (0,)), ((), ())), preferred_element_type=jnp.float32)


def column_sum(x):
    return jnp.sum(x.astype(jnp.float32), 0)


def norm_forward(x):
    centre = x - jnp.mean(x, -1, keepdims=True)
    inverse = lax.rsqrt(jnp.mean(centre * centre, -1, keepdims=True) + EPSILON)
    return centre * inverse, inverse


def norm_backward(upstream, factor, hat, inverse):
    scaled = upstream * factor
    return inverse * (
        scaled
        - jnp.mean(scaled, -1, keepdims=True)
        - hat * jnp.mean(scaled * hat, -1, keepdims=True)
    )


GELU_A = 0.7978845608028654
GELU_B = 0.044715


MESH_ID = pl.DeviceIdType.MESH
VMEM_SPACE = pltpu.VMEM
VMEM_ASK = 60 * 1024 * 1024


def greet(peers):
    barrier = pltpu.get_barrier_semaphore()
    count = 0
    for present, who in peers:
        if present is None:
            pl.semaphore_signal(barrier, inc=1, device_id=who, device_id_type=MESH_ID)
            count = count + 1
        else:

            @pl.when(present)
            def _(who=who):
                pl.semaphore_signal(barrier, inc=1, device_id=who, device_id_type=MESH_ID)

            count = count + present.astype(jnp.int32)
    pl.semaphore_wait(barrier, count)


def maybe(condition, action):
    if condition is None:
        action()
    else:
        pl.when(condition)(action)


def remote(source, target, send, receive, who):
    return pltpu.make_async_remote_copy(
        src_ref=source,
        dst_ref=target,
        send_sem=send,
        recv_sem=receive,
        device_id=who,
        device_id_type=MESH_ID,
    )


OWN, ACROSS_X, ACROSS_Y, DIAGONAL = 0, 1, 2, 3


def cuts_of(rows):
    tail = max(32, round(rows * 0.22 / 32) * 32)
    head = rows - tail
    return ((0, head), (head, rows))


def half_of(span, which):
    low, high = span
    middle = (low + high) // 2
    return (low, middle) if which == 0 else (middle, high)


def places():
    z, f = lax.axis_index("dp"), lax.axis_index("fsdp")
    q, c = f // 2, lax.rem(f, 2)
    qx = q + 1 - 2 * lax.rem(q, 2)
    qy = lax.rem(q + 2, 4)
    qd = qx + qy - q
    return z, c, (q, qx, qy, qd)


def gather_stages(planes, rows, members, x, outs, buf, sems, where, opening):
    out_sem, send, recv, side_send, side_recv = sems
    z, c, cols = where
    cuts = cuts_of(rows)
    at_x, at_y, mate = (z, cols[1] * 2 + c), (z, cols[2] * 2 + c), (z, cols[0] * 2 + 1 - c)
    above, below = z < planes - 1, z > 0
    up, down = (z + 1, cols[0] * 2 + c), (z - 1, cols[0] * 2 + c)
    sent = []

    def block(zs, col, core, span):
        return buf.at[zs, cols[col], core, pl.ds(span[0], span[1] - span[0])]

    def push(condition, zs, col, span, who, slot, receive, mine=False):
        def make():
            here = block(zs, col, c, span)
            source = x.at[pl.ds(span[0], span[1] - span[0])] if mine else here
            return remote(source, here, send.at[slot[0], zs, slot[1]], receive, who)

        maybe(condition, lambda: make().start())
        sent.append((condition, make))

    def await_block(zs, col, span, receive, core=None):
        here = block(zs, col, c if core is None else core, span)
        remote(here, here, send.at[0, 0, 0], receive, mate).wait_recv()

    def deliver(zs, col, core, span):
        for index, (out, (low, high)) in enumerate(zip(outs, members)):
            first, last = max(low, span[0]), min(high, span[1])
            if first < last:
                pltpu.make_async_copy(
                    buf.at[zs, cols[col], core, pl.ds(first, last - first)],
                    out.at[zs, cols[col], core, pl.ds(first - low, last - first)],
                    out_sem.at[index],
                ).start()

    def share(condition, part, zs, col, span, kind, mine=False):
        def make():
            here = block(zs, col, c, span)
            source = x.at[pl.ds(span[0], span[1] - span[0])] if mine else here
            return remote(
                source, here, side_send.at[part, zs, kind], side_recv.at[part, zs, kind], mate
            )

        def action():
            make().start()
            if not mine:
                deliver(zs, col, c, span)

        maybe(condition, action)
        sent.append((condition, make))
        shared.append((condition, part, zs, col, span, kind))

    shared = []
    whole = [cuts[0], cuts[1]]
    for part in (0, 1):
        push(above, z, OWN, whole[part], up, (part, 2), recv.at[part, z, OWN], True)
        push(below, z, OWN, whole[part], down, (part, 3), recv.at[part, z, OWN], True)
    for part in (1, 0):
        if part == 0:
            opening()
        push(None, z, OWN, whole[part], at_x, (part, 0), recv.at[part, z, ACROSS_X], True)
        push(None, z, OWN, whole[part], at_y, (part, 1), recv.at[part, z, ACROSS_Y], True)
    for part in (0, 1):
        share(None, part, z, OWN, whole[part], 0, True)
    own_copy = pltpu.make_async_copy(x, buf.at[z, cols[0], c], out_sem.at[len(members)])
    own_copy.start()

    def turn(condition, part, zs):
        span = whole[part]
        for col, which, who, slot in ((ACROSS_X, 1, at_y, 4), (ACROSS_Y, 0, at_x, 5)):
            maybe(
                condition,
                lambda col=col: await_block(zs, col, span, recv.at[part, zs, col]),
            )
            push(condition, zs, col, half_of(span, which), who, (part, slot), recv.at[part, zs, 4 + which])
            if part == 1:
                push(above, zs, col, span, up, (1, 4 + 2 * col), recv.at[1, zs, col])
                push(below, zs, col, span, down, (1, 5 + 2 * col), recv.at[1, zs, col])
            share(condition, part, zs, col, span, col)

    yield
    turn(None, 1, z)
    yield
    for which in (0, 1):
        await_block(z, DIAGONAL, half_of(whole[1], which), recv.at[1, z, 4 + which])
    push(above, z, DIAGONAL, whole[1], up, (1, 10), recv.at[1, z, DIAGONAL])
    push(below, z, DIAGONAL, whole[1], down, (1, 11), recv.at[1, z, DIAGONAL])
    share(None, 1, z, DIAGONAL, whole[1], 3)
    yield
    turn(None, 0, z)

    def settle(upto):
        while len(shared) > upto:
            condition, part, zs, col, span, kind = shared.pop(0)

            def action():
                await_block(zs, col, span, side_recv.at[part, zs, kind], 1 - c)
                deliver(zs, col, 1 - c, span)

            maybe(condition, action)

    for step in range(1, planes):
        yield
        ways = ((z - step >= 0, z - step, above, up), (z + step < planes, z + step, below, down))
        for valid, zs, further, onward in ways:
            go = jnp.logical_and(valid, further)
            pl.when(valid)(
                lambda zs=zs: await_block(zs, OWN, whole[0], recv.at[0, zs, OWN])
            )
            push(go, zs, OWN, whole[0], onward, (0, 2), recv.at[0, zs, OWN])
            push(valid, zs, OWN, whole[0], at_x, (0, 0), recv.at[0, zs, ACROSS_X])
            push(valid, zs, OWN, whole[0], at_y, (0, 1), recv.at[0, zs, ACROSS_Y])
            share(valid, 0, zs, OWN, whole[0], 0)
        yield
        for valid, zs, further, onward in ways:
            go = jnp.logical_and(valid, further)
            for col in (OWN, ACROSS_X, ACROSS_Y, DIAGONAL):
                pl.when(valid)(
                    lambda zs=zs, col=col: await_block(zs, col, whole[1], recv.at[1, zs, col])
                )
                push(go, zs, col, whole[1], onward, (1, col), recv.at[1, zs, col])
                share(valid, 1, zs, col, whole[1], col)
        yield
        for valid, zs, further, onward in ways:
            turn(valid, 0, zs)
        settle(8)
    yield
    own_copy.wait()
    deliver(z, OWN, c, (0, rows))
    everywhere = [(None, z)] + [
        (valid, zs)
        for step in range(1, planes)
        for valid, zs in ((z - step >= 0, z - step), (z + step < planes, z + step))
    ]
    for condition, zs in everywhere:
        for which in (0, 1):
            span = half_of(whole[0], which)
            maybe(
                condition,
                lambda zs=zs, which=which, span=span: await_block(
                    zs, DIAGONAL, span, recv.at[0, zs, 4 + which]
                ),
            )
            share(condition, 0, zs, DIAGONAL, span, 3 + which)
    settle(0)
    for condition, make in sent:
        maybe(condition, lambda make=make: make().wait_send())
    for index, (out, (low, high)) in enumerate(zip(outs, members)):
        pltpu.make_async_copy(
            buf.at[:, :, :, pl.ds(low, high - low)], out, out_sem.at[index]
        ).wait()


def select_stages(planes, facts, own_word, found, refs, where, offset):
    part, side, plane_in, middle, line_in, turned, sems_send, sems_recv = refs
    z, c, cols = where
    q = cols[0]
    f = q * 2 + c
    mate = (z, q * 2 + 1 - c)
    words = own_word.shape[0]
    line = [(lax.rem(z + d, planes), f) for d in range(1, planes)]
    turned[...] = to_half(own_word[...].T)
    yield

    def mate_message(col):
        return remote(
            part.at[:, col, 1 - c], side.at[:, col], sems_send.at[0, col], sems_recv.at[0, col], mate
        )

    def plane_message(col):
        return remote(
            part.at[:, col, c],
            plane_in.at[col],
            sems_send.at[1, col],
            sems_recv.at[1, col],
            (z, cols[col] * 2 + c),
        )

    def line_message(d, who):
        return remote(
            middle.at[who[0]], line_in.at[d], sems_send.at[2, d], sems_recv.at[2, d], who
        )

    def merge(col):
        mate_message(col).wait_recv()
        for zt in range(planes):
            part[zt, col, c] = part[zt, col, c] + side[zt, col]
        if col != OWN:
            plane_message(col).start()

    order = (DIAGONAL, ACROSS_X, ACROSS_Y, OWN)
    for place, col in enumerate(order):

        def body(n, unused, col=col):
            zt, core = n // 2, lax.rem(n, 2)
            ids = facts[zt, cols[col] * 2 + core]
            row = lax.broadcasted_iota(jnp.int32, (words, BUCKET), 0) + offset
            picks = jnp.concatenate(
                [to_half((row == ids[i : i + 1, :]).astype(jnp.float32)) for i in (0, 1)], 1
            )
            part[zt, col, core] = to_half(nn(turned[...], picks))
            return unused

        lax.fori_loop(0, 2 * planes, body, 0)
        mate_message(col).start()
        if place > 0:
            merge(order[place - 1])
        yield
    merge(OWN)
    total = part[:, OWN, c]
    yield
    for col in order[:3]:
        plane_message(col).wait_recv()
        total = total + plane_in[col]
    middle[...] = total
    for d, who in enumerate(line):
        line_message(d, who).start()
    yield
    total = middle[z]
    for d, who in enumerate(line):
        line_message(d, who).wait_recv()
        total = total + line_in[d]
    found[...] = total.astype(jnp.float32).T
    for col in order:
        mate_message(col).wait_send()
    for col in order[:3]:
        plane_message(col).wait_send()
    for d, who in enumerate(line):
        line_message(d, who).wait_send()


PLAN = (1, 1, 1, 1, 1, 1, 1, 1, 1, 1, 1, 1, 1, 1)


def start_kernel(
    planes,
    rows,
    members,
    own_wide,
    own_tall,
    own_head,
    own_word,
    own_facts,
    own_place,
    *refs,
):
    width = 8
    count = len(members)
    outs, (facts, place, found) = refs[:count], refs[count : count + 3]
    x, buf = refs[count + 3 : count + 5]
    gather_sems = refs[count + 5 : count + 10]
    select_refs = refs[count + 10 : count + 18]
    line_send, line_recv, plane_send, plane_recv = refs[count + 18 :]
    where = places()
    z, c, cols = where
    f = cols[0] * 2 + c
    line = [(lax.rem(z + d, planes), f) for d in range(1, planes)]
    plane = [(z, lax.rem(f + d, width)) for d in range(1, width)]
    facts[z, f] = own_facts[...]
    place[z, f] = to_half(own_place[...]).astype(jnp.float32)
    greet([(None, who) for who in line + plane])
    pairs = (facts, place)

    def along(i, d, who):
        here = pairs[i].at[z, f]
        return remote(here, here, line_send.at[i, d], line_recv.at[i, d], who)

    def around(i, d, who, source):
        here = pairs[i].at[:, source]
        return remote(here, here, plane_send.at[i, d], plane_recv.at[i, d], who)

    for d, who in enumerate(line):
        for i in (0, 1):
            along(i, d, who).start()
    for (low, high), piece in zip(members, (own_wide[...], own_tall[...], own_head[...])):
        x[low:high] = to_half(piece)

    def opening():
        for d, who in enumerate(line):
            for i in (0, 1):
                source = pairs[i].at[lax.rem(z - d - 1 + planes, planes), f]
                remote(source, source, line_send.at[i, d], line_recv.at[i, d], who).wait_recv()
        for d, who in enumerate(plane):
            for i in (0, 1):
                around(i, d, who, f).start()

    gather = gather_stages(planes, rows, members, x, outs, buf, gather_sems, where, opening)
    offset = (z * width + f) * own_word.shape[0]
    select = select_stages(planes, facts, own_word, found, select_refs, where, offset)
    done = object()
    next(gather)
    next(select)
    for d in range(1, width):
        source = lax.rem(f - d + width, width)
        for i in (0, 1):
            around(i, d - 1, mate_of(where), source).wait_recv()
    for number in range(64):
        for unused in range(PLAN[number] if number < len(PLAN) else 1):
            next(select, done)
        if next(gather, done) is done:
            break
    for unused in select:
        pass
    for d, who in enumerate(line):
        for i in (0, 1):
            along(i, d, who).wait_send()
    for d, who in enumerate(plane):
        for i in (0, 1):
            around(i, d, who, f).wait_send()


def mate_of(where):
    z, c, cols = where
    return (z, cols[0] * 2 + 1 - c)


def run_start(shards, own_word, own_facts, own_place, mesh_shape, identity):
    planes, width = mesh_shape
    heights = tuple(shard.shape[0] for shard in shards)
    rows, columns = sum(heights), shards[1].shape[1]
    members, low = [], 0
    for height in heights:
        members.append((low, low + height))
        low += height
    half, single = jnp.bfloat16, jnp.float32
    vmem = pl.BlockSpec(memory_space=VMEM_SPACE)
    dma = pltpu.SemaphoreType.DMA
    words, features = own_word.shape
    block = (features, ROWS)
    *outs, facts, place, found = pl.pallas_call(
        functools.partial(start_kernel, planes, rows, tuple(members)),
        out_shape=[
            jax.ShapeDtypeStruct((planes, width // 2, 2, height, columns), half)
            for height in heights
        ]
        + [
            jax.ShapeDtypeStruct((planes, width, *own_facts.shape), own_facts.dtype),
            jax.ShapeDtypeStruct((planes, width, *own_place.shape), own_place.dtype),
            jax.ShapeDtypeStruct((ROWS, features), single),
        ],
        in_specs=[vmem] * 6,
        out_specs=[pl.BlockSpec(memory_space=pl.ANY)] * len(heights) + [vmem] * 3,
        scratch_shapes=[
            VMEM_SPACE((rows, columns), half),
            VMEM_SPACE((planes, width // 2, 2, rows, columns), half),
            dma((len(heights) + 1,)),
            dma((2, planes, 12)),
            dma((2, planes, 6)),
            dma((2, planes, 5)),
            dma((2, planes, 5)),
            VMEM_SPACE((planes, 4, 2, *block), half),
            VMEM_SPACE((planes, 4, *block), half),
            VMEM_SPACE((4, planes, *block), half),
            VMEM_SPACE((planes, *block), half),
            VMEM_SPACE((planes - 1, *block), half),
            VMEM_SPACE((features, words), half),
            dma((3, 4)),
            dma((3, 4)),
            dma((2, planes)),
            dma((2, planes)),
            dma((2, width)),
            dma((2, width)),
        ],
        compiler_params=pltpu.CompilerParams(
            collective_id=identity, has_side_effects=True, vmem_limit_bytes=VMEM_ASK
        ),
    )(*shards, own_word, own_facts, own_place)
    weights = [out.reshape(-1, columns) for out in outs]
    devices = planes * width
    return (
        weights,
        facts.reshape(devices, *own_facts.shape),
        place.reshape(devices, *own_place.shape),
        found,
    )


def accumulate(target, sources, height):
    step = 32

    def body(i, unused):
        rows = pl.ds(pl.multiple_of(i * step, step), step)
        total = sources[0][rows].astype(jnp.float32)
        for source in sources[1:]:
            total = total + source[rows].astype(jnp.float32)
        target[rows] = total.astype(target.dtype)
        return unused

    lax.fori_loop(0, height // step, body, 0)


ROWS_AT = 1
MATE_AT = 9


def far_first(i, z, planes):
    low = (2 * z < planes).astype(jnp.int32)
    falling = planes - 1 - i - (i >= planes - 1 - z).astype(jnp.int32)
    rising = i + (i >= z).astype(jnp.int32)
    last = (jnp.int32(i) == planes - 1).astype(jnp.int32)
    return last * z + (1 - last) * (low * falling + (1 - low) * rising)


def finish_kernel(
    planes,
    heights,
    split,
    left_wide,
    left_tall,
    rights,
    outer,
    head_grad,
    own_rows,
    vector_terms,
    facts,
    base_word,
    back_decoder,
    totals,
    out,
    word_grad,
    place_grad,
    last,
    ends,
    all_rows,
    both,
    side,
    half_in,
    full_in,
    line_in,
    tail_line,
    tail_half,
    tail_full,
    wide_buf,
    tall_buf,
    vector_in,
    vector_mid,
    vector_last,
    fetch,
    head_load,
    side_send,
    side_recv,
    send,
    recv,
    tail_send,
    tail_recv,
    row_send,
    row_recv,
    vec_send,
    vec_recv,
    end_send,
    end_recv,
):
    width = 8
    wide_height, tall_height, head_height = heights
    rows = wide_height + tall_height + head_height
    z, c, cols = places()
    q = cols[0]
    f = q * 2 + c
    x, y = lax.rem(q, 2), q // 2
    cuts = cuts_of(rows)
    head, tail = cuts
    head_rows, tail_rows = head[1] - head[0], tail[1] - tail[0]
    at_x, at_y, mate = (z, cols[1] * 2 + c), (z, cols[2] * 2 + c), (z, q * 2 + 1 - c)
    above, below = z < planes - 1, z > 0
    up, down = (z + 1, f), (z - 1, f)
    line = [(lax.rem(z + d, planes), f) for d in range(1, planes)]
    plane = [(z, lax.rem(f + d, width)) for d in range(1, width)]
    greet([(None, who) for who in line + plane])
    order = (DIAGONAL, ACROSS_X, ACROSS_Y, OWN)
    sent = []

    def push(condition, make):
        maybe(condition, lambda: make().start())
        sent.append((condition, make))

    def piece(ref, span):
        return ref.at[pl.ds(span[0], span[1] - span[0])]

    def plane_at(i):
        return far_first(i, z, planes)

    def turn_of(n):
        m = n - 1 - 3 * (n == 0).astype(jnp.int32) + (n > 4 * planes - 4).astype(jnp.int32)
        group, j = (m + 4) // 4 - 1, lax.rem(m + 4, 4)
        ahead = (j == 0).astype(jnp.int32)
        return group + ahead, DIAGONAL * ahead + j * (j < 3).astype(jnp.int32)

    def chip_of(n):
        i, col = turn_of(n)
        flip_x, flip_y = lax.rem(col, 2), col // 2
        return plane_at(i) * 4 + 2 * lax.rem(y + flip_y, 2) + lax.rem(x + flip_x, 2)

    def fetches(n):
        k, slot = chip_of(n), lax.rem(n, 2)
        wide_rows = pl.ds(pl.multiple_of(k * 2 * wide_height, 16), 2 * wide_height)
        tall_rows = pl.ds(pl.multiple_of(k * 2 * tall_height, 16), 2 * tall_height)
        return (
            pltpu.make_async_copy(
                left_wide.at[wide_rows], wide_buf.at[slot], fetch.at[0, slot]
            ),
            pltpu.make_async_copy(
                left_tall.at[tall_rows], tall_buf.at[slot], fetch.at[1, slot]
            ),
        )

    for copy in fetches(jnp.int32(0)):
        copy.start()

    def vector_first(d, who):
        return remote(
            vector_terms.at[:, who[1]], vector_in.at[d], vec_send.at[0, d], vec_recv.at[0, d], who
        )

    def vector_second(d, who):
        return remote(
            vector_mid.at[who[0]], vector_last.at[d], vec_send.at[1, d], vec_recv.at[1, d], who
        )

    def row_line(d, who):
        return remote(
            own_rows, all_rows.at[z, q, c], row_send.at[0, d], row_recv.at[0, d], who
        )

    def row_plane(col):
        return remote(
            all_rows.at[:, q, c],
            all_rows.at[:, q, c],
            row_send.at[1, col],
            row_recv.at[1, col],
            (z, cols[col] * 2 + c),
        )

    def row_mate():
        return remote(
            all_rows.at[:, :, c], all_rows.at[:, :, c], row_send.at[2, 0], row_recv.at[2, 0], mate
        )

    for d, who in enumerate(line):
        push(None, functools.partial(row_line, d, who))
    for d, who in enumerate(plane):
        push(None, functools.partial(vector_first, d, who))
    all_rows[z, q, c] = own_rows[...]
    head_copies = []
    for col in order:
        copy = pltpu.make_async_copy(
            head_grad.at[:, cols[col]],
            both.at[:, col, :, pl.ds(wide_height + tall_height, head_height)],
            head_load.at[col],
        )
        copy.start()
        head_copies.append(copy)

    def side_message(zt, col):
        return remote(
            both.at[zt, col, 1 - c],
            side.at[zt, col],
            side_send.at[col, zt],
            side_recv.at[col, zt],
            mate,
        )

    def half_message(zt, which):
        return remote(
            piece(both.at[zt, DIAGONAL, c], half_of(head, which)),
            half_in.at[which, zt],
            send.at[0, which, zt],
            recv.at[0, which, zt],
            (at_x, at_y)[which],
        )

    def full_message(zt, which):
        return remote(
            piece(both.at[zt, (ACROSS_X, ACROSS_Y)[which], c], head),
            full_in.at[which, zt],
            send.at[1, which, zt],
            recv.at[1, which, zt],
            (at_x, at_y)[which],
        )

    def line_message(zt, way):
        return remote(
            piece(both.at[zt, OWN, c], head),
            line_in.at[way, zt],
            send.at[2, way, zt],
            recv.at[2, way, zt],
            (up, down)[way],
        )

    def tail_message(zt, way):
        return remote(
            both.at[zt, :, c, pl.ds(tail[0], tail_rows)],
            tail_line.at[way, zt],
            tail_send.at[way, zt],
            tail_recv.at[way, zt],
            (up, down)[way],
        )

    def merged(zt, col):
        side_message(zt, col).wait_recv()
        mine = both.at[zt, col, c]
        accumulate(mine, [mine, side.at[zt, col]], rows)

    def second(zt):
        for which, col in ((0, ACROSS_X), (1, ACROSS_Y)):
            half_message(zt, 1 - which).wait_recv()
            target = piece(both.at[zt, col, c], half_of(head, 1 - which))
            accumulate(target, [target, half_in.at[1 - which, zt]], head_rows // 2)
            full_message(zt, which).start()

    def tail_add(zt, way):
        tail_message(zt, way).wait_recv()
        for col in range(4):
            target = piece(both.at[zt, col, c], tail)
            accumulate(target, [target, tail_line.at[way, zt, col]], tail_rows)

    def onward(zt, add, message):
        for way, valid in ((0, zt > z), (1, zt < z)):
            behind = (below, above)[way]
            pl.when(jnp.logical_and(valid, behind))(functools.partial(add, zt, way))
            pl.when(valid)(lambda way=way: message(zt, way).start())

    def tail_step(zt):
        onward(zt, tail_add, tail_message)

    def line_add(zt, way):
        line_message(zt, way).wait_recv()
        mine = piece(both.at[zt, OWN, c], head)
        accumulate(mine, [mine, line_in.at[way, zt]], head_rows)

    def third(zt):
        for which in (0, 1):
            full_message(zt, which).wait_recv()
        base = [piece(both.at[zt, OWN, c], head), full_in.at[0, zt], full_in.at[1, zt]]
        accumulate(base[0], base, head_rows)
        onward(zt, line_add, line_message)

    def after(n):
        i, col = turn_of(n)
        zt = plane_at(i)
        merged(zt, col)

        @pl.when(col == DIAGONAL)
        def _():
            half_message(zt, 0).start()
            half_message(zt, 1).start()

        @pl.when(col == OWN)
        def _():
            second(zt)
            pl.when(i < planes - 1)(lambda: tail_step(zt))
            pl.when(i > 0)(lambda: third(plane_at(i - 1)))

    for copy in head_copies:
        copy.wait()

    def await_plane_rows():
        for step in (ACROSS_X, ACROSS_Y, DIAGONAL):
            here = all_rows.at[:, cols[step], c]
            remote(here, here, row_send.at[1, step], row_recv.at[1, step], mate).wait_recv()

    def body(n, unused):
        for copy in fetches(n):
            copy.wait()

        @pl.when(n + 1 < 4 * planes)
        def _():
            for copy in fetches(n + 1):
                copy.start()

        (i, col), k, slot = turn_of(n), chip_of(n), lax.rem(n, 2)
        zt = plane_at(i)
        region = (k >= split[0]).astype(jnp.int32) + (k >= split[1]).astype(jnp.int32)
        product_wide = to_half(nn(wide_buf[slot], rights[region]))
        both[zt, col, 0, :wide_height] = product_wide[:wide_height]
        both[zt, col, 1, :wide_height] = product_wide[wide_height:]
        product_tall = to_half(nn(tall_buf[slot], outer[...]))
        here = slice(wide_height, wide_height + tall_height)
        both[zt, col, 0, here] = product_tall[:tall_height]
        both[zt, col, 1, here] = product_tall[tall_height:]
        side_message(zt, col).start()
        pl.when(n > 0)(lambda: after(n - 1))

        @pl.when(n == ROWS_AT)
        def _():
            for d, who in enumerate(line):
                row_line(d, who).wait_recv()
            for step in (ACROSS_X, ACROSS_Y, DIAGONAL):
                row_plane(step).start()
            total = vector_terms[:, f]
            for d, who in enumerate(plane):
                vector_first(d, who).wait_recv()
                total = total + vector_in[d]
            vector_mid[...] = total
            for d, who in enumerate(line):
                vector_second(d, who).start()

        @pl.when(n == MATE_AT)
        def _():
            await_plane_rows()
            row_mate().start()

        return unused

    lax.fori_loop(0, 4 * planes, body, 0)
    after(jnp.int32(4 * planes - 1))
    here = all_rows.at[:, :, 1 - c]
    remote(here, here, row_send.at[2, 0], row_recv.at[2, 0], mate).wait_recv()
    words = word_grad.shape[0]
    offset = (z * width + f) * words

    def look_back(first, after):
        def body(n, unused):
            zt, chip = n // 4, lax.rem(n, 4)
            row = lax.broadcasted_iota(jnp.int32, (words, BUCKET), 0) + offset
            total = word_grad[...]
            for core in (0, 1):
                ids = facts[zt, chip * 2 + core]
                picks = jnp.concatenate(
                    [to_half((row == ids[i : i + 1, :]).astype(jnp.float32)) for i in (0, 1)], 1
                )
                total = total + nn(picks, all_rows[zt, chip, core])
            word_grad[...] = total
            return unused

        lax.fori_loop(first, after, body, 0)

    word_grad[...] = base_word[...]
    look_back(0, 2 * planes)
    targets = [plane_at(i) for i in range(planes)]

    def tail_half_message(which):
        return remote(
            piece(both.at[z, DIAGONAL, c], half_of(tail, which)),
            tail_half.at[which],
            tail_send.at[2, which],
            tail_recv.at[2, which],
            (at_x, at_y)[which],
        )

    def tail_full_message(which):
        return remote(
            piece(both.at[z, (ACROSS_X, ACROSS_Y)[which], c], tail),
            tail_full.at[which],
            tail_send.at[3, which],
            tail_recv.at[3, which],
            (at_x, at_y)[which],
        )

    pl.when(below)(lambda: tail_add(z, 0))
    pl.when(above)(lambda: tail_add(z, 1))
    for which in (0, 1):
        push(None, functools.partial(tail_half_message, which))
    look_back(2 * planes, 4 * planes)
    for which, col in ((1, ACROSS_X), (0, ACROSS_Y)):
        tail_half_message(which).wait_recv()
        target = piece(both.at[z, col, c], half_of(tail, which))
        accumulate(target, [target, tail_half.at[which]], tail_rows // 2)
    for which in (0, 1):
        push(None, functools.partial(tail_full_message, which))
    for which in (0, 1):
        full_message(z, which).wait_recv()
    goal = piece(out, head)
    accumulate(
        goal, [piece(both.at[z, OWN, c], head), full_in.at[0, z], full_in.at[1, z]], head_rows
    )
    for present, way in ((below, 0), (above, 1)):

        def add(way=way):
            line_message(z, way).wait_recv()
            accumulate(goal, [goal, line_in.at[way, z]], head_rows)

        pl.when(present)(add)
    for which in (0, 1):
        tail_full_message(which).wait_recv()
    accumulate(
        piece(out, tail),
        [piece(both.at[z, OWN, c], tail), tail_full.at[0], tail_full.at[1]],
        tail_rows,
    )
    total = vector_mid[z]
    for d, who in enumerate(line):
        vector_second(d, who).wait_recv()
        total = total + vector_last[d]
    height = place_grad.shape[0]
    own = z * width + f
    low_half = (own * height < BUCKET).astype(jnp.float32)
    high_half = (own * height < 2 * BUCKET).astype(jnp.float32) - low_half
    slot = pl.multiple_of(lax.rem(own * height, BUCKET), height)
    lane = lax.broadcasted_iota(jnp.int32, (1, 128), 1)
    grad = jnp.zeros((height, 128), jnp.float32)
    for zt in range(planes):
        for chip in range(4):
            for core in (0, 1):
                note = facts[zt, chip * 2 + core, 4:5, :]
                two = jnp.sum(
                    jnp.where(lane == 1, (note > 0).astype(jnp.float32), 0.0), 1, keepdims=True
                )
                lower = all_rows[zt, chip, core, pl.ds(slot, height)].astype(jnp.float32)
                upper = all_rows[zt, chip, core, pl.ds(BUCKET + slot, height)].astype(jnp.float32)
                grad = grad + low_half * (lower + two * upper) + high_half * (1.0 - two) * upper
    place_grad[...] = grad
    squares = jnp.sum(grad * grad) + jnp.sum(back_decoder[...] * back_decoder[...])
    squares = squares + jnp.sum(word_grad[...] * word_grad[...])
    squares = squares + jnp.sum(out[...] * out[...])
    last[z, f, 0:8] = total
    last[z, f, 8:16] = jnp.concatenate(
        [totals[...], jnp.where(lane == 0, squares, 0.0), jnp.zeros((6, 128), jnp.float32)], 0
    )
    first_copies, second_copies = [], []
    for d, who in enumerate(line):
        here = last.at[z, f]
        first_copies.append(remote(here, here, end_send.at[0, d], end_recv.at[0, d], who))
        first_copies[-1].start()
    for d, who in enumerate(line):
        here = last.at[lax.rem(z - d - 1 + planes, planes), f]
        remote(here, here, end_send.at[0, d], end_recv.at[0, d], who).wait_recv()
    for d, who in enumerate(plane):
        here = last.at[:, f]
        second_copies.append(remote(here, here, end_send.at[1, d], end_recv.at[1, d], who))
        second_copies[-1].start()
    for d, who in enumerate(plane):
        here = last.at[:, lax.rem(f - d - 1 + width, width)]
        remote(here, here, end_send.at[1, d], end_recv.at[1, d], who).wait_recv()
    summed = last[...]
    tails = jnp.sum(jnp.sum(summed[:, :, 8:16], 0), 0)
    squares = jnp.sum(summed[:, :, 0:8] * summed[:, :, 0:8]) + jnp.sum(tails[1:2, :])
    norm = jnp.sqrt(jnp.broadcast_to(squares, (1, 128)))
    factor = jnp.minimum(1.0, CLIP_NORM / (norm + NORM_EPSILON))
    mlm = totals[0:1, :] - jnp.sum(jnp.where(lane == 1, tails[0:1, :], 0.0))
    sop = jnp.zeros((1, 128), jnp.float32) + jnp.sum(jnp.where(lane == 2, tails[0:1, :], 0.0))
    ends[...] = jnp.concatenate(
        [norm, factor, mlm, sop, jnp.zeros((4, 128), jnp.float32)], 0
    )
    for copy in first_copies + second_copies:
        copy.wait_send()
    row_mate().wait_send()
    for condition, make in sent:
        maybe(condition, lambda make=make: make().wait_send())
    for zt in targets:
        for col in order:
            side_message(zt, col).wait_send()
        for which in (0, 1):
            half_message(zt, which).wait_send()
            full_message(zt, which).wait_send()
        for way, valid in ((0, zt > z), (1, zt < z)):

            def done(zt=zt, way=way):
                tail_message(zt, way).wait_send()
                line_message(zt, way).wait_send()

            pl.when(valid)(done)
    for step in (ACROSS_X, ACROSS_Y, DIAGONAL):
        row_plane(step).wait_send()
    for d, who in enumerate(line):
        vector_second(d, who).wait_send()


def run_finish(
    left_wide,
    left_tall,
    rights,
    outer,
    head_grad,
    own_rows,
    vector_terms,
    facts,
    base_word,
    back_decoder,
    totals,
    places_count,
    mesh_shape,
    identity,
):
    planes, width = mesh_shape
    devices = planes * width
    columns = outer.shape[1]
    heights = (
        left_wide.shape[0] // devices,
        left_tall.shape[0] // devices,
        head_grad.shape[0] // devices,
    )
    rows = sum(heights)
    long = left_wide.shape[1]
    split = (3 * D // (2 * heights[0]), 4 * D // (2 * heights[0]))
    head, tail = (high - low for low, high in cuts_of(rows))
    half, single = jnp.bfloat16, jnp.float32
    block = vector_terms.shape[1:]
    vmem = pl.BlockSpec(memory_space=VMEM_SPACE)
    any_space = pl.BlockSpec(memory_space=pl.ANY)
    dma = pltpu.SemaphoreType.DMA
    out, word_grad, place_grad, last, ends = pl.pallas_call(
        functools.partial(finish_kernel, planes, heights, split),
        out_shape=[
            jax.ShapeDtypeStruct((rows, columns), single),
            jax.ShapeDtypeStruct(base_word.shape, single),
            jax.ShapeDtypeStruct((places_count, 128), single),
            jax.ShapeDtypeStruct((planes, width, 16, 128), single),
            jax.ShapeDtypeStruct((8, 128), single),
        ],
        in_specs=[any_space, any_space, vmem, vmem, any_space, vmem, vmem] + [vmem] * 4,
        out_specs=[vmem] * 5,
        scratch_shapes=[
            VMEM_SPACE((planes, width // 2, 2, *own_rows.shape), half),
            VMEM_SPACE((planes, 4, 2, rows, columns), half),
            VMEM_SPACE((planes, 4, rows, columns), half),
            VMEM_SPACE((2, planes, head // 2, columns), half),
            VMEM_SPACE((2, planes, head, columns), half),
            VMEM_SPACE((2, planes, head, columns), half),
            VMEM_SPACE((2, planes, 4, tail, columns), half),
            VMEM_SPACE((2, tail // 2, columns), half),
            VMEM_SPACE((2, tail, columns), half),
            VMEM_SPACE((2, 2 * heights[0], long), half),
            VMEM_SPACE((2, 2 * heights[1], long), half),
            VMEM_SPACE((width - 1, planes, *block), single),
            VMEM_SPACE((planes, *block), single),
            VMEM_SPACE((planes - 1, *block), single),
            dma((2, 2)),
            dma((4,)),
            dma((4, planes)),
            dma((4, planes)),
            dma((3, 2, planes)),
            dma((3, 2, planes)),
            dma((4, planes)),
            dma((4, planes)),
            dma((3, 4)),
            dma((3, 4)),
            dma((2, width)),
            dma((2, width)),
            dma((2, width)),
            dma((2, width)),
        ],
        compiler_params=pltpu.CompilerParams(
            collective_id=identity, has_side_effects=True, vmem_limit_bytes=VMEM_ASK
        ),
    )(
        left_wide,
        left_tall,
        rights,
        outer,
        head_grad.reshape(planes, width // 2, 2, heights[2], columns),
        own_rows,
        vector_terms.reshape(planes, width, *block),
        facts.reshape(planes, width, *facts.shape[1:]),
        base_word,
        back_decoder,
        totals,
    )
    return out, heights, word_grad, place_grad, last, ends


LIFT = 128
WIRE = 48


def exact_rows(pick, values):
    first = to_half(values)
    rest = values - first.astype(jnp.float32)
    second = to_half(rest)
    third = to_half(rest - second.astype(jnp.float32))
    return nn(pick, first) + nn(pick, second) + nn(pick, third)


def lanes_to_rows(x):
    return jnp.concatenate([x[:, i : i + 128] for i in range(0, x.shape[1], 128)], 0)


def rows_to_lanes(x):
    return jnp.concatenate([x[i : i + 1] for i in range(x.shape[0])], 1)


def head_kernel(
    planes,
    lengths,
    sop_labels,
    final,
    head,
    word,
    decoder,
    facts,
    own_facts,
    vec,
    back_final,
    back_word,
    back_decoder,
    back_head,
    wide_sums,
    small_sums,
    totals,
    all_t,
    stats,
    powers,
    back_t,
    plane_in,
    middle,
    line_in,
    word_half,
    sends,
    recvs,
):
    width = 8
    z, c, cols = places()
    f = cols[0] * 2 + c
    line = [(lax.rem(z + d, planes), f) for d in range(1, planes)]
    plane = [(z, lax.rem(f + d, width)) for d in range(1, width)]
    greet([(None, who) for who in line + plane])
    offset = (z * width + f) * word.shape[0]
    words, slots = word.shape[0], planes * width * WIRE
    single = jnp.float32

    def gather_line(ref, kind):
        here = ref.at[z, f]
        return [
            remote(here, here, sends.at[kind, d], recvs.at[kind, d], who)
            for d, who in enumerate(line)
        ]

    def gather_plane(ref, kind):
        here = ref.at[:, f]
        return [
            remote(here, here, sends.at[kind, d], recvs.at[kind, d], who)
            for d, who in enumerate(plane)
        ]

    def await_line(ref, kind):
        for d in range(planes - 1):
            here = ref.at[lax.rem(z - d - 1 + planes, planes), f]
            remote(here, here, sends.at[kind, d], recvs.at[kind, d], line[d]).wait_recv()

    def await_plane(ref, kind):
        for d in range(width - 1):
            here = ref.at[:, lax.rem(f - d - 1 + width, width)]
            remote(here, here, sends.at[kind, d], recvs.at[kind, d], plane[d]).wait_recv()

    started = []
    lane = lax.broadcasted_iota(jnp.int32, (1, 128), 1)
    notes = facts[...]
    labels = jnp.concatenate([notes[i, 2:3, :WIRE] for i in range(planes * width)], 1)
    used = (lanes_to_rows(labels) >= 0).astype(single)
    mlm_count = jnp.sum(used)
    seconds = jnp.where(lane == 1, (notes[:, 4, :] > 0).astype(single), 0.0)
    sop_count = planes * width + jnp.sum(seconds)
    mlm_scale = 1.0 / jnp.broadcast_to(mlm_count, (1, 1))
    sop_scale = 1.0 / jnp.broadcast_to(sop_count, (1, 1))

    def start(copies):
        for copy in copies:
            copy.start()
        started.extend(copies)

    final_half = to_half(final[...])
    place = lax.broadcasted_iota(jnp.int32, (ROWS, LIFT), 0)
    scatter = to_half((place == own_facts[3:4, :]).astype(single))
    pick = scatter.T
    picked = to_half(nn(pick, final_half))
    dense = nt(picked, head[:E, :]) + short_row(vec, MLM_B)
    bend = jnp.tanh(GELU_A * dense * (1.0 + GELU_B * dense * dense))
    hat, inverse = norm_forward(0.5 * dense * (1.0 + bend))
    slope = 0.5 * (1.0 + bend) + (0.5 * GELU_A) * dense * (1.0 - bend * bend) * (
        1.0 + 3.0 * GELU_B * dense * dense
    )
    rows_half = to_half(hat * short_row(vec, MLM_G) + short_row(vec, MLM_LB))
    all_t[z, f] = rows_half[:WIRE]
    start(gather_line(all_t, 0))

    word_half[...] = to_half(word[...])
    row16 = lax.broadcasted_iota(jnp.int32, (16, ROWS), 0)
    col16 = lax.broadcasted_iota(jnp.int32, (16, ROWS), 1)
    leads = to_half(
        (jnp.logical_and(row16 < 2, col16 == row16 * BUCKET)).astype(single)
    )
    firsts = to_half(nn(leads, final_half))
    pooled = jnp.tanh(nt(firsts, head[E : E + D, :]) + wide_row(vec, POOL_B))
    await_line(all_t, 0)
    start(gather_plane(all_t, 1))
    zero_class, one_class = lanes_of(vec, CLS_AT, D // 128), lanes_of(vec, CLS_AT + D // 128, D // 128)
    c0 = jnp.sum(pooled * zero_class, -1, keepdims=True)
    c1 = jnp.sum(pooled * one_class, -1, keepdims=True)
    class_top = jnp.maximum(c0, c1)
    e0, e1 = jnp.exp(c0 - class_top), jnp.exp(c1 - class_top)
    class_total = e0 + e1
    which = lax.broadcasted_iota(jnp.int32, (16, 1), 0)
    label = jnp.where(which == 0, sop_labels[0], sop_labels[1])
    hit = (label == 1).astype(single)
    two = (lengths[1] > 0).astype(single)
    present = jnp.where(which == 0, 1.0, jnp.where(which == 1, two, 0.0))
    losses = (jnp.log(class_total) + class_top - (c0 + hit * (c1 - c0))) * present
    weight = present * sop_scale
    back_c0 = (e0 / class_total - (1.0 - hit)) * weight
    back_c1 = (e1 / class_total - hit) * weight
    wide_sums[1:2, :] = jnp.sum(back_c0 * pooled, 0, keepdims=True)
    wide_sums[2:3, :] = jnp.sum(back_c1 * pooled, 0, keepdims=True)
    pre_half = to_half((back_c0 * zero_class + back_c1 * one_class) * (1.0 - pooled * pooled))
    wide_sums[0:1, :] = jnp.sum(pre_half.astype(single), 0, keepdims=True)
    back_head[E : E + D, :] = to_half(tn(pre_half, firsts))
    back_firsts = nn(pre_half, head[E : E + D, :])
    await_plane(all_t, 1)

    row = lax.broadcasted_iota(jnp.int32, (words, 128), 0) + offset
    bias = jnp.broadcast_to(to_half(decoder[...]).astype(single), (8, words)).T[:, 0:1]
    tops, sums, targets = [], [], []
    chunk = width * WIRE
    flat_t = all_t[...].reshape(slots, E)
    for low in range(0, slots, chunk):
        logits = nt(word_half[...], flat_t[low : low + chunk]) + bias
        top = jnp.max(logits, 0, keepdims=True)
        power = jnp.exp(logits - top)
        powers[:, pl.ds(low, chunk)] = power
        tops.append(top)
        sums.append(jnp.sum(power, 0, keepdims=True))
        for at in range(0, chunk, 128):
            mark = row == labels[:, low + at : low + at + 128]
            targets.append(
                jnp.sum(jnp.where(mark, logits[:, at : at + 128], 0.0), 0, keepdims=True)
            )
    own_top = lanes_to_rows(jnp.concatenate(tops, 1))
    groups = slots // 128
    stats[z, f, 0:groups] = own_top
    stats[z, f, groups : 2 * groups] = lanes_to_rows(jnp.concatenate(sums, 1))
    start(gather_line(stats, 2))
    target = jnp.sum(jnp.concatenate(targets, 0) * used)
    await_line(stats, 2)
    start(gather_plane(stats, 3))
    await_plane(stats, 3)
    every = stats[...].reshape(planes * width, 2 * groups, 128)
    top = jnp.max(every[:, :groups], 0)
    total = jnp.sum(every[:, groups:] * jnp.exp(every[:, :groups] - top[None]), 0)
    log_sum = jnp.sum((jnp.log(total) + top) * used)
    weight = used * mlm_scale
    factor = rows_to_lanes(weight * jnp.exp(own_top - top) / total)
    weight = rows_to_lanes(weight)

    def slot_terms(zz, d, who):
        return remote(
            back_t.at[zz, who[1]],
            plane_in.at[d, zz],
            sends.at[4 + zz, d],
            recvs.at[4 + zz, d],
            who,
        )

    words_total = jnp.zeros((words, E), single)
    word_sums = jnp.zeros((8, words), single)
    ones = jnp.ones((8, width * WIRE), jnp.bfloat16)
    for low in range(0, slots, chunk):
        parts = []
        for at in range(low, low + chunk, 128):
            mark = row == labels[:, at : at + 128]
            part = powers[:, pl.ds(at, 128)] * factor[:, at : at + 128] - jnp.where(
                mark, weight[:, at : at + 128], 0.0
            )
            parts.append(to_half(part))
        half = jnp.concatenate(parts, 1)
        word_sums = word_sums + nt(ones, half)
        words_total = words_total + nn(half, flat_t[low : low + chunk])
        zz = low // chunk
        back_t[zz] = tn(half, word_half[...]).reshape(width, WIRE, E)
        start([slot_terms(zz, d, who) for d, who in enumerate(plane)])
    back_word[...] = words_total
    back_decoder[...] = word_sums[0:1]

    for zz in range(planes):
        total = back_t[zz, f]
        for d in range(width - 1):
            slot_terms(zz, d, plane[d]).wait_recv()
            total = total + plane_in[d, zz]
        middle[zz] = total
    start(
        [
            remote(middle.at[who[0]], line_in.at[d], sends.at[4 + planes, d], recvs.at[4 + planes, d], who)
            for d, who in enumerate(line)
        ]
    )
    total = middle[z]
    for d in range(planes - 1):
        remote(
            line_in.at[d], line_in.at[d], sends.at[4 + planes, d], recvs.at[4 + planes, d], line[d]
        ).wait_recv()
        total = total + line_in[d]
    back_rows = jnp.concatenate([total, jnp.zeros((LIFT - WIRE, E), single)], 0)
    small_sums[1:2, :] = jnp.sum(back_rows * hat, 0, keepdims=True)
    small_sums[2:3, :] = jnp.sum(back_rows, 0, keepdims=True)
    dense_half = to_half(norm_backward(back_rows, short_row(vec, MLM_G), hat, inverse) * slope)
    small_sums[0:1, :] = jnp.sum(dense_half.astype(single), 0, keepdims=True)
    back_head[:E, :] = to_half(tn(dense_half, picked))
    back_final[...] = exact_rows(scatter, nn(dense_half, head[:E, :]))
    back_final[0:1, :] = back_final[0:1, :] + back_firsts[0:1]
    back_final[BUCKET : BUCKET + 1, :] = back_final[BUCKET : BUCKET + 1, :] + back_firsts[1:2]
    sop_sum = jnp.sum(losses)
    ends = jnp.zeros((1, 128), single)
    for at, value in enumerate((log_sum, target, sop_sum, mlm_count, sop_count)):
        ends = ends + jnp.where(lane == at, value, 0.0)
    totals[...] = ends
    for copy in started:
        copy.wait_send()


def run_head(
    lengths, sop_labels, final, head, word, decoder, facts, own_facts, vec, mesh_shape, identity
):
    planes, width = mesh_shape
    words = word.shape[0]
    slots = planes * width * WIRE
    groups = slots // 128
    single, half = jnp.float32, jnp.bfloat16
    vmem = pl.BlockSpec(memory_space=VMEM_SPACE)
    smem = pl.BlockSpec(memory_space=pltpu.SMEM)
    dma = pltpu.SemaphoreType.DMA
    return pl.pallas_call(
        functools.partial(head_kernel, planes),
        out_shape=[
            jax.ShapeDtypeStruct((ROWS, D), single),
            jax.ShapeDtypeStruct((words, E), single),
            jax.ShapeDtypeStruct((1, words), single),
            jax.ShapeDtypeStruct(head.shape, half),
            jax.ShapeDtypeStruct((3, D), single),
            jax.ShapeDtypeStruct((3, E), single),
            jax.ShapeDtypeStruct((1, 128), single),
        ],
        in_specs=[smem] * 2 + [vmem] * 7,
        out_specs=[vmem] * 7,
        scratch_shapes=[
            VMEM_SPACE((planes, width, WIRE, E), half),
            VMEM_SPACE((planes, width, 2 * groups, 128), single),
            VMEM_SPACE((words, slots), single),
            VMEM_SPACE((planes, width, WIRE, E), single),
            VMEM_SPACE((width - 1, planes, WIRE, E), single),
            VMEM_SPACE((planes, WIRE, E), single),
            VMEM_SPACE((planes - 1, WIRE, E), single),
            VMEM_SPACE((words, E), half),
            dma((5 + planes, width)),
            dma((5 + planes, width)),
        ],
        compiler_params=pltpu.CompilerParams(
            collective_id=identity, has_side_effects=True, vmem_limit_bytes=VMEM_ASK
        ),
    )(lengths, sop_labels, final, head, word, decoder, facts, own_facts, vec)


def adam_update(weight, gradient, first, second, rate):
    first = BETA_ONE * first + (1 - BETA_ONE) * gradient
    second = BETA_TWO * second + (1 - BETA_TWO) * gradient * gradient
    first_hat = first / (1 - BETA_ONE**STEP)
    second_hat = second / (1 - BETA_TWO**STEP)
    updated = weight - rate * (
        first_hat / (jnp.sqrt(second_hat) + ADAM_EPSILON) + WEIGHT_DECAY * weight
    )
    return (updated, first, second)


def adam_kernel(blocks, rates, *refs):
    count = len(rates)
    ends, refs = refs[0], refs[1:]
    ins, outs = refs[: 4 * count], refs[4 * count :]
    factor = ends[1:2, 0:1]

    def update(number):
        weight, first, second, gradient = ins[4 * number : 4 * number + 4]
        grad = gradient[...]
        if grad.ndim > 2:
            grad = grad[:, :, :8].reshape(-1, 128)[: weight.shape[0]]
        results = adam_update(
            weight[...], factor * grad, first[...], second[...], rates[number]
        )
        for out, result in zip(outs[3 * number : 3 * number + 3], results):
            out[...] = result

    for number in range(blocks):
        update(number)

    @pl.when(pl.program_id(0) == 0)
    def _():
        for number in range(blocks, count):
            update(number)


def run_adam(ends, groups, steps):
    in_specs = [pl.BlockSpec(ends.shape, lambda i: (0, 0))]
    out_specs, shapes, given = [], [], [ends]
    blocks = 0
    for weight, first, second, gradient, low, rate in groups:
        rows, columns = weight.shape
        if low is None:
            spec = pl.BlockSpec(weight.shape, lambda i: (0, 0))
            zero = (0,) * gradient.ndim
            grad_spec = pl.BlockSpec(gradient.shape, lambda i, zero=zero: zero)
        else:
            blocks += 1
            height = rows // steps
            spec = pl.BlockSpec((height, columns), lambda i: (i, 0))
            grad_spec = pl.BlockSpec(
                (height, columns), lambda i, start=low // height: (start + i, 0)
            )
        in_specs += [spec] * 3 + [grad_spec]
        out_specs += [spec] * 3
        shapes += [jax.ShapeDtypeStruct(weight.shape, jnp.float32)] * 3
        given += [weight, first, second, gradient]
    return pl.pallas_call(
        functools.partial(adam_kernel, blocks, tuple(group[5] for group in groups)),
        grid=(steps,),
        out_shape=shapes,
        in_specs=in_specs,
        out_specs=out_specs,
        compiler_params=pltpu.CompilerParams(
            dimension_semantics=("arbitrary",), vmem_limit_bytes=VMEM_ASK
        ),
    )(*given)


class Network:
    def __init__(self, mesh):
        self.shape = (mesh.shape["dp"], mesh.shape["fsdp"])
        self.devices = self.shape[0] * self.shape[1]
        self.kernels = self.shape[1] == 8
        self.calls = 0

    def identity(self):
        self.calls += 1
        return self.calls

    def start(self, shards, own_word, own_facts, own_place):
        if self.kernels:
            return run_start(
                shards, own_word, own_facts, own_place, self.shape, self.identity()
            )
        weights = [lax.all_gather(to_half(w), AXES, axis=0, tiled=True) for w in shards]
        facts = lax.all_gather(own_facts, AXES)
        place = lax.all_gather(to_half(own_place), AXES).astype(jnp.float32)
        words = own_word.shape[0]
        ids = facts[:, : ROWS // 128].reshape(-1) - lax.axis_index(AXES) * words
        column = jnp.arange(words, dtype=jnp.int32)
        select = to_half(ids[:, None] == column[None, :])
        terms = product(select, to_half(own_word))
        found = lax.psum_scatter(terms, AXES, scatter_dimension=0, tiled=True)
        return weights, facts, place, found

    def head(self, lengths, sop_labels, final, head, word, decoder, facts, own_facts, vec):
        decoder = decoder[None]
        given = (lengths, sop_labels, final, head, word, decoder, facts, own_facts, vec)
        if self.kernels:
            return run_head(*given, self.shape, self.identity())
        return self.plain_head(*given)

    def plain_head(self, lengths, sop_labels, final, head, word, decoder, facts, own_facts, vec):
        short, cls = vec[SHORT_AT:], vec[CLS_AT:FF_AT].reshape(2, D)
        pool_b = vec[POOL_B * D // 128 : CLS_AT].reshape(D)
        labels = facts[:, 2, :WIRE].reshape(1, -1)
        mlm_count = jnp.sum((labels >= 0).astype(jnp.float32))
        sop_count = self.devices + jnp.sum((facts[:, 4, 1] > 0).astype(jnp.float32))
        single = jnp.float32
        offset = lax.axis_index(AXES) * word.shape[0]
        word_half, final_half = to_half(word), to_half(final)
        rows = own_facts[3, :WIRE]
        pick = (rows[:, None] == jnp.arange(ROWS, dtype=jnp.int32)[None]).astype(single)
        picked = to_half(product(to_half(pick), final_half))
        dense = times_transpose(picked, head[:E]) + short[MLM_B]
        bend = jnp.tanh(GELU_A * dense * (1.0 + GELU_B * dense * dense))
        hat, inverse = norm_forward(0.5 * dense * (1.0 + bend))
        slope = 0.5 * (1.0 + bend) + (0.5 * GELU_A) * dense * (1.0 - bend * bend) * (
            1.0 + 3.0 * GELU_B * dense * dense
        )
        rows_half = to_half(hat * short[MLM_G] + short[MLM_LB])
        all_rows = lax.all_gather(rows_half, AXES, axis=0, tiled=True)
        logits = times_transpose(word_half, all_rows) + to_half(decoder).astype(single).T
        mark = jnp.arange(word.shape[0], dtype=jnp.int32)[:, None] + offset == labels
        own_top = jnp.max(logits, 0)
        own_total = jnp.sum(jnp.exp(logits - own_top), 0)
        used = (labels[0] >= 0).astype(single)
        target = jnp.sum(jnp.sum(jnp.where(mark, logits, 0.0), 0) * used)
        top = lax.pmax(own_top, AXES)
        total = lax.psum(own_total * jnp.exp(own_top - top), AXES)
        log_sum = jnp.sum((jnp.log(total) + top) * used)
        weight = used / mlm_count
        half = to_half((jnp.exp(logits - top) / total - mark.astype(single)) * weight)
        back_rows = lax.psum_scatter(
            transpose_times(half, word_half), AXES, scatter_dimension=0, tiled=True
        )
        dense_half = to_half(norm_backward(back_rows, short[MLM_G], hat, inverse) * slope)
        back_final = lax.dot_general(
            pick, product(dense_half, head[:E]), (((0,), (0,)), ((), ())), precision=PRECISE
        )
        firsts = jnp.stack([final_half[0], final_half[BUCKET]])
        pooled = jnp.tanh(times_transpose(firsts, head[E : E + D]) + pool_b)
        classes = jnp.sum(pooled[:, None] * cls[None], -1)
        powers = jnp.exp(classes - jnp.max(classes, -1, keepdims=True))
        totals = jnp.sum(powers, -1, keepdims=True)
        onehot = jnp.stack([1 - sop_labels, sop_labels], 1).astype(single)
        present = jnp.stack([jnp.float32(1.0), (lengths[1] > 0).astype(single)])
        losses = jnp.log(totals[:, 0]) + jnp.max(classes, -1) - jnp.sum(classes * onehot, -1)
        back_classes = (powers / totals - onehot) * (present / sop_count)[:, None]
        back_pooled = jnp.sum(back_classes[:, :, None] * cls[None], 1)
        pre_half = to_half(back_pooled * (1.0 - pooled * pooled))
        back_firsts = product(pre_half, head[E : E + D])
        back_final = back_final.at[0].add(back_firsts[0]).at[BUCKET].add(back_firsts[1])
        back_cls = jnp.sum(back_classes[:, :, None] * pooled[:, None], 0)
        small_sums = [column_sum(dense_half), jnp.sum(back_rows * hat, 0), jnp.sum(back_rows, 0)]
        back_head = [transpose_times(dense_half, picked), transpose_times(pre_half, firsts)]
        ends = jnp.stack([log_sum, target, jnp.sum(losses * present), mlm_count, sop_count])
        return (
            back_final,
            product(half, all_rows),
            column_sum(half.T)[None],
            to_half(jnp.pad(jnp.concatenate(back_head, 0), ((0, E), (0, 0)))),
            jnp.concatenate([column_sum(pre_half)[None], back_cls], 0),
            jnp.stack(small_sums),
            jnp.pad(ends, (0, 123))[None],
        )

    def adam(self, ends, groups):
        if self.kernels:
            updates = run_adam(ends, groups, 4)
            return [updates[i : i + 3] for i in range(0, len(updates), 3)]
        updates = []
        for weight, first, second, gradient, low, rate in groups:
            rows = weight.shape[0]
            if low is not None:
                gradient = gradient[low : low + rows]
            gradient = gradient.reshape(-1, weight.shape[1])[:rows]
            updates.append(adam_update(weight, ends[1, 0] * gradient, first, second, rate))
        return updates

    def finish(
        self,
        left_wide,
        left_tall,
        rights,
        outer,
        head_grad,
        own_rows,
        vector,
        facts,
        base_word,
        back_decoder,
        totals,
        places_count,
    ):
        devices = self.devices
        if self.kernels:
            out, heights, word_grad, place_grad, last, ends = run_finish(
                left_wide,
                left_tall,
                rights,
                outer,
                head_grad,
                own_rows,
                vector,
                facts,
                base_word,
                back_decoder,
                totals,
                places_count,
                self.shape,
                self.identity(),
            )
            return out, heights, word_grad, place_grad, last, ends
        back_wide = jnp.concatenate(
            [
                product(left_wide[: 3 * D], rights[0]),
                product(left_wide[3 * D : 4 * D], rights[1]),
                product(left_wide[4 * D :], rights[2]),
            ],
            0,
        )
        sums = [
            lax.psum_scatter(p.astype(jnp.float32), AXES, scatter_dimension=0, tiled=True)
            for p in (back_wide, product(left_tall, outer), head_grad)
        ]
        all_rows = lax.all_gather(own_rows, AXES, axis=0, tiled=True)
        own, words = lax.axis_index(AXES), base_word.shape[0]
        ids = facts[:, : ROWS // 128].reshape(-1) - own * words
        select = to_half(ids[:, None] == jnp.arange(words, dtype=jnp.int32)[None, :])
        word_grad = base_word + transpose_times(select, all_rows)
        by_device = all_rows.reshape(devices, ROWS, E).astype(jnp.float32)
        two = (facts[:, 4, 1] > 0)[:, None, None]
        lower, upper = by_device[:, :BUCKET], by_device[:, BUCKET:]
        lower = jnp.sum(lower + jnp.where(two, upper, 0.0), 0)
        upper = jnp.sum(jnp.where(two, 0.0, upper), 0)
        every = jnp.concatenate([lower, upper], 0)
        every = jnp.pad(every, ((0, places_count * devices - ROWS), (0, 0)))
        place_grad = lax.dynamic_slice(every, (own * places_count, 0), (places_count, E))
        squares = sum(jnp.sum(g * g) for g in (*sums, word_grad, place_grad, back_decoder))
        reduced, tails, squares = lax.psum((vector, totals, squares), AXES)
        norm = jnp.sqrt(squares + jnp.sum(reduced * reduced))
        factor = jnp.minimum(1.0, CLIP_NORM / (norm + NORM_EPSILON))
        ends = jnp.stack([norm, factor, totals[0, 0] - tails[0, 1], tails[0, 2]])
        ends = jnp.broadcast_to(ends[:, None], (4, 128))
        heights = tuple(total.shape[0] for total in sums)
        return jnp.concatenate(sums, 0), heights, word_grad, place_grad, reduced, ends


CLS_AT, FF_AT, SHORT_AT = 10 * D // 128, 12 * D // 128, (12 * D + FF) // 128


def lanes_of(vec, first, count):
    return jnp.concatenate([vec[pl.ds(first + i, 1), :] for i in range(count)], 1)


def wide_row(vec, index):
    return lanes_of(vec, index * (D // 128), D // 128)


def short_row(vec, index):
    return vec[pl.ds(SHORT_AT + index, 1), :]


def nt(a, b):
    return lax.dot_general(a, b, (((1,), (1,)), ((), ())), preferred_element_type=jnp.float32)


def nn(a, b):
    return jnp.dot(a, b, preferred_element_type=jnp.float32)


def tn(a, b):
    return lax.dot_general(a, b, (((0,), (0,)), ((), ())), preferred_element_type=jnp.float32)


CHUNK = 512
PAIR = 2 * HEAD_DIM
PROJ_B, Q_B, V_B, O_B, LN1_G, LN1_B, FFO_B, LN2_G, LN2_B, POOL_B = range(10)


def allowed_block(lengths):
    shape = (ROWS, ROWS)
    row = lax.broadcasted_iota(jnp.int32, shape, 0)
    col = lax.broadcasted_iota(jnp.int32, shape, 1)
    two = lengths[1] > 0
    row_second = jnp.logical_and(row >= BUCKET, two).astype(jnp.int32)
    col_second = jnp.logical_and(col >= BUCKET, two).astype(jnp.int32)
    length = jnp.where(col_second == 1, lengths[1], lengths[0])
    live = col - BUCKET * col_second < length
    return jnp.logical_and(row_second == col_second, live)


def halves(x):
    lane = lax.broadcasted_iota(jnp.int32, x.shape, 1)
    zero = jnp.zeros_like(x)
    return jnp.where(lane < HEAD_DIM, x, zero), jnp.where(lane < HEAD_DIM, zero, x)


def kinds(lengths):
    row = lax.broadcasted_iota(jnp.int32, (ROWS, 1), 0)
    second = jnp.logical_and(row >= BUCKET, lengths[1] > 0).astype(jnp.int32)
    length = jnp.where(second == 1, lengths[1], lengths[0])
    return (row - BUCKET * second >= length // 2).astype(jnp.float32)


EMB_G, EMB_B, MLM_B, MLM_G, MLM_LB, TYPE_ZERO, TYPE_ONE = range(7)


def forward_kernel(
    lengths,
    found,
    place,
    lift,
    wide,
    tall,
    vec,
    final,
    embed_hat,
    embed_inverse,
    normed_half,
    rights,
    projected,
    weighting,
    hat_one,
    inverse_one,
    slope,
    active,
    hat_two,
    inverse_two,
    hidden,
):
    layer = pl.program_id(0)

    def row(index):
        return wide_row(vec, index)

    @pl.when(layer == 0)
    def _():
        two = (lengths[1] > 0).astype(jnp.float32)
        kind = kinds(lengths)
        lower = place[pl.ds(BUCKET, BUCKET), :]
        lower = jnp.where(two > 0, place[pl.ds(0, BUCKET), :], lower)
        embedded = found[...] + jnp.concatenate([place[pl.ds(0, BUCKET), :], lower], 0)
        zero, one = short_row(vec, TYPE_ZERO), short_row(vec, TYPE_ONE)
        hat, inverse = norm_forward(embedded + jnp.where(kind > 0, one, zero))
        embed_hat[...] = hat
        embed_inverse[...] = inverse
        normed = to_half(hat * short_row(vec, EMB_G) + short_row(vec, EMB_B))
        normed_half[...] = normed
        hidden[...] = nn(normed, lift[...]) + row(PROJ_B)

    half = to_half(hidden[...])
    rights[0] = half
    for part, bias in ((0, Q_B), (1, None), (2, V_B)):
        for low in range(0, D, 256):
            here = part * D + low
            value = nt(half, wide[pl.ds(here, 256), :])
            if bias is not None:
                value = value + lanes_of(vec, (bias * D + low) // 128, 2)
            projected[:, pl.ds(here, 256)] = to_half(value)
    allowed = allowed_block(lengths)
    for pair in range(HEADS // 2):
        lanes = pair * PAIR
        queries = halves(projected[:, pl.ds(lanes, PAIR)])
        keys = projected[:, pl.ds(D + lanes, PAIR)]
        values = halves(projected[:, pl.ds(2 * D + lanes, PAIR)])
        total = jnp.zeros((ROWS, PAIR), jnp.float32)
        for side in (0, 1):
            scores = jnp.where(allowed, nt(queries[side], keys) * SCALE, MASKED)
            powers = jnp.exp(scores - jnp.max(scores, -1, keepdims=True))
            weights = powers * (1.0 / jnp.sum(powers, -1, keepdims=True))
            weighting[2 * pair + side] = weights
            total = total + nn(to_half(weights), values[side])
        rights[1, :, pl.ds(lanes, PAIR)] = to_half(total)
    first_sum = hidden[...] + nt(rights[1], wide[pl.ds(3 * D, D), :]) + row(O_B)
    hat, inverse = norm_forward(first_sum)
    hat_one[...] = hat
    inverse_one[...] = inverse
    middle = hat * row(LN1_G) + row(LN1_B)
    half = to_half(middle)
    rights[2] = half
    total = middle + row(FFO_B)
    for low in range(0, FF, CHUNK):
        bias = lanes_of(vec, FF_AT + low // 128, CHUNK // 128)
        inner = nt(half, wide[pl.ds(4 * D + low, CHUNK), :]) + bias
        square = inner * inner
        bend = jnp.tanh(GELU_A * inner * (1.0 + GELU_B * square))
        act = to_half(0.5 * inner * (1.0 + bend))
        slope[:, pl.ds(low, CHUNK)] = 0.5 * (1.0 + bend) + (0.5 * GELU_A) * inner * (
            1.0 - bend * bend
        ) * (1.0 + 3.0 * GELU_B * square)
        active[pl.ds(low, CHUNK), :] = act.T
        total = total + nn(act, tall[pl.ds(low, CHUNK), :])
    hat, inverse = norm_forward(total)
    hat_two[...] = hat
    inverse_two[...] = inverse
    output = hat * row(LN2_G) + row(LN2_B)
    hidden[...] = output
    final[...] = output


def whole_spec():
    return pl.BlockSpec(memory_space=VMEM_SPACE, pipeline_mode=pl.Buffered(1))


def lift_spec():
    return pl.BlockSpec((E, D), lambda i: ((E + D) // E, 0), pipeline_mode=pl.Buffered(1))


def by_layer(*shape, order=lambda i: i):
    return pl.BlockSpec(
        (None, *shape), lambda i: (order(i),) + (0,) * len(shape), memory_space=VMEM_SPACE
    )


def run_forward(lengths, found, place, head, wide, tall, vec):
    def kept(*shape, dtype=jnp.bfloat16):
        return jax.ShapeDtypeStruct((LAYERS, *shape), dtype)

    single = jnp.float32
    names = (
        "final",
        "embed_hat",
        "embed_inverse",
        "normed_half",
        "rights",
        "projected",
        "weighting",
        "hat_one",
        "inverse_one",
        "slope",
        "active",
        "hat_two",
        "inverse_two",
    )
    outs = pl.pallas_call(
        forward_kernel,
        grid=(LAYERS,),
        out_shape=[
            jax.ShapeDtypeStruct((ROWS, D), single),
            jax.ShapeDtypeStruct((ROWS, E), single),
            jax.ShapeDtypeStruct((ROWS, 1), single),
            jax.ShapeDtypeStruct((ROWS, E), jnp.bfloat16),
            jax.ShapeDtypeStruct((3, LAYERS, ROWS, D), jnp.bfloat16),
            kept(ROWS, 3 * D),
            kept(HEADS, ROWS, ROWS, dtype=single),
            kept(ROWS, D, dtype=single),
            kept(ROWS, 1, dtype=single),
            kept(ROWS, FF, dtype=single),
            jax.ShapeDtypeStruct((FF, LAYERS * ROWS), jnp.bfloat16),
            kept(ROWS, D, dtype=single),
            kept(ROWS, 1, dtype=single),
        ],
        in_specs=[pl.BlockSpec(memory_space=pltpu.SMEM)]
        + [whole_spec()] * 2
        + [lift_spec()]
        + [whole_spec()] * 3,
        out_specs=[
            pl.BlockSpec((ROWS, D), lambda i: (0, 0)),
            pl.BlockSpec((ROWS, E), lambda i: (0, 0)),
            pl.BlockSpec((ROWS, 1), lambda i: (0, 0)),
            pl.BlockSpec((ROWS, E), lambda i: (0, 0)),
            pl.BlockSpec((3, None, ROWS, D), lambda i: (0, i, 0, 0)),
            by_layer(ROWS, 3 * D),
            by_layer(HEADS, ROWS, ROWS),
            by_layer(ROWS, D),
            by_layer(ROWS, 1),
            by_layer(ROWS, FF),
            pl.BlockSpec((FF, ROWS), lambda i: (0, i)),
            by_layer(ROWS, D),
            by_layer(ROWS, 1),
        ],
        scratch_shapes=[VMEM_SPACE((ROWS, D), single)],
        compiler_params=pltpu.CompilerParams(
            dimension_semantics=("arbitrary",), vmem_limit_bytes=VMEM_ASK
        ),
    )(lengths, found, place, head, wide, tall, vec)
    return dict(zip(names, outs))


def backward_kernel(
    lengths,
    start,
    wide_sums,
    small_sums,
    embed_hat,
    embed_inverse,
    normed_half,
    lift,
    head_in,
    wide,
    tall,
    vec,
    projected,
    weighting,
    hat_one,
    inverse_one,
    slope,
    hat_two,
    inverse_two,
    rows_out,
    back_lift,
    turned,
    outer,
    vector,
    sums,
    ff_sum,
    upstream,
    back_mixed,
    joint,
):
    step = pl.program_id(0)

    @pl.when(step == 0)
    def _():
        upstream[...] = start[...]
        sums[...] = jnp.zeros_like(sums)
        ff_sum[...] = jnp.zeros_like(ff_sum)

    def row(index):
        return wide_row(vec, index)

    def add_sum(index, value):
        here = pl.ds(index - Q_B, 1)
        sums[here, :] = sums[here, :] + jnp.sum(value, 0, keepdims=True)

    up = upstream[...]
    hat = hat_two[...]
    add_sum(LN2_G, up * hat)
    add_sum(LN2_B, up)
    back_second = norm_backward(up, row(LN2_G), hat, inverse_two[...])
    half = to_half(back_second)
    outer[...] = half
    add_sum(FFO_B, half.astype(jnp.float32))
    total = back_second
    for low in range(0, FF, CHUNK):
        lanes = pl.ds(low, CHUNK)
        inner = to_half(nt(half, tall[lanes, :]) * slope[:, lanes])
        ff_sum[:, lanes] = ff_sum[:, lanes] + jnp.sum(
            inner.astype(jnp.float32), 0, keepdims=True
        )
        turned[pl.ds(4 * D + low, CHUNK), :] = inner.T
        total = total + nn(inner, wide[pl.ds(4 * D + low, CHUNK), :])
    hat = hat_one[...]
    add_sum(LN1_G, total * hat)
    add_sum(LN1_B, total)
    back_first = norm_backward(total, row(LN1_G), hat, inverse_one[...])
    upstream[...] = back_first
    half = to_half(back_first)
    add_sum(O_B, half.astype(jnp.float32))
    turned[pl.ds(3 * D, D), :] = half.T
    back_mixed[...] = to_half(nn(half, wide[pl.ds(3 * D, D), :]))
    for pair in range(HEADS // 2):
        lanes = pair * PAIR
        queries = halves(projected[:, pl.ds(lanes, PAIR)])
        keys = halves(projected[:, pl.ds(D + lanes, PAIR)])
        values = projected[:, pl.ds(2 * D + lanes, PAIR)]
        grads = halves(back_mixed[:, pl.ds(lanes, PAIR)])
        zero = jnp.zeros((ROWS, PAIR), jnp.float32)
        back_query, back_key, back_value = zero, zero, zero
        for side in (0, 1):
            weights = weighting[2 * pair + side]
            soft = nt(grads[side], values)
            scores = to_half(
                weights * (soft - jnp.sum(weights * soft, -1, keepdims=True))
            )
            back_query = back_query + nn(scores, keys[side])
            back_key = back_key + tn(scores, queries[side])
            back_value = back_value + tn(to_half(weights), grads[side])
        joint[:, pl.ds(lanes, PAIR)] = to_half(back_query * SCALE)
        joint[:, pl.ds(D + lanes, PAIR)] = to_half(back_key * SCALE)
        joint[:, pl.ds(2 * D + lanes, PAIR)] = to_half(back_value)
    total = upstream[...]
    for part, bias in ((0, Q_B), (1, None), (2, V_B)):
        here = pl.ds(part * D, D)
        value = joint[:, here]
        if bias is not None:
            add_sum(bias, value.astype(jnp.float32))
        turned[here, :] = value.T
        total = total + nn(value, wide[here, :])
    upstream[...] = total

    @pl.when(step == LAYERS - 1)
    def _():
        half = to_half(upstream[...])
        back_lift[...] = to_half(tn(normed_half[...], half))
        back_normed = nt(half, lift[...])
        hat = embed_hat[...]
        back = norm_backward(back_normed, short_row(vec, EMB_G), hat, embed_inverse[...])
        rows_out[...] = to_half(back)
        kind = kinds(lengths)
        ones = jnp.sum(back * kind, 0, keepdims=True)
        zeros = jnp.sum(back * (1.0 - kind), 0, keepdims=True)
        vector[...] = jnp.zeros_like(vector)
        parts = [jnp.sum(half.astype(jnp.float32), 0, keepdims=True)]
        parts += [sums[pl.ds(i, 1), :] for i in range(8)]
        parts += [wide_sums[pl.ds(i, 1), :] for i in range(3)]
        parts += [ff_sum[...]]
        parts += [
            jnp.sum(back_normed * hat, 0, keepdims=True),
            jnp.sum(back_normed, 0, keepdims=True),
        ]
        parts += [small_sums[pl.ds(i, 1), :] for i in range(3)]
        parts += [zeros, ones]
        at = 0
        for part in parts:
            for low in range(0, part.shape[1], 128):
                vector[pl.ds(at, 1), :] = part[:, low : low + 128]
                at += 1


def run_backward(lengths, start, wide_sums, small_sums, head, back_head, wide, tall, vec, kept, lines):
    single, half = jnp.float32, jnp.bfloat16
    last = LAYERS - 1

    def order(i):
        return last - i

    return pl.pallas_call(
        backward_kernel,
        grid=(LAYERS,),
        out_shape=[
            jax.ShapeDtypeStruct((ROWS, E), half),
            jax.ShapeDtypeStruct(back_head.shape, half),
            jax.ShapeDtypeStruct((4 * D + FF, LAYERS * ROWS), half),
            jax.ShapeDtypeStruct((LAYERS, ROWS, D), half),
            jax.ShapeDtypeStruct((lines, 128), single),
        ],
        in_specs=[pl.BlockSpec(memory_space=pltpu.SMEM)]
        + [whole_spec()] * 6
        + [lift_spec(), pl.BlockSpec(memory_space=pl.ANY)]
        + [whole_spec()] * 3
        + [
            by_layer(ROWS, 3 * D, order=order),
            by_layer(HEADS, ROWS, ROWS, order=order),
            by_layer(ROWS, D, order=order),
            by_layer(ROWS, 1, order=order),
            by_layer(ROWS, FF, order=order),
            by_layer(ROWS, D, order=order),
            by_layer(ROWS, 1, order=order),
        ],
        out_specs=[
            pl.BlockSpec((ROWS, E), lambda i: (0, 0)),
            pl.BlockSpec((E, D), lambda i: ((E + D) // E, 0)),
            pl.BlockSpec((4 * D + FF, ROWS), lambda i: (0, order(i))),
            by_layer(ROWS, D, order=order),
            pl.BlockSpec((lines, 128), lambda i: (0, 0)),
        ],
        input_output_aliases={8: 1},
        scratch_shapes=[
            VMEM_SPACE((8, D), single),
            VMEM_SPACE((1, FF), single),
            VMEM_SPACE((ROWS, D), single),
            VMEM_SPACE((ROWS, D), half),
            VMEM_SPACE((ROWS, 3 * D), half),
        ],
        compiler_params=pltpu.CompilerParams(
            dimension_semantics=("arbitrary",), vmem_limit_bytes=VMEM_ASK
        ),
    )(
        lengths,
        start,
        wide_sums,
        small_sums,
        kept["embed_hat"],
        kept["embed_inverse"],
        kept["normed_half"],
        head,
        back_head,
        wide,
        tall,
        vec,
        kept["projected"],
        kept["weighting"],
        kept["hat_one"],
        kept["inverse_one"],
        kept["slope"],
        kept["hat_two"],
        kept["inverse_two"],
    )


def local(
    mesh,
    word_table,
    position_table,
    head_weights,
    decoder_bias,
    layer_wide,
    layer_tall,
    vectors,
    word_first,
    word_second,
    position_first,
    position_second,
    head_first,
    head_second,
    decoder_first,
    decoder_second,
    wide_first,
    wide_second,
    tall_first,
    tall_second,
    vector_first,
    vector_second,
    token_ids,
    seq_lengths,
    mlm_rows,
    mlm_labels,
    sop_labels,
):
    network = Network(mesh)

    def fill(count, value):
        return jnp.full((count,), value, jnp.int32)

    slots = mlm_labels.shape[0]
    facts = jnp.concatenate(
        [
            token_ids,
            mlm_labels,
            fill(128 - slots, -1),
            mlm_rows,
            fill(128 - slots, -1),
            seq_lengths,
            sop_labels,
            fill(3 * 128 + 124, 0),
        ]
    ).reshape(8, 128)
    (wide, tall, head), all_facts, place, found = network.start(
        (layer_wide.T, layer_tall, head_weights.T), word_table, facts, position_table
    )
    devices = all_facts.shape[0]
    place = place.reshape(-1, E)
    vec = vectors.reshape(-1, 128)
    kept = run_forward(seq_lengths, found, place, head, wide, tall, vec)
    (back_final, back_word_head, back_decoder, back_head, wide_sums, small_sums, totals) = (
        network.head(
            seq_lengths,
            sop_labels,
            kept["final"],
            head,
            word_table,
            decoder_bias,
            all_facts,
            facts,
            vec,
        )
    )
    mlm_count, sop_count = totals[0, 3], totals[0, 4]
    total = vectors.shape[0]
    share = -(-total // (devices * 1024)) * 1024
    back_rows, back_head, turned, outer, vector_grad = run_backward(
        seq_lengths,
        back_final,
        wide_sums,
        small_sums,
        head,
        back_head,
        wide,
        tall,
        vec,
        kept,
        devices * share // 128,
    )
    sums, heights, back_word, back_place, last, ends = network.finish(
        turned,
        kept["active"],
        kept["rights"].reshape(3, -1, D),
        outer.reshape(-1, D),
        back_head,
        back_rows,
        vector_grad.reshape(devices, -1, 128),
        all_facts,
        back_word_head,
        back_decoder,
        totals,
        position_table.shape[0],
    )
    wide_at, tall_at, head_at = 0, heights[0], heights[0] + heights[1]

    def turned_group(weight, first, second, low):
        return (weight.T, first.T, second.T, sums, low, LEARN_RATE)

    def flat(x):
        return x[None]

    def lines(x):
        return x.reshape(-1, 128)

    groups = (
        (word_table, word_first, word_second, back_word, 0, LEARN_RATE),
        turned_group(layer_wide, wide_first, wide_second, wide_at),
        (layer_tall, tall_first, tall_second, sums, tall_at, LEARN_RATE),
        turned_group(head_weights, head_first, head_second, head_at),
        (position_table, position_first, position_second, back_place, None, LEARN_RATE),
        (flat(decoder_bias), flat(decoder_first), flat(decoder_second), back_decoder, None)
        + (LEARN_RATE,),
        (lines(vectors), lines(vector_first), lines(vector_second), last, None, SMALL_RATE),
    )
    word, wide, tall, head, position, decoder, vector = network.adam(ends, groups)

    def turn(arrays):
        return [x.T for x in arrays]

    def plain(arrays):
        return [x.reshape(-1) for x in arrays]

    updates = (*word, *position, *turn(head), *plain(decoder), *turn(wide), *tall, *plain(vector))
    grad_norm, mlm_sum, sop_total = ends[0, 0], ends[2, 0], ends[3, 0]
    return (*updates, mlm_sum, mlm_count, sop_total, sop_count, grad_norm)


def solution(mesh):
    rows = P(AXES, None)
    columns = P(None, AXES)
    flat = P(AXES)
    whole = P()
    return jax.shard_map(
        functools.partial(local, mesh),
        mesh=mesh,
        in_specs=(rows, rows, columns, flat, columns, rows, whole)
        + (rows, rows) * 2
        + (columns, columns, flat, flat, columns, columns, rows, rows, whole, whole)
        + (flat,) * 5,
        out_specs=(rows,) * 6
        + (columns,) * 3
        + (flat,) * 3
        + (columns,) * 3
        + (rows,) * 3
        + (whole,) * 8,
        check_vma=False,
    )
```

```python
import functools

import jax
import jax.numpy as jnp
from jax import lax
from jax.experimental import pallas as pl
from jax.experimental.pallas import tpu as pltpu
from jax.sharding import PartitionSpec as P

D = 768
HEADS = 12
HEAD_DIM = 64
FF = 3072
E = 128
LAYERS = 4
STEP = 10
BUCKET = 128
ROWS = 2 * BUCKET

PRECISE = lax.Precision.HIGHEST
EPSILON = 1e-06
LEARN_RATE = 0.1
SMALL_RATE = 0.5
BETA_ONE = 0.9
BETA_TWO = 0.999
ADAM_EPSILON = 1e-08
WEIGHT_DECAY = 0.01
CLIP_NORM = 0.005
NORM_EPSILON = 1e-06
MASKED = -1e30
SCALE = HEAD_DIM ** (-0.5)
AXES = ("dp", "fsdp")


def to_half(x):
    return x.astype(jnp.bfloat16)


def product(a, b):
    return jnp.dot(a, b, preferred_element_type=jnp.float32)


def times_transpose(a, b):
    return lax.dot_general(a, b, (((1,), (1,)), ((), ())), preferred_element_type=jnp.float32)


def transpose_times(a, b):
    return lax.dot_general(a, b, (((0,), (0,)), ((), ())), preferred_element_type=jnp.float32)


def column_sum(x):
    return jnp.sum(x.astype(jnp.float32), 0)


def norm_forward(x):
    centre = x - jnp.mean(x, -1, keepdims=True)
    inverse = lax.rsqrt(jnp.mean(centre * centre, -1, keepdims=True) + EPSILON)
    return centre * inverse, inverse


def norm_backward(upstream, factor, hat, inverse):
    scaled = upstream * factor
    return inverse * (
        scaled
        - jnp.mean(scaled, -1, keepdims=True)
        - hat * jnp.mean(scaled * hat, -1, keepdims=True)
    )


GELU_A = 0.7978845608028654
GELU_B = 0.044715


MESH_ID = pl.DeviceIdType.MESH
VMEM_SPACE = pltpu.VMEM
VMEM_ASK = 60 * 1024 * 1024


def greet(peers):
    barrier = pltpu.get_barrier_semaphore()
    count = 0
    for present, who in peers:
        if present is None:
            pl.semaphore_signal(barrier, inc=1, device_id=who, device_id_type=MESH_ID)
            count = count + 1
        else:

            @pl.when(present)
            def _(who=who):
                pl.semaphore_signal(barrier, inc=1, device_id=who, device_id_type=MESH_ID)

            count = count + present.astype(jnp.int32)
    pl.semaphore_wait(barrier, count)


def maybe(condition, action):
    if condition is None:
        action()
    else:
        pl.when(condition)(action)


def remote(source, target, send, receive, who):
    return pltpu.make_async_remote_copy(
        src_ref=source,
        dst_ref=target,
        send_sem=send,
        recv_sem=receive,
        device_id=who,
        device_id_type=MESH_ID,
    )


OWN, ACROSS_X, ACROSS_Y, DIAGONAL = 0, 1, 2, 3


def cuts_of(rows, share):
    tail = max(32, round(rows * share / 32) * 32)
    head = rows - tail
    return ((0, head), (head, rows))


GATHER_TAIL, FINISH_TAIL = 0.3, 0.2


def half_of(span, which):
    low, high = span
    middle = (low + high) // 2
    return (low, middle) if which == 0 else (middle, high)


def places():
    z, f = lax.axis_index("dp"), lax.axis_index("fsdp")
    q, c = f // 2, lax.rem(f, 2)
    qx = q + 1 - 2 * lax.rem(q, 2)
    qy = lax.rem(q + 2, 4)
    qd = qx + qy - q
    return z, c, (q, qx, qy, qd)


def gather_stages(planes, rows, members, x, outs, buf, sems, where, opening):
    out_sem, send, recv, side_send, side_recv = sems
    z, c, cols = where
    cuts = cuts_of(rows, GATHER_TAIL)
    at_x, at_y, mate = (z, cols[1] * 2 + c), (z, cols[2] * 2 + c), (z, cols[0] * 2 + 1 - c)
    above, below = z < planes - 1, z > 0
    up, down = (z + 1, cols[0] * 2 + c), (z - 1, cols[0] * 2 + c)
    sent = []

    def block(zs, col, core, span):
        return buf.at[zs, cols[col], core, pl.ds(span[0], span[1] - span[0])]

    def push(condition, zs, col, span, who, slot, receive, mine=False):
        def make():
            here = block(zs, col, c, span)
            source = x.at[pl.ds(span[0], span[1] - span[0])] if mine else here
            return remote(source, here, send.at[slot[0], zs, slot[1]], receive, who)

        maybe(condition, lambda: make().start())
        sent.append((condition, make))

    def await_block(zs, col, span, receive, core=None):
        here = block(zs, col, c if core is None else core, span)
        remote(here, here, send.at[0, 0, 0], receive, mate).wait_recv()

    def deliver(zs, col, core, span):
        for index, (out, (low, high)) in enumerate(zip(outs, members)):
            first, last = max(low, span[0]), min(high, span[1])
            if first < last:
                pltpu.make_async_copy(
                    buf.at[zs, cols[col], core, pl.ds(first, last - first)],
                    out.at[zs, cols[col], core, pl.ds(first - low, last - first)],
                    out_sem.at[index],
                ).start()

    def share(condition, part, zs, col, span, kind, mine=False):
        def make():
            here = block(zs, col, c, span)
            source = x.at[pl.ds(span[0], span[1] - span[0])] if mine else here
            return remote(
                source, here, side_send.at[part, zs, kind], side_recv.at[part, zs, kind], mate
            )

        def action():
            make().start()
            if not mine:
                deliver(zs, col, c, span)

        maybe(condition, action)
        sent.append((condition, make))
        shared.append((condition, part, zs, col, span, kind))

    shared = []
    whole = [cuts[0], cuts[1]]
    for part in (0, 1):
        push(above, z, OWN, whole[part], up, (part, 2), recv.at[part, z, OWN], True)
        push(below, z, OWN, whole[part], down, (part, 3), recv.at[part, z, OWN], True)
    for part in (1, 0):
        if part == 0:
            opening()
        push(None, z, OWN, whole[part], at_x, (part, 0), recv.at[part, z, ACROSS_X], True)
        push(None, z, OWN, whole[part], at_y, (part, 1), recv.at[part, z, ACROSS_Y], True)
    for part in (0, 1):
        share(None, part, z, OWN, whole[part], 0, True)
    own_copy = pltpu.make_async_copy(x, buf.at[z, cols[0], c], out_sem.at[len(members)])
    own_copy.start()

    def turn(condition, part, zs):
        span = whole[part]
        for col, which, who, slot in ((ACROSS_X, 1, at_y, 4), (ACROSS_Y, 0, at_x, 5)):
            maybe(
                condition,
                lambda col=col: await_block(zs, col, span, recv.at[part, zs, col]),
            )
            push(condition, zs, col, half_of(span, which), who, (part, slot), recv.at[part, zs, 4 + which])
            if part == 1:
                push(above, zs, col, span, up, (1, 4 + 2 * col), recv.at[1, zs, col])
                push(below, zs, col, span, down, (1, 5 + 2 * col), recv.at[1, zs, col])
            share(condition, part, zs, col, span, col)

    yield
    turn(None, 1, z)
    yield
    for which in (0, 1):
        await_block(z, DIAGONAL, half_of(whole[1], which), recv.at[1, z, 4 + which])
    push(above, z, DIAGONAL, whole[1], up, (1, 10), recv.at[1, z, DIAGONAL])
    push(below, z, DIAGONAL, whole[1], down, (1, 11), recv.at[1, z, DIAGONAL])
    share(None, 1, z, DIAGONAL, whole[1], 3)
    yield
    turn(None, 0, z)

    def settle(upto):
        while len(shared) > upto:
            condition, part, zs, col, span, kind = shared.pop(0)

            def action():
                await_block(zs, col, span, side_recv.at[part, zs, kind], 1 - c)
                deliver(zs, col, 1 - c, span)

            maybe(condition, action)

    for step in range(1, planes):
        yield
        ways = ((z - step >= 0, z - step, above, up), (z + step < planes, z + step, below, down))
        for valid, zs, further, onward in ways:
            go = jnp.logical_and(valid, further)
            pl.when(valid)(
                lambda zs=zs: await_block(zs, OWN, whole[0], recv.at[0, zs, OWN])
            )
            push(go, zs, OWN, whole[0], onward, (0, 2), recv.at[0, zs, OWN])
            push(valid, zs, OWN, whole[0], at_x, (0, 0), recv.at[0, zs, ACROSS_X])
            push(valid, zs, OWN, whole[0], at_y, (0, 1), recv.at[0, zs, ACROSS_Y])
            share(valid, 0, zs, OWN, whole[0], 0)
        yield
        for valid, zs, further, onward in ways:
            go = jnp.logical_and(valid, further)
            for col in (OWN, ACROSS_X, ACROSS_Y, DIAGONAL):
                pl.when(valid)(
                    lambda zs=zs, col=col: await_block(zs, col, whole[1], recv.at[1, zs, col])
                )
                push(go, zs, col, whole[1], onward, (1, col), recv.at[1, zs, col])
                share(valid, 1, zs, col, whole[1], col)
        yield
        for valid, zs, further, onward in ways:
            turn(valid, 0, zs)
        settle(8)
    yield
    own_copy.wait()
    deliver(z, OWN, c, (0, rows))
    everywhere = [(None, z)] + [
        (valid, zs)
        for step in range(1, planes)
        for valid, zs in ((z - step >= 0, z - step), (z + step < planes, z + step))
    ]
    for condition, zs in everywhere:
        for which in (0, 1):
            span = half_of(whole[0], which)
            maybe(
                condition,
                lambda zs=zs, which=which, span=span: await_block(
                    zs, DIAGONAL, span, recv.at[0, zs, 4 + which]
                ),
            )
            share(condition, 0, zs, DIAGONAL, span, 3 + which)
    settle(0)
    for condition, make in sent:
        maybe(condition, lambda make=make: make().wait_send())
    for index, (out, (low, high)) in enumerate(zip(outs, members)):
        pltpu.make_async_copy(
            buf.at[:, :, :, pl.ds(low, high - low)], out, out_sem.at[index]
        ).wait()


def select_stages(planes, facts, own_word, found, refs, where, offset):
    part, side, plane_in, middle, line_in, turned, sems_send, sems_recv = refs
    z, c, cols = where
    q = cols[0]
    f = q * 2 + c
    mate = (z, q * 2 + 1 - c)
    words = own_word.shape[0]
    line = [(lax.rem(z + d, planes), f) for d in range(1, planes)]
    turned[...] = to_half(own_word[...].T)
    yield

    def mate_message(col):
        return remote(
            part.at[:, col, 1 - c], side.at[:, col], sems_send.at[0, col], sems_recv.at[0, col], mate
        )

    def plane_message(col):
        return remote(
            part.at[:, col, c],
            plane_in.at[col],
            sems_send.at[1, col],
            sems_recv.at[1, col],
            (z, cols[col] * 2 + c),
        )

    def line_message(d, who):
        return remote(
            middle.at[who[0]], line_in.at[d], sems_send.at[2, d], sems_recv.at[2, d], who
        )

    def merge(col):
        mate_message(col).wait_recv()
        for zt in range(planes):
            part[zt, col, c] = part[zt, col, c] + side[zt, col]
        if col != OWN:
            plane_message(col).start()

    order = (DIAGONAL, ACROSS_X, ACROSS_Y, OWN)
    for place, col in enumerate(order):

        def body(n, unused, col=col):
            zt, core = n // 2, lax.rem(n, 2)
            ids = facts[zt, cols[col] * 2 + core]
            row = lax.broadcasted_iota(jnp.int32, (words, BUCKET), 0) + offset
            picks = jnp.concatenate(
                [to_half((row == ids[i : i + 1, :]).astype(jnp.float32)) for i in (0, 1)], 1
            )
            part[zt, col, core] = to_half(nn(turned[...], picks))
            return unused

        lax.fori_loop(0, 2 * planes, body, 0)
        mate_message(col).start()
        if place > 0:
            merge(order[place - 1])
        yield
    merge(OWN)
    total = part[:, OWN, c]
    yield
    for col in order[:3]:
        plane_message(col).wait_recv()
        total = total + plane_in[col]
    middle[...] = total
    for d, who in enumerate(line):
        line_message(d, who).start()
    yield
    total = middle[z]
    for d, who in enumerate(line):
        line_message(d, who).wait_recv()
        total = total + line_in[d]
    found[...] = total.astype(jnp.float32).T
    for col in order:
        mate_message(col).wait_send()
    for col in order[:3]:
        plane_message(col).wait_send()
    for d, who in enumerate(line):
        line_message(d, who).wait_send()


PLAN = (1, 1, 1, 1, 1, 1, 1, 1, 1, 1, 1, 1, 1, 1)


def start_kernel(
    planes,
    rows,
    members,
    own_wide,
    own_tall,
    own_head,
    own_word,
    own_place,
    ids,
    labels,
    slot_rows,
    lengths,
    sop_labels,
    *refs,
):
    width = 8
    count = len(members)
    outs, (facts, place, found) = refs[:count], refs[count : count + 3]
    x, buf = refs[count + 3 : count + 5]
    gather_sems = refs[count + 5 : count + 10]
    select_refs = refs[count + 10 : count + 18]
    line_send, line_recv, plane_send, plane_recv = refs[count + 18 :]
    where = places()
    z, c, cols = where
    f = cols[0] * 2 + c
    line = [(lax.rem(z + d, planes), f) for d in range(1, planes)]
    plane = [(z, lax.rem(f + d, width)) for d in range(1, width)]
    lane = lax.broadcasted_iota(jnp.int32, (1, 128), 1)
    rest = jnp.full((1, 128 - labels.shape[1]), -1, jnp.int32)
    note = jnp.zeros((1, 128), jnp.int32)
    for at, value in enumerate((lengths[0], lengths[1], sop_labels[0], sop_labels[1])):
        note = note + jnp.where(lane == at, value, 0)
    facts[z, f] = jnp.concatenate(
        [
            ids[:, :128],
            ids[:, 128:],
            jnp.concatenate([labels[...], rest], 1),
            jnp.concatenate([slot_rows[...], rest], 1),
            note,
            jnp.zeros((3, 128), jnp.int32),
        ],
        0,
    )
    place[z, f] = to_half(own_place[...])
    greet([(None, who) for who in line + plane])
    pairs = (facts, place)

    def along(i, d, who):
        here = pairs[i].at[z, f]
        return remote(here, here, line_send.at[i, d], line_recv.at[i, d], who)

    def around(i, d, who, source):
        here = pairs[i].at[:, source]
        return remote(here, here, plane_send.at[i, d], plane_recv.at[i, d], who)

    for d, who in enumerate(line):
        for i in (0, 1):
            along(i, d, who).start()
    for (low, high), piece in zip(members, (own_wide[...], own_tall[...], own_head[...])):
        x[low:high] = to_half(piece)

    def opening():
        for d, who in enumerate(line):
            for i in (0, 1):
                source = pairs[i].at[lax.rem(z - d - 1 + planes, planes), f]
                remote(source, source, line_send.at[i, d], line_recv.at[i, d], who).wait_recv()
        for d, who in enumerate(plane):
            for i in (0, 1):
                around(i, d, who, f).start()

    gather = gather_stages(planes, rows, members, x, outs, buf, gather_sems, where, opening)
    offset = (z * width + f) * own_word.shape[0]
    select = select_stages(planes, facts, own_word, found, select_refs, where, offset)
    done = object()
    next(gather)
    next(select)
    for d in range(1, width):
        source = lax.rem(f - d + width, width)
        for i in (0, 1):
            around(i, d - 1, mate_of(where), source).wait_recv()
    for number in range(64):
        for unused in range(PLAN[number] if number < len(PLAN) else 1):
            next(select, done)
        if next(gather, done) is done:
            break
    for unused in select:
        pass
    for d, who in enumerate(line):
        for i in (0, 1):
            along(i, d, who).wait_send()
    for d, who in enumerate(plane):
        for i in (0, 1):
            around(i, d, who, f).wait_send()


def mate_of(where):
    z, c, cols = where
    return (z, cols[0] * 2 + 1 - c)


def run_start(shards, own_word, own_place, batch, mesh_shape, identity):
    planes, width = mesh_shape
    heights = tuple(shard.shape[0] for shard in shards)
    rows, columns = sum(heights), shards[1].shape[1]
    members, low = [], 0
    for height in heights:
        members.append((low, low + height))
        low += height
    half, single = jnp.bfloat16, jnp.float32
    vmem = pl.BlockSpec(memory_space=VMEM_SPACE)
    dma = pltpu.SemaphoreType.DMA
    words, features = own_word.shape
    block = (features, ROWS)
    *outs, facts, place, found = pl.pallas_call(
        functools.partial(start_kernel, planes, rows, tuple(members)),
        out_shape=[
            jax.ShapeDtypeStruct((planes, width // 2, 2, height, columns), half)
            for height in heights
        ]
        + [
            jax.ShapeDtypeStruct((planes, width, 8, 128), jnp.int32),
            jax.ShapeDtypeStruct((planes, width, *own_place.shape), half),
            jax.ShapeDtypeStruct((ROWS, features), single),
        ],
        in_specs=[vmem] * 8 + [pl.BlockSpec(memory_space=pltpu.SMEM)] * 2,
        out_specs=[pl.BlockSpec(memory_space=pl.ANY)] * len(heights) + [vmem] * 3,
        scratch_shapes=[
            VMEM_SPACE((rows, columns), half),
            VMEM_SPACE((planes, width // 2, 2, rows, columns), half),
            dma((len(heights) + 1,)),
            dma((2, planes, 12)),
            dma((2, planes, 6)),
            dma((2, planes, 5)),
            dma((2, planes, 5)),
            VMEM_SPACE((planes, 4, 2, *block), half),
            VMEM_SPACE((planes, 4, *block), half),
            VMEM_SPACE((4, planes, *block), half),
            VMEM_SPACE((planes, *block), half),
            VMEM_SPACE((planes - 1, *block), half),
            VMEM_SPACE((features, words), half),
            dma((3, 4)),
            dma((3, 4)),
            dma((2, planes)),
            dma((2, planes)),
            dma((2, width)),
            dma((2, width)),
        ],
        compiler_params=pltpu.CompilerParams(
            collective_id=identity, has_side_effects=True, vmem_limit_bytes=VMEM_ASK
        ),
    )(*shards, own_word, own_place, *[x[None] for x in batch[:3]], *batch[3:])
    weights = [out.reshape(-1, columns) for out in outs]
    devices = planes * width
    return (
        weights,
        facts.reshape(devices, 8, 128),
        place.reshape(devices, *own_place.shape),
        found,
    )


def accumulate(target, sources, height):
    step = 32

    def body(i, unused):
        rows = pl.ds(pl.multiple_of(i * step, step), step)
        total = sources[0][rows].astype(jnp.float32)
        for source in sources[1:]:
            total = total + source[rows].astype(jnp.float32)
        target[rows] = total.astype(target.dtype)
        return unused

    lax.fori_loop(0, height // step, body, 0)


ROWS_AT = 1
TURN_AT = 5
MATE_AT = 9


def far_first(i, z, planes):
    low = (2 * z < planes).astype(jnp.int32)
    falling = planes - 1 - i - (i >= planes - 1 - z).astype(jnp.int32)
    rising = i + (i >= z).astype(jnp.int32)
    last = (jnp.int32(i) == planes - 1).astype(jnp.int32)
    return last * z + (1 - last) * (low * falling + (1 - low) * rising)


def finish_kernel(
    planes,
    heights,
    split,
    left_wide,
    left_tall,
    rights_from,
    outer_from,
    head_grad,
    own_rows,
    vector_terms,
    facts,
    base_word,
    back_decoder,
    totals,
    out,
    word_grad,
    place_grad,
    last,
    ends,
    all_rows,
    both,
    side,
    half_in,
    full_in,
    line_in,
    tail_line,
    tail_half,
    tail_full,
    wide_buf,
    tall_buf,
    vector_in,
    vector_mid,
    vector_last,
    fetch,
    head_load,
    side_send,
    side_recv,
    send,
    recv,
    tail_send,
    tail_recv,
    row_send,
    row_recv,
    vec_send,
    vec_recv,
    end_send,
    end_recv,
    rights,
    outer,
    right_load,
):
    width = 8
    right_copies = [
        pltpu.make_async_copy(rights_from.at[i], rights.at[i], right_load.at[i]) for i in range(3)
    ]
    right_copies.append(pltpu.make_async_copy(outer_from, outer, right_load.at[3]))
    for copy in right_copies:
        copy.start()
    wide_height, tall_height, head_height = heights
    rows = wide_height + tall_height + head_height
    z, c, cols = places()
    q = cols[0]
    f = q * 2 + c
    x, y = lax.rem(q, 2), q // 2
    cuts = cuts_of(rows, FINISH_TAIL)
    head, tail = cuts
    head_rows, tail_rows = head[1] - head[0], tail[1] - tail[0]
    at_x, at_y, mate = (z, cols[1] * 2 + c), (z, cols[2] * 2 + c), (z, q * 2 + 1 - c)
    above, below = z < planes - 1, z > 0
    up, down = (z + 1, f), (z - 1, f)
    line = [(lax.rem(z + d, planes), f) for d in range(1, planes)]
    plane = [(z, lax.rem(f + d, width)) for d in range(1, width)]
    greet([(None, who) for who in line + plane])
    order = (DIAGONAL, ACROSS_X, ACROSS_Y, OWN)
    sent = []

    def push(condition, make):
        maybe(condition, lambda: make().start())
        sent.append((condition, make))

    def piece(ref, span):
        return ref.at[pl.ds(span[0], span[1] - span[0])]

    def plane_at(i):
        return far_first(i, z, planes)

    def turn_of(n):
        m = n - 1 - 3 * (n == 0).astype(jnp.int32) + (n > 4 * planes - 4).astype(jnp.int32)
        group, j = (m + 4) // 4 - 1, lax.rem(m + 4, 4)
        ahead = (j == 0).astype(jnp.int32)
        return group + ahead, DIAGONAL * ahead + j * (j < 3).astype(jnp.int32)

    def chip_of(n):
        i, col = turn_of(n)
        flip_x, flip_y = lax.rem(col, 2), col // 2
        return plane_at(i) * 4 + 2 * lax.rem(y + flip_y, 2) + lax.rem(x + flip_x, 2)

    def fetches(n):
        k, slot = chip_of(n), lax.rem(n, 2)
        wide_rows = pl.ds(pl.multiple_of(k * 2 * wide_height, 16), 2 * wide_height)
        tall_rows = pl.ds(pl.multiple_of(k * 2 * tall_height, 16), 2 * tall_height)
        return (
            pltpu.make_async_copy(
                left_wide.at[wide_rows], wide_buf.at[slot], fetch.at[0, slot]
            ),
            pltpu.make_async_copy(
                left_tall.at[tall_rows], tall_buf.at[slot], fetch.at[1, slot]
            ),
        )

    for copy in fetches(jnp.int32(0)):
        copy.start()

    def vector_first(d, who):
        return remote(
            vector_terms.at[:, who[1]], vector_in.at[d], vec_send.at[0, d], vec_recv.at[0, d], who
        )

    def vector_second(d, who):
        return remote(
            vector_mid.at[who[0]], vector_last.at[d], vec_send.at[1, d], vec_recv.at[1, d], who
        )

    def row_line(d, who):
        return remote(
            own_rows, all_rows.at[z, q, c], row_send.at[0, d], row_recv.at[0, d], who
        )

    def row_plane(col):
        return remote(
            all_rows.at[:, q, c],
            all_rows.at[:, q, c],
            row_send.at[1, col],
            row_recv.at[1, col],
            (z, cols[col] * 2 + c),
        )

    def row_turn(which):
        col, who = ((ACROSS_Y, at_x), (ACROSS_X, at_y))[which]
        here = all_rows.at[:, cols[col], c, pl.ds(which * BUCKET, BUCKET)]
        return remote(here, here, row_send.at[2, 1 + which], row_recv.at[2, 1 + which], who)

    def row_mate():
        return remote(
            all_rows.at[:, :, c], all_rows.at[:, :, c], row_send.at[2, 0], row_recv.at[2, 0], mate
        )

    for d, who in enumerate(line):
        push(None, functools.partial(row_line, d, who))
    for d, who in enumerate(plane):
        push(None, functools.partial(vector_first, d, who))
    all_rows[z, q, c] = own_rows[...]
    head_copies = []
    for col in order:
        copy = pltpu.make_async_copy(
            head_grad.at[:, cols[col]],
            both.at[:, col, :, pl.ds(wide_height + tall_height, head_height)],
            head_load.at[col],
        )
        copy.start()
        head_copies.append(copy)

    def side_message(zt, col):
        return remote(
            both.at[zt, col, 1 - c],
            side.at[zt, col],
            side_send.at[col, zt],
            side_recv.at[col, zt],
            mate,
        )

    def half_message(zt, which):
        return remote(
            piece(both.at[zt, DIAGONAL, c], half_of(head, which)),
            half_in.at[which, zt],
            send.at[0, which, zt],
            recv.at[0, which, zt],
            (at_x, at_y)[which],
        )

    def full_message(zt, which):
        return remote(
            piece(both.at[zt, (ACROSS_X, ACROSS_Y)[which], c], head),
            full_in.at[which, zt],
            send.at[1, which, zt],
            recv.at[1, which, zt],
            (at_x, at_y)[which],
        )

    def line_message(zt, way):
        return remote(
            piece(both.at[zt, OWN, c], head),
            line_in.at[way, zt],
            send.at[2, way, zt],
            recv.at[2, way, zt],
            (up, down)[way],
        )

    def tail_message(zt, way):
        return remote(
            both.at[zt, :, c, pl.ds(tail[0], tail_rows)],
            tail_line.at[way, zt],
            tail_send.at[way, zt],
            tail_recv.at[way, zt],
            (up, down)[way],
        )

    def merged(zt, col):
        side_message(zt, col).wait_recv()
        mine = both.at[zt, col, c]
        accumulate(mine, [mine, side.at[zt, col]], rows)

    def second(zt):
        for which, col in ((0, ACROSS_X), (1, ACROSS_Y)):
            half_message(zt, 1 - which).wait_recv()
            target = piece(both.at[zt, col, c], half_of(head, 1 - which))
            accumulate(target, [target, half_in.at[1 - which, zt]], head_rows // 2)
            full_message(zt, which).start()

    def tail_add(zt, way):
        tail_message(zt, way).wait_recv()
        for col in range(4):
            target = piece(both.at[zt, col, c], tail)
            accumulate(target, [target, tail_line.at[way, zt, col]], tail_rows)

    def ways(zt):
        return ((0, zt > z, below), (1, zt < z, above))

    def tail_open(zt):
        for way, valid, behind in ways(zt):
            go = jnp.logical_and(valid, jnp.logical_not(behind))
            pl.when(go)(lambda way=way: tail_message(zt, way).start())

    def tail_pass(zt):
        for way, valid, behind in ways(zt):

            def action(way=way):
                tail_add(zt, way)
                tail_message(zt, way).start()

            pl.when(jnp.logical_and(valid, behind))(action)

    def line_add(zt, way):
        line_message(zt, way).wait_recv()
        mine = piece(both.at[zt, OWN, c], head)
        accumulate(mine, [mine, line_in.at[way, zt]], head_rows)

    def third(zt):
        for which in (0, 1):
            full_message(zt, which).wait_recv()
        base = [piece(both.at[zt, OWN, c], head), full_in.at[0, zt], full_in.at[1, zt]]
        accumulate(base[0], base, head_rows)
        for way, valid, behind in ways(zt):
            go = jnp.logical_and(valid, jnp.logical_not(behind))
            pl.when(go)(lambda way=way: line_message(zt, way).start())

    def line_pass(zt):
        for way, valid, behind in ways(zt):

            def action(way=way):
                line_add(zt, way)
                line_message(zt, way).start()

            pl.when(jnp.logical_and(valid, behind))(action)

    def after(n):
        i, col = turn_of(n)
        zt = plane_at(i)
        merged(zt, col)

        @pl.when(col == DIAGONAL)
        def _():
            half_message(zt, 0).start()
            half_message(zt, 1).start()

        @pl.when(col == OWN)
        def _():
            second(zt)
            pl.when(i < planes - 1)(lambda: tail_open(zt))
            pl.when(i > 0)(lambda: tail_pass(plane_at(i - 1)))
            pl.when(i > 0)(lambda: third(plane_at(i - 1)))
            pl.when(i > 1)(lambda: line_pass(plane_at(i - 2)))

    for copy in head_copies + right_copies:
        copy.wait()

    def turn_rows():
        for step in (ACROSS_X, ACROSS_Y):
            here = all_rows.at[:, cols[step], c]
            remote(here, here, row_send.at[1, step], row_recv.at[1, step], mate).wait_recv()
        for which in (0, 1):
            row_turn(which).start()

    def share_rows():
        for which in (0, 1):
            here = all_rows.at[:, cols[DIAGONAL], c, pl.ds(which * BUCKET, BUCKET)]
            remote(
                here, here, row_send.at[2, 1 + which], row_recv.at[2, 1 + which], mate
            ).wait_recv()
        row_mate().start()

    def sum_vector():
        total = vector_mid[z]
        for d, who in enumerate(line):
            vector_second(d, who).wait_recv()
            total = total + vector_last[d]
        last[z, f, 0:8] = total

    def body(n, unused):
        for copy in fetches(n):
            copy.wait()

        @pl.when(n + 1 < 4 * planes)
        def _():
            for copy in fetches(n + 1):
                copy.start()

        (i, col), k, slot = turn_of(n), chip_of(n), lax.rem(n, 2)
        zt = plane_at(i)
        region = (k >= split[0]).astype(jnp.int32) + (k >= split[1]).astype(jnp.int32)
        product_wide = to_half(nn(wide_buf[slot], rights[region]))
        both[zt, col, 0, :wide_height] = product_wide[:wide_height]
        both[zt, col, 1, :wide_height] = product_wide[wide_height:]
        product_tall = to_half(nn(tall_buf[slot], outer[...]))
        here = slice(wide_height, wide_height + tall_height)
        both[zt, col, 0, here] = product_tall[:tall_height]
        both[zt, col, 1, here] = product_tall[tall_height:]
        side_message(zt, col).start()
        pl.when(n > 0)(lambda: after(n - 1))

        @pl.when(n == ROWS_AT)
        def _():
            for d, who in enumerate(line):
                row_line(d, who).wait_recv()
            for step in (ACROSS_X, ACROSS_Y):
                row_plane(step).start()
            total = vector_terms[:, f]
            for d, who in enumerate(plane):
                vector_first(d, who).wait_recv()
                total = total + vector_in[d]
            vector_mid[...] = total
            for d, who in enumerate(line):
                vector_second(d, who).start()

        pl.when(n == TURN_AT)(turn_rows)
        pl.when(n == MATE_AT)(share_rows)

        return unused

    lax.fori_loop(0, 4 * planes, body, 0)
    after(jnp.int32(4 * planes - 1))
    targets = [plane_at(i) for i in range(planes)]
    sum_vector()
    here = all_rows.at[:, :, 1 - c]
    remote(here, here, row_send.at[2, 0], row_recv.at[2, 0], mate).wait_recv()
    words = word_grad.shape[0]
    offset = (z * width + f) * words

    def look_back(first, after):
        def body(n, unused):
            zt, chip = n // 4, lax.rem(n, 4)
            row = lax.broadcasted_iota(jnp.int32, (words, BUCKET), 0) + offset
            total = word_grad[...]
            for core in (0, 1):
                ids = facts[zt, chip * 2 + core]
                picks = jnp.concatenate(
                    [to_half((row == ids[i : i + 1, :]).astype(jnp.float32)) for i in (0, 1)], 1
                )
                total = total + nn(picks, all_rows[zt, chip, core])
            word_grad[...] = total
            return unused

        lax.fori_loop(first, after, body, 0)

    word_grad[...] = base_word[...]

    def tail_half_message(which):
        return remote(
            piece(both.at[z, DIAGONAL, c], half_of(tail, which)),
            tail_half.at[which],
            tail_send.at[2, which],
            tail_recv.at[2, which],
            (at_x, at_y)[which],
        )

    def tail_full_message(which):
        return remote(
            piece(both.at[z, (ACROSS_X, ACROSS_Y)[which], c], tail),
            tail_full.at[which],
            tail_send.at[3, which],
            tail_recv.at[3, which],
            (at_x, at_y)[which],
        )

    pl.when(below)(lambda: tail_add(z, 0))
    pl.when(above)(lambda: tail_add(z, 1))
    for which in (0, 1):
        push(None, functools.partial(tail_half_message, which))
    line_pass(targets[planes - 2])
    look_back(0, 4 * planes)
    for which, col in ((1, ACROSS_X), (0, ACROSS_Y)):
        tail_half_message(which).wait_recv()
        target = piece(both.at[z, col, c], half_of(tail, which))
        accumulate(target, [target, tail_half.at[which]], tail_rows // 2)
    for which in (0, 1):
        push(None, functools.partial(tail_full_message, which))
    for which in (0, 1):
        full_message(z, which).wait_recv()
    goal = piece(out, head)
    accumulate(
        goal, [piece(both.at[z, OWN, c], head), full_in.at[0, z], full_in.at[1, z]], head_rows
    )
    for present, way in ((below, 0), (above, 1)):

        def add(way=way):
            line_message(z, way).wait_recv()
            accumulate(goal, [goal, line_in.at[way, z]], head_rows)

        pl.when(present)(add)
    for which in (0, 1):
        tail_full_message(which).wait_recv()
    accumulate(
        piece(out, tail),
        [piece(both.at[z, OWN, c], tail), tail_full.at[0], tail_full.at[1]],
        tail_rows,
    )
    height = place_grad.shape[0]
    own = z * width + f
    low_half = (own * height < BUCKET).astype(jnp.float32)
    high_half = (own * height < 2 * BUCKET).astype(jnp.float32) - low_half
    slot = pl.multiple_of(lax.rem(own * height, BUCKET), height)
    lane = lax.broadcasted_iota(jnp.int32, (1, 128), 1)
    grad = jnp.zeros((height, 128), jnp.float32)
    for zt in range(planes):
        for chip in range(4):
            for core in (0, 1):
                note = facts[zt, chip * 2 + core, 4:5, :]
                two = jnp.sum(
                    jnp.where(lane == 1, (note > 0).astype(jnp.float32), 0.0), 1, keepdims=True
                )
                lower = all_rows[zt, chip, core, pl.ds(slot, height)].astype(jnp.float32)
                upper = all_rows[zt, chip, core, pl.ds(BUCKET + slot, height)].astype(jnp.float32)
                grad = grad + low_half * (lower + two * upper) + high_half * (1.0 - two) * upper
    place_grad[...] = grad
    squares = jnp.sum(grad * grad) + jnp.sum(back_decoder[...] * back_decoder[...])
    squares = squares + jnp.sum(word_grad[...] * word_grad[...])
    squares = squares + jnp.sum(out[...] * out[...])
    last[z, f, 8:16] = jnp.concatenate(
        [totals[...], jnp.where(lane == 0, squares, 0.0), jnp.zeros((6, 128), jnp.float32)], 0
    )
    first_copies, second_copies = [], []
    for d, who in enumerate(line):
        here = last.at[z, f]
        first_copies.append(remote(here, here, end_send.at[0, d], end_recv.at[0, d], who))
        first_copies[-1].start()
    for d, who in enumerate(line):
        here = last.at[lax.rem(z - d - 1 + planes, planes), f]
        remote(here, here, end_send.at[0, d], end_recv.at[0, d], who).wait_recv()
    for d, who in enumerate(plane):
        here = last.at[:, f]
        second_copies.append(remote(here, here, end_send.at[1, d], end_recv.at[1, d], who))
        second_copies[-1].start()
    for d, who in enumerate(plane):
        here = last.at[:, lax.rem(f - d - 1 + width, width)]
        remote(here, here, end_send.at[1, d], end_recv.at[1, d], who).wait_recv()
    summed = last[...]
    tails = jnp.sum(jnp.sum(summed[:, :, 8:16], 0), 0)
    squares = jnp.sum(summed[:, :, 0:8] * summed[:, :, 0:8]) + jnp.sum(tails[1:2, :])
    norm = jnp.sqrt(jnp.broadcast_to(squares, (1, 128)))
    factor = jnp.minimum(1.0, CLIP_NORM / (norm + NORM_EPSILON))
    mlm = totals[0:1, :] - jnp.sum(jnp.where(lane == 1, tails[0:1, :], 0.0))
    def count(at):
        own = jnp.where(lane == at, totals[0:1, :], 0.0)
        return jnp.broadcast_to(jnp.sum(own, 1, keepdims=True), (1, 128))

    sop = jnp.zeros((1, 128), jnp.float32) + jnp.sum(jnp.where(lane == 2, tails[0:1, :], 0.0))
    ends[...] = jnp.concatenate(
        [norm, factor, mlm, sop, count(3), count(4), jnp.zeros((2, 128), jnp.float32)], 0
    )
    for copy in first_copies + second_copies:
        copy.wait_send()
    row_mate().wait_send()
    for condition, make in sent:
        maybe(condition, lambda make=make: make().wait_send())
    for zt in targets:
        for col in order:
            side_message(zt, col).wait_send()
        for which in (0, 1):
            half_message(zt, which).wait_send()
            full_message(zt, which).wait_send()
        for way, valid in ((0, zt > z), (1, zt < z)):

            def done(zt=zt, way=way):
                tail_message(zt, way).wait_send()
                line_message(zt, way).wait_send()

            pl.when(valid)(done)
    for step in (ACROSS_X, ACROSS_Y):
        row_plane(step).wait_send()
    for which in (0, 1):
        row_turn(which).wait_send()
    for d, who in enumerate(line):
        vector_second(d, who).wait_send()


def run_finish(
    left_wide,
    left_tall,
    rights,
    outer,
    head_grad,
    own_rows,
    vector_terms,
    facts,
    base_word,
    back_decoder,
    totals,
    places_count,
    mesh_shape,
    identity,
):
    planes, width = mesh_shape
    devices = planes * width
    columns = outer.shape[1]
    heights = (
        left_wide.shape[0] // devices,
        left_tall.shape[0] // devices,
        head_grad.shape[0] // devices,
    )
    rows = sum(heights)
    long = left_wide.shape[1]
    split = (3 * D // (2 * heights[0]), 4 * D // (2 * heights[0]))
    head, tail = (high - low for low, high in cuts_of(rows, FINISH_TAIL))
    half, single = jnp.bfloat16, jnp.float32
    block = vector_terms.shape[1:]
    vmem = pl.BlockSpec(memory_space=VMEM_SPACE)
    any_space = pl.BlockSpec(memory_space=pl.ANY)
    dma = pltpu.SemaphoreType.DMA
    out, word_grad, place_grad, last, ends = pl.pallas_call(
        functools.partial(finish_kernel, planes, heights, split),
        out_shape=[
            jax.ShapeDtypeStruct((rows, columns), single),
            jax.ShapeDtypeStruct(base_word.shape, single),
            jax.ShapeDtypeStruct((places_count, 128), single),
            jax.ShapeDtypeStruct((planes, width, 16, 128), single),
            jax.ShapeDtypeStruct((8, 128), single),
        ],
        in_specs=[any_space] * 5 + [vmem] * 6,
        out_specs=[vmem] * 5,
        scratch_shapes=[
            VMEM_SPACE((planes, width // 2, 2, *own_rows.shape), half),
            VMEM_SPACE((planes, 4, 2, rows, columns), half),
            VMEM_SPACE((planes, 4, rows, columns), half),
            VMEM_SPACE((2, planes, head // 2, columns), half),
            VMEM_SPACE((2, planes, head, columns), half),
            VMEM_SPACE((2, planes, head, columns), half),
            VMEM_SPACE((2, planes, 4, tail, columns), half),
            VMEM_SPACE((2, tail // 2, columns), half),
            VMEM_SPACE((2, tail, columns), half),
            VMEM_SPACE((2, 2 * heights[0], long), half),
            VMEM_SPACE((2, 2 * heights[1], long), half),
            VMEM_SPACE((width - 1, planes, *block), single),
            VMEM_SPACE((planes, *block), single),
            VMEM_SPACE((planes - 1, *block), single),
            dma((2, 2)),
            dma((4,)),
            dma((4, planes)),
            dma((4, planes)),
            dma((3, 2, planes)),
            dma((3, 2, planes)),
            dma((4, planes)),
            dma((4, planes)),
            dma((3, 4)),
            dma((3, 4)),
            dma((2, width)),
            dma((2, width)),
            dma((2, width)),
            dma((2, width)),
            VMEM_SPACE(rights.shape, half),
            VMEM_SPACE(outer.shape, half),
            dma((4,)),
        ],
        compiler_params=pltpu.CompilerParams(
            collective_id=identity, has_side_effects=True, vmem_limit_bytes=VMEM_ASK
        ),
    )(
        left_wide,
        left_tall,
        rights,
        outer,
        head_grad.reshape(planes, width // 2, 2, heights[2], columns),
        own_rows,
        vector_terms.reshape(planes, width, *block),
        facts.reshape(planes, width, *facts.shape[1:]),
        base_word,
        back_decoder,
        totals,
    )
    return out, heights, word_grad, place_grad, last, ends


LIFT = 128
WIRE = 48


def exact_rows(pick, values):
    first = to_half(values)
    rest = values - first.astype(jnp.float32)
    second = to_half(rest)
    third = to_half(rest - second.astype(jnp.float32))
    return nn(pick, first) + nn(pick, second) + nn(pick, third)


def lanes_to_rows(x):
    return jnp.concatenate([x[:, i : i + 128] for i in range(0, x.shape[1], 128)], 0)


def rows_to_lanes(x):
    return jnp.concatenate([x[i : i + 1] for i in range(x.shape[0])], 1)


def head_kernel(
    planes,
    lengths,
    sop_labels,
    final,
    head,
    word,
    decoder,
    facts,
    vec,
    back_final,
    back_word,
    back_decoder,
    back_head,
    wide_sums,
    small_sums,
    totals,
    all_t,
    stats,
    powers,
    back_t,
    plane_in,
    middle,
    line_in,
    word_half,
    sends,
    recvs,
):
    width = 8
    z, c, cols = places()
    f = cols[0] * 2 + c
    line = [(lax.rem(z + d, planes), f) for d in range(1, planes)]
    plane = [(z, lax.rem(f + d, width)) for d in range(1, width)]
    greet([(None, who) for who in line + plane])
    offset = (z * width + f) * word.shape[0]
    words, slots = word.shape[0], planes * width * WIRE
    single = jnp.float32

    def gather_line(ref, kind):
        here = ref.at[z, f]
        return [
            remote(here, here, sends.at[kind, d], recvs.at[kind, d], who)
            for d, who in enumerate(line)
        ]

    def gather_plane(ref, kind):
        here = ref.at[:, f]
        return [
            remote(here, here, sends.at[kind, d], recvs.at[kind, d], who)
            for d, who in enumerate(plane)
        ]

    def await_line(ref, kind):
        for d in range(planes - 1):
            here = ref.at[lax.rem(z - d - 1 + planes, planes), f]
            remote(here, here, sends.at[kind, d], recvs.at[kind, d], line[d]).wait_recv()

    def await_plane(ref, kind):
        for d in range(width - 1):
            here = ref.at[:, lax.rem(f - d - 1 + width, width)]
            remote(here, here, sends.at[kind, d], recvs.at[kind, d], plane[d]).wait_recv()

    started = []
    lane = lax.broadcasted_iota(jnp.int32, (1, 128), 1)
    notes = facts[...]
    labels = jnp.concatenate([notes[i, 2:3, :WIRE] for i in range(planes * width)], 1)
    used = (lanes_to_rows(labels) >= 0).astype(single)
    mlm_count = jnp.sum(used)
    seconds = jnp.where(lane == 1, (notes[:, 4, :] > 0).astype(single), 0.0)
    sop_count = planes * width + jnp.sum(seconds)
    mlm_scale = 1.0 / jnp.broadcast_to(mlm_count, (1, 1))
    sop_scale = 1.0 / jnp.broadcast_to(sop_count, (1, 1))

    def start(copies):
        for copy in copies:
            copy.start()
        started.extend(copies)

    final_half = to_half(final[...])
    place = lax.broadcasted_iota(jnp.int32, (ROWS, LIFT), 0)
    scatter = to_half((place == facts[z * width + f, 3:4, :]).astype(single))
    pick = scatter.T
    picked = to_half(nn(pick, final_half))
    dense = nt(picked, head[:E, :]) + short_row(vec, MLM_B)
    bend = jnp.tanh(GELU_A * dense * (1.0 + GELU_B * dense * dense))
    hat, inverse = norm_forward(0.5 * dense * (1.0 + bend))
    slope = 0.5 * (1.0 + bend) + (0.5 * GELU_A) * dense * (1.0 - bend * bend) * (
        1.0 + 3.0 * GELU_B * dense * dense
    )
    rows_half = to_half(hat * short_row(vec, MLM_G) + short_row(vec, MLM_LB))
    all_t[z, f] = rows_half[:WIRE]
    start(gather_line(all_t, 0))

    word_half[...] = to_half(word[...])
    row16 = lax.broadcasted_iota(jnp.int32, (16, ROWS), 0)
    col16 = lax.broadcasted_iota(jnp.int32, (16, ROWS), 1)
    leads = to_half(
        (jnp.logical_and(row16 < 2, col16 == row16 * BUCKET)).astype(single)
    )
    firsts = to_half(nn(leads, final_half))
    pooled = jnp.tanh(nt(firsts, head[E : E + D, :]) + wide_row(vec, POOL_B))
    await_line(all_t, 0)
    start(gather_plane(all_t, 1))
    zero_class, one_class = lanes_of(vec, CLS_AT, D // 128), lanes_of(vec, CLS_AT + D // 128, D // 128)
    c0 = jnp.sum(pooled * zero_class, -1, keepdims=True)
    c1 = jnp.sum(pooled * one_class, -1, keepdims=True)
    class_top = jnp.maximum(c0, c1)
    e0, e1 = jnp.exp(c0 - class_top), jnp.exp(c1 - class_top)
    class_total = e0 + e1
    which = lax.broadcasted_iota(jnp.int32, (16, 1), 0)
    label = jnp.where(which == 0, sop_labels[0], sop_labels[1])
    hit = (label == 1).astype(single)
    two = (lengths[1] > 0).astype(single)
    present = jnp.where(which == 0, 1.0, jnp.where(which == 1, two, 0.0))
    losses = (jnp.log(class_total) + class_top - (c0 + hit * (c1 - c0))) * present
    weight = present * sop_scale
    back_c0 = (e0 / class_total - (1.0 - hit)) * weight
    back_c1 = (e1 / class_total - hit) * weight
    wide_sums[1:2, :] = jnp.sum(back_c0 * pooled, 0, keepdims=True)
    wide_sums[2:3, :] = jnp.sum(back_c1 * pooled, 0, keepdims=True)
    pre_half = to_half((back_c0 * zero_class + back_c1 * one_class) * (1.0 - pooled * pooled))
    wide_sums[0:1, :] = jnp.sum(pre_half.astype(single), 0, keepdims=True)
    back_head[E : E + D, :] = to_half(tn(pre_half, firsts))
    back_firsts = nn(pre_half, head[E : E + D, :])
    await_plane(all_t, 1)

    row = lax.broadcasted_iota(jnp.int32, (words, 128), 0) + offset
    bias = jnp.broadcast_to(to_half(decoder[...]).astype(single), (8, words)).T[:, 0:1]
    tops, sums, targets = [], [], []
    chunk = width * WIRE
    flat_t = all_t[...].reshape(slots, E)
    for low in range(0, slots, chunk):
        logits = nt(word_half[...], flat_t[low : low + chunk]) + bias
        top = jnp.max(logits, 0, keepdims=True)
        power = jnp.exp(logits - top)
        powers[:, pl.ds(low, chunk)] = power
        tops.append(top)
        sums.append(jnp.sum(power, 0, keepdims=True))
        for at in range(0, chunk, 128):
            mark = row == labels[:, low + at : low + at + 128]
            targets.append(
                jnp.sum(jnp.where(mark, logits[:, at : at + 128], 0.0), 0, keepdims=True)
            )
    own_top = lanes_to_rows(jnp.concatenate(tops, 1))
    groups = slots // 128
    stats[z, f, 0:groups] = own_top
    stats[z, f, groups : 2 * groups] = lanes_to_rows(jnp.concatenate(sums, 1))
    start(gather_line(stats, 2))
    target = jnp.sum(jnp.concatenate(targets, 0) * used)
    await_line(stats, 2)
    start(gather_plane(stats, 3))
    await_plane(stats, 3)
    every = stats[...].reshape(planes * width, 2 * groups, 128)
    top = jnp.max(every[:, :groups], 0)
    total = jnp.sum(every[:, groups:] * jnp.exp(every[:, :groups] - top[None]), 0)
    log_sum = jnp.sum((jnp.log(total) + top) * used)
    weight = used * mlm_scale
    factor = rows_to_lanes(weight * jnp.exp(own_top - top) / total)
    weight = rows_to_lanes(weight)

    def slot_terms(zz, d, who):
        return remote(
            back_t.at[zz, who[1]],
            plane_in.at[d, zz],
            sends.at[4 + zz, d],
            recvs.at[4 + zz, d],
            who,
        )

    words_total = jnp.zeros((words, E), single)
    word_sums = jnp.zeros((8, words), single)
    ones = jnp.ones((8, width * WIRE), jnp.bfloat16)
    for low in range(0, slots, chunk):
        parts = []
        for at in range(low, low + chunk, 128):
            mark = row == labels[:, at : at + 128]
            part = powers[:, pl.ds(at, 128)] * factor[:, at : at + 128] - jnp.where(
                mark, weight[:, at : at + 128], 0.0
            )
            parts.append(to_half(part))
        half = jnp.concatenate(parts, 1)
        word_sums = word_sums + nt(ones, half)
        words_total = words_total + nn(half, flat_t[low : low + chunk])
        zz = low // chunk
        back_t[zz] = tn(half, word_half[...]).reshape(width, WIRE, E)
        start([slot_terms(zz, d, who) for d, who in enumerate(plane)])
    back_word[...] = words_total
    back_decoder[...] = word_sums[0:1]

    for zz in range(planes):
        total = back_t[zz, f]
        for d in range(width - 1):
            slot_terms(zz, d, plane[d]).wait_recv()
            total = total + plane_in[d, zz]
        middle[zz] = total
    start(
        [
            remote(middle.at[who[0]], line_in.at[d], sends.at[4 + planes, d], recvs.at[4 + planes, d], who)
            for d, who in enumerate(line)
        ]
    )
    total = middle[z]
    for d in range(planes - 1):
        remote(
            line_in.at[d], line_in.at[d], sends.at[4 + planes, d], recvs.at[4 + planes, d], line[d]
        ).wait_recv()
        total = total + line_in[d]
    back_rows = jnp.concatenate([total, jnp.zeros((LIFT - WIRE, E), single)], 0)
    small_sums[1:2, :] = jnp.sum(back_rows * hat, 0, keepdims=True)
    small_sums[2:3, :] = jnp.sum(back_rows, 0, keepdims=True)
    dense_half = to_half(norm_backward(back_rows, short_row(vec, MLM_G), hat, inverse) * slope)
    small_sums[0:1, :] = jnp.sum(dense_half.astype(single), 0, keepdims=True)
    back_head[:E, :] = to_half(tn(dense_half, picked))
    back_final[...] = exact_rows(scatter, nn(dense_half, head[:E, :]))
    back_final[0:1, :] = back_final[0:1, :] + back_firsts[0:1]
    back_final[BUCKET : BUCKET + 1, :] = back_final[BUCKET : BUCKET + 1, :] + back_firsts[1:2]
    sop_sum = jnp.sum(losses)
    ends = jnp.zeros((1, 128), single)
    for at, value in enumerate((log_sum, target, sop_sum, mlm_count, sop_count)):
        ends = ends + jnp.where(lane == at, value, 0.0)
    totals[...] = ends
    for copy in started:
        copy.wait_send()


def run_head(
    lengths, sop_labels, final, head, word, decoder, facts, vec, mesh_shape, identity
):
    planes, width = mesh_shape
    words = word.shape[0]
    slots = planes * width * WIRE
    groups = slots // 128
    single, half = jnp.float32, jnp.bfloat16
    vmem = pl.BlockSpec(memory_space=VMEM_SPACE)
    smem = pl.BlockSpec(memory_space=pltpu.SMEM)
    dma = pltpu.SemaphoreType.DMA
    return pl.pallas_call(
        functools.partial(head_kernel, planes),
        out_shape=[
            jax.ShapeDtypeStruct((ROWS, D), single),
            jax.ShapeDtypeStruct((words, E), single),
            jax.ShapeDtypeStruct((1, words), single),
            jax.ShapeDtypeStruct(head.shape, half),
            jax.ShapeDtypeStruct((3, D), single),
            jax.ShapeDtypeStruct((3, E), single),
            jax.ShapeDtypeStruct((1, 128), single),
        ],
        in_specs=[smem] * 2 + [vmem] * 6,
        out_specs=[vmem] * 7,
        scratch_shapes=[
            VMEM_SPACE((planes, width, WIRE, E), half),
            VMEM_SPACE((planes, width, 2 * groups, 128), single),
            VMEM_SPACE((words, slots), single),
            VMEM_SPACE((planes, width, WIRE, E), single),
            VMEM_SPACE((width - 1, planes, WIRE, E), single),
            VMEM_SPACE((planes, WIRE, E), single),
            VMEM_SPACE((planes - 1, WIRE, E), single),
            VMEM_SPACE((words, E), half),
            dma((5 + planes, width)),
            dma((5 + planes, width)),
        ],
        compiler_params=pltpu.CompilerParams(
            collective_id=identity, has_side_effects=True, vmem_limit_bytes=VMEM_ASK
        ),
    )(lengths, sop_labels, final, head, word, decoder, facts, vec)


def adam_update(weight, gradient, first, second, rate):
    first = BETA_ONE * first + (1 - BETA_ONE) * gradient
    second = BETA_TWO * second + (1 - BETA_TWO) * gradient * gradient
    first_hat = first / (1 - BETA_ONE**STEP)
    second_hat = second / (1 - BETA_TWO**STEP)
    updated = weight - rate * (
        first_hat / (jnp.sqrt(second_hat) + ADAM_EPSILON) + WEIGHT_DECAY * weight
    )
    return (updated, first, second)


def adam_kernel(blocks, rates, *refs):
    count = len(rates)
    ends, refs = refs[0], refs[1:]
    ins, outs, scalars = refs[: 4 * count], refs[4 * count : 7 * count], refs[7 * count :]
    factor = ends[1:2, 0:1]

    def update(number):
        weight, first, second, gradient = ins[4 * number : 4 * number + 4]
        grad = gradient[...]
        if grad.ndim > 2:
            grad = grad[:, :, :8].reshape(-1, 128)[: weight.shape[0]]
        results = adam_update(
            weight[...], factor * grad, first[...], second[...], rates[number]
        )
        for out, result in zip(outs[3 * number : 3 * number + 3], results):
            out[...] = result

    for number in range(blocks):
        update(number)

    @pl.when(pl.program_id(0) == 0)
    def _():
        for number in range(blocks, count):
            update(number)
        lane = lax.broadcasted_iota(jnp.int32, (1, 128), 1)
        for at, scalar in enumerate(scalars):
            scalar[0] = jnp.sum(jnp.where(lane == 0, ends[at : at + 1, :], 0.0))


def run_adam(ends, groups, steps):
    in_specs = [pl.BlockSpec(ends.shape, lambda i: (0, 0))]
    out_specs, shapes, given = [], [], [ends]
    blocks = 0
    for weight, first, second, gradient, low, rate in groups:
        rows, columns = weight.shape
        if low is None:
            spec = pl.BlockSpec(weight.shape, lambda i: (0, 0))
            zero = (0,) * gradient.ndim
            grad_spec = pl.BlockSpec(gradient.shape, lambda i, zero=zero: zero)
        else:
            blocks += 1
            height = rows // steps
            spec = pl.BlockSpec((height, columns), lambda i: (i, 0))
            grad_spec = pl.BlockSpec(
                (height, columns), lambda i, start=low // height: (start + i, 0)
            )
        in_specs += [spec] * 3 + [grad_spec]
        out_specs += [spec] * 3
        shapes += [jax.ShapeDtypeStruct(weight.shape, jnp.float32)] * 3
        given += [weight, first, second, gradient]
    out_specs += [pl.BlockSpec(memory_space=pltpu.SMEM)] * 6
    shapes += [jax.ShapeDtypeStruct((1,), jnp.float32)] * 6
    return pl.pallas_call(
        functools.partial(adam_kernel, blocks, tuple(group[5] for group in groups)),
        grid=(steps,),
        out_shape=shapes,
        in_specs=in_specs,
        out_specs=out_specs,
        compiler_params=pltpu.CompilerParams(
            dimension_semantics=("arbitrary",), vmem_limit_bytes=VMEM_ASK
        ),
    )(*given)


class Network:
    def __init__(self, mesh):
        self.shape = (mesh.shape["dp"], mesh.shape["fsdp"])
        self.devices = self.shape[0] * self.shape[1]
        self.kernels = self.shape[1] == 8
        self.calls = 0

    def identity(self):
        self.calls += 1
        return self.calls

    def start(self, shards, own_word, own_place, batch):
        if self.kernels:
            return run_start(shards, own_word, own_place, batch, self.shape, self.identity())
        token_ids, labels, slot_rows, lengths, sop_labels = batch

        def fill(count, value):
            return jnp.full((count,), value, jnp.int32)

        rest = fill(128 - labels.shape[0], -1)
        own_facts = [token_ids, labels, rest, slot_rows, rest, lengths, sop_labels]
        own_facts = jnp.concatenate([*own_facts, fill(3 * 128 + 124, 0)]).reshape(8, 128)
        weights = [lax.all_gather(to_half(w), AXES, axis=0, tiled=True) for w in shards]
        facts = lax.all_gather(own_facts, AXES)
        place = lax.all_gather(to_half(own_place), AXES)
        words = own_word.shape[0]
        ids = facts[:, : ROWS // 128].reshape(-1) - lax.axis_index(AXES) * words
        column = jnp.arange(words, dtype=jnp.int32)
        select = to_half(ids[:, None] == column[None, :])
        terms = product(select, to_half(own_word))
        found = lax.psum_scatter(terms, AXES, scatter_dimension=0, tiled=True)
        return weights, facts, place, found

    def head(self, lengths, sop_labels, final, head, word, decoder, facts, vec):
        decoder = decoder[None]
        given = (lengths, sop_labels, final, head, word, decoder, facts, vec)
        if self.kernels:
            return run_head(*given, self.shape, self.identity())
        return self.plain_head(*given)

    def plain_head(self, lengths, sop_labels, final, head, word, decoder, facts, vec):
        short, cls = vec[SHORT_AT:], vec[CLS_AT:FF_AT].reshape(2, D)
        pool_b = vec[POOL_B * D // 128 : CLS_AT].reshape(D)
        labels = facts[:, 2, :WIRE].reshape(1, -1)
        mlm_count = jnp.sum((labels >= 0).astype(jnp.float32))
        sop_count = self.devices + jnp.sum((facts[:, 4, 1] > 0).astype(jnp.float32))
        single = jnp.float32
        offset = lax.axis_index(AXES) * word.shape[0]
        word_half, final_half = to_half(word), to_half(final)
        rows = facts[lax.axis_index(AXES), 3, :WIRE]
        pick = (rows[:, None] == jnp.arange(ROWS, dtype=jnp.int32)[None]).astype(single)
        picked = to_half(product(to_half(pick), final_half))
        dense = times_transpose(picked, head[:E]) + short[MLM_B]
        bend = jnp.tanh(GELU_A * dense * (1.0 + GELU_B * dense * dense))
        hat, inverse = norm_forward(0.5 * dense * (1.0 + bend))
        slope = 0.5 * (1.0 + bend) + (0.5 * GELU_A) * dense * (1.0 - bend * bend) * (
            1.0 + 3.0 * GELU_B * dense * dense
        )
        rows_half = to_half(hat * short[MLM_G] + short[MLM_LB])
        all_rows = lax.all_gather(rows_half, AXES, axis=0, tiled=True)
        logits = times_transpose(word_half, all_rows) + to_half(decoder).astype(single).T
        mark = jnp.arange(word.shape[0], dtype=jnp.int32)[:, None] + offset == labels
        own_top = jnp.max(logits, 0)
        own_total = jnp.sum(jnp.exp(logits - own_top), 0)
        used = (labels[0] >= 0).astype(single)
        target = jnp.sum(jnp.sum(jnp.where(mark, logits, 0.0), 0) * used)
        top = lax.pmax(own_top, AXES)
        total = lax.psum(own_total * jnp.exp(own_top - top), AXES)
        log_sum = jnp.sum((jnp.log(total) + top) * used)
        weight = used / mlm_count
        half = to_half((jnp.exp(logits - top) / total - mark.astype(single)) * weight)
        back_rows = lax.psum_scatter(
            transpose_times(half, word_half), AXES, scatter_dimension=0, tiled=True
        )
        dense_half = to_half(norm_backward(back_rows, short[MLM_G], hat, inverse) * slope)
        back_final = lax.dot_general(
            pick, product(dense_half, head[:E]), (((0,), (0,)), ((), ())), precision=PRECISE
        )
        firsts = jnp.stack([final_half[0], final_half[BUCKET]])
        pooled = jnp.tanh(times_transpose(firsts, head[E : E + D]) + pool_b)
        classes = jnp.sum(pooled[:, None] * cls[None], -1)
        powers = jnp.exp(classes - jnp.max(classes, -1, keepdims=True))
        totals = jnp.sum(powers, -1, keepdims=True)
        onehot = jnp.stack([1 - sop_labels, sop_labels], 1).astype(single)
        present = jnp.stack([jnp.float32(1.0), (lengths[1] > 0).astype(single)])
        losses = jnp.log(totals[:, 0]) + jnp.max(classes, -1) - jnp.sum(classes * onehot, -1)
        back_classes = (powers / totals - onehot) * (present / sop_count)[:, None]
        back_pooled = jnp.sum(back_classes[:, :, None] * cls[None], 1)
        pre_half = to_half(back_pooled * (1.0 - pooled * pooled))
        back_firsts = product(pre_half, head[E : E + D])
        back_final = back_final.at[0].add(back_firsts[0]).at[BUCKET].add(back_firsts[1])
        back_cls = jnp.sum(back_classes[:, :, None] * pooled[:, None], 0)
        small_sums = [column_sum(dense_half), jnp.sum(back_rows * hat, 0), jnp.sum(back_rows, 0)]
        back_head = [transpose_times(dense_half, picked), transpose_times(pre_half, firsts)]
        ends = jnp.stack([log_sum, target, jnp.sum(losses * present), mlm_count, sop_count])
        return (
            back_final,
            product(half, all_rows),
            column_sum(half.T)[None],
            to_half(jnp.pad(jnp.concatenate(back_head, 0), ((0, E), (0, 0)))),
            jnp.concatenate([column_sum(pre_half)[None], back_cls], 0),
            jnp.stack(small_sums),
            jnp.pad(ends, (0, 123))[None],
        )

    def adam(self, ends, groups):
        if self.kernels:
            updates = run_adam(ends, groups, 4)
            scalars = [x.reshape(()) for x in updates[-6:]]
            return [updates[i : i + 3] for i in range(0, 3 * len(groups), 3)], scalars
        updates = []
        for weight, first, second, gradient, low, rate in groups:
            rows = weight.shape[0]
            if low is not None:
                gradient = gradient[low : low + rows]
            gradient = gradient.reshape(-1, weight.shape[1])[:rows]
            updates.append(adam_update(weight, ends[1, 0] * gradient, first, second, rate))
        return updates, [ends[i, 0] for i in range(6)]

    def finish(
        self,
        left_wide,
        left_tall,
        rights,
        outer,
        head_grad,
        own_rows,
        vector,
        facts,
        base_word,
        back_decoder,
        totals,
        places_count,
    ):
        devices = self.devices
        if self.kernels:
            out, heights, word_grad, place_grad, last, ends = run_finish(
                left_wide,
                left_tall,
                rights,
                outer,
                head_grad,
                own_rows,
                vector,
                facts,
                base_word,
                back_decoder,
                totals,
                places_count,
                self.shape,
                self.identity(),
            )
            return out, heights, word_grad, place_grad, last, ends
        back_wide = jnp.concatenate(
            [
                product(left_wide[: 3 * D], rights[0]),
                product(left_wide[3 * D : 4 * D], rights[1]),
                product(left_wide[4 * D :], rights[2]),
            ],
            0,
        )
        sums = [
            lax.psum_scatter(p.astype(jnp.float32), AXES, scatter_dimension=0, tiled=True)
            for p in (back_wide, product(left_tall, outer), head_grad)
        ]
        all_rows = lax.all_gather(own_rows, AXES, axis=0, tiled=True)
        own, words = lax.axis_index(AXES), base_word.shape[0]
        ids = facts[:, : ROWS // 128].reshape(-1) - own * words
        select = to_half(ids[:, None] == jnp.arange(words, dtype=jnp.int32)[None, :])
        word_grad = base_word + transpose_times(select, all_rows)
        by_device = all_rows.reshape(devices, ROWS, E).astype(jnp.float32)
        two = (facts[:, 4, 1] > 0)[:, None, None]
        lower, upper = by_device[:, :BUCKET], by_device[:, BUCKET:]
        lower = jnp.sum(lower + jnp.where(two, upper, 0.0), 0)
        upper = jnp.sum(jnp.where(two, 0.0, upper), 0)
        every = jnp.concatenate([lower, upper], 0)
        every = jnp.pad(every, ((0, places_count * devices - ROWS), (0, 0)))
        place_grad = lax.dynamic_slice(every, (own * places_count, 0), (places_count, E))
        squares = sum(jnp.sum(g * g) for g in (*sums, word_grad, place_grad, back_decoder))
        reduced, tails, squares = lax.psum((vector, totals, squares), AXES)
        norm = jnp.sqrt(squares + jnp.sum(reduced * reduced))
        factor = jnp.minimum(1.0, CLIP_NORM / (norm + NORM_EPSILON))
        ends = [norm, factor, totals[0, 0] - tails[0, 1], tails[0, 2]]
        ends = jnp.stack([*ends, totals[0, 3], totals[0, 4]])
        ends = jnp.broadcast_to(ends[:, None], (6, 128))
        heights = tuple(total.shape[0] for total in sums)
        return jnp.concatenate(sums, 0), heights, word_grad, place_grad, reduced, ends


CLS_AT, FF_AT, SHORT_AT = 10 * D // 128, 12 * D // 128, (12 * D + FF) // 128


def lanes_of(vec, first, count):
    return jnp.concatenate([vec[pl.ds(first + i, 1), :] for i in range(count)], 1)


def wide_row(vec, index):
    return lanes_of(vec, index * (D // 128), D // 128)


def short_row(vec, index):
    return vec[pl.ds(SHORT_AT + index, 1), :]


def nt(a, b):
    return lax.dot_general(a, b, (((1,), (1,)), ((), ())), preferred_element_type=jnp.float32)


def nn(a, b):
    return jnp.dot(a, b, preferred_element_type=jnp.float32)


def tn(a, b):
    return lax.dot_general(a, b, (((0,), (0,)), ((), ())), preferred_element_type=jnp.float32)


CHUNK = 512
PAIR = 2 * HEAD_DIM
PROJ_B, Q_B, V_B, O_B, LN1_G, LN1_B, FFO_B, LN2_G, LN2_B, POOL_B = range(10)


def allowed_block(lengths):
    shape = (ROWS, ROWS)
    key = lax.broadcasted_iota(jnp.int32, shape, 0)
    query = lax.broadcasted_iota(jnp.int32, shape, 1)
    two = lengths[1] > 0
    key_second = jnp.logical_and(key >= BUCKET, two).astype(jnp.int32)
    query_second = jnp.logical_and(query >= BUCKET, two).astype(jnp.int32)
    length = jnp.where(key_second == 1, lengths[1], lengths[0])
    live = key - BUCKET * key_second < length
    return jnp.logical_and(query_second == key_second, live)


def halves_down(x):
    row = lax.broadcasted_iota(jnp.int32, x.shape, 0)
    zero = jnp.zeros_like(x)
    return jnp.where(row < HEAD_DIM, x, zero), jnp.where(row < HEAD_DIM, zero, x)


def halves(x):
    lane = lax.broadcasted_iota(jnp.int32, x.shape, 1)
    zero = jnp.zeros_like(x)
    return jnp.where(lane < HEAD_DIM, x, zero), jnp.where(lane < HEAD_DIM, zero, x)


def kinds(lengths):
    row = lax.broadcasted_iota(jnp.int32, (ROWS, 1), 0)
    second = jnp.logical_and(row >= BUCKET, lengths[1] > 0).astype(jnp.int32)
    length = jnp.where(second == 1, lengths[1], lengths[0])
    return (row - BUCKET * second >= length // 2).astype(jnp.float32)


EMB_G, EMB_B, MLM_B, MLM_G, MLM_LB, TYPE_ZERO, TYPE_ONE = range(7)


def forward_kernel(
    lengths,
    found,
    place,
    lift,
    wide,
    tall,
    vec,
    final,
    embed_hat,
    embed_inverse,
    normed_half,
    rights,
    projected,
    weighting,
    hat_one,
    inverse_one,
    slope,
    active,
    hat_two,
    inverse_two,
    hidden,
):
    layer = pl.program_id(0)

    def row(index):
        return wide_row(vec, index)

    @pl.when(layer == 0)
    def _():
        two = (lengths[1] > 0).astype(jnp.float32)
        kind = kinds(lengths)
        upper = place[pl.ds(0, BUCKET), :].astype(jnp.float32)
        lower = jnp.where(two > 0, upper, place[pl.ds(BUCKET, BUCKET), :].astype(jnp.float32))
        embedded = found[...] + jnp.concatenate([upper, lower], 0)
        zero, one = short_row(vec, TYPE_ZERO), short_row(vec, TYPE_ONE)
        hat, inverse = norm_forward(embedded + jnp.where(kind > 0, one, zero))
        embed_hat[...] = hat
        embed_inverse[...] = inverse
        normed = to_half(hat * short_row(vec, EMB_G) + short_row(vec, EMB_B))
        normed_half[...] = normed
        hidden[...] = nn(normed, lift[...]) + row(PROJ_B)

    half = to_half(hidden[...])
    rights[0] = half
    for part, bias in ((0, Q_B), (1, None), (2, V_B)):
        for low in range(0, D, 256):
            here = part * D + low
            value = nt(half, wide[pl.ds(here, 256), :])
            if bias is not None:
                value = value + lanes_of(vec, (bias * D + low) // 128, 2)
            projected[:, pl.ds(here, 256)] = to_half(value)
    allowed = allowed_block(lengths)
    for pair in range(HEADS // 2):
        lanes = pair * PAIR
        queries = halves(projected[:, pl.ds(lanes, PAIR)])
        keys = projected[:, pl.ds(D + lanes, PAIR)]
        values = halves_down(projected[:, pl.ds(2 * D + lanes, PAIR)].T)
        total = jnp.zeros((PAIR, ROWS), jnp.float32)
        for side in (0, 1):
            scores = jnp.where(allowed, nt(keys, queries[side]) * SCALE, MASKED)
            powers = jnp.exp(scores - jnp.max(scores, 0, keepdims=True))
            weights = powers * (1.0 / jnp.sum(powers, 0, keepdims=True))
            weighting[2 * pair + side] = weights
            total = total + nn(values[side], to_half(weights))
        rights[1, :, pl.ds(lanes, PAIR)] = to_half(total).T
    first_sum = hidden[...] + nt(rights[1], wide[pl.ds(3 * D, D), :]) + row(O_B)
    hat, inverse = norm_forward(first_sum)
    hat_one[...] = hat
    inverse_one[...] = inverse
    middle = hat * row(LN1_G) + row(LN1_B)
    half = to_half(middle)
    rights[2] = half
    total = middle + row(FFO_B)
    for low in range(0, FF, CHUNK):
        bias = lanes_of(vec, FF_AT + low // 128, CHUNK // 128)
        inner = nt(half, wide[pl.ds(4 * D + low, CHUNK), :]) + bias
        square = inner * inner
        bend = jnp.tanh(GELU_A * inner * (1.0 + GELU_B * square))
        act = to_half(0.5 * inner * (1.0 + bend))
        slope[:, pl.ds(low, CHUNK)] = 0.5 * (1.0 + bend) + (0.5 * GELU_A) * inner * (
            1.0 - bend * bend
        ) * (1.0 + 3.0 * GELU_B * square)
        active[pl.ds(low, CHUNK), :] = act.T
        total = total + nn(act, tall[pl.ds(low, CHUNK), :])
    hat, inverse = norm_forward(total)
    hat_two[...] = hat
    inverse_two[...] = inverse
    output = hat * row(LN2_G) + row(LN2_B)
    hidden[...] = output
    final[...] = output


def whole_spec():
    return pl.BlockSpec(memory_space=VMEM_SPACE, pipeline_mode=pl.Buffered(1))


def lift_spec():
    return pl.BlockSpec((E, D), lambda i: ((E + D) // E, 0), pipeline_mode=pl.Buffered(1))


def by_layer(*shape, order=lambda i: i):
    return pl.BlockSpec(
        (None, *shape), lambda i: (order(i),) + (0,) * len(shape), memory_space=VMEM_SPACE
    )


def run_forward(lengths, found, place, head, wide, tall, vec):
    def kept(*shape, dtype=jnp.bfloat16):
        return jax.ShapeDtypeStruct((LAYERS, *shape), dtype)

    single = jnp.float32
    names = (
        "final",
        "embed_hat",
        "embed_inverse",
        "normed_half",
        "rights",
        "projected",
        "weighting",
        "hat_one",
        "inverse_one",
        "slope",
        "active",
        "hat_two",
        "inverse_two",
    )
    outs = pl.pallas_call(
        forward_kernel,
        grid=(LAYERS,),
        out_shape=[
            jax.ShapeDtypeStruct((ROWS, D), single),
            jax.ShapeDtypeStruct((ROWS, E), single),
            jax.ShapeDtypeStruct((ROWS, 1), single),
            jax.ShapeDtypeStruct((ROWS, E), jnp.bfloat16),
            jax.ShapeDtypeStruct((3, LAYERS, ROWS, D), jnp.bfloat16),
            kept(ROWS, 3 * D),
            kept(HEADS, ROWS, ROWS, dtype=single),
            kept(ROWS, D, dtype=single),
            kept(ROWS, 1, dtype=single),
            kept(ROWS, FF, dtype=single),
            jax.ShapeDtypeStruct((FF, LAYERS * ROWS), jnp.bfloat16),
            kept(ROWS, D, dtype=single),
            kept(ROWS, 1, dtype=single),
        ],
        in_specs=[pl.BlockSpec(memory_space=pltpu.SMEM)]
        + [whole_spec()] * 2
        + [lift_spec()]
        + [whole_spec()] * 3,
        out_specs=[
            pl.BlockSpec((ROWS, D), lambda i: (0, 0)),
            pl.BlockSpec((ROWS, E), lambda i: (0, 0)),
            pl.BlockSpec((ROWS, 1), lambda i: (0, 0)),
            pl.BlockSpec((ROWS, E), lambda i: (0, 0)),
            pl.BlockSpec((3, None, ROWS, D), lambda i: (0, i, 0, 0)),
            by_layer(ROWS, 3 * D),
            by_layer(HEADS, ROWS, ROWS),
            by_layer(ROWS, D),
            by_layer(ROWS, 1),
            by_layer(ROWS, FF),
            pl.BlockSpec((FF, ROWS), lambda i: (0, i)),
            by_layer(ROWS, D),
            by_layer(ROWS, 1),
        ],
        scratch_shapes=[VMEM_SPACE((ROWS, D), single)],
        compiler_params=pltpu.CompilerParams(
            dimension_semantics=("arbitrary",), vmem_limit_bytes=VMEM_ASK
        ),
    )(lengths, found, place, head, wide, tall, vec)
    return dict(zip(names, outs))


def backward_kernel(
    lengths,
    start,
    wide_sums,
    small_sums,
    embed_hat,
    embed_inverse,
    normed_half,
    lift,
    head_in,
    wide,
    tall,
    vec,
    projected,
    weighting,
    hat_one,
    inverse_one,
    slope,
    hat_two,
    inverse_two,
    rows_out,
    back_lift,
    turned,
    outer,
    vector,
    sums,
    ff_sum,
    upstream,
    back_mixed,
    joint,
):
    step = pl.program_id(0)

    @pl.when(step == 0)
    def _():
        upstream[...] = start[...]
        sums[...] = jnp.zeros_like(sums)
        ff_sum[...] = jnp.zeros_like(ff_sum)

    def row(index):
        return wide_row(vec, index)

    def add_sum(index, value):
        here = pl.ds(index - Q_B, 1)
        sums[here, :] = sums[here, :] + jnp.sum(value, 0, keepdims=True)

    up = upstream[...]
    hat = hat_two[...]
    add_sum(LN2_G, up * hat)
    add_sum(LN2_B, up)
    back_second = norm_backward(up, row(LN2_G), hat, inverse_two[...])
    half = to_half(back_second)
    outer[...] = half
    add_sum(FFO_B, half.astype(jnp.float32))
    total = back_second
    for low in range(0, FF, CHUNK):
        lanes = pl.ds(low, CHUNK)
        inner = to_half(nt(half, tall[lanes, :]) * slope[:, lanes])
        ff_sum[:, lanes] = ff_sum[:, lanes] + jnp.sum(
            inner.astype(jnp.float32), 0, keepdims=True
        )
        turned[pl.ds(4 * D + low, CHUNK), :] = inner.T
        total = total + nn(inner, wide[pl.ds(4 * D + low, CHUNK), :])
    hat = hat_one[...]
    add_sum(LN1_G, total * hat)
    add_sum(LN1_B, total)
    back_first = norm_backward(total, row(LN1_G), hat, inverse_one[...])
    upstream[...] = back_first
    half = to_half(back_first)
    add_sum(O_B, half.astype(jnp.float32))
    turned[pl.ds(3 * D, D), :] = half.T
    back_mixed[...] = to_half(nn(half, wide[pl.ds(3 * D, D), :]))
    for pair in range(HEADS // 2):
        lanes = pair * PAIR
        queries = halves(projected[:, pl.ds(lanes, PAIR)])
        keys = halves_down(projected[:, pl.ds(D + lanes, PAIR)].T)
        values = projected[:, pl.ds(2 * D + lanes, PAIR)]
        grads = halves(back_mixed[:, pl.ds(lanes, PAIR)])
        zero = jnp.zeros((ROWS, PAIR), jnp.float32)
        back_query, back_key, back_value = jnp.zeros((PAIR, ROWS), jnp.float32), zero, zero
        for side in (0, 1):
            weights = weighting[2 * pair + side]
            soft = nt(values, grads[side])
            scores = to_half(weights * (soft - jnp.sum(weights * soft, 0, keepdims=True)))
            back_query = back_query + nn(keys[side], scores)
            back_key = back_key + nn(scores, queries[side])
            back_value = back_value + nn(to_half(weights), grads[side])
        query_half = to_half(back_query * SCALE)
        key_half, value_half = to_half(back_key * SCALE), to_half(back_value)
        joint[:, pl.ds(lanes, PAIR)] = query_half.T
        joint[:, pl.ds(D + lanes, PAIR)] = key_half
        joint[:, pl.ds(2 * D + lanes, PAIR)] = value_half
        turned[pl.ds(lanes, PAIR), :] = query_half
        turned[pl.ds(D + lanes, PAIR), :] = key_half.T
        turned[pl.ds(2 * D + lanes, PAIR), :] = value_half.T
    total = upstream[...]
    for part, bias in ((0, Q_B), (1, None), (2, V_B)):
        here = pl.ds(part * D, D)
        value = joint[:, here]
        if bias is not None:
            add_sum(bias, value.astype(jnp.float32))
        total = total + nn(value, wide[here, :])
    upstream[...] = total

    @pl.when(step == LAYERS - 1)
    def _():
        half = to_half(upstream[...])
        back_lift[...] = to_half(tn(normed_half[...], half))
        back_normed = nt(half, lift[...])
        hat = embed_hat[...]
        back = norm_backward(back_normed, short_row(vec, EMB_G), hat, embed_inverse[...])
        rows_out[...] = to_half(back)
        kind = kinds(lengths)
        ones = jnp.sum(back * kind, 0, keepdims=True)
        zeros = jnp.sum(back * (1.0 - kind), 0, keepdims=True)
        vector[...] = jnp.zeros_like(vector)
        parts = [jnp.sum(half.astype(jnp.float32), 0, keepdims=True)]
        parts += [sums[pl.ds(i, 1), :] for i in range(8)]
        parts += [wide_sums[pl.ds(i, 1), :] for i in range(3)]
        parts += [ff_sum[...]]
        parts += [
            jnp.sum(back_normed * hat, 0, keepdims=True),
            jnp.sum(back_normed, 0, keepdims=True),
        ]
        parts += [small_sums[pl.ds(i, 1), :] for i in range(3)]
        parts += [zeros, ones]
        at = 0
        for part in parts:
            for low in range(0, part.shape[1], 128):
                vector[pl.ds(at, 1), :] = part[:, low : low + 128]
                at += 1


def run_backward(lengths, start, wide_sums, small_sums, head, back_head, wide, tall, vec, kept, lines):
    single, half = jnp.float32, jnp.bfloat16
    last = LAYERS - 1

    def order(i):
        return last - i

    return pl.pallas_call(
        backward_kernel,
        grid=(LAYERS,),
        out_shape=[
            jax.ShapeDtypeStruct((ROWS, E), half),
            jax.ShapeDtypeStruct(back_head.shape, half),
            jax.ShapeDtypeStruct((4 * D + FF, LAYERS * ROWS), half),
            jax.ShapeDtypeStruct((LAYERS, ROWS, D), half),
            jax.ShapeDtypeStruct((lines, 128), single),
        ],
        in_specs=[pl.BlockSpec(memory_space=pltpu.SMEM)]
        + [whole_spec()] * 6
        + [lift_spec(), pl.BlockSpec(memory_space=pl.ANY)]
        + [whole_spec()] * 3
        + [
            by_layer(ROWS, 3 * D, order=order),
            by_layer(HEADS, ROWS, ROWS, order=order),
            by_layer(ROWS, D, order=order),
            by_layer(ROWS, 1, order=order),
            by_layer(ROWS, FF, order=order),
            by_layer(ROWS, D, order=order),
            by_layer(ROWS, 1, order=order),
        ],
        out_specs=[
            pl.BlockSpec((ROWS, E), lambda i: (0, 0)),
            pl.BlockSpec((E, D), lambda i: ((E + D) // E, 0)),
            pl.BlockSpec((4 * D + FF, ROWS), lambda i: (0, order(i))),
            by_layer(ROWS, D, order=order),
            pl.BlockSpec((lines, 128), lambda i: (0, 0)),
        ],
        input_output_aliases={8: 1},
        scratch_shapes=[
            VMEM_SPACE((8, D), single),
            VMEM_SPACE((1, FF), single),
            VMEM_SPACE((ROWS, D), single),
            VMEM_SPACE((ROWS, D), half),
            VMEM_SPACE((ROWS, 3 * D), half),
        ],
        compiler_params=pltpu.CompilerParams(
            dimension_semantics=("arbitrary",), vmem_limit_bytes=VMEM_ASK
        ),
    )(
        lengths,
        start,
        wide_sums,
        small_sums,
        kept["embed_hat"],
        kept["embed_inverse"],
        kept["normed_half"],
        head,
        back_head,
        wide,
        tall,
        vec,
        kept["projected"],
        kept["weighting"],
        kept["hat_one"],
        kept["inverse_one"],
        kept["slope"],
        kept["hat_two"],
        kept["inverse_two"],
    )


def local(
    mesh,
    word_table,
    position_table,
    head_weights,
    decoder_bias,
    layer_wide,
    layer_tall,
    vectors,
    word_first,
    word_second,
    position_first,
    position_second,
    head_first,
    head_second,
    decoder_first,
    decoder_second,
    wide_first,
    wide_second,
    tall_first,
    tall_second,
    vector_first,
    vector_second,
    token_ids,
    seq_lengths,
    mlm_rows,
    mlm_labels,
    sop_labels,
):
    network = Network(mesh)

    (wide, tall, head), all_facts, place, found = network.start(
        (layer_wide.T, layer_tall, head_weights.T),
        word_table,
        position_table,
        (token_ids, mlm_labels, mlm_rows, seq_lengths, sop_labels),
    )
    devices = all_facts.shape[0]
    place = place.reshape(-1, E)
    vec = vectors.reshape(-1, 128)
    kept = run_forward(seq_lengths, found, place, head, wide, tall, vec)
    (back_final, back_word_head, back_decoder, back_head, wide_sums, small_sums, totals) = (
        network.head(
            seq_lengths,
            sop_labels,
            kept["final"],
            head,
            word_table,
            decoder_bias,
            all_facts,
            vec,
        )
    )
    total = vectors.shape[0]
    share = -(-total // (devices * 1024)) * 1024
    back_rows, back_head, turned, outer, vector_grad = run_backward(
        seq_lengths,
        back_final,
        wide_sums,
        small_sums,
        head,
        back_head,
        wide,
        tall,
        vec,
        kept,
        devices * share // 128,
    )
    sums, heights, back_word, back_place, last, ends = network.finish(
        turned,
        kept["active"],
        kept["rights"].reshape(3, -1, D),
        outer.reshape(-1, D),
        back_head,
        back_rows,
        vector_grad.reshape(devices, -1, 128),
        all_facts,
        back_word_head,
        back_decoder,
        totals,
        position_table.shape[0],
    )
    wide_at, tall_at, head_at = 0, heights[0], heights[0] + heights[1]

    def turned_group(weight, first, second, low):
        return (weight.T, first.T, second.T, sums, low, LEARN_RATE)

    def flat(x):
        return x[None]

    def lines(x):
        return x.reshape(-1, 128)

    groups = (
        (word_table, word_first, word_second, back_word, 0, LEARN_RATE),
        turned_group(layer_wide, wide_first, wide_second, wide_at),
        (layer_tall, tall_first, tall_second, sums, tall_at, LEARN_RATE),
        turned_group(head_weights, head_first, head_second, head_at),
        (position_table, position_first, position_second, back_place, None, LEARN_RATE),
        (flat(decoder_bias), flat(decoder_first), flat(decoder_second), back_decoder, None)
        + (LEARN_RATE,),
        (lines(vectors), lines(vector_first), lines(vector_second), last, None, SMALL_RATE),
    )
    arrays, scalars = network.adam(ends, groups)
    word, wide, tall, head, position, decoder, vector = arrays
    grad_norm, unused, mlm_sum, sop_total, mlm_count, sop_count = scalars

    def turn(arrays):
        return [x.T for x in arrays]

    def plain(arrays):
        return [x.reshape(-1) for x in arrays]

    updates = (*word, *position, *turn(head), *plain(decoder), *turn(wide), *tall, *plain(vector))
    return (*updates, mlm_sum, mlm_count, sop_total, sop_count, grad_norm)


def solution(mesh):
    rows = P(AXES, None)
    columns = P(None, AXES)
    flat = P(AXES)
    whole = P()
    return jax.shard_map(
        functools.partial(local, mesh),
        mesh=mesh,
        in_specs=(rows, rows, columns, flat, columns, rows, whole)
        + (rows, rows) * 2
        + (columns, columns, flat, flat, columns, columns, rows, rows, whole, whole)
        + (flat,) * 5,
        out_specs=(rows,) * 6
        + (columns,) * 3
        + (flat,) * 3
        + (columns,) * 3
        + (rows,) * 3
        + (whole,) * 8,
        check_vma=False,
    )
```

```python
import functools

import jax
import jax.numpy as jnp
from jax import lax
from jax.experimental import pallas as pl
from jax.experimental.pallas import tpu as pltpu
from jax.sharding import PartitionSpec as P

D = 768
HEADS = 12
HEAD_DIM = 64
FF = 3072
E = 128
LAYERS = 4
STEP = 10
BUCKET = 128
ROWS = 2 * BUCKET

PRECISE = lax.Precision.HIGHEST
EPSILON = 1e-06
LEARN_RATE = 0.1
SMALL_RATE = 0.5
BETA_ONE = 0.9
BETA_TWO = 0.999
ADAM_EPSILON = 1e-08
WEIGHT_DECAY = 0.01
CLIP_NORM = 0.005
NORM_EPSILON = 1e-06
MASKED = -1e30
SCALE = HEAD_DIM ** (-0.5)
AXES = ("dp", "fsdp")


def to_half(x):
    return x.astype(jnp.bfloat16)


def product(a, b):
    return jnp.dot(a, b, preferred_element_type=jnp.float32)


def times_transpose(a, b):
    return lax.dot_general(a, b, (((1,), (1,)), ((), ())), preferred_element_type=jnp.float32)


def transpose_times(a, b):
    return lax.dot_general(a, b, (((0,), (0,)), ((), ())), preferred_element_type=jnp.float32)


def column_sum(x):
    return jnp.sum(x.astype(jnp.float32), 0)


def norm_forward(x):
    centre = x - jnp.mean(x, -1, keepdims=True)
    inverse = lax.rsqrt(jnp.mean(centre * centre, -1, keepdims=True) + EPSILON)
    return centre * inverse, inverse


def norm_backward(upstream, factor, hat, inverse):
    scaled = upstream * factor
    return inverse * (
        scaled
        - jnp.mean(scaled, -1, keepdims=True)
        - hat * jnp.mean(scaled * hat, -1, keepdims=True)
    )


GELU_A = 0.7978845608028654
GELU_B = 0.044715


MESH_ID = pl.DeviceIdType.MESH
VMEM_SPACE = pltpu.VMEM
VMEM_ASK = 60 * 1024 * 1024


def greet(peers):
    barrier = pltpu.get_barrier_semaphore()
    count = 0
    for present, who in peers:
        if present is None:
            pl.semaphore_signal(barrier, inc=1, device_id=who, device_id_type=MESH_ID)
            count = count + 1
        else:

            @pl.when(present)
            def _(who=who):
                pl.semaphore_signal(barrier, inc=1, device_id=who, device_id_type=MESH_ID)

            count = count + present.astype(jnp.int32)
    pl.semaphore_wait(barrier, count)


def maybe(condition, action):
    if condition is None:
        action()
    else:
        pl.when(condition)(action)


def remote(source, target, send, receive, who):
    return pltpu.make_async_remote_copy(
        src_ref=source,
        dst_ref=target,
        send_sem=send,
        recv_sem=receive,
        device_id=who,
        device_id_type=MESH_ID,
    )


OWN, ACROSS_X, ACROSS_Y, DIAGONAL = 0, 1, 2, 3


def cuts_of(rows, share):
    tail = max(32, round(rows * share / 32) * 32)
    head = rows - tail
    return ((0, head), (head, rows))


GATHER_TAIL, FINISH_TAIL = 0.3, 0.2


def half_of(span, which):
    low, high = span
    middle = (low + high) // 2
    return (low, middle) if which == 0 else (middle, high)


def places():
    z, f = lax.axis_index("dp"), lax.axis_index("fsdp")
    q, c = f // 2, lax.rem(f, 2)
    qx = q + 1 - 2 * lax.rem(q, 2)
    qy = lax.rem(q + 2, 4)
    qd = qx + qy - q
    return z, c, (q, qx, qy, qd)


def gather_stages(planes, rows, members, x, outs, buf, sems, where, opening):
    out_sem, send, recv, side_send, side_recv = sems
    z, c, cols = where
    cuts = cuts_of(rows, GATHER_TAIL)
    at_x, at_y, mate = (z, cols[1] * 2 + c), (z, cols[2] * 2 + c), (z, cols[0] * 2 + 1 - c)
    above, below = z < planes - 1, z > 0
    up, down = (z + 1, cols[0] * 2 + c), (z - 1, cols[0] * 2 + c)
    sent = []

    def block(zs, col, core, span):
        return buf.at[zs, cols[col], core, pl.ds(span[0], span[1] - span[0])]

    def push(condition, zs, col, span, who, slot, receive, mine=False):
        def make():
            here = block(zs, col, c, span)
            source = x.at[pl.ds(span[0], span[1] - span[0])] if mine else here
            return remote(source, here, send.at[slot[0], zs, slot[1]], receive, who)

        maybe(condition, lambda: make().start())
        sent.append((condition, make))

    def await_block(zs, col, span, receive, core=None):
        here = block(zs, col, c if core is None else core, span)
        remote(here, here, send.at[0, 0, 0], receive, mate).wait_recv()

    def deliver(zs, col, core, span):
        for index, (out, (low, high)) in enumerate(zip(outs, members)):
            first, last = max(low, span[0]), min(high, span[1])
            if first < last:
                pltpu.make_async_copy(
                    buf.at[zs, cols[col], core, pl.ds(first, last - first)],
                    out.at[zs, cols[col], core, pl.ds(first - low, last - first)],
                    out_sem.at[index],
                ).start()

    def share(condition, part, zs, col, span, kind, mine=False):
        def make():
            here = block(zs, col, c, span)
            source = x.at[pl.ds(span[0], span[1] - span[0])] if mine else here
            return remote(
                source, here, side_send.at[part, zs, kind], side_recv.at[part, zs, kind], mate
            )

        def action():
            make().start()
            if not mine:
                deliver(zs, col, c, span)

        maybe(condition, action)
        sent.append((condition, make))
        shared.append((condition, part, zs, col, span, kind))

    shared = []
    whole = [cuts[0], cuts[1]]
    for part in (0, 1):
        push(above, z, OWN, whole[part], up, (part, 2), recv.at[part, z, OWN], True)
        push(below, z, OWN, whole[part], down, (part, 3), recv.at[part, z, OWN], True)
    for part in (1, 0):
        if part == 0:
            opening()
        push(None, z, OWN, whole[part], at_x, (part, 0), recv.at[part, z, ACROSS_X], True)
        push(None, z, OWN, whole[part], at_y, (part, 1), recv.at[part, z, ACROSS_Y], True)
    for part in (0, 1):
        share(None, part, z, OWN, whole[part], 0, True)
    own_copy = pltpu.make_async_copy(x, buf.at[z, cols[0], c], out_sem.at[len(members)])
    own_copy.start()

    def turn(condition, part, zs):
        span = whole[part]
        for col, which, who, slot in ((ACROSS_X, 1, at_y, 4), (ACROSS_Y, 0, at_x, 5)):
            maybe(
                condition,
                lambda col=col: await_block(zs, col, span, recv.at[part, zs, col]),
            )
            push(condition, zs, col, half_of(span, which), who, (part, slot), recv.at[part, zs, 4 + which])
            if part == 1:
                push(above, zs, col, span, up, (1, 4 + 2 * col), recv.at[1, zs, col])
                push(below, zs, col, span, down, (1, 5 + 2 * col), recv.at[1, zs, col])
            share(condition, part, zs, col, span, col)

    yield
    turn(None, 1, z)
    yield
    for which in (0, 1):
        await_block(z, DIAGONAL, half_of(whole[1], which), recv.at[1, z, 4 + which])
    push(above, z, DIAGONAL, whole[1], up, (1, 10), recv.at[1, z, DIAGONAL])
    push(below, z, DIAGONAL, whole[1], down, (1, 11), recv.at[1, z, DIAGONAL])
    share(None, 1, z, DIAGONAL, whole[1], 3)
    yield
    turn(None, 0, z)

    def settle(upto):
        while len(shared) > upto:
            condition, part, zs, col, span, kind = shared.pop(0)

            def action():
                await_block(zs, col, span, side_recv.at[part, zs, kind], 1 - c)
                deliver(zs, col, 1 - c, span)

            maybe(condition, action)

    for step in range(1, planes):
        yield
        ways = ((z - step >= 0, z - step, above, up), (z + step < planes, z + step, below, down))
        for valid, zs, further, onward in ways:
            go = jnp.logical_and(valid, further)
            pl.when(valid)(
                lambda zs=zs: await_block(zs, OWN, whole[0], recv.at[0, zs, OWN])
            )
            push(go, zs, OWN, whole[0], onward, (0, 2), recv.at[0, zs, OWN])
            push(valid, zs, OWN, whole[0], at_x, (0, 0), recv.at[0, zs, ACROSS_X])
            push(valid, zs, OWN, whole[0], at_y, (0, 1), recv.at[0, zs, ACROSS_Y])
            share(valid, 0, zs, OWN, whole[0], 0)
        yield
        for valid, zs, further, onward in ways:
            go = jnp.logical_and(valid, further)
            for col in (OWN, ACROSS_X, ACROSS_Y, DIAGONAL):
                pl.when(valid)(
                    lambda zs=zs, col=col: await_block(zs, col, whole[1], recv.at[1, zs, col])
                )
                push(go, zs, col, whole[1], onward, (1, col), recv.at[1, zs, col])
                share(valid, 1, zs, col, whole[1], col)
        yield
        for valid, zs, further, onward in ways:
            turn(valid, 0, zs)
        settle(8)
    yield
    own_copy.wait()
    deliver(z, OWN, c, (0, rows))
    everywhere = [(None, z)] + [
        (valid, zs)
        for step in range(1, planes)
        for valid, zs in ((z - step >= 0, z - step), (z + step < planes, z + step))
    ]
    for condition, zs in everywhere:
        for which in (0, 1):
            span = half_of(whole[0], which)
            maybe(
                condition,
                lambda zs=zs, which=which, span=span: await_block(
                    zs, DIAGONAL, span, recv.at[0, zs, 4 + which]
                ),
            )
            share(condition, 0, zs, DIAGONAL, span, 3 + which)
    settle(0)
    for condition, make in sent:
        maybe(condition, lambda make=make: make().wait_send())
    for index, (out, (low, high)) in enumerate(zip(outs, members)):
        pltpu.make_async_copy(
            buf.at[:, :, :, pl.ds(low, high - low)], out, out_sem.at[index]
        ).wait()


def select_stages(planes, facts, own_word, found, refs, where, offset):
    part, side, plane_in, middle, line_in, turned, sems_send, sems_recv = refs
    z, c, cols = where
    q = cols[0]
    f = q * 2 + c
    mate = (z, q * 2 + 1 - c)
    words = own_word.shape[0]
    line = [(lax.rem(z + d, planes), f) for d in range(1, planes)]
    turned[...] = to_half(own_word[...].T)
    yield

    def mate_message(col):
        return remote(
            part.at[:, col, 1 - c], side.at[:, col], sems_send.at[0, col], sems_recv.at[0, col], mate
        )

    def plane_message(col):
        return remote(
            part.at[:, col, c],
            plane_in.at[col],
            sems_send.at[1, col],
            sems_recv.at[1, col],
            (z, cols[col] * 2 + c),
        )

    def line_message(d, who):
        return remote(
            middle.at[who[0]], line_in.at[d], sems_send.at[2, d], sems_recv.at[2, d], who
        )

    def merge(col):
        mate_message(col).wait_recv()
        for zt in range(planes):
            part[zt, col, c] = part[zt, col, c] + side[zt, col]
        if col != OWN:
            plane_message(col).start()

    order = (DIAGONAL, ACROSS_X, ACROSS_Y, OWN)
    for place, col in enumerate(order):

        def body(n, unused, col=col):
            zt, core = n // 2, lax.rem(n, 2)
            ids = facts[zt, cols[col] * 2 + core]
            row = lax.broadcasted_iota(jnp.int32, (words, BUCKET), 0) + offset
            picks = jnp.concatenate(
                [to_half((row == ids[i : i + 1, :]).astype(jnp.float32)) for i in (0, 1)], 1
            )
            part[zt, col, core] = to_half(nn(turned[...], picks))
            return unused

        lax.fori_loop(0, 2 * planes, body, 0)
        mate_message(col).start()
        if place > 0:
            merge(order[place - 1])
        yield
    merge(OWN)
    total = part[:, OWN, c]
    yield
    for col in order[:3]:
        plane_message(col).wait_recv()
        total = total + plane_in[col]
    middle[...] = total
    for d, who in enumerate(line):
        line_message(d, who).start()
    yield
    total = middle[z]
    for d, who in enumerate(line):
        line_message(d, who).wait_recv()
        total = total + line_in[d]
    found[...] = total.astype(jnp.float32).T
    for col in order:
        mate_message(col).wait_send()
    for col in order[:3]:
        plane_message(col).wait_send()
    for d, who in enumerate(line):
        line_message(d, who).wait_send()


PLAN = (1, 1, 1, 1, 1, 1, 1, 1, 1, 1, 1, 1, 1, 1)


def start_kernel(
    planes,
    rows,
    members,
    own_wide,
    own_tall,
    own_head,
    own_word,
    own_place,
    ids,
    labels,
    slot_rows,
    lengths,
    sop_labels,
    *refs,
):
    width = 8
    count = len(members)
    outs, (facts, place, found) = refs[:count], refs[count : count + 3]
    x, buf = refs[count + 3 : count + 5]
    gather_sems = refs[count + 5 : count + 10]
    select_refs = refs[count + 10 : count + 18]
    line_send, line_recv, plane_send, plane_recv = refs[count + 18 :]
    where = places()
    z, c, cols = where
    f = cols[0] * 2 + c
    line = [(lax.rem(z + d, planes), f) for d in range(1, planes)]
    plane = [(z, lax.rem(f + d, width)) for d in range(1, width)]
    lane = lax.broadcasted_iota(jnp.int32, (1, 128), 1)
    rest = jnp.full((1, 128 - labels.shape[1]), -1, jnp.int32)
    note = jnp.zeros((1, 128), jnp.int32)
    for at, value in enumerate((lengths[0], lengths[1], sop_labels[0], sop_labels[1])):
        note = note + jnp.where(lane == at, value, 0)
    facts[z, f] = jnp.concatenate(
        [
            ids[:, :128],
            ids[:, 128:],
            jnp.concatenate([labels[...], rest], 1),
            jnp.concatenate([slot_rows[...], rest], 1),
            note,
            jnp.zeros((3, 128), jnp.int32),
        ],
        0,
    )
    place[z, f] = to_half(own_place[...])
    greet([(None, who) for who in line + plane])
    pairs = (facts, place)

    def along(i, d, who):
        here = pairs[i].at[z, f]
        return remote(here, here, line_send.at[i, d], line_recv.at[i, d], who)

    def around(i, d, who, source):
        here = pairs[i].at[:, source]
        return remote(here, here, plane_send.at[i, d], plane_recv.at[i, d], who)

    for d, who in enumerate(line):
        for i in (0, 1):
            along(i, d, who).start()
    for (low, high), piece in zip(members, (own_wide[...], own_tall[...], own_head[...])):
        x[low:high] = to_half(piece)

    def opening():
        for d, who in enumerate(line):
            for i in (0, 1):
                source = pairs[i].at[lax.rem(z - d - 1 + planes, planes), f]
                remote(source, source, line_send.at[i, d], line_recv.at[i, d], who).wait_recv()
        for d, who in enumerate(plane):
            for i in (0, 1):
                around(i, d, who, f).start()

    gather = gather_stages(planes, rows, members, x, outs, buf, gather_sems, where, opening)
    offset = (z * width + f) * own_word.shape[0]
    select = select_stages(planes, facts, own_word, found, select_refs, where, offset)
    done = object()
    next(gather)
    next(select)
    for d in range(1, width):
        source = lax.rem(f - d + width, width)
        for i in (0, 1):
            around(i, d - 1, mate_of(where), source).wait_recv()
    for number in range(64):
        for unused in range(PLAN[number] if number < len(PLAN) else 1):
            next(select, done)
        if next(gather, done) is done:
            break
    for unused in select:
        pass
    for d, who in enumerate(line):
        for i in (0, 1):
            along(i, d, who).wait_send()
    for d, who in enumerate(plane):
        for i in (0, 1):
            around(i, d, who, f).wait_send()


def mate_of(where):
    z, c, cols = where
    return (z, cols[0] * 2 + 1 - c)


def run_start(shards, own_word, own_place, batch, mesh_shape, identity):
    planes, width = mesh_shape
    heights = tuple(shard.shape[0] for shard in shards)
    rows, columns = sum(heights), shards[1].shape[1]
    members, low = [], 0
    for height in heights:
        members.append((low, low + height))
        low += height
    half, single = jnp.bfloat16, jnp.float32
    vmem = pl.BlockSpec(memory_space=VMEM_SPACE)
    dma = pltpu.SemaphoreType.DMA
    words, features = own_word.shape
    block = (features, ROWS)
    *outs, facts, place, found = pl.pallas_call(
        functools.partial(start_kernel, planes, rows, tuple(members)),
        out_shape=[
            jax.ShapeDtypeStruct((planes, width // 2, 2, height, columns), half)
            for height in heights
        ]
        + [
            jax.ShapeDtypeStruct((planes, width, 8, 128), jnp.int32),
            jax.ShapeDtypeStruct((planes, width, *own_place.shape), half),
            jax.ShapeDtypeStruct((ROWS, features), single),
        ],
        in_specs=[vmem] * 8 + [pl.BlockSpec(memory_space=pltpu.SMEM)] * 2,
        out_specs=[pl.BlockSpec(memory_space=pl.ANY)] * len(heights) + [vmem] * 3,
        scratch_shapes=[
            VMEM_SPACE((rows, columns), half),
            VMEM_SPACE((planes, width // 2, 2, rows, columns), half),
            dma((len(heights) + 1,)),
            dma((2, planes, 12)),
            dma((2, planes, 6)),
            dma((2, planes, 5)),
            dma((2, planes, 5)),
            VMEM_SPACE((planes, 4, 2, *block), half),
            VMEM_SPACE((planes, 4, *block), half),
            VMEM_SPACE((4, planes, *block), half),
            VMEM_SPACE((planes, *block), half),
            VMEM_SPACE((planes - 1, *block), half),
            VMEM_SPACE((features, words), half),
            dma((3, 4)),
            dma((3, 4)),
            dma((2, planes)),
            dma((2, planes)),
            dma((2, width)),
            dma((2, width)),
        ],
        compiler_params=pltpu.CompilerParams(
            collective_id=identity, has_side_effects=True, vmem_limit_bytes=VMEM_ASK
        ),
    )(*shards, own_word, own_place, *[x[None] for x in batch[:3]], *batch[3:])
    weights = [out.reshape(-1, columns) for out in outs]
    devices = planes * width
    return (
        weights,
        facts.reshape(devices, 8, 128),
        place.reshape(devices, *own_place.shape),
        found,
    )


def accumulate(target, sources, height):
    step = 32

    def body(i, unused):
        rows = pl.ds(pl.multiple_of(i * step, step), step)
        total = sources[0][rows].astype(jnp.float32)
        for source in sources[1:]:
            total = total + source[rows].astype(jnp.float32)
        target[rows] = total.astype(target.dtype)
        return unused

    lax.fori_loop(0, height // step, body, 0)


ROWS_AT = 1
TURN_AT = 5
MATE_AT = 9


def far_first(i, z, planes):
    low = (2 * z < planes).astype(jnp.int32)
    falling = planes - 1 - i - (i >= planes - 1 - z).astype(jnp.int32)
    rising = i + (i >= z).astype(jnp.int32)
    last = (jnp.int32(i) == planes - 1).astype(jnp.int32)
    return last * z + (1 - last) * (low * falling + (1 - low) * rising)


def finish_kernel(
    planes,
    heights,
    split,
    left_wide,
    left_tall,
    rights_from,
    outer_from,
    head_grad,
    own_rows,
    vector_terms,
    facts,
    base_word,
    back_decoder,
    totals,
    out,
    word_grad,
    place_grad,
    last,
    ends,
    all_rows,
    both,
    side,
    half_in,
    full_in,
    line_in,
    tail_line,
    tail_half,
    tail_full,
    wide_buf,
    tall_buf,
    vector_in,
    vector_mid,
    vector_last,
    fetch,
    head_load,
    side_send,
    side_recv,
    send,
    recv,
    tail_send,
    tail_recv,
    row_send,
    row_recv,
    vec_send,
    vec_recv,
    end_send,
    end_recv,
    rights,
    outer,
    right_load,
):
    width = 8
    right_copies = [
        pltpu.make_async_copy(rights_from.at[i], rights.at[i], right_load.at[i]) for i in range(3)
    ]
    right_copies.append(pltpu.make_async_copy(outer_from, outer, right_load.at[3]))
    for copy in right_copies:
        copy.start()
    wide_height, tall_height, head_height = heights
    rows = wide_height + tall_height + head_height
    z, c, cols = places()
    q = cols[0]
    f = q * 2 + c
    x, y = lax.rem(q, 2), q // 2
    cuts = cuts_of(rows, FINISH_TAIL)
    head, tail = cuts
    head_rows, tail_rows = head[1] - head[0], tail[1] - tail[0]
    at_x, at_y, mate = (z, cols[1] * 2 + c), (z, cols[2] * 2 + c), (z, q * 2 + 1 - c)
    above, below = z < planes - 1, z > 0
    up, down = (z + 1, f), (z - 1, f)
    line = [(lax.rem(z + d, planes), f) for d in range(1, planes)]
    plane = [(z, lax.rem(f + d, width)) for d in range(1, width)]
    greet([(None, who) for who in line + plane])
    order = (DIAGONAL, ACROSS_X, ACROSS_Y, OWN)
    sent = []

    def push(condition, make):
        maybe(condition, lambda: make().start())
        sent.append((condition, make))

    def piece(ref, span):
        return ref.at[pl.ds(span[0], span[1] - span[0])]

    def plane_at(i):
        return far_first(i, z, planes)

    def turn_of(n):
        m = n - 1 - 3 * (n == 0).astype(jnp.int32) + (n > 4 * planes - 4).astype(jnp.int32)
        group, j = (m + 4) // 4 - 1, lax.rem(m + 4, 4)
        ahead = (j == 0).astype(jnp.int32)
        return group + ahead, DIAGONAL * ahead + j * (j < 3).astype(jnp.int32)

    def chip_of(n):
        i, col = turn_of(n)
        flip_x, flip_y = lax.rem(col, 2), col // 2
        return plane_at(i) * 4 + 2 * lax.rem(y + flip_y, 2) + lax.rem(x + flip_x, 2)

    def fetches(n):
        k, slot = chip_of(n), lax.rem(n, 2)
        wide_rows = pl.ds(pl.multiple_of(k * 2 * wide_height, 16), 2 * wide_height)
        tall_rows = pl.ds(pl.multiple_of(k * 2 * tall_height, 16), 2 * tall_height)
        return (
            pltpu.make_async_copy(
                left_wide.at[wide_rows], wide_buf.at[slot], fetch.at[0, slot]
            ),
            pltpu.make_async_copy(
                left_tall.at[tall_rows], tall_buf.at[slot], fetch.at[1, slot]
            ),
        )

    for copy in fetches(jnp.int32(0)):
        copy.start()

    def vector_first(d, who):
        return remote(
            vector_terms.at[:, who[1]], vector_in.at[d], vec_send.at[0, d], vec_recv.at[0, d], who
        )

    def vector_second(d, who):
        return remote(
            vector_mid.at[who[0]], vector_last.at[d], vec_send.at[1, d], vec_recv.at[1, d], who
        )

    def row_line(d, who):
        return remote(
            own_rows, all_rows.at[z, q, c], row_send.at[0, d], row_recv.at[0, d], who
        )

    def row_plane(col):
        return remote(
            all_rows.at[:, q, c],
            all_rows.at[:, q, c],
            row_send.at[1, col],
            row_recv.at[1, col],
            (z, cols[col] * 2 + c),
        )

    def row_turn(which):
        col, who = ((ACROSS_Y, at_x), (ACROSS_X, at_y))[which]
        here = all_rows.at[:, cols[col], c, pl.ds(which * BUCKET, BUCKET)]
        return remote(here, here, row_send.at[2, 1 + which], row_recv.at[2, 1 + which], who)

    def row_mate():
        return remote(
            all_rows.at[:, :, c], all_rows.at[:, :, c], row_send.at[2, 0], row_recv.at[2, 0], mate
        )

    for d, who in enumerate(line):
        push(None, functools.partial(row_line, d, who))
    for d, who in enumerate(plane):
        push(None, functools.partial(vector_first, d, who))
    all_rows[z, q, c] = own_rows[...]
    head_copies = []
    for col in order:
        copy = pltpu.make_async_copy(
            head_grad.at[:, cols[col]],
            both.at[:, col, :, pl.ds(wide_height + tall_height, head_height)],
            head_load.at[col],
        )
        copy.start()
        head_copies.append(copy)

    def side_message(zt, col):
        return remote(
            both.at[zt, col, 1 - c],
            side.at[zt, col],
            side_send.at[col, zt],
            side_recv.at[col, zt],
            mate,
        )

    def half_message(zt, which):
        return remote(
            piece(both.at[zt, DIAGONAL, c], half_of(head, which)),
            half_in.at[which, zt],
            send.at[0, which, zt],
            recv.at[0, which, zt],
            (at_x, at_y)[which],
        )

    def full_message(zt, which):
        return remote(
            piece(both.at[zt, (ACROSS_X, ACROSS_Y)[which], c], head),
            full_in.at[which, zt],
            send.at[1, which, zt],
            recv.at[1, which, zt],
            (at_x, at_y)[which],
        )

    def line_message(zt, way):
        return remote(
            piece(both.at[zt, OWN, c], head),
            line_in.at[way, zt],
            send.at[2, way, zt],
            recv.at[2, way, zt],
            (up, down)[way],
        )

    def tail_message(zt, way):
        return remote(
            both.at[zt, :, c, pl.ds(tail[0], tail_rows)],
            tail_line.at[way, zt],
            tail_send.at[way, zt],
            tail_recv.at[way, zt],
            (up, down)[way],
        )

    def merged(zt, col):
        side_message(zt, col).wait_recv()
        mine = both.at[zt, col, c]
        accumulate(mine, [mine, side.at[zt, col]], rows)

    def second(zt):
        for which, col in ((0, ACROSS_X), (1, ACROSS_Y)):
            half_message(zt, 1 - which).wait_recv()
            target = piece(both.at[zt, col, c], half_of(head, 1 - which))
            accumulate(target, [target, half_in.at[1 - which, zt]], head_rows // 2)
            full_message(zt, which).start()

    def tail_add(zt, way):
        tail_message(zt, way).wait_recv()
        for col in range(4):
            target = piece(both.at[zt, col, c], tail)
            accumulate(target, [target, tail_line.at[way, zt, col]], tail_rows)

    def ways(zt):
        return ((0, zt > z, below), (1, zt < z, above))

    def tail_open(zt):
        for way, valid, behind in ways(zt):
            go = jnp.logical_and(valid, jnp.logical_not(behind))
            pl.when(go)(lambda way=way: tail_message(zt, way).start())

    def tail_pass(zt):
        for way, valid, behind in ways(zt):

            def action(way=way):
                tail_add(zt, way)
                tail_message(zt, way).start()

            pl.when(jnp.logical_and(valid, behind))(action)

    def line_add(zt, way):
        line_message(zt, way).wait_recv()
        mine = piece(both.at[zt, OWN, c], head)
        accumulate(mine, [mine, line_in.at[way, zt]], head_rows)

    def third(zt):
        for which in (0, 1):
            full_message(zt, which).wait_recv()
        base = [piece(both.at[zt, OWN, c], head), full_in.at[0, zt], full_in.at[1, zt]]
        accumulate(base[0], base, head_rows)
        for way, valid, behind in ways(zt):
            go = jnp.logical_and(valid, jnp.logical_not(behind))
            pl.when(go)(lambda way=way: line_message(zt, way).start())

    def line_pass(zt):
        for way, valid, behind in ways(zt):

            def action(way=way):
                line_add(zt, way)
                line_message(zt, way).start()

            pl.when(jnp.logical_and(valid, behind))(action)

    def after(n):
        i, col = turn_of(n)
        zt = plane_at(i)
        merged(zt, col)

        @pl.when(col == DIAGONAL)
        def _():
            half_message(zt, 0).start()
            half_message(zt, 1).start()

        @pl.when(col == OWN)
        def _():
            second(zt)
            pl.when(i < planes - 1)(lambda: tail_open(zt))
            pl.when(i > 0)(lambda: tail_pass(plane_at(i - 1)))
            pl.when(i > 0)(lambda: third(plane_at(i - 1)))
            pl.when(i > 1)(lambda: line_pass(plane_at(i - 2)))

    for copy in head_copies + right_copies:
        copy.wait()

    def turn_rows():
        for step in (ACROSS_X, ACROSS_Y):
            here = all_rows.at[:, cols[step], c]
            remote(here, here, row_send.at[1, step], row_recv.at[1, step], mate).wait_recv()
        for which in (0, 1):
            row_turn(which).start()

    def share_rows():
        for which in (0, 1):
            here = all_rows.at[:, cols[DIAGONAL], c, pl.ds(which * BUCKET, BUCKET)]
            remote(
                here, here, row_send.at[2, 1 + which], row_recv.at[2, 1 + which], mate
            ).wait_recv()
        row_mate().start()

    def sum_vector():
        total = vector_mid[z]
        for d, who in enumerate(line):
            vector_second(d, who).wait_recv()
            total = total + vector_last[d]
        last[z, f, 0:8] = total

    def body(n, unused):
        for copy in fetches(n):
            copy.wait()

        @pl.when(n + 1 < 4 * planes)
        def _():
            for copy in fetches(n + 1):
                copy.start()

        (i, col), k, slot = turn_of(n), chip_of(n), lax.rem(n, 2)
        zt = plane_at(i)
        region = (k >= split[0]).astype(jnp.int32) + (k >= split[1]).astype(jnp.int32)
        product_wide = to_half(nn(wide_buf[slot], rights[region]))
        both[zt, col, 0, :wide_height] = product_wide[:wide_height]
        both[zt, col, 1, :wide_height] = product_wide[wide_height:]
        product_tall = to_half(nn(tall_buf[slot], outer[...]))
        here = slice(wide_height, wide_height + tall_height)
        both[zt, col, 0, here] = product_tall[:tall_height]
        both[zt, col, 1, here] = product_tall[tall_height:]
        side_message(zt, col).start()
        pl.when(n > 0)(lambda: after(n - 1))

        @pl.when(n == ROWS_AT)
        def _():
            for d, who in enumerate(line):
                row_line(d, who).wait_recv()
            for step in (ACROSS_X, ACROSS_Y):
                row_plane(step).start()
            total = vector_terms[:, f]
            for d, who in enumerate(plane):
                vector_first(d, who).wait_recv()
                total = total + vector_in[d]
            vector_mid[...] = total
            for d, who in enumerate(line):
                vector_second(d, who).start()

        pl.when(n == TURN_AT)(turn_rows)
        pl.when(n == MATE_AT)(share_rows)

        return unused

    lax.fori_loop(0, 4 * planes, body, 0)
    after(jnp.int32(4 * planes - 1))
    targets = [plane_at(i) for i in range(planes)]
    sum_vector()
    here = all_rows.at[:, :, 1 - c]
    remote(here, here, row_send.at[2, 0], row_recv.at[2, 0], mate).wait_recv()
    words = word_grad.shape[0]
    offset = (z * width + f) * words

    def look_back(first, after):
        def body(n, unused):
            zt, chip = n // 4, lax.rem(n, 4)
            row = lax.broadcasted_iota(jnp.int32, (words, BUCKET), 0) + offset
            total = word_grad[...]
            for core in (0, 1):
                ids = facts[zt, chip * 2 + core]
                picks = jnp.concatenate(
                    [to_half((row == ids[i : i + 1, :]).astype(jnp.float32)) for i in (0, 1)], 1
                )
                total = total + nn(picks, all_rows[zt, chip, core])
            word_grad[...] = total
            return unused

        lax.fori_loop(first, after, body, 0)

    word_grad[...] = base_word[...]

    def tail_half_message(which):
        return remote(
            piece(both.at[z, DIAGONAL, c], half_of(tail, which)),
            tail_half.at[which],
            tail_send.at[2, which],
            tail_recv.at[2, which],
            (at_x, at_y)[which],
        )

    def tail_full_message(which):
        return remote(
            piece(both.at[z, (ACROSS_X, ACROSS_Y)[which], c], tail),
            tail_full.at[which],
            tail_send.at[3, which],
            tail_recv.at[3, which],
            (at_x, at_y)[which],
        )

    pl.when(below)(lambda: tail_add(z, 0))
    pl.when(above)(lambda: tail_add(z, 1))
    for which in (0, 1):
        push(None, functools.partial(tail_half_message, which))
    line_pass(targets[planes - 2])
    look_back(0, 4 * planes)
    for which, col in ((1, ACROSS_X), (0, ACROSS_Y)):
        tail_half_message(which).wait_recv()
        target = piece(both.at[z, col, c], half_of(tail, which))
        accumulate(target, [target, tail_half.at[which]], tail_rows // 2)
    for which in (0, 1):
        push(None, functools.partial(tail_full_message, which))
    for which in (0, 1):
        full_message(z, which).wait_recv()
    goal = piece(out, head)
    accumulate(
        goal, [piece(both.at[z, OWN, c], head), full_in.at[0, z], full_in.at[1, z]], head_rows
    )
    for present, way in ((below, 0), (above, 1)):

        def add(way=way):
            line_message(z, way).wait_recv()
            accumulate(goal, [goal, line_in.at[way, z]], head_rows)

        pl.when(present)(add)
    for which in (0, 1):
        tail_full_message(which).wait_recv()
    accumulate(
        piece(out, tail),
        [piece(both.at[z, OWN, c], tail), tail_full.at[0], tail_full.at[1]],
        tail_rows,
    )
    height = place_grad.shape[0]
    own = z * width + f
    low_half = (own * height < BUCKET).astype(jnp.float32)
    high_half = (own * height < 2 * BUCKET).astype(jnp.float32) - low_half
    slot = pl.multiple_of(lax.rem(own * height, BUCKET), height)
    lane = lax.broadcasted_iota(jnp.int32, (1, 128), 1)
    grad = jnp.zeros((height, 128), jnp.float32)
    for zt in range(planes):
        for chip in range(4):
            for core in (0, 1):
                note = facts[zt, chip * 2 + core, 4:5, :]
                two = jnp.sum(
                    jnp.where(lane == 1, (note > 0).astype(jnp.float32), 0.0), 1, keepdims=True
                )
                lower = all_rows[zt, chip, core, pl.ds(slot, height)].astype(jnp.float32)
                upper = all_rows[zt, chip, core, pl.ds(BUCKET + slot, height)].astype(jnp.float32)
                grad = grad + low_half * (lower + two * upper) + high_half * (1.0 - two) * upper
    place_grad[...] = grad
    squares = jnp.sum(grad * grad) + jnp.sum(back_decoder[...] * back_decoder[...])
    squares = squares + jnp.sum(word_grad[...] * word_grad[...])
    squares = squares + jnp.sum(out[...] * out[...])
    last[z, f, 8:16] = jnp.concatenate(
        [totals[...], jnp.where(lane == 0, squares, 0.0), jnp.zeros((6, 128), jnp.float32)], 0
    )
    first_copies, second_copies = [], []
    for d, who in enumerate(line):
        here = last.at[z, f]
        first_copies.append(remote(here, here, end_send.at[0, d], end_recv.at[0, d], who))
        first_copies[-1].start()
    for d, who in enumerate(line):
        here = last.at[lax.rem(z - d - 1 + planes, planes), f]
        remote(here, here, end_send.at[0, d], end_recv.at[0, d], who).wait_recv()
    for d, who in enumerate(plane):
        here = last.at[:, f]
        second_copies.append(remote(here, here, end_send.at[1, d], end_recv.at[1, d], who))
        second_copies[-1].start()
    for d, who in enumerate(plane):
        here = last.at[:, lax.rem(f - d - 1 + width, width)]
        remote(here, here, end_send.at[1, d], end_recv.at[1, d], who).wait_recv()
    summed = last[...]
    tails = jnp.sum(jnp.sum(summed[:, :, 8:16], 0), 0)
    squares = jnp.sum(summed[:, :, 0:8] * summed[:, :, 0:8]) + jnp.sum(tails[1:2, :])
    norm = jnp.sqrt(jnp.broadcast_to(squares, (1, 128)))
    factor = jnp.minimum(1.0, CLIP_NORM / (norm + NORM_EPSILON))
    mlm = totals[0:1, :] - jnp.sum(jnp.where(lane == 1, tails[0:1, :], 0.0))
    def count(at):
        own = jnp.where(lane == at, totals[0:1, :], 0.0)
        return jnp.broadcast_to(jnp.sum(own, 1, keepdims=True), (1, 128))

    sop = jnp.zeros((1, 128), jnp.float32) + jnp.sum(jnp.where(lane == 2, tails[0:1, :], 0.0))
    ends[...] = jnp.concatenate(
        [norm, factor, mlm, sop, count(3), count(4), jnp.zeros((2, 128), jnp.float32)], 0
    )
    for copy in first_copies + second_copies:
        copy.wait_send()
    row_mate().wait_send()
    for condition, make in sent:
        maybe(condition, lambda make=make: make().wait_send())
    for zt in targets:
        for col in order:
            side_message(zt, col).wait_send()
        for which in (0, 1):
            half_message(zt, which).wait_send()
            full_message(zt, which).wait_send()
        for way, valid in ((0, zt > z), (1, zt < z)):

            def done(zt=zt, way=way):
                tail_message(zt, way).wait_send()
                line_message(zt, way).wait_send()

            pl.when(valid)(done)
    for step in (ACROSS_X, ACROSS_Y):
        row_plane(step).wait_send()
    for which in (0, 1):
        row_turn(which).wait_send()
    for d, who in enumerate(line):
        vector_second(d, who).wait_send()


def run_finish(
    left_wide,
    left_tall,
    rights,
    outer,
    head_grad,
    own_rows,
    vector_terms,
    facts,
    base_word,
    back_decoder,
    totals,
    places_count,
    mesh_shape,
    identity,
):
    planes, width = mesh_shape
    devices = planes * width
    columns = outer.shape[1]
    heights = (
        left_wide.shape[0] // devices,
        left_tall.shape[0] // devices,
        head_grad.shape[0] // devices,
    )
    rows = sum(heights)
    long = left_wide.shape[1]
    split = (3 * D // (2 * heights[0]), 4 * D // (2 * heights[0]))
    head, tail = (high - low for low, high in cuts_of(rows, FINISH_TAIL))
    half, single = jnp.bfloat16, jnp.float32
    block = vector_terms.shape[1:]
    vmem = pl.BlockSpec(memory_space=VMEM_SPACE)
    any_space = pl.BlockSpec(memory_space=pl.ANY)
    dma = pltpu.SemaphoreType.DMA
    out, word_grad, place_grad, last, ends = pl.pallas_call(
        functools.partial(finish_kernel, planes, heights, split),
        out_shape=[
            jax.ShapeDtypeStruct((rows, columns), single),
            jax.ShapeDtypeStruct(base_word.shape, single),
            jax.ShapeDtypeStruct((places_count, 128), single),
            jax.ShapeDtypeStruct((planes, width, 16, 128), single),
            jax.ShapeDtypeStruct((8, 128), single),
        ],
        in_specs=[any_space] * 5 + [vmem] * 6,
        out_specs=[vmem] * 5,
        scratch_shapes=[
            VMEM_SPACE((planes, width // 2, 2, *own_rows.shape), half),
            VMEM_SPACE((planes, 4, 2, rows, columns), half),
            VMEM_SPACE((planes, 4, rows, columns), half),
            VMEM_SPACE((2, planes, head // 2, columns), half),
            VMEM_SPACE((2, planes, head, columns), half),
            VMEM_SPACE((2, planes, head, columns), half),
            VMEM_SPACE((2, planes, 4, tail, columns), half),
            VMEM_SPACE((2, tail // 2, columns), half),
            VMEM_SPACE((2, tail, columns), half),
            VMEM_SPACE((2, 2 * heights[0], long), half),
            VMEM_SPACE((2, 2 * heights[1], long), half),
            VMEM_SPACE((width - 1, planes, *block), single),
            VMEM_SPACE((planes, *block), single),
            VMEM_SPACE((planes - 1, *block), single),
            dma((2, 2)),
            dma((4,)),
            dma((4, planes)),
            dma((4, planes)),
            dma((3, 2, planes)),
            dma((3, 2, planes)),
            dma((4, planes)),
            dma((4, planes)),
            dma((3, 4)),
            dma((3, 4)),
            dma((2, width)),
            dma((2, width)),
            dma((2, width)),
            dma((2, width)),
            VMEM_SPACE(rights.shape, half),
            VMEM_SPACE(outer.shape, half),
            dma((4,)),
        ],
        compiler_params=pltpu.CompilerParams(
            collective_id=identity, has_side_effects=True, vmem_limit_bytes=VMEM_ASK
        ),
    )(
        left_wide,
        left_tall,
        rights,
        outer,
        head_grad.reshape(planes, width // 2, 2, heights[2], columns),
        own_rows,
        vector_terms.reshape(planes, width, *block),
        facts.reshape(planes, width, *facts.shape[1:]),
        base_word,
        back_decoder,
        totals,
    )
    return out, heights, word_grad, place_grad, last, ends


LIFT = 128
WIRE = 48


def exact_rows(pick, values):
    first = to_half(values)
    rest = values - first.astype(jnp.float32)
    second = to_half(rest)
    third = to_half(rest - second.astype(jnp.float32))
    return nn(pick, first) + nn(pick, second) + nn(pick, third)


def lanes_to_rows(x):
    return jnp.concatenate([x[:, i : i + 128] for i in range(0, x.shape[1], 128)], 0)


def rows_to_lanes(x):
    return jnp.concatenate([x[i : i + 1] for i in range(x.shape[0])], 1)


def head_kernel(
    planes,
    lengths,
    sop_labels,
    final,
    head,
    word,
    decoder,
    facts,
    vec,
    back_final,
    back_word,
    back_decoder,
    back_head,
    wide_sums,
    small_sums,
    totals,
    all_t,
    stats,
    powers,
    back_t,
    plane_in,
    middle,
    line_in,
    word_half,
    sends,
    recvs,
):
    width = 8
    z, c, cols = places()
    f = cols[0] * 2 + c
    line = [(lax.rem(z + d, planes), f) for d in range(1, planes)]
    plane = [(z, lax.rem(f + d, width)) for d in range(1, width)]
    greet([(None, who) for who in line + plane])
    offset = (z * width + f) * word.shape[0]
    words, slots = word.shape[0], planes * width * WIRE
    single = jnp.float32

    def gather_line(ref, kind):
        here = ref.at[z, f]
        return [
            remote(here, here, sends.at[kind, d], recvs.at[kind, d], who)
            for d, who in enumerate(line)
        ]

    def gather_plane(ref, kind):
        here = ref.at[:, f]
        return [
            remote(here, here, sends.at[kind, d], recvs.at[kind, d], who)
            for d, who in enumerate(plane)
        ]

    def await_line(ref, kind):
        for d in range(planes - 1):
            here = ref.at[lax.rem(z - d - 1 + planes, planes), f]
            remote(here, here, sends.at[kind, d], recvs.at[kind, d], line[d]).wait_recv()

    def await_plane(ref, kind):
        for d in range(width - 1):
            here = ref.at[:, lax.rem(f - d - 1 + width, width)]
            remote(here, here, sends.at[kind, d], recvs.at[kind, d], plane[d]).wait_recv()

    started = []
    lane = lax.broadcasted_iota(jnp.int32, (1, 128), 1)
    notes = facts[...]
    labels = jnp.concatenate([notes[i, 2:3, :WIRE] for i in range(planes * width)], 1)
    used = (lanes_to_rows(labels) >= 0).astype(single)
    mlm_count = jnp.sum(used)
    seconds = jnp.where(lane == 1, (notes[:, 4, :] > 0).astype(single), 0.0)
    sop_count = planes * width + jnp.sum(seconds)
    mlm_scale = 1.0 / jnp.broadcast_to(mlm_count, (1, 1))
    sop_scale = 1.0 / jnp.broadcast_to(sop_count, (1, 1))

    def start(copies):
        for copy in copies:
            copy.start()
        started.extend(copies)

    final_half = to_half(final[...])
    place = lax.broadcasted_iota(jnp.int32, (ROWS, LIFT), 0)
    scatter = to_half((place == facts[z * width + f, 3:4, :]).astype(single))
    pick = scatter.T
    picked = to_half(nn(pick, final_half))
    dense = nt(picked, head[:E, :]) + short_row(vec, MLM_B)
    bend = jnp.tanh(GELU_A * dense * (1.0 + GELU_B * dense * dense))
    hat, inverse = norm_forward(0.5 * dense * (1.0 + bend))
    slope = 0.5 * (1.0 + bend) + (0.5 * GELU_A) * dense * (1.0 - bend * bend) * (
        1.0 + 3.0 * GELU_B * dense * dense
    )
    rows_half = to_half(hat * short_row(vec, MLM_G) + short_row(vec, MLM_LB))
    all_t[z, f] = rows_half[:WIRE]
    start(gather_line(all_t, 0))

    word_half[...] = to_half(word[...])
    row16 = lax.broadcasted_iota(jnp.int32, (16, ROWS), 0)
    col16 = lax.broadcasted_iota(jnp.int32, (16, ROWS), 1)
    leads = to_half(
        (jnp.logical_and(row16 < 2, col16 == row16 * BUCKET)).astype(single)
    )
    firsts = to_half(nn(leads, final_half))
    pooled = jnp.tanh(nt(firsts, head[E : E + D, :]) + wide_row(vec, POOL_B))
    await_line(all_t, 0)
    start(gather_plane(all_t, 1))
    zero_class, one_class = lanes_of(vec, CLS_AT, D // 128), lanes_of(vec, CLS_AT + D // 128, D // 128)
    c0 = jnp.sum(pooled * zero_class, -1, keepdims=True)
    c1 = jnp.sum(pooled * one_class, -1, keepdims=True)
    class_top = jnp.maximum(c0, c1)
    e0, e1 = jnp.exp(c0 - class_top), jnp.exp(c1 - class_top)
    class_total = e0 + e1
    which = lax.broadcasted_iota(jnp.int32, (16, 1), 0)
    label = jnp.where(which == 0, sop_labels[0], sop_labels[1])
    hit = (label == 1).astype(single)
    two = (lengths[1] > 0).astype(single)
    present = jnp.where(which == 0, 1.0, jnp.where(which == 1, two, 0.0))
    losses = (jnp.log(class_total) + class_top - (c0 + hit * (c1 - c0))) * present
    weight = present * sop_scale
    back_c0 = (e0 / class_total - (1.0 - hit)) * weight
    back_c1 = (e1 / class_total - hit) * weight
    wide_sums[1:2, :] = jnp.sum(back_c0 * pooled, 0, keepdims=True)
    wide_sums[2:3, :] = jnp.sum(back_c1 * pooled, 0, keepdims=True)
    pre_half = to_half((back_c0 * zero_class + back_c1 * one_class) * (1.0 - pooled * pooled))
    wide_sums[0:1, :] = jnp.sum(pre_half.astype(single), 0, keepdims=True)
    back_head[E : E + D, :] = to_half(tn(pre_half, firsts))
    back_firsts = nn(pre_half, head[E : E + D, :])
    await_plane(all_t, 1)

    row = lax.broadcasted_iota(jnp.int32, (words, 128), 0) + offset
    bias = jnp.broadcast_to(to_half(decoder[...]).astype(single), (8, words)).T[:, 0:1]
    tops, sums, targets = [], [], []
    chunk = width * WIRE
    flat_t = all_t[...].reshape(slots, E)

    def logits_of(low):
        return nt(word_half[...], flat_t[low : low + chunk])

    coming = logits_of(0)
    for low in range(0, slots, chunk):
        logits = coming + bias
        if low + chunk < slots:
            coming = logits_of(low + chunk)
        top = jnp.max(logits, 0, keepdims=True)
        power = jnp.exp(logits - top)
        powers[:, pl.ds(low, chunk)] = power
        tops.append(top)
        sums.append(jnp.sum(power, 0, keepdims=True))
        for at in range(0, chunk, 128):
            mark = row == labels[:, low + at : low + at + 128]
            targets.append(
                jnp.sum(jnp.where(mark, logits[:, at : at + 128], 0.0), 0, keepdims=True)
            )
    own_top = lanes_to_rows(jnp.concatenate(tops, 1))
    groups = slots // 128
    stats[z, f, 0:groups] = own_top
    stats[z, f, groups : 2 * groups] = lanes_to_rows(jnp.concatenate(sums, 1))
    start(gather_line(stats, 2))
    target = jnp.sum(jnp.concatenate(targets, 0) * used)
    await_line(stats, 2)
    start(gather_plane(stats, 3))
    await_plane(stats, 3)
    every = stats[...].reshape(planes * width, 2 * groups, 128)
    top = jnp.max(every[:, :groups], 0)
    total = jnp.sum(every[:, groups:] * jnp.exp(every[:, :groups] - top[None]), 0)
    log_sum = jnp.sum((jnp.log(total) + top) * used)
    weight = used * mlm_scale
    factor = rows_to_lanes(weight * jnp.exp(own_top - top) / total)
    weight = rows_to_lanes(weight)

    def slot_terms(zz, d, who):
        return remote(
            back_t.at[zz, who[1]],
            plane_in.at[d, zz],
            sends.at[4 + zz, d],
            recvs.at[4 + zz, d],
            who,
        )

    def spread(word_sums, words_total, low, half):
        zz = low // chunk
        back_t[zz] = tn(half, word_half[...]).reshape(width, WIRE, E)
        start([slot_terms(zz, d, who) for d, who in enumerate(plane)])
        return word_sums + nt(ones, half), words_total + nn(half, flat_t[low : low + chunk])

    ready = []
    words_total = jnp.zeros((words, E), single)
    word_sums = jnp.zeros((8, words), single)
    ones = jnp.ones((8, width * WIRE), jnp.bfloat16)
    for low in range(0, slots, chunk):
        parts = []
        for at in range(low, low + chunk, 128):
            mark = row == labels[:, at : at + 128]
            part = powers[:, pl.ds(at, 128)] * factor[:, at : at + 128] - jnp.where(
                mark, weight[:, at : at + 128], 0.0
            )
            parts.append(to_half(part))
        if ready:
            word_sums, words_total = spread(word_sums, words_total, *ready.pop())
        ready.append((low, jnp.concatenate(parts, 1)))
    word_sums, words_total = spread(word_sums, words_total, *ready.pop())
    back_word[...] = words_total
    back_decoder[...] = word_sums[0:1]

    for zz in range(planes):
        total = back_t[zz, f]
        for d in range(width - 1):
            slot_terms(zz, d, plane[d]).wait_recv()
            total = total + plane_in[d, zz]
        middle[zz] = total
    start(
        [
            remote(middle.at[who[0]], line_in.at[d], sends.at[4 + planes, d], recvs.at[4 + planes, d], who)
            for d, who in enumerate(line)
        ]
    )
    total = middle[z]
    for d in range(planes - 1):
        remote(
            line_in.at[d], line_in.at[d], sends.at[4 + planes, d], recvs.at[4 + planes, d], line[d]
        ).wait_recv()
        total = total + line_in[d]
    back_rows = jnp.concatenate([total, jnp.zeros((LIFT - WIRE, E), single)], 0)
    small_sums[1:2, :] = jnp.sum(back_rows * hat, 0, keepdims=True)
    small_sums[2:3, :] = jnp.sum(back_rows, 0, keepdims=True)
    dense_half = to_half(norm_backward(back_rows, short_row(vec, MLM_G), hat, inverse) * slope)
    small_sums[0:1, :] = jnp.sum(dense_half.astype(single), 0, keepdims=True)
    back_head[:E, :] = to_half(tn(dense_half, picked))
    back_final[...] = exact_rows(scatter, nn(dense_half, head[:E, :]))
    back_final[0:1, :] = back_final[0:1, :] + back_firsts[0:1]
    back_final[BUCKET : BUCKET + 1, :] = back_final[BUCKET : BUCKET + 1, :] + back_firsts[1:2]
    sop_sum = jnp.sum(losses)
    ends = jnp.zeros((1, 128), single)
    for at, value in enumerate((log_sum, target, sop_sum, mlm_count, sop_count)):
        ends = ends + jnp.where(lane == at, value, 0.0)
    totals[...] = ends
    for copy in started:
        copy.wait_send()


def run_head(
    lengths, sop_labels, final, head, word, decoder, facts, vec, mesh_shape, identity
):
    planes, width = mesh_shape
    words = word.shape[0]
    slots = planes * width * WIRE
    groups = slots // 128
    single, half = jnp.float32, jnp.bfloat16
    vmem = pl.BlockSpec(memory_space=VMEM_SPACE)
    smem = pl.BlockSpec(memory_space=pltpu.SMEM)
    dma = pltpu.SemaphoreType.DMA
    return pl.pallas_call(
        functools.partial(head_kernel, planes),
        out_shape=[
            jax.ShapeDtypeStruct((ROWS, D), single),
            jax.ShapeDtypeStruct((words, E), single),
            jax.ShapeDtypeStruct((1, words), single),
            jax.ShapeDtypeStruct(head.shape, half),
            jax.ShapeDtypeStruct((3, D), single),
            jax.ShapeDtypeStruct((3, E), single),
            jax.ShapeDtypeStruct((1, 128), single),
        ],
        in_specs=[smem] * 2 + [vmem] * 6,
        out_specs=[vmem] * 7,
        scratch_shapes=[
            VMEM_SPACE((planes, width, WIRE, E), half),
            VMEM_SPACE((planes, width, 2 * groups, 128), single),
            VMEM_SPACE((words, slots), single),
            VMEM_SPACE((planes, width, WIRE, E), single),
            VMEM_SPACE((width - 1, planes, WIRE, E), single),
            VMEM_SPACE((planes, WIRE, E), single),
            VMEM_SPACE((planes - 1, WIRE, E), single),
            VMEM_SPACE((words, E), half),
            dma((5 + planes, width)),
            dma((5 + planes, width)),
        ],
        compiler_params=pltpu.CompilerParams(
            collective_id=identity, has_side_effects=True, vmem_limit_bytes=VMEM_ASK
        ),
    )(lengths, sop_labels, final, head, word, decoder, facts, vec)


def adam_update(weight, gradient, first, second, rate):
    first = BETA_ONE * first + (1 - BETA_ONE) * gradient
    second = BETA_TWO * second + (1 - BETA_TWO) * gradient * gradient
    first_hat = first / (1 - BETA_ONE**STEP)
    second_hat = second / (1 - BETA_TWO**STEP)
    updated = weight - rate * (
        first_hat / (jnp.sqrt(second_hat) + ADAM_EPSILON) + WEIGHT_DECAY * weight
    )
    return (updated, first, second)


def adam_kernel(blocks, rates, *refs):
    count = len(rates)
    ends, refs = refs[0], refs[1:]
    ins, outs, scalars = refs[: 4 * count], refs[4 * count : 7 * count], refs[7 * count :]
    factor = ends[1:2, 0:1]

    def update(number):
        weight, first, second, gradient = ins[4 * number : 4 * number + 4]
        grad = gradient[...]
        if grad.ndim > 2:
            grad = grad[:, :, :8].reshape(-1, 128)[: weight.shape[0]]
        results = adam_update(
            weight[...], factor * grad, first[...], second[...], rates[number]
        )
        for out, result in zip(outs[3 * number : 3 * number + 3], results):
            out[...] = result

    for number in range(blocks):
        update(number)

    @pl.when(pl.program_id(0) == 0)
    def _():
        for number in range(blocks, count):
            update(number)
        lane = lax.broadcasted_iota(jnp.int32, (1, 128), 1)
        for at, scalar in enumerate(scalars):
            scalar[0] = jnp.sum(jnp.where(lane == 0, ends[at : at + 1, :], 0.0))


def run_adam(ends, groups, steps):
    in_specs = [pl.BlockSpec(ends.shape, lambda i: (0, 0))]
    out_specs, shapes, given = [], [], [ends]
    blocks = 0
    for weight, first, second, gradient, low, rate in groups:
        rows, columns = weight.shape
        if low is None:
            spec = pl.BlockSpec(weight.shape, lambda i: (0, 0))
            zero = (0,) * gradient.ndim
            grad_spec = pl.BlockSpec(gradient.shape, lambda i, zero=zero: zero)
        else:
            blocks += 1
            height = rows // steps
            spec = pl.BlockSpec((height, columns), lambda i: (i, 0))
            grad_spec = pl.BlockSpec(
                (height, columns), lambda i, start=low // height: (start + i, 0)
            )
        in_specs += [spec] * 3 + [grad_spec]
        out_specs += [spec] * 3
        shapes += [jax.ShapeDtypeStruct(weight.shape, jnp.float32)] * 3
        given += [weight, first, second, gradient]
    out_specs += [pl.BlockSpec(memory_space=pltpu.SMEM)] * 6
    shapes += [jax.ShapeDtypeStruct((1,), jnp.float32)] * 6
    return pl.pallas_call(
        functools.partial(adam_kernel, blocks, tuple(group[5] for group in groups)),
        grid=(steps,),
        out_shape=shapes,
        in_specs=in_specs,
        out_specs=out_specs,
        compiler_params=pltpu.CompilerParams(
            dimension_semantics=("arbitrary",), vmem_limit_bytes=VMEM_ASK
        ),
    )(*given)


class Network:
    def __init__(self, mesh):
        self.shape = (mesh.shape["dp"], mesh.shape["fsdp"])
        self.devices = self.shape[0] * self.shape[1]
        self.kernels = self.shape[1] == 8
        self.calls = 0

    def identity(self):
        self.calls += 1
        return self.calls

    def start(self, shards, own_word, own_place, batch):
        if self.kernels:
            return run_start(shards, own_word, own_place, batch, self.shape, self.identity())
        token_ids, labels, slot_rows, lengths, sop_labels = batch

        def fill(count, value):
            return jnp.full((count,), value, jnp.int32)

        rest = fill(128 - labels.shape[0], -1)
        own_facts = [token_ids, labels, rest, slot_rows, rest, lengths, sop_labels]
        own_facts = jnp.concatenate([*own_facts, fill(3 * 128 + 124, 0)]).reshape(8, 128)
        weights = [lax.all_gather(to_half(w), AXES, axis=0, tiled=True) for w in shards]
        facts = lax.all_gather(own_facts, AXES)
        place = lax.all_gather(to_half(own_place), AXES)
        words = own_word.shape[0]
        ids = facts[:, : ROWS // 128].reshape(-1) - lax.axis_index(AXES) * words
        column = jnp.arange(words, dtype=jnp.int32)
        select = to_half(ids[:, None] == column[None, :])
        terms = product(select, to_half(own_word))
        found = lax.psum_scatter(terms, AXES, scatter_dimension=0, tiled=True)
        return weights, facts, place, found

    def head(self, lengths, sop_labels, final, head, word, decoder, facts, vec):
        decoder = decoder[None]
        given = (lengths, sop_labels, final, head, word, decoder, facts, vec)
        if self.kernels:
            return run_head(*given, self.shape, self.identity())
        return self.plain_head(*given)

    def plain_head(self, lengths, sop_labels, final, head, word, decoder, facts, vec):
        short, cls = vec[SHORT_AT:], vec[CLS_AT:FF_AT].reshape(2, D)
        pool_b = vec[POOL_B * D // 128 : CLS_AT].reshape(D)
        labels = facts[:, 2, :WIRE].reshape(1, -1)
        mlm_count = jnp.sum((labels >= 0).astype(jnp.float32))
        sop_count = self.devices + jnp.sum((facts[:, 4, 1] > 0).astype(jnp.float32))
        single = jnp.float32
        offset = lax.axis_index(AXES) * word.shape[0]
        word_half, final_half = to_half(word), to_half(final)
        rows = facts[lax.axis_index(AXES), 3, :WIRE]
        pick = (rows[:, None] == jnp.arange(ROWS, dtype=jnp.int32)[None]).astype(single)
        picked = to_half(product(to_half(pick), final_half))
        dense = times_transpose(picked, head[:E]) + short[MLM_B]
        bend = jnp.tanh(GELU_A * dense * (1.0 + GELU_B * dense * dense))
        hat, inverse = norm_forward(0.5 * dense * (1.0 + bend))
        slope = 0.5 * (1.0 + bend) + (0.5 * GELU_A) * dense * (1.0 - bend * bend) * (
            1.0 + 3.0 * GELU_B * dense * dense
        )
        rows_half = to_half(hat * short[MLM_G] + short[MLM_LB])
        all_rows = lax.all_gather(rows_half, AXES, axis=0, tiled=True)
        logits = times_transpose(word_half, all_rows) + to_half(decoder).astype(single).T
        mark = jnp.arange(word.shape[0], dtype=jnp.int32)[:, None] + offset == labels
        own_top = jnp.max(logits, 0)
        own_total = jnp.sum(jnp.exp(logits - own_top), 0)
        used = (labels[0] >= 0).astype(single)
        target = jnp.sum(jnp.sum(jnp.where(mark, logits, 0.0), 0) * used)
        top = lax.pmax(own_top, AXES)
        total = lax.psum(own_total * jnp.exp(own_top - top), AXES)
        log_sum = jnp.sum((jnp.log(total) + top) * used)
        weight = used / mlm_count
        half = to_half((jnp.exp(logits - top) / total - mark.astype(single)) * weight)
        back_rows = lax.psum_scatter(
            transpose_times(half, word_half), AXES, scatter_dimension=0, tiled=True
        )
        dense_half = to_half(norm_backward(back_rows, short[MLM_G], hat, inverse) * slope)
        back_final = lax.dot_general(
            pick, product(dense_half, head[:E]), (((0,), (0,)), ((), ())), precision=PRECISE
        )
        firsts = jnp.stack([final_half[0], final_half[BUCKET]])
        pooled = jnp.tanh(times_transpose(firsts, head[E : E + D]) + pool_b)
        classes = jnp.sum(pooled[:, None] * cls[None], -1)
        powers = jnp.exp(classes - jnp.max(classes, -1, keepdims=True))
        totals = jnp.sum(powers, -1, keepdims=True)
        onehot = jnp.stack([1 - sop_labels, sop_labels], 1).astype(single)
        present = jnp.stack([jnp.float32(1.0), (lengths[1] > 0).astype(single)])
        losses = jnp.log(totals[:, 0]) + jnp.max(classes, -1) - jnp.sum(classes * onehot, -1)
        back_classes = (powers / totals - onehot) * (present / sop_count)[:, None]
        back_pooled = jnp.sum(back_classes[:, :, None] * cls[None], 1)
        pre_half = to_half(back_pooled * (1.0 - pooled * pooled))
        back_firsts = product(pre_half, head[E : E + D])
        back_final = back_final.at[0].add(back_firsts[0]).at[BUCKET].add(back_firsts[1])
        back_cls = jnp.sum(back_classes[:, :, None] * pooled[:, None], 0)
        small_sums = [column_sum(dense_half), jnp.sum(back_rows * hat, 0), jnp.sum(back_rows, 0)]
        back_head = [transpose_times(dense_half, picked), transpose_times(pre_half, firsts)]
        ends = jnp.stack([log_sum, target, jnp.sum(losses * present), mlm_count, sop_count])
        return (
            back_final,
            product(half, all_rows),
            column_sum(half.T)[None],
            to_half(jnp.pad(jnp.concatenate(back_head, 0), ((0, E), (0, 0)))),
            jnp.concatenate([column_sum(pre_half)[None], back_cls], 0),
            jnp.stack(small_sums),
            jnp.pad(ends, (0, 123))[None],
        )

    def adam(self, ends, groups):
        if self.kernels:
            updates = run_adam(ends, groups, 4)
            scalars = [x.reshape(()) for x in updates[-6:]]
            return [updates[i : i + 3] for i in range(0, 3 * len(groups), 3)], scalars
        updates = []
        for weight, first, second, gradient, low, rate in groups:
            rows = weight.shape[0]
            if low is not None:
                gradient = gradient[low : low + rows]
            gradient = gradient.reshape(-1, weight.shape[1])[:rows]
            updates.append(adam_update(weight, ends[1, 0] * gradient, first, second, rate))
        return updates, [ends[i, 0] for i in range(6)]

    def finish(
        self,
        left_wide,
        left_tall,
        rights,
        outer,
        head_grad,
        own_rows,
        vector,
        facts,
        base_word,
        back_decoder,
        totals,
        places_count,
    ):
        devices = self.devices
        if self.kernels:
            out, heights, word_grad, place_grad, last, ends = run_finish(
                left_wide,
                left_tall,
                rights,
                outer,
                head_grad,
                own_rows,
                vector,
                facts,
                base_word,
                back_decoder,
                totals,
                places_count,
                self.shape,
                self.identity(),
            )
            return out, heights, word_grad, place_grad, last, ends
        back_wide = jnp.concatenate(
            [
                product(left_wide[: 3 * D], rights[0]),
                product(left_wide[3 * D : 4 * D], rights[1]),
                product(left_wide[4 * D :], rights[2]),
            ],
            0,
        )
        sums = [
            lax.psum_scatter(p.astype(jnp.float32), AXES, scatter_dimension=0, tiled=True)
            for p in (back_wide, product(left_tall, outer), head_grad)
        ]
        all_rows = lax.all_gather(own_rows, AXES, axis=0, tiled=True)
        own, words = lax.axis_index(AXES), base_word.shape[0]
        ids = facts[:, : ROWS // 128].reshape(-1) - own * words
        select = to_half(ids[:, None] == jnp.arange(words, dtype=jnp.int32)[None, :])
        word_grad = base_word + transpose_times(select, all_rows)
        by_device = all_rows.reshape(devices, ROWS, E).astype(jnp.float32)
        two = (facts[:, 4, 1] > 0)[:, None, None]
        lower, upper = by_device[:, :BUCKET], by_device[:, BUCKET:]
        lower = jnp.sum(lower + jnp.where(two, upper, 0.0), 0)
        upper = jnp.sum(jnp.where(two, 0.0, upper), 0)
        every = jnp.concatenate([lower, upper], 0)
        every = jnp.pad(every, ((0, places_count * devices - ROWS), (0, 0)))
        place_grad = lax.dynamic_slice(every, (own * places_count, 0), (places_count, E))
        squares = sum(jnp.sum(g * g) for g in (*sums, word_grad, place_grad, back_decoder))
        reduced, tails, squares = lax.psum((vector, totals, squares), AXES)
        norm = jnp.sqrt(squares + jnp.sum(reduced * reduced))
        factor = jnp.minimum(1.0, CLIP_NORM / (norm + NORM_EPSILON))
        ends = [norm, factor, totals[0, 0] - tails[0, 1], tails[0, 2]]
        ends = jnp.stack([*ends, totals[0, 3], totals[0, 4]])
        ends = jnp.broadcast_to(ends[:, None], (6, 128))
        heights = tuple(total.shape[0] for total in sums)
        return jnp.concatenate(sums, 0), heights, word_grad, place_grad, reduced, ends


CLS_AT, FF_AT, SHORT_AT = 10 * D // 128, 12 * D // 128, (12 * D + FF) // 128


def lanes_of(vec, first, count):
    return jnp.concatenate([vec[pl.ds(first + i, 1), :] for i in range(count)], 1)


def wide_row(vec, index):
    return lanes_of(vec, index * (D // 128), D // 128)


def short_row(vec, index):
    return vec[pl.ds(SHORT_AT + index, 1), :]


def nt(a, b):
    return lax.dot_general(a, b, (((1,), (1,)), ((), ())), preferred_element_type=jnp.float32)


def nn(a, b):
    return jnp.dot(a, b, preferred_element_type=jnp.float32)


def tn(a, b):
    return lax.dot_general(a, b, (((0,), (0,)), ((), ())), preferred_element_type=jnp.float32)


FORWARD_CHUNK, BACKWARD_CHUNK = 1024, 256
PAIR = 2 * HEAD_DIM
PROJ_B, Q_B, V_B, O_B, LN1_G, LN1_B, FFO_B, LN2_G, LN2_B, POOL_B = range(10)


def allowed_block(lengths):
    shape = (ROWS, ROWS)
    key = lax.broadcasted_iota(jnp.int32, shape, 0)
    query = lax.broadcasted_iota(jnp.int32, shape, 1)
    two = lengths[1] > 0
    key_second = jnp.logical_and(key >= BUCKET, two).astype(jnp.int32)
    query_second = jnp.logical_and(query >= BUCKET, two).astype(jnp.int32)
    length = jnp.where(key_second == 1, lengths[1], lengths[0])
    live = key - BUCKET * key_second < length
    return jnp.logical_and(query_second == key_second, live)


def halves_down(x):
    row = lax.broadcasted_iota(jnp.int32, x.shape, 0)
    zero = jnp.zeros_like(x)
    return jnp.where(row < HEAD_DIM, x, zero), jnp.where(row < HEAD_DIM, zero, x)


def halves(x):
    lane = lax.broadcasted_iota(jnp.int32, x.shape, 1)
    zero = jnp.zeros_like(x)
    return jnp.where(lane < HEAD_DIM, x, zero), jnp.where(lane < HEAD_DIM, zero, x)


def kinds(lengths):
    row = lax.broadcasted_iota(jnp.int32, (ROWS, 1), 0)
    second = jnp.logical_and(row >= BUCKET, lengths[1] > 0).astype(jnp.int32)
    length = jnp.where(second == 1, lengths[1], lengths[0])
    return (row - BUCKET * second >= length // 2).astype(jnp.float32)


EMB_G, EMB_B, MLM_B, MLM_G, MLM_LB, TYPE_ZERO, TYPE_ONE = range(7)


def forward_kernel(
    lengths,
    found,
    place,
    lift,
    wide,
    tall,
    vec,
    final,
    embed_hat,
    embed_inverse,
    normed_half,
    rights,
    projected,
    weighting,
    hat_one,
    inverse_one,
    slope,
    active,
    hat_two,
    inverse_two,
    hidden,
):
    layer = pl.program_id(0)

    def row(index):
        return wide_row(vec, index)

    @pl.when(layer == 0)
    def _():
        two = (lengths[1] > 0).astype(jnp.float32)
        kind = kinds(lengths)
        upper = place[pl.ds(0, BUCKET), :].astype(jnp.float32)
        lower = jnp.where(two > 0, upper, place[pl.ds(BUCKET, BUCKET), :].astype(jnp.float32))
        embedded = found[...] + jnp.concatenate([upper, lower], 0)
        zero, one = short_row(vec, TYPE_ZERO), short_row(vec, TYPE_ONE)
        hat, inverse = norm_forward(embedded + jnp.where(kind > 0, one, zero))
        embed_hat[...] = hat
        embed_inverse[...] = inverse
        normed = to_half(hat * short_row(vec, EMB_G) + short_row(vec, EMB_B))
        normed_half[...] = normed
        hidden[...] = nn(normed, lift[...]) + row(PROJ_B)

    half = to_half(hidden[...])
    rights[0] = half
    for part, bias in ((0, Q_B), (1, None), (2, V_B)):
        for low in range(0, D, 256):
            here = part * D + low
            value = nt(half, wide[pl.ds(here, 256), :])
            if bias is not None:
                value = value + lanes_of(vec, (bias * D + low) // 128, 2)
            projected[:, pl.ds(here, 256)] = to_half(value)
    allowed = allowed_block(lengths)
    def scores_of(head):
        lanes = head // 2 * PAIR
        queries = halves(projected[:, pl.ds(lanes, PAIR)])[head % 2]
        return nt(projected[:, pl.ds(D + lanes, PAIR)], queries)

    def mix(head, weights):
        lanes = head // 2 * PAIR
        values = halves_down(projected[:, pl.ds(2 * D + lanes, PAIR)].T)[head % 2]
        part = nn(values, weights)
        if head % 2:
            rights[1, :, pl.ds(lanes, PAIR)] = to_half(mixes.pop() + part).T
        else:
            mixes.append(part)

    mixes, waiting, coming = [], None, scores_of(0)
    for head in range(HEADS):
        products = coming
        if head + 1 < HEADS:
            coming = scores_of(head + 1)
        scores = jnp.where(allowed, products * SCALE, MASKED)
        powers = jnp.exp(scores - jnp.max(scores, 0, keepdims=True))
        weights = powers * (1.0 / jnp.sum(powers, 0, keepdims=True))
        weighting[head] = weights
        if waiting is not None:
            mix(head - 1, waiting)
        waiting = to_half(weights)
    mix(HEADS - 1, waiting)
    first_sum = hidden[...] + nt(rights[1], wide[pl.ds(3 * D, D), :]) + row(O_B)
    hat, inverse = norm_forward(first_sum)
    hat_one[...] = hat
    inverse_one[...] = inverse
    middle = hat * row(LN1_G) + row(LN1_B)
    half = to_half(middle)
    rights[2] = half
    total = middle + row(FFO_B)

    def inner_of(low):
        return nt(half, wide[pl.ds(4 * D + low, FORWARD_CHUNK), :])

    coming = inner_of(0)
    for low in range(0, FF, FORWARD_CHUNK):
        inner = coming + lanes_of(vec, FF_AT + low // 128, FORWARD_CHUNK // 128)
        if low + FORWARD_CHUNK < FF:
            coming = inner_of(low + FORWARD_CHUNK)
        square = inner * inner
        bend = jnp.tanh(GELU_A * inner * (1.0 + GELU_B * square))
        act = to_half(0.5 * inner * (1.0 + bend))
        slope[:, pl.ds(low, FORWARD_CHUNK)] = 0.5 * (1.0 + bend) + (0.5 * GELU_A) * inner * (
            1.0 - bend * bend
        ) * (1.0 + 3.0 * GELU_B * square)
        active[pl.ds(low, FORWARD_CHUNK), :] = act.T
        total = total + nn(act, tall[pl.ds(low, FORWARD_CHUNK), :])
    hat, inverse = norm_forward(total)
    hat_two[...] = hat
    inverse_two[...] = inverse
    output = hat * row(LN2_G) + row(LN2_B)
    hidden[...] = output
    final[...] = output


def whole_spec():
    return pl.BlockSpec(memory_space=VMEM_SPACE, pipeline_mode=pl.Buffered(1))


def lift_spec():
    return pl.BlockSpec((E, D), lambda i: ((E + D) // E, 0), pipeline_mode=pl.Buffered(1))


def by_layer(*shape, order=lambda i: i):
    return pl.BlockSpec(
        (None, *shape), lambda i: (order(i),) + (0,) * len(shape), memory_space=VMEM_SPACE
    )


def run_forward(lengths, found, place, head, wide, tall, vec):
    def kept(*shape, dtype=jnp.bfloat16):
        return jax.ShapeDtypeStruct((LAYERS, *shape), dtype)

    single = jnp.float32
    names = (
        "final",
        "embed_hat",
        "embed_inverse",
        "normed_half",
        "rights",
        "projected",
        "weighting",
        "hat_one",
        "inverse_one",
        "slope",
        "active",
        "hat_two",
        "inverse_two",
    )
    outs = pl.pallas_call(
        forward_kernel,
        grid=(LAYERS,),
        out_shape=[
            jax.ShapeDtypeStruct((ROWS, D), single),
            jax.ShapeDtypeStruct((ROWS, E), single),
            jax.ShapeDtypeStruct((ROWS, 1), single),
            jax.ShapeDtypeStruct((ROWS, E), jnp.bfloat16),
            jax.ShapeDtypeStruct((3, LAYERS, ROWS, D), jnp.bfloat16),
            kept(ROWS, 3 * D),
            kept(HEADS, ROWS, ROWS, dtype=single),
            kept(ROWS, D, dtype=single),
            kept(ROWS, 1, dtype=single),
            kept(ROWS, FF, dtype=single),
            jax.ShapeDtypeStruct((FF, LAYERS * ROWS), jnp.bfloat16),
            kept(ROWS, D, dtype=single),
            kept(ROWS, 1, dtype=single),
        ],
        in_specs=[pl.BlockSpec(memory_space=pltpu.SMEM)]
        + [whole_spec()] * 2
        + [lift_spec()]
        + [whole_spec()] * 3,
        out_specs=[
            pl.BlockSpec((ROWS, D), lambda i: (0, 0)),
            pl.BlockSpec((ROWS, E), lambda i: (0, 0)),
            pl.BlockSpec((ROWS, 1), lambda i: (0, 0)),
            pl.BlockSpec((ROWS, E), lambda i: (0, 0)),
            pl.BlockSpec((3, None, ROWS, D), lambda i: (0, i, 0, 0)),
            by_layer(ROWS, 3 * D),
            by_layer(HEADS, ROWS, ROWS),
            by_layer(ROWS, D),
            by_layer(ROWS, 1),
            by_layer(ROWS, FF),
            pl.BlockSpec((FF, ROWS), lambda i: (0, i)),
            by_layer(ROWS, D),
            by_layer(ROWS, 1),
        ],
        scratch_shapes=[VMEM_SPACE((ROWS, D), single)],
        compiler_params=pltpu.CompilerParams(
            dimension_semantics=("arbitrary",), vmem_limit_bytes=VMEM_ASK
        ),
    )(lengths, found, place, head, wide, tall, vec)
    return dict(zip(names, outs))


def backward_kernel(
    lengths,
    start,
    wide_sums,
    small_sums,
    embed_hat,
    embed_inverse,
    normed_half,
    lift,
    head_in,
    wide,
    tall,
    vec,
    projected,
    weighting,
    hat_one,
    inverse_one,
    slope,
    hat_two,
    inverse_two,
    rows_out,
    back_lift,
    turned,
    outer,
    vector,
    sums,
    ff_sum,
    upstream,
    back_mixed,
    joint,
):
    step = pl.program_id(0)

    @pl.when(step == 0)
    def _():
        upstream[...] = start[...]
        sums[...] = jnp.zeros_like(sums)
        ff_sum[...] = jnp.zeros_like(ff_sum)

    def row(index):
        return wide_row(vec, index)

    def add_sum(index, value):
        here = pl.ds(index - Q_B, 1)
        sums[here, :] = sums[here, :] + jnp.sum(value, 0, keepdims=True)

    up = upstream[...]
    hat = hat_two[...]
    add_sum(LN2_G, up * hat)
    add_sum(LN2_B, up)
    back_second = norm_backward(up, row(LN2_G), hat, inverse_two[...])
    half = to_half(back_second)
    outer[...] = half
    add_sum(FFO_B, half.astype(jnp.float32))
    total = back_second

    def back_active(low):
        return nt(half, tall[pl.ds(low, BACKWARD_CHUNK), :])

    coming = back_active(0)
    for low in range(0, FF, BACKWARD_CHUNK):
        lanes = pl.ds(low, BACKWARD_CHUNK)
        product = coming
        if low + BACKWARD_CHUNK < FF:
            coming = back_active(low + BACKWARD_CHUNK)
        inner = to_half(product * slope[:, lanes])
        ff_sum[:, lanes] = ff_sum[:, lanes] + jnp.sum(
            inner.astype(jnp.float32), 0, keepdims=True
        )
        turned[pl.ds(4 * D + low, BACKWARD_CHUNK), :] = inner.T
        total = total + nn(inner, wide[pl.ds(4 * D + low, BACKWARD_CHUNK), :])
    hat = hat_one[...]
    add_sum(LN1_G, total * hat)
    add_sum(LN1_B, total)
    back_first = norm_backward(total, row(LN1_G), hat, inverse_one[...])
    upstream[...] = back_first
    half = to_half(back_first)
    add_sum(O_B, half.astype(jnp.float32))
    turned[pl.ds(3 * D, D), :] = half.T
    back_mixed[...] = to_half(nn(half, wide[pl.ds(3 * D, D), :]))

    def soft_of(head):
        lanes = head // 2 * PAIR
        grads = halves(back_mixed[:, pl.ds(lanes, PAIR)])[head % 2]
        return nt(projected[:, pl.ds(2 * D + lanes, PAIR)], grads)

    def spread(head, scores, weights):
        lanes, side = head // 2 * PAIR, head % 2
        queries = halves(projected[:, pl.ds(lanes, PAIR)])[side]
        keys = halves_down(projected[:, pl.ds(D + lanes, PAIR)].T)[side]
        grads = halves(back_mixed[:, pl.ds(lanes, PAIR)])[side]
        parts = nn(keys, scores), nn(scores, queries), nn(weights, grads)
        if side == 0:
            sides.extend(parts)
            return
        value_half = to_half(sides.pop() + parts[2])
        key_half = to_half((sides.pop() + parts[1]) * SCALE)
        query_half = to_half((sides.pop() + parts[0]) * SCALE)
        joint[:, pl.ds(lanes, PAIR)] = query_half.T
        joint[:, pl.ds(D + lanes, PAIR)] = key_half
        joint[:, pl.ds(2 * D + lanes, PAIR)] = value_half
        turned[pl.ds(lanes, PAIR), :] = query_half
        turned[pl.ds(D + lanes, PAIR), :] = key_half.T
        turned[pl.ds(2 * D + lanes, PAIR), :] = value_half.T

    sides, waiting, coming = [], None, soft_of(0)
    for head in range(HEADS):
        soft = coming
        if head + 1 < HEADS:
            coming = soft_of(head + 1)
        weights = weighting[head]
        scores = to_half(weights * (soft - jnp.sum(weights * soft, 0, keepdims=True)))
        if waiting is not None:
            spread(head - 1, *waiting)
        waiting = (scores, to_half(weights))
    spread(HEADS - 1, *waiting)
    total = upstream[...]
    for part, bias in ((0, Q_B), (1, None), (2, V_B)):
        here = pl.ds(part * D, D)
        value = joint[:, here]
        if bias is not None:
            add_sum(bias, value.astype(jnp.float32))
        total = total + nn(value, wide[here, :])
    upstream[...] = total

    @pl.when(step == LAYERS - 1)
    def _():
        half = to_half(upstream[...])
        back_lift[...] = to_half(tn(normed_half[...], half))
        back_normed = nt(half, lift[...])
        hat = embed_hat[...]
        back = norm_backward(back_normed, short_row(vec, EMB_G), hat, embed_inverse[...])
        rows_out[...] = to_half(back)
        kind = kinds(lengths)
        ones = jnp.sum(back * kind, 0, keepdims=True)
        zeros = jnp.sum(back * (1.0 - kind), 0, keepdims=True)
        vector[...] = jnp.zeros_like(vector)
        parts = [jnp.sum(half.astype(jnp.float32), 0, keepdims=True)]
        parts += [sums[pl.ds(i, 1), :] for i in range(8)]
        parts += [wide_sums[pl.ds(i, 1), :] for i in range(3)]
        parts += [ff_sum[...]]
        parts += [
            jnp.sum(back_normed * hat, 0, keepdims=True),
            jnp.sum(back_normed, 0, keepdims=True),
        ]
        parts += [small_sums[pl.ds(i, 1), :] for i in range(3)]
        parts += [zeros, ones]
        at = 0
        for part in parts:
            for low in range(0, part.shape[1], 128):
                vector[pl.ds(at, 1), :] = part[:, low : low + 128]
                at += 1


def run_backward(lengths, start, wide_sums, small_sums, head, back_head, wide, tall, vec, kept, lines):
    single, half = jnp.float32, jnp.bfloat16
    last = LAYERS - 1

    def order(i):
        return last - i

    return pl.pallas_call(
        backward_kernel,
        grid=(LAYERS,),
        out_shape=[
            jax.ShapeDtypeStruct((ROWS, E), half),
            jax.ShapeDtypeStruct(back_head.shape, half),
            jax.ShapeDtypeStruct((4 * D + FF, LAYERS * ROWS), half),
            jax.ShapeDtypeStruct((LAYERS, ROWS, D), half),
            jax.ShapeDtypeStruct((lines, 128), single),
        ],
        in_specs=[pl.BlockSpec(memory_space=pltpu.SMEM)]
        + [whole_spec()] * 6
        + [lift_spec(), pl.BlockSpec(memory_space=pl.ANY)]
        + [whole_spec()] * 3
        + [
            by_layer(ROWS, 3 * D, order=order),
            by_layer(HEADS, ROWS, ROWS, order=order),
            by_layer(ROWS, D, order=order),
            by_layer(ROWS, 1, order=order),
            by_layer(ROWS, FF, order=order),
            by_layer(ROWS, D, order=order),
            by_layer(ROWS, 1, order=order),
        ],
        out_specs=[
            pl.BlockSpec((ROWS, E), lambda i: (0, 0)),
            pl.BlockSpec((E, D), lambda i: ((E + D) // E, 0)),
            pl.BlockSpec((4 * D + FF, ROWS), lambda i: (0, order(i))),
            by_layer(ROWS, D, order=order),
            pl.BlockSpec((lines, 128), lambda i: (0, 0)),
        ],
        input_output_aliases={8: 1},
        scratch_shapes=[
            VMEM_SPACE((8, D), single),
            VMEM_SPACE((1, FF), single),
            VMEM_SPACE((ROWS, D), single),
            VMEM_SPACE((ROWS, D), half),
            VMEM_SPACE((ROWS, 3 * D), half),
        ],
        compiler_params=pltpu.CompilerParams(
            dimension_semantics=("arbitrary",), vmem_limit_bytes=VMEM_ASK
        ),
    )(
        lengths,
        start,
        wide_sums,
        small_sums,
        kept["embed_hat"],
        kept["embed_inverse"],
        kept["normed_half"],
        head,
        back_head,
        wide,
        tall,
        vec,
        kept["projected"],
        kept["weighting"],
        kept["hat_one"],
        kept["inverse_one"],
        kept["slope"],
        kept["hat_two"],
        kept["inverse_two"],
    )


def local(
    mesh,
    word_table,
    position_table,
    head_weights,
    decoder_bias,
    layer_wide,
    layer_tall,
    vectors,
    word_first,
    word_second,
    position_first,
    position_second,
    head_first,
    head_second,
    decoder_first,
    decoder_second,
    wide_first,
    wide_second,
    tall_first,
    tall_second,
    vector_first,
    vector_second,
    token_ids,
    seq_lengths,
    mlm_rows,
    mlm_labels,
    sop_labels,
):
    network = Network(mesh)

    (wide, tall, head), all_facts, place, found = network.start(
        (layer_wide.T, layer_tall, head_weights.T),
        word_table,
        position_table,
        (token_ids, mlm_labels, mlm_rows, seq_lengths, sop_labels),
    )
    devices = all_facts.shape[0]
    place = place.reshape(-1, E)
    vec = vectors.reshape(-1, 128)
    kept = run_forward(seq_lengths, found, place, head, wide, tall, vec)
    (back_final, back_word_head, back_decoder, back_head, wide_sums, small_sums, totals) = (
        network.head(
            seq_lengths,
            sop_labels,
            kept["final"],
            head,
            word_table,
            decoder_bias,
            all_facts,
            vec,
        )
    )
    total = vectors.shape[0]
    share = -(-total // (devices * 1024)) * 1024
    back_rows, back_head, turned, outer, vector_grad = run_backward(
        seq_lengths,
        back_final,
        wide_sums,
        small_sums,
        head,
        back_head,
        wide,
        tall,
        vec,
        kept,
        devices * share // 128,
    )
    sums, heights, back_word, back_place, last, ends = network.finish(
        turned,
        kept["active"],
        kept["rights"].reshape(3, -1, D),
        outer.reshape(-1, D),
        back_head,
        back_rows,
        vector_grad.reshape(devices, -1, 128),
        all_facts,
        back_word_head,
        back_decoder,
        totals,
        position_table.shape[0],
    )
    wide_at, tall_at, head_at = 0, heights[0], heights[0] + heights[1]

    def turned_group(weight, first, second, low):
        return (weight.T, first.T, second.T, sums, low, LEARN_RATE)

    def flat(x):
        return x[None]

    def lines(x):
        return x.reshape(-1, 128)

    groups = (
        (word_table, word_first, word_second, back_word, 0, LEARN_RATE),
        turned_group(layer_wide, wide_first, wide_second, wide_at),
        (layer_tall, tall_first, tall_second, sums, tall_at, LEARN_RATE),
        turned_group(head_weights, head_first, head_second, head_at),
        (position_table, position_first, position_second, back_place, None, LEARN_RATE),
        (flat(decoder_bias), flat(decoder_first), flat(decoder_second), back_decoder, None)
        + (LEARN_RATE,),
        (lines(vectors), lines(vector_first), lines(vector_second), last, None, SMALL_RATE),
    )
    arrays, scalars = network.adam(ends, groups)
    word, wide, tall, head, position, decoder, vector = arrays
    grad_norm, unused, mlm_sum, sop_total, mlm_count, sop_count = scalars

    def turn(arrays):
        return [x.T for x in arrays]

    def plain(arrays):
        return [x.reshape(-1) for x in arrays]

    updates = (*word, *position, *turn(head), *plain(decoder), *turn(wide), *tall, *plain(vector))
    return (*updates, mlm_sum, mlm_count, sop_total, sop_count, grad_norm)


def solution(mesh):
    rows = P(AXES, None)
    columns = P(None, AXES)
    flat = P(AXES)
    whole = P()
    return jax.shard_map(
        functools.partial(local, mesh),
        mesh=mesh,
        in_specs=(rows, rows, columns, flat, columns, rows, whole)
        + (rows, rows) * 2
        + (columns, columns, flat, flat, columns, columns, rows, rows, whole, whole)
        + (flat,) * 5,
        out_specs=(rows,) * 6
        + (columns,) * 3
        + (flat,) * 3
        + (columns,) * 3
        + (rows,) * 3
        + (whole,) * 8,
        check_vma=False,
    )
```

```python
import functools

import jax
import jax.numpy as jnp
from jax import lax
from jax.experimental import pallas as pl
from jax.experimental.pallas import tpu as pltpu
from jax.sharding import PartitionSpec as P

D = 768
HEADS = 12
HEAD_DIM = 64
FF = 3072
E = 128
LAYERS = 4
STEP = 10
BUCKET = 128
ROWS = 2 * BUCKET

PRECISE = lax.Precision.HIGHEST
EPSILON = 1e-06
LEARN_RATE = 0.1
SMALL_RATE = 0.5
BETA_ONE = 0.9
BETA_TWO = 0.999
ADAM_EPSILON = 1e-08
WEIGHT_DECAY = 0.01
CLIP_NORM = 0.005
NORM_EPSILON = 1e-06
MASKED = -1e30
SCALE = HEAD_DIM ** (-0.5)
AXES = ("dp", "fsdp")


def to_half(x):
    return x.astype(jnp.bfloat16)


def product(a, b):
    return jnp.dot(a, b, preferred_element_type=jnp.float32)


def times_transpose(a, b):
    return lax.dot_general(a, b, (((1,), (1,)), ((), ())), preferred_element_type=jnp.float32)


def transpose_times(a, b):
    return lax.dot_general(a, b, (((0,), (0,)), ((), ())), preferred_element_type=jnp.float32)


def column_sum(x):
    return jnp.sum(x.astype(jnp.float32), 0)


def norm_forward(x):
    centre = x - jnp.mean(x, -1, keepdims=True)
    inverse = lax.rsqrt(jnp.mean(centre * centre, -1, keepdims=True) + EPSILON)
    return centre * inverse, inverse


def norm_backward(upstream, factor, hat, inverse):
    scaled = upstream * factor
    return inverse * (
        scaled
        - jnp.mean(scaled, -1, keepdims=True)
        - hat * jnp.mean(scaled * hat, -1, keepdims=True)
    )


GELU_A = 0.7978845608028654
GELU_B = 0.044715


MESH_ID = pl.DeviceIdType.MESH
VMEM_SPACE = pltpu.VMEM
VMEM_ASK = 60 * 1024 * 1024


def greet(peers):
    barrier = pltpu.get_barrier_semaphore()
    count = 0
    for present, who in peers:
        if present is None:
            pl.semaphore_signal(barrier, inc=1, device_id=who, device_id_type=MESH_ID)
            count = count + 1
        else:

            @pl.when(present)
            def _(who=who):
                pl.semaphore_signal(barrier, inc=1, device_id=who, device_id_type=MESH_ID)

            count = count + present.astype(jnp.int32)
    pl.semaphore_wait(barrier, count)


def maybe(condition, action):
    if condition is None:
        action()
    else:
        pl.when(condition)(action)


def remote(source, target, send, receive, who):
    return pltpu.make_async_remote_copy(
        src_ref=source,
        dst_ref=target,
        send_sem=send,
        recv_sem=receive,
        device_id=who,
        device_id_type=MESH_ID,
    )


OWN, ACROSS_X, ACROSS_Y, DIAGONAL = 0, 1, 2, 3


def cuts_of(rows, share):
    tail = max(32, round(rows * share / 32) * 32)
    head = rows - tail
    return ((0, head), (head, rows))


GATHER_TAIL, FINISH_TAIL = 0.3, 0.2


def half_of(span, which):
    low, high = span
    middle = (low + high) // 2
    return (low, middle) if which == 0 else (middle, high)


def places():
    z, f = lax.axis_index("dp"), lax.axis_index("fsdp")
    q, c = f // 2, lax.rem(f, 2)
    qx = q + 1 - 2 * lax.rem(q, 2)
    qy = lax.rem(q + 2, 4)
    qd = qx + qy - q
    return z, c, (q, qx, qy, qd)


def gather_stages(planes, rows, members, x, outs, buf, sems, where, opening):
    out_sem, send, recv, side_send, side_recv = sems
    z, c, cols = where
    cuts = cuts_of(rows, GATHER_TAIL)
    at_x, at_y, mate = (z, cols[1] * 2 + c), (z, cols[2] * 2 + c), (z, cols[0] * 2 + 1 - c)
    above, below = z < planes - 1, z > 0
    up, down = (z + 1, cols[0] * 2 + c), (z - 1, cols[0] * 2 + c)
    sent = []

    def block(zs, col, core, span):
        return buf.at[zs, cols[col], core, pl.ds(span[0], span[1] - span[0])]

    def push(condition, zs, col, span, who, slot, receive, mine=False):
        def make():
            here = block(zs, col, c, span)
            source = x.at[pl.ds(span[0], span[1] - span[0])] if mine else here
            return remote(source, here, send.at[slot[0], zs, slot[1]], receive, who)

        maybe(condition, lambda: make().start())
        sent.append((condition, make))

    def await_block(zs, col, span, receive, core=None):
        here = block(zs, col, c if core is None else core, span)
        remote(here, here, send.at[0, 0, 0], receive, mate).wait_recv()

    def deliver(zs, col, core, span):
        for index, (out, (low, high)) in enumerate(zip(outs, members)):
            first, last = max(low, span[0]), min(high, span[1])
            if first < last:
                pltpu.make_async_copy(
                    buf.at[zs, cols[col], core, pl.ds(first, last - first)],
                    out.at[zs, cols[col], core, pl.ds(first - low, last - first)],
                    out_sem.at[index],
                ).start()

    def share(condition, part, zs, col, span, kind, mine=False):
        def make():
            here = block(zs, col, c, span)
            source = x.at[pl.ds(span[0], span[1] - span[0])] if mine else here
            return remote(
                source, here, side_send.at[part, zs, kind], side_recv.at[part, zs, kind], mate
            )

        def action():
            make().start()
            if not mine:
                deliver(zs, col, c, span)

        maybe(condition, action)
        sent.append((condition, make))
        shared.append((condition, part, zs, col, span, kind))

    shared = []
    whole = [cuts[0], cuts[1]]
    for part in (0, 1):
        push(above, z, OWN, whole[part], up, (part, 2), recv.at[part, z, OWN], True)
        push(below, z, OWN, whole[part], down, (part, 3), recv.at[part, z, OWN], True)
    for part in (1, 0):
        if part == 0:
            opening()
        push(None, z, OWN, whole[part], at_x, (part, 0), recv.at[part, z, ACROSS_X], True)
        push(None, z, OWN, whole[part], at_y, (part, 1), recv.at[part, z, ACROSS_Y], True)
    for part in (0, 1):
        share(None, part, z, OWN, whole[part], 0, True)
    own_copy = pltpu.make_async_copy(x, buf.at[z, cols[0], c], out_sem.at[len(members)])
    own_copy.start()

    def turn(condition, part, zs):
        span = whole[part]
        for col, which, who, slot in ((ACROSS_X, 1, at_y, 4), (ACROSS_Y, 0, at_x, 5)):
            maybe(
                condition,
                lambda col=col: await_block(zs, col, span, recv.at[part, zs, col]),
            )
            push(condition, zs, col, half_of(span, which), who, (part, slot), recv.at[part, zs, 4 + which])
            if part == 1:
                push(above, zs, col, span, up, (1, 4 + 2 * col), recv.at[1, zs, col])
                push(below, zs, col, span, down, (1, 5 + 2 * col), recv.at[1, zs, col])
            share(condition, part, zs, col, span, col)

    yield
    turn(None, 1, z)
    yield
    for which in (0, 1):
        await_block(z, DIAGONAL, half_of(whole[1], which), recv.at[1, z, 4 + which])
    push(above, z, DIAGONAL, whole[1], up, (1, 10), recv.at[1, z, DIAGONAL])
    push(below, z, DIAGONAL, whole[1], down, (1, 11), recv.at[1, z, DIAGONAL])
    share(None, 1, z, DIAGONAL, whole[1], 3)
    yield
    turn(None, 0, z)

    def settle(upto):
        while len(shared) > upto:
            condition, part, zs, col, span, kind = shared.pop(0)

            def action():
                await_block(zs, col, span, side_recv.at[part, zs, kind], 1 - c)
                deliver(zs, col, 1 - c, span)

            maybe(condition, action)

    for step in range(1, planes):
        yield
        ways = ((z - step >= 0, z - step, above, up), (z + step < planes, z + step, below, down))
        for valid, zs, further, onward in ways:
            go = jnp.logical_and(valid, further)
            pl.when(valid)(
                lambda zs=zs: await_block(zs, OWN, whole[0], recv.at[0, zs, OWN])
            )
            push(go, zs, OWN, whole[0], onward, (0, 2), recv.at[0, zs, OWN])
            push(valid, zs, OWN, whole[0], at_x, (0, 0), recv.at[0, zs, ACROSS_X])
            push(valid, zs, OWN, whole[0], at_y, (0, 1), recv.at[0, zs, ACROSS_Y])
            share(valid, 0, zs, OWN, whole[0], 0)
        yield
        for valid, zs, further, onward in ways:
            go = jnp.logical_and(valid, further)
            for col in (OWN, ACROSS_X, ACROSS_Y, DIAGONAL):
                pl.when(valid)(
                    lambda zs=zs, col=col: await_block(zs, col, whole[1], recv.at[1, zs, col])
                )
                push(go, zs, col, whole[1], onward, (1, col), recv.at[1, zs, col])
                share(valid, 1, zs, col, whole[1], col)
        yield
        for valid, zs, further, onward in ways:
            turn(valid, 0, zs)
        settle(8)
    yield
    own_copy.wait()
    deliver(z, OWN, c, (0, rows))
    everywhere = [(None, z)] + [
        (valid, zs)
        for step in range(1, planes)
        for valid, zs in ((z - step >= 0, z - step), (z + step < planes, z + step))
    ]
    for condition, zs in everywhere:
        for which in (0, 1):
            span = half_of(whole[0], which)
            maybe(
                condition,
                lambda zs=zs, which=which, span=span: await_block(
                    zs, DIAGONAL, span, recv.at[0, zs, 4 + which]
                ),
            )
            share(condition, 0, zs, DIAGONAL, span, 3 + which)
    settle(0)
    for condition, make in sent:
        maybe(condition, lambda make=make: make().wait_send())
    for index, (out, (low, high)) in enumerate(zip(outs, members)):
        pltpu.make_async_copy(
            buf.at[:, :, :, pl.ds(low, high - low)], out, out_sem.at[index]
        ).wait()


def select_stages(planes, facts, own_word, found, refs, where, offset):
    part, side, plane_in, middle, line_in, turned, sems_send, sems_recv = refs
    z, c, cols = where
    q = cols[0]
    f = q * 2 + c
    mate = (z, q * 2 + 1 - c)
    words = own_word.shape[0]
    line = [(lax.rem(z + d, planes), f) for d in range(1, planes)]
    turned[...] = to_half(own_word[...].T)
    yield

    def mate_message(col):
        return remote(
            part.at[:, col, 1 - c], side.at[:, col], sems_send.at[0, col], sems_recv.at[0, col], mate
        )

    def plane_message(col):
        return remote(
            part.at[:, col, c],
            plane_in.at[col],
            sems_send.at[1, col],
            sems_recv.at[1, col],
            (z, cols[col] * 2 + c),
        )

    def line_message(d, who):
        return remote(
            middle.at[who[0]], line_in.at[d], sems_send.at[2, d], sems_recv.at[2, d], who
        )

    def merge(col):
        mate_message(col).wait_recv()
        for zt in range(planes):
            part[zt, col, c] = part[zt, col, c] + side[zt, col]
        if col != OWN:
            plane_message(col).start()

    order = (DIAGONAL, ACROSS_X, ACROSS_Y, OWN)
    for place, col in enumerate(order):

        def body(n, unused, col=col):
            zt, core = n // 2, lax.rem(n, 2)
            ids = facts[zt, cols[col] * 2 + core]
            row = lax.broadcasted_iota(jnp.int32, (words, BUCKET), 0) + offset
            picks = jnp.concatenate(
                [to_half((row == ids[i : i + 1, :]).astype(jnp.float32)) for i in (0, 1)], 1
            )
            part[zt, col, core] = to_half(nn(turned[...], picks))
            return unused

        lax.fori_loop(0, 2 * planes, body, 0)
        mate_message(col).start()
        if place > 0:
            merge(order[place - 1])
        yield
    merge(OWN)
    total = part[:, OWN, c]
    yield
    for col in order[:3]:
        plane_message(col).wait_recv()
        total = total + plane_in[col]
    middle[...] = total
    for d, who in enumerate(line):
        line_message(d, who).start()
    yield
    total = middle[z]
    for d, who in enumerate(line):
        line_message(d, who).wait_recv()
        total = total + line_in[d]
    found[...] = total.astype(jnp.float32).T
    for col in order:
        mate_message(col).wait_send()
    for col in order[:3]:
        plane_message(col).wait_send()
    for d, who in enumerate(line):
        line_message(d, who).wait_send()


PLAN = (1, 2, 1, 1, 0, 1, 0, 0, 0, 0, 1)


def start_kernel(
    planes,
    rows,
    members,
    own_wide,
    own_tall,
    own_head,
    own_word,
    own_place,
    ids,
    labels,
    slot_rows,
    lengths,
    sop_labels,
    *refs,
):
    width = 8
    count = len(members)
    outs, (facts, place, found) = refs[:count], refs[count : count + 3]
    x, buf = refs[count + 3 : count + 5]
    gather_sems = refs[count + 5 : count + 10]
    select_refs = refs[count + 10 : count + 18]
    line_send, line_recv, plane_send, plane_recv = refs[count + 18 :]
    where = places()
    z, c, cols = where
    f = cols[0] * 2 + c
    line = [(lax.rem(z + d, planes), f) for d in range(1, planes)]
    plane = [(z, lax.rem(f + d, width)) for d in range(1, width)]
    lane = lax.broadcasted_iota(jnp.int32, (1, 128), 1)
    rest = jnp.full((1, 128 - labels.shape[1]), -1, jnp.int32)
    note = jnp.zeros((1, 128), jnp.int32)
    for at, value in enumerate((lengths[0], lengths[1], sop_labels[0], sop_labels[1])):
        note = note + jnp.where(lane == at, value, 0)
    facts[z, f] = jnp.concatenate(
        [
            ids[:, :128],
            ids[:, 128:],
            jnp.concatenate([labels[...], rest], 1),
            jnp.concatenate([slot_rows[...], rest], 1),
            note,
            jnp.zeros((3, 128), jnp.int32),
        ],
        0,
    )
    place[z, f] = to_half(own_place[...])
    greet([(None, who) for who in line + plane])
    pairs = (facts, place)

    def along(i, d, who):
        here = pairs[i].at[z, f]
        return remote(here, here, line_send.at[i, d], line_recv.at[i, d], who)

    def around(i, d, who, source):
        here = pairs[i].at[:, source]
        return remote(here, here, plane_send.at[i, d], plane_recv.at[i, d], who)

    for d, who in enumerate(line):
        for i in (0, 1):
            along(i, d, who).start()
    for (low, high), piece in zip(members, (own_wide[...], own_tall[...], own_head[...])):
        x[low:high] = to_half(piece)

    def opening():
        for d, who in enumerate(line):
            for i in (0, 1):
                source = pairs[i].at[lax.rem(z - d - 1 + planes, planes), f]
                remote(source, source, line_send.at[i, d], line_recv.at[i, d], who).wait_recv()
        for d, who in enumerate(plane):
            for i in (0, 1):
                around(i, d, who, f).start()

    gather = gather_stages(planes, rows, members, x, outs, buf, gather_sems, where, opening)
    offset = (z * width + f) * own_word.shape[0]
    select = select_stages(planes, facts, own_word, found, select_refs, where, offset)
    done = object()
    next(gather)
    next(select)
    for d in range(1, width):
        source = lax.rem(f - d + width, width)
        for i in (0, 1):
            around(i, d - 1, mate_of(where), source).wait_recv()
    for number in range(64):
        for unused in range(PLAN[number] if number < len(PLAN) else 1):
            next(select, done)
        if next(gather, done) is done:
            break
    for unused in select:
        pass
    for d, who in enumerate(line):
        for i in (0, 1):
            along(i, d, who).wait_send()
    for d, who in enumerate(plane):
        for i in (0, 1):
            around(i, d, who, f).wait_send()


def mate_of(where):
    z, c, cols = where
    return (z, cols[0] * 2 + 1 - c)


def run_start(shards, own_word, own_place, batch, mesh_shape, identity):
    planes, width = mesh_shape
    heights = tuple(shard.shape[0] for shard in shards)
    rows, columns = sum(heights), shards[1].shape[1]
    members, low = [], 0
    for height in heights:
        members.append((low, low + height))
        low += height
    half, single = jnp.bfloat16, jnp.float32
    vmem = pl.BlockSpec(memory_space=VMEM_SPACE)
    dma = pltpu.SemaphoreType.DMA
    words, features = own_word.shape
    block = (features, ROWS)
    *outs, facts, place, found = pl.pallas_call(
        functools.partial(start_kernel, planes, rows, tuple(members)),
        out_shape=[
            jax.ShapeDtypeStruct((planes, width // 2, 2, height, columns), half)
            for height in heights
        ]
        + [
            jax.ShapeDtypeStruct((planes, width, 8, 128), jnp.int32),
            jax.ShapeDtypeStruct((planes, width, *own_place.shape), half),
            jax.ShapeDtypeStruct((ROWS, features), single),
        ],
        in_specs=[vmem] * 8 + [pl.BlockSpec(memory_space=pltpu.SMEM)] * 2,
        out_specs=[pl.BlockSpec(memory_space=pl.ANY)] * len(heights) + [vmem] * 3,
        scratch_shapes=[
            VMEM_SPACE((rows, columns), half),
            VMEM_SPACE((planes, width // 2, 2, rows, columns), half),
            dma((len(heights) + 1,)),
            dma((2, planes, 12)),
            dma((2, planes, 6)),
            dma((2, planes, 5)),
            dma((2, planes, 5)),
            VMEM_SPACE((planes, 4, 2, *block), half),
            VMEM_SPACE((planes, 4, *block), half),
            VMEM_SPACE((4, planes, *block), half),
            VMEM_SPACE((planes, *block), half),
            VMEM_SPACE((planes - 1, *block), half),
            VMEM_SPACE((features, words), half),
            dma((3, 4)),
            dma((3, 4)),
            dma((2, planes)),
            dma((2, planes)),
            dma((2, width)),
            dma((2, width)),
        ],
        compiler_params=pltpu.CompilerParams(
            collective_id=identity, has_side_effects=True, vmem_limit_bytes=VMEM_ASK
        ),
    )(*shards, own_word, own_place, *[x[None] for x in batch[:3]], *batch[3:])
    weights = [out.reshape(-1, columns) for out in outs]
    devices = planes * width
    return (
        weights,
        facts.reshape(devices, 8, 128),
        place.reshape(devices, *own_place.shape),
        found,
    )


def accumulate(target, sources, height):
    step = 32

    def body(i, unused):
        rows = pl.ds(pl.multiple_of(i * step, step), step)
        total = sources[0][rows].astype(jnp.float32)
        for source in sources[1:]:
            total = total + source[rows].astype(jnp.float32)
        target[rows] = total.astype(target.dtype)
        return unused

    lax.fori_loop(0, height // step, body, 0)


ROWS_AT = 1
TURN_AT = 5
MATE_AT = 9


def far_first(i, z, planes):
    low = (2 * z < planes).astype(jnp.int32)
    falling = planes - 1 - i - (i >= planes - 1 - z).astype(jnp.int32)
    rising = i + (i >= z).astype(jnp.int32)
    last = (jnp.int32(i) == planes - 1).astype(jnp.int32)
    return last * z + (1 - last) * (low * falling + (1 - low) * rising)


def finish_kernel(
    planes,
    heights,
    split,
    left_wide,
    left_tall,
    rights_from,
    outer_from,
    head_grad,
    own_rows,
    vector_terms,
    facts,
    base_word,
    back_decoder,
    totals,
    out,
    word_grad,
    place_grad,
    last,
    ends,
    all_rows,
    both,
    side,
    half_in,
    full_in,
    line_in,
    tail_line,
    tail_half,
    tail_full,
    wide_buf,
    tall_buf,
    vector_in,
    vector_mid,
    vector_last,
    fetch,
    head_load,
    side_send,
    side_recv,
    send,
    recv,
    tail_send,
    tail_recv,
    row_send,
    row_recv,
    vec_send,
    vec_recv,
    end_send,
    end_recv,
    rights,
    outer,
    right_load,
):
    width = 8
    right_copies = [
        pltpu.make_async_copy(rights_from.at[i], rights.at[i], right_load.at[i]) for i in range(3)
    ]
    right_copies.append(pltpu.make_async_copy(outer_from, outer, right_load.at[3]))
    for copy in right_copies:
        copy.start()
    wide_height, tall_height, head_height = heights
    rows = wide_height + tall_height + head_height
    z, c, cols = places()
    q = cols[0]
    f = q * 2 + c
    x, y = lax.rem(q, 2), q // 2
    cuts = cuts_of(rows, FINISH_TAIL)
    head, tail = cuts
    head_rows, tail_rows = head[1] - head[0], tail[1] - tail[0]
    at_x, at_y, mate = (z, cols[1] * 2 + c), (z, cols[2] * 2 + c), (z, q * 2 + 1 - c)
    above, below = z < planes - 1, z > 0
    up, down = (z + 1, f), (z - 1, f)
    line = [(lax.rem(z + d, planes), f) for d in range(1, planes)]
    plane = [(z, lax.rem(f + d, width)) for d in range(1, width)]
    greet([(None, who) for who in line + plane])
    order = (DIAGONAL, ACROSS_X, ACROSS_Y, OWN)
    sent = []

    def push(condition, make):
        maybe(condition, lambda: make().start())
        sent.append((condition, make))

    def piece(ref, span):
        return ref.at[pl.ds(span[0], span[1] - span[0])]

    def plane_at(i):
        return far_first(i, z, planes)

    def turn_of(n):
        m = n - 1 - 3 * (n == 0).astype(jnp.int32) + (n > 4 * planes - 4).astype(jnp.int32)
        group, j = (m + 4) // 4 - 1, lax.rem(m + 4, 4)
        ahead = (j == 0).astype(jnp.int32)
        return group + ahead, DIAGONAL * ahead + j * (j < 3).astype(jnp.int32)

    def chip_of(n):
        i, col = turn_of(n)
        flip_x, flip_y = lax.rem(col, 2), col // 2
        return plane_at(i) * 4 + 2 * lax.rem(y + flip_y, 2) + lax.rem(x + flip_x, 2)

    def fetches(n):
        k, slot = chip_of(n), lax.rem(n, 2)
        wide_rows = pl.ds(pl.multiple_of(k * 2 * wide_height, 16), 2 * wide_height)
        tall_rows = pl.ds(pl.multiple_of(k * 2 * tall_height, 16), 2 * tall_height)
        return (
            pltpu.make_async_copy(
                left_wide.at[wide_rows], wide_buf.at[slot], fetch.at[0, slot]
            ),
            pltpu.make_async_copy(
                left_tall.at[tall_rows], tall_buf.at[slot], fetch.at[1, slot]
            ),
        )

    for copy in fetches(jnp.int32(0)):
        copy.start()

    def vector_first(d, who):
        return remote(
            vector_terms.at[:, who[1]], vector_in.at[d], vec_send.at[0, d], vec_recv.at[0, d], who
        )

    def vector_second(d, who):
        return remote(
            vector_mid.at[who[0]], vector_last.at[d], vec_send.at[1, d], vec_recv.at[1, d], who
        )

    def row_line(d, who):
        return remote(
            own_rows, all_rows.at[z, q, c], row_send.at[0, d], row_recv.at[0, d], who
        )

    def row_plane(col):
        return remote(
            all_rows.at[:, q, c],
            all_rows.at[:, q, c],
            row_send.at[1, col],
            row_recv.at[1, col],
            (z, cols[col] * 2 + c),
        )

    def row_turn(which):
        col, who = ((ACROSS_Y, at_x), (ACROSS_X, at_y))[which]
        here = all_rows.at[:, cols[col], c, pl.ds(which * BUCKET, BUCKET)]
        return remote(here, here, row_send.at[2, 1 + which], row_recv.at[2, 1 + which], who)

    def row_mate():
        return remote(
            all_rows.at[:, :, c], all_rows.at[:, :, c], row_send.at[2, 0], row_recv.at[2, 0], mate
        )

    for d, who in enumerate(line):
        push(None, functools.partial(row_line, d, who))
    for d, who in enumerate(plane):
        push(None, functools.partial(vector_first, d, who))
    all_rows[z, q, c] = own_rows[...]
    head_copies = []
    for col in order:
        copy = pltpu.make_async_copy(
            head_grad.at[:, cols[col]],
            both.at[:, col, :, pl.ds(wide_height + tall_height, head_height)],
            head_load.at[col],
        )
        copy.start()
        head_copies.append(copy)

    def side_message(zt, col):
        return remote(
            both.at[zt, col, 1 - c],
            side.at[zt, col],
            side_send.at[col, zt],
            side_recv.at[col, zt],
            mate,
        )

    def half_message(zt, which):
        return remote(
            piece(both.at[zt, DIAGONAL, c], half_of(head, which)),
            half_in.at[which, zt],
            send.at[0, which, zt],
            recv.at[0, which, zt],
            (at_x, at_y)[which],
        )

    def full_message(zt, which):
        return remote(
            piece(both.at[zt, (ACROSS_X, ACROSS_Y)[which], c], head),
            full_in.at[which, zt],
            send.at[1, which, zt],
            recv.at[1, which, zt],
            (at_x, at_y)[which],
        )

    def line_message(zt, way):
        return remote(
            piece(both.at[zt, OWN, c], head),
            line_in.at[way, zt],
            send.at[2, way, zt],
            recv.at[2, way, zt],
            (up, down)[way],
        )

    def tail_message(zt, way):
        return remote(
            both.at[zt, :, c, pl.ds(tail[0], tail_rows)],
            tail_line.at[way, zt],
            tail_send.at[way, zt],
            tail_recv.at[way, zt],
            (up, down)[way],
        )

    def merged(zt, col):
        side_message(zt, col).wait_recv()
        mine = both.at[zt, col, c]
        accumulate(mine, [mine, side.at[zt, col]], rows)

    def second(zt):
        for which, col in ((0, ACROSS_X), (1, ACROSS_Y)):
            half_message(zt, 1 - which).wait_recv()
            target = piece(both.at[zt, col, c], half_of(head, 1 - which))
            accumulate(target, [target, half_in.at[1 - which, zt]], head_rows // 2)
            full_message(zt, which).start()

    def tail_add(zt, way):
        tail_message(zt, way).wait_recv()
        for col in range(4):
            target = piece(both.at[zt, col, c], tail)
            accumulate(target, [target, tail_line.at[way, zt, col]], tail_rows)

    def ways(zt):
        return ((0, zt > z, below), (1, zt < z, above))

    def tail_open(zt):
        for way, valid, behind in ways(zt):
            go = jnp.logical_and(valid, jnp.logical_not(behind))
            pl.when(go)(lambda way=way: tail_message(zt, way).start())

    def tail_pass(zt):
        for way, valid, behind in ways(zt):

            def action(way=way):
                tail_add(zt, way)
                tail_message(zt, way).start()

            pl.when(jnp.logical_and(valid, behind))(action)

    def line_add(zt, way):
        line_message(zt, way).wait_recv()
        mine = piece(both.at[zt, OWN, c], head)
        accumulate(mine, [mine, line_in.at[way, zt]], head_rows)

    def third(zt):
        for which in (0, 1):
            full_message(zt, which).wait_recv()
        base = [piece(both.at[zt, OWN, c], head), full_in.at[0, zt], full_in.at[1, zt]]
        accumulate(base[0], base, head_rows)
        for way, valid, behind in ways(zt):
            go = jnp.logical_and(valid, jnp.logical_not(behind))
            pl.when(go)(lambda way=way: line_message(zt, way).start())

    def line_pass(zt):
        for way, valid, behind in ways(zt):

            def action(way=way):
                line_add(zt, way)
                line_message(zt, way).start()

            pl.when(jnp.logical_and(valid, behind))(action)

    def after(n):
        i, col = turn_of(n)
        zt = plane_at(i)
        merged(zt, col)

        @pl.when(col == DIAGONAL)
        def _():
            half_message(zt, 0).start()
            half_message(zt, 1).start()

        @pl.when(col == OWN)
        def _():
            second(zt)
            pl.when(i < planes - 1)(lambda: tail_open(zt))
            pl.when(i > 0)(lambda: tail_pass(plane_at(i - 1)))
            pl.when(i > 0)(lambda: third(plane_at(i - 1)))
            pl.when(i > 1)(lambda: line_pass(plane_at(i - 2)))

    for copy in head_copies + right_copies:
        copy.wait()

    def turn_rows():
        for step in (ACROSS_X, ACROSS_Y):
            here = all_rows.at[:, cols[step], c]
            remote(here, here, row_send.at[1, step], row_recv.at[1, step], mate).wait_recv()
        for which in (0, 1):
            row_turn(which).start()

    def share_rows():
        for which in (0, 1):
            here = all_rows.at[:, cols[DIAGONAL], c, pl.ds(which * BUCKET, BUCKET)]
            remote(
                here, here, row_send.at[2, 1 + which], row_recv.at[2, 1 + which], mate
            ).wait_recv()
        row_mate().start()

    def sum_vector():
        total = vector_mid[z]
        for d, who in enumerate(line):
            vector_second(d, who).wait_recv()
            total = total + vector_last[d]
        last[z, f, 0:8] = total

    def body(n, unused):
        for copy in fetches(n):
            copy.wait()

        @pl.when(n + 1 < 4 * planes)
        def _():
            for copy in fetches(n + 1):
                copy.start()

        (i, col), k, slot = turn_of(n), chip_of(n), lax.rem(n, 2)
        zt = plane_at(i)
        region = (k >= split[0]).astype(jnp.int32) + (k >= split[1]).astype(jnp.int32)
        product_wide = to_half(nn(wide_buf[slot], rights[region]))
        both[zt, col, 0, :wide_height] = product_wide[:wide_height]
        both[zt, col, 1, :wide_height] = product_wide[wide_height:]
        product_tall = to_half(nn(tall_buf[slot], outer[...]))
        here = slice(wide_height, wide_height + tall_height)
        both[zt, col, 0, here] = product_tall[:tall_height]
        both[zt, col, 1, here] = product_tall[tall_height:]
        side_message(zt, col).start()
        pl.when(n > 0)(lambda: after(n - 1))

        @pl.when(n == ROWS_AT)
        def _():
            for d, who in enumerate(line):
                row_line(d, who).wait_recv()
            for step in (ACROSS_X, ACROSS_Y):
                row_plane(step).start()
            total = vector_terms[:, f]
            for d, who in enumerate(plane):
                vector_first(d, who).wait_recv()
                total = total + vector_in[d]
            vector_mid[...] = total
            for d, who in enumerate(line):
                vector_second(d, who).start()

        pl.when(n == TURN_AT)(turn_rows)
        pl.when(n == MATE_AT)(share_rows)

        return unused

    lax.fori_loop(0, 4 * planes, body, 0)
    after(jnp.int32(4 * planes - 1))
    targets = [plane_at(i) for i in range(planes)]
    sum_vector()
    here = all_rows.at[:, :, 1 - c]
    remote(here, here, row_send.at[2, 0], row_recv.at[2, 0], mate).wait_recv()
    words = word_grad.shape[0]
    offset = (z * width + f) * words

    def look_back(first, after):
        def body(n, unused):
            zt, chip = n // 4, lax.rem(n, 4)
            row = lax.broadcasted_iota(jnp.int32, (words, BUCKET), 0) + offset
            total = word_grad[...]
            for core in (0, 1):
                ids = facts[zt, chip * 2 + core]
                picks = jnp.concatenate(
                    [to_half((row == ids[i : i + 1, :]).astype(jnp.float32)) for i in (0, 1)], 1
                )
                total = total + nn(picks, all_rows[zt, chip, core])
            word_grad[...] = total
            return unused

        lax.fori_loop(first, after, body, 0)

    word_grad[...] = base_word[...]

    def tail_half_message(which):
        return remote(
            piece(both.at[z, DIAGONAL, c], half_of(tail, which)),
            tail_half.at[which],
            tail_send.at[2, which],
            tail_recv.at[2, which],
            (at_x, at_y)[which],
        )

    def tail_full_message(which):
        return remote(
            piece(both.at[z, (ACROSS_X, ACROSS_Y)[which], c], tail),
            tail_full.at[which],
            tail_send.at[3, which],
            tail_recv.at[3, which],
            (at_x, at_y)[which],
        )

    pl.when(below)(lambda: tail_add(z, 0))
    pl.when(above)(lambda: tail_add(z, 1))
    for which in (0, 1):
        push(None, functools.partial(tail_half_message, which))
    line_pass(targets[planes - 2])
    look_back(0, 4 * planes)
    for which, col in ((1, ACROSS_X), (0, ACROSS_Y)):
        tail_half_message(which).wait_recv()
        target = piece(both.at[z, col, c], half_of(tail, which))
        accumulate(target, [target, tail_half.at[which]], tail_rows // 2)
    for which in (0, 1):
        push(None, functools.partial(tail_full_message, which))
    for which in (0, 1):
        full_message(z, which).wait_recv()
    goal = piece(out, head)
    accumulate(
        goal, [piece(both.at[z, OWN, c], head), full_in.at[0, z], full_in.at[1, z]], head_rows
    )
    for present, way in ((below, 0), (above, 1)):

        def add(way=way):
            line_message(z, way).wait_recv()
            accumulate(goal, [goal, line_in.at[way, z]], head_rows)

        pl.when(present)(add)
    for which in (0, 1):
        tail_full_message(which).wait_recv()
    accumulate(
        piece(out, tail),
        [piece(both.at[z, OWN, c], tail), tail_full.at[0], tail_full.at[1]],
        tail_rows,
    )
    height = place_grad.shape[0]
    own = z * width + f
    low_half = (own * height < BUCKET).astype(jnp.float32)
    high_half = (own * height < 2 * BUCKET).astype(jnp.float32) - low_half
    slot = pl.multiple_of(lax.rem(own * height, BUCKET), height)
    lane = lax.broadcasted_iota(jnp.int32, (1, 128), 1)
    grad = jnp.zeros((height, 128), jnp.float32)
    for zt in range(planes):
        for chip in range(4):
            for core in (0, 1):
                note = facts[zt, chip * 2 + core, 4:5, :]
                two = jnp.sum(
                    jnp.where(lane == 1, (note > 0).astype(jnp.float32), 0.0), 1, keepdims=True
                )
                lower = all_rows[zt, chip, core, pl.ds(slot, height)].astype(jnp.float32)
                upper = all_rows[zt, chip, core, pl.ds(BUCKET + slot, height)].astype(jnp.float32)
                grad = grad + low_half * (lower + two * upper) + high_half * (1.0 - two) * upper
    place_grad[...] = grad
    squares = jnp.sum(grad * grad) + jnp.sum(back_decoder[...] * back_decoder[...])
    squares = squares + jnp.sum(word_grad[...] * word_grad[...])
    squares = squares + jnp.sum(out[...] * out[...])
    last[z, f, 8:16] = jnp.concatenate(
        [totals[...], jnp.where(lane == 0, squares, 0.0), jnp.zeros((6, 128), jnp.float32)], 0
    )
    first_copies, second_copies = [], []
    for d, who in enumerate(line):
        here = last.at[z, f]
        first_copies.append(remote(here, here, end_send.at[0, d], end_recv.at[0, d], who))
        first_copies[-1].start()
    for d, who in enumerate(line):
        here = last.at[lax.rem(z - d - 1 + planes, planes), f]
        remote(here, here, end_send.at[0, d], end_recv.at[0, d], who).wait_recv()
    for d, who in enumerate(plane):
        here = last.at[:, f]
        second_copies.append(remote(here, here, end_send.at[1, d], end_recv.at[1, d], who))
        second_copies[-1].start()
    for d, who in enumerate(plane):
        here = last.at[:, lax.rem(f - d - 1 + width, width)]
        remote(here, here, end_send.at[1, d], end_recv.at[1, d], who).wait_recv()
    summed = last[...]
    tails = jnp.sum(jnp.sum(summed[:, :, 8:16], 0), 0)
    squares = jnp.sum(summed[:, :, 0:8] * summed[:, :, 0:8]) + jnp.sum(tails[1:2, :])
    norm = jnp.sqrt(jnp.broadcast_to(squares, (1, 128)))
    factor = jnp.minimum(1.0, CLIP_NORM / (norm + NORM_EPSILON))
    mlm = totals[0:1, :] - jnp.sum(jnp.where(lane == 1, tails[0:1, :], 0.0))
    def count(at):
        own = jnp.where(lane == at, totals[0:1, :], 0.0)
        return jnp.broadcast_to(jnp.sum(own, 1, keepdims=True), (1, 128))

    sop = jnp.zeros((1, 128), jnp.float32) + jnp.sum(jnp.where(lane == 2, tails[0:1, :], 0.0))
    ends[...] = jnp.concatenate(
        [norm, factor, mlm, sop, count(3), count(4), jnp.zeros((2, 128), jnp.float32)], 0
    )
    for copy in first_copies + second_copies:
        copy.wait_send()
    row_mate().wait_send()
    for condition, make in sent:
        maybe(condition, lambda make=make: make().wait_send())
    for zt in targets:
        for col in order:
            side_message(zt, col).wait_send()
        for which in (0, 1):
            half_message(zt, which).wait_send()
            full_message(zt, which).wait_send()
        for way, valid in ((0, zt > z), (1, zt < z)):

            def done(zt=zt, way=way):
                tail_message(zt, way).wait_send()
                line_message(zt, way).wait_send()

            pl.when(valid)(done)
    for step in (ACROSS_X, ACROSS_Y):
        row_plane(step).wait_send()
    for which in (0, 1):
        row_turn(which).wait_send()
    for d, who in enumerate(line):
        vector_second(d, who).wait_send()


def run_finish(
    left_wide,
    left_tall,
    rights,
    outer,
    head_grad,
    own_rows,
    vector_terms,
    facts,
    base_word,
    back_decoder,
    totals,
    places_count,
    mesh_shape,
    identity,
):
    planes, width = mesh_shape
    devices = planes * width
    columns = outer.shape[1]
    heights = (
        left_wide.shape[0] // devices,
        left_tall.shape[0] // devices,
        head_grad.shape[0] // devices,
    )
    rows = sum(heights)
    long = left_wide.shape[1]
    split = (3 * D // (2 * heights[0]), 4 * D // (2 * heights[0]))
    head, tail = (high - low for low, high in cuts_of(rows, FINISH_TAIL))
    half, single = jnp.bfloat16, jnp.float32
    block = vector_terms.shape[1:]
    vmem = pl.BlockSpec(memory_space=VMEM_SPACE)
    any_space = pl.BlockSpec(memory_space=pl.ANY)
    dma = pltpu.SemaphoreType.DMA
    out, word_grad, place_grad, last, ends = pl.pallas_call(
        functools.partial(finish_kernel, planes, heights, split),
        out_shape=[
            jax.ShapeDtypeStruct((rows, columns), single),
            jax.ShapeDtypeStruct(base_word.shape, single),
            jax.ShapeDtypeStruct((places_count, 128), single),
            jax.ShapeDtypeStruct((planes, width, 16, 128), single),
            jax.ShapeDtypeStruct((8, 128), single),
        ],
        in_specs=[any_space] * 5 + [vmem] * 6,
        out_specs=[vmem] * 5,
        scratch_shapes=[
            VMEM_SPACE((planes, width // 2, 2, *own_rows.shape), half),
            VMEM_SPACE((planes, 4, 2, rows, columns), half),
            VMEM_SPACE((planes, 4, rows, columns), half),
            VMEM_SPACE((2, planes, head // 2, columns), half),
            VMEM_SPACE((2, planes, head, columns), half),
            VMEM_SPACE((2, planes, head, columns), half),
            VMEM_SPACE((2, planes, 4, tail, columns), half),
            VMEM_SPACE((2, tail // 2, columns), half),
            VMEM_SPACE((2, tail, columns), half),
            VMEM_SPACE((2, 2 * heights[0], long), half),
            VMEM_SPACE((2, 2 * heights[1], long), half),
            VMEM_SPACE((width - 1, planes, *block), single),
            VMEM_SPACE((planes, *block), single),
            VMEM_SPACE((planes - 1, *block), single),
            dma((2, 2)),
            dma((4,)),
            dma((4, planes)),
            dma((4, planes)),
            dma((3, 2, planes)),
            dma((3, 2, planes)),
            dma((4, planes)),
            dma((4, planes)),
            dma((3, 4)),
            dma((3, 4)),
            dma((2, width)),
            dma((2, width)),
            dma((2, width)),
            dma((2, width)),
            VMEM_SPACE(rights.shape, half),
            VMEM_SPACE(outer.shape, half),
            dma((4,)),
        ],
        compiler_params=pltpu.CompilerParams(
            collective_id=identity, has_side_effects=True, vmem_limit_bytes=VMEM_ASK
        ),
    )(
        left_wide,
        left_tall,
        rights,
        outer,
        head_grad.reshape(planes, width // 2, 2, heights[2], columns),
        own_rows,
        vector_terms.reshape(planes, width, *block),
        facts.reshape(planes, width, *facts.shape[1:]),
        base_word,
        back_decoder,
        totals,
    )
    return out, heights, word_grad, place_grad, last, ends


LIFT = 128
WIRE = 48


def exact_rows(pick, values):
    first = to_half(values)
    rest = values - first.astype(jnp.float32)
    second = to_half(rest)
    third = to_half(rest - second.astype(jnp.float32))
    return nn(pick, first) + nn(pick, second) + nn(pick, third)


def lanes_to_rows(x):
    return jnp.concatenate([x[:, i : i + 128] for i in range(0, x.shape[1], 128)], 0)


def rows_to_lanes(x):
    return jnp.concatenate([x[i : i + 1] for i in range(x.shape[0])], 1)


def head_kernel(
    planes,
    lengths,
    sop_labels,
    final,
    head,
    word,
    decoder,
    facts,
    vec,
    back_final,
    back_word,
    back_decoder,
    back_head,
    wide_sums,
    small_sums,
    totals,
    all_t,
    stats,
    powers,
    back_t,
    plane_in,
    middle,
    line_in,
    word_half,
    sends,
    recvs,
):
    width = 8
    z, c, cols = places()
    f = cols[0] * 2 + c
    line = [(lax.rem(z + d, planes), f) for d in range(1, planes)]
    plane = [(z, lax.rem(f + d, width)) for d in range(1, width)]
    greet([(None, who) for who in line + plane])
    offset = (z * width + f) * word.shape[0]
    words, slots = word.shape[0], planes * width * WIRE
    single = jnp.float32

    def gather_line(ref, kind):
        here = ref.at[z, f]
        return [
            remote(here, here, sends.at[kind, d], recvs.at[kind, d], who)
            for d, who in enumerate(line)
        ]

    def gather_plane(ref, kind):
        here = ref.at[:, f]
        return [
            remote(here, here, sends.at[kind, d], recvs.at[kind, d], who)
            for d, who in enumerate(plane)
        ]

    def await_line(ref, kind):
        for d in range(planes - 1):
            here = ref.at[lax.rem(z - d - 1 + planes, planes), f]
            remote(here, here, sends.at[kind, d], recvs.at[kind, d], line[d]).wait_recv()

    def await_plane(ref, kind):
        for d in range(width - 1):
            here = ref.at[:, lax.rem(f - d - 1 + width, width)]
            remote(here, here, sends.at[kind, d], recvs.at[kind, d], plane[d]).wait_recv()

    started = []
    lane = lax.broadcasted_iota(jnp.int32, (1, 128), 1)
    notes = facts[...]
    labels = jnp.concatenate([notes[i, 2:3, :WIRE] for i in range(planes * width)], 1)
    used = (lanes_to_rows(labels) >= 0).astype(single)
    mlm_count = jnp.sum(used)
    seconds = jnp.where(lane == 1, (notes[:, 4, :] > 0).astype(single), 0.0)
    sop_count = planes * width + jnp.sum(seconds)
    mlm_scale = 1.0 / jnp.broadcast_to(mlm_count, (1, 1))
    sop_scale = 1.0 / jnp.broadcast_to(sop_count, (1, 1))

    def start(copies):
        for copy in copies:
            copy.start()
        started.extend(copies)

    final_half = to_half(final[...])
    place = lax.broadcasted_iota(jnp.int32, (ROWS, LIFT), 0)
    scatter = to_half((place == facts[z * width + f, 3:4, :]).astype(single))
    pick = scatter.T
    picked = to_half(nn(pick, final_half))
    dense = nt(picked, head[:E, :]) + short_row(vec, MLM_B)
    bend = jnp.tanh(GELU_A * dense * (1.0 + GELU_B * dense * dense))
    hat, inverse = norm_forward(0.5 * dense * (1.0 + bend))
    slope = 0.5 * (1.0 + bend) + (0.5 * GELU_A) * dense * (1.0 - bend * bend) * (
        1.0 + 3.0 * GELU_B * dense * dense
    )
    rows_half = to_half(hat * short_row(vec, MLM_G) + short_row(vec, MLM_LB))
    all_t[z, f] = rows_half[:WIRE]
    start(gather_line(all_t, 0))

    word_half[...] = to_half(word[...])
    row16 = lax.broadcasted_iota(jnp.int32, (16, ROWS), 0)
    col16 = lax.broadcasted_iota(jnp.int32, (16, ROWS), 1)
    leads = to_half(
        (jnp.logical_and(row16 < 2, col16 == row16 * BUCKET)).astype(single)
    )
    firsts = to_half(nn(leads, final_half))
    pooled = jnp.tanh(nt(firsts, head[E : E + D, :]) + wide_row(vec, POOL_B))
    await_line(all_t, 0)
    start(gather_plane(all_t, 1))
    zero_class, one_class = lanes_of(vec, CLS_AT, D // 128), lanes_of(vec, CLS_AT + D // 128, D // 128)
    c0 = jnp.sum(pooled * zero_class, -1, keepdims=True)
    c1 = jnp.sum(pooled * one_class, -1, keepdims=True)
    class_top = jnp.maximum(c0, c1)
    e0, e1 = jnp.exp(c0 - class_top), jnp.exp(c1 - class_top)
    class_total = e0 + e1
    which = lax.broadcasted_iota(jnp.int32, (16, 1), 0)
    label = jnp.where(which == 0, sop_labels[0], sop_labels[1])
    hit = (label == 1).astype(single)
    two = (lengths[1] > 0).astype(single)
    present = jnp.where(which == 0, 1.0, jnp.where(which == 1, two, 0.0))
    losses = (jnp.log(class_total) + class_top - (c0 + hit * (c1 - c0))) * present
    weight = present * sop_scale
    back_c0 = (e0 / class_total - (1.0 - hit)) * weight
    back_c1 = (e1 / class_total - hit) * weight
    wide_sums[1:2, :] = jnp.sum(back_c0 * pooled, 0, keepdims=True)
    wide_sums[2:3, :] = jnp.sum(back_c1 * pooled, 0, keepdims=True)
    pre_half = to_half((back_c0 * zero_class + back_c1 * one_class) * (1.0 - pooled * pooled))
    wide_sums[0:1, :] = jnp.sum(pre_half.astype(single), 0, keepdims=True)
    back_head[E : E + D, :] = to_half(tn(pre_half, firsts))
    back_firsts = nn(pre_half, head[E : E + D, :])
    await_plane(all_t, 1)

    row = lax.broadcasted_iota(jnp.int32, (words, 128), 0) + offset
    bias = jnp.broadcast_to(to_half(decoder[...]).astype(single), (8, words)).T[:, 0:1]
    tops, sums, targets = [], [], []
    chunk = width * WIRE
    flat_t = all_t[...].reshape(slots, E)

    def logits_of(low):
        return nt(word_half[...], flat_t[low : low + chunk])

    coming = logits_of(0)
    for low in range(0, slots, chunk):
        logits = coming + bias
        if low + chunk < slots:
            coming = logits_of(low + chunk)
        top = jnp.max(logits, 0, keepdims=True)
        power = jnp.exp(logits - top)
        powers[:, pl.ds(low, chunk)] = power
        tops.append(top)
        sums.append(jnp.sum(power, 0, keepdims=True))
        for at in range(0, chunk, 128):
            mark = row == labels[:, low + at : low + at + 128]
            targets.append(
                jnp.sum(jnp.where(mark, logits[:, at : at + 128], 0.0), 0, keepdims=True)
            )
    own_top = lanes_to_rows(jnp.concatenate(tops, 1))
    groups = slots // 128
    stats[z, f, 0:groups] = own_top
    stats[z, f, groups : 2 * groups] = lanes_to_rows(jnp.concatenate(sums, 1))
    start(gather_line(stats, 2))
    target = jnp.sum(jnp.concatenate(targets, 0) * used)
    await_line(stats, 2)
    start(gather_plane(stats, 3))
    await_plane(stats, 3)
    every = stats[...].reshape(planes * width, 2 * groups, 128)
    top = jnp.max(every[:, :groups], 0)
    total = jnp.sum(every[:, groups:] * jnp.exp(every[:, :groups] - top[None]), 0)
    log_sum = jnp.sum((jnp.log(total) + top) * used)
    weight = used * mlm_scale
    factor = rows_to_lanes(weight * jnp.exp(own_top - top) / total)
    weight = rows_to_lanes(weight)

    def slot_terms(zz, d, who):
        return remote(
            back_t.at[zz, who[1]],
            plane_in.at[d, zz],
            sends.at[4 + zz, d],
            recvs.at[4 + zz, d],
            who,
        )

    def spread(word_sums, words_total, low, half):
        zz = low // chunk
        back_t[zz] = tn(half, word_half[...]).reshape(width, WIRE, E)
        start([slot_terms(zz, d, who) for d, who in enumerate(plane)])
        return word_sums + nt(ones, half), words_total + nn(half, flat_t[low : low + chunk])

    ready = []
    words_total = jnp.zeros((words, E), single)
    word_sums = jnp.zeros((8, words), single)
    ones = jnp.ones((8, width * WIRE), jnp.bfloat16)
    for low in range(0, slots, chunk):
        parts = []
        for at in range(low, low + chunk, 128):
            mark = row == labels[:, at : at + 128]
            part = powers[:, pl.ds(at, 128)] * factor[:, at : at + 128] - jnp.where(
                mark, weight[:, at : at + 128], 0.0
            )
            parts.append(to_half(part))
        if ready:
            word_sums, words_total = spread(word_sums, words_total, *ready.pop())
        ready.append((low, jnp.concatenate(parts, 1)))
    word_sums, words_total = spread(word_sums, words_total, *ready.pop())
    back_word[...] = words_total
    back_decoder[...] = word_sums[0:1]

    for zz in range(planes):
        total = back_t[zz, f]
        for d in range(width - 1):
            slot_terms(zz, d, plane[d]).wait_recv()
            total = total + plane_in[d, zz]
        middle[zz] = total
    start(
        [
            remote(middle.at[who[0]], line_in.at[d], sends.at[4 + planes, d], recvs.at[4 + planes, d], who)
            for d, who in enumerate(line)
        ]
    )
    total = middle[z]
    for d in range(planes - 1):
        remote(
            line_in.at[d], line_in.at[d], sends.at[4 + planes, d], recvs.at[4 + planes, d], line[d]
        ).wait_recv()
        total = total + line_in[d]
    back_rows = jnp.concatenate([total, jnp.zeros((LIFT - WIRE, E), single)], 0)
    small_sums[1:2, :] = jnp.sum(back_rows * hat, 0, keepdims=True)
    small_sums[2:3, :] = jnp.sum(back_rows, 0, keepdims=True)
    dense_half = to_half(norm_backward(back_rows, short_row(vec, MLM_G), hat, inverse) * slope)
    small_sums[0:1, :] = jnp.sum(dense_half.astype(single), 0, keepdims=True)
    back_head[:E, :] = to_half(tn(dense_half, picked))
    back_final[...] = exact_rows(scatter, nn(dense_half, head[:E, :]))
    back_final[0:1, :] = back_final[0:1, :] + back_firsts[0:1]
    back_final[BUCKET : BUCKET + 1, :] = back_final[BUCKET : BUCKET + 1, :] + back_firsts[1:2]
    sop_sum = jnp.sum(losses)
    ends = jnp.zeros((1, 128), single)
    for at, value in enumerate((log_sum, target, sop_sum, mlm_count, sop_count)):
        ends = ends + jnp.where(lane == at, value, 0.0)
    totals[...] = ends
    for copy in started:
        copy.wait_send()


def run_head(
    lengths, sop_labels, final, head, word, decoder, facts, vec, mesh_shape, identity
):
    planes, width = mesh_shape
    words = word.shape[0]
    slots = planes * width * WIRE
    groups = slots // 128
    single, half = jnp.float32, jnp.bfloat16
    vmem = pl.BlockSpec(memory_space=VMEM_SPACE)
    smem = pl.BlockSpec(memory_space=pltpu.SMEM)
    dma = pltpu.SemaphoreType.DMA
    return pl.pallas_call(
        functools.partial(head_kernel, planes),
        out_shape=[
            jax.ShapeDtypeStruct((ROWS, D), single),
            jax.ShapeDtypeStruct((words, E), single),
            jax.ShapeDtypeStruct((1, words), single),
            jax.ShapeDtypeStruct(head.shape, half),
            jax.ShapeDtypeStruct((3, D), single),
            jax.ShapeDtypeStruct((3, E), single),
            jax.ShapeDtypeStruct((1, 128), single),
        ],
        in_specs=[smem] * 2 + [vmem] * 6,
        out_specs=[vmem] * 7,
        scratch_shapes=[
            VMEM_SPACE((planes, width, WIRE, E), half),
            VMEM_SPACE((planes, width, 2 * groups, 128), single),
            VMEM_SPACE((words, slots), single),
            VMEM_SPACE((planes, width, WIRE, E), single),
            VMEM_SPACE((width - 1, planes, WIRE, E), single),
            VMEM_SPACE((planes, WIRE, E), single),
            VMEM_SPACE((planes - 1, WIRE, E), single),
            VMEM_SPACE((words, E), half),
            dma((5 + planes, width)),
            dma((5 + planes, width)),
        ],
        compiler_params=pltpu.CompilerParams(
            collective_id=identity, has_side_effects=True, vmem_limit_bytes=VMEM_ASK
        ),
    )(lengths, sop_labels, final, head, word, decoder, facts, vec)


def adam_update(weight, gradient, first, second, rate):
    first = BETA_ONE * first + (1 - BETA_ONE) * gradient
    second = BETA_TWO * second + (1 - BETA_TWO) * gradient * gradient
    first_hat = first / (1 - BETA_ONE**STEP)
    second_hat = second / (1 - BETA_TWO**STEP)
    updated = weight - rate * (
        first_hat / (jnp.sqrt(second_hat) + ADAM_EPSILON) + WEIGHT_DECAY * weight
    )
    return (updated, first, second)


def adam_kernel(blocks, rates, *refs):
    count = len(rates)
    ends, refs = refs[0], refs[1:]
    ins, outs, scalars = refs[: 4 * count], refs[4 * count : 7 * count], refs[7 * count :]
    factor = ends[1:2, 0:1]

    def update(number):
        weight, first, second, gradient = ins[4 * number : 4 * number + 4]
        grad = gradient[...]
        if grad.ndim > 2:
            grad = grad[:, :, :8].reshape(-1, 128)[: weight.shape[0]]
        results = adam_update(
            weight[...], factor * grad, first[...], second[...], rates[number]
        )
        for out, result in zip(outs[3 * number : 3 * number + 3], results):
            out[...] = result

    for number in range(blocks):
        update(number)

    @pl.when(pl.program_id(0) == 0)
    def _():
        for number in range(blocks, count):
            update(number)
        lane = lax.broadcasted_iota(jnp.int32, (1, 128), 1)
        for at, scalar in enumerate(scalars):
            scalar[0] = jnp.sum(jnp.where(lane == 0, ends[at : at + 1, :], 0.0))


ADAM_STEPS = 2


def run_adam(ends, groups, steps):
    in_specs = [pl.BlockSpec(ends.shape, lambda i: (0, 0))]
    out_specs, shapes, given = [], [], [ends]
    blocks = 0
    for weight, first, second, gradient, low, rate in groups:
        rows, columns = weight.shape
        if low is None:
            spec = pl.BlockSpec(weight.shape, lambda i: (0, 0))
            zero = (0,) * gradient.ndim
            grad_spec = pl.BlockSpec(gradient.shape, lambda i, zero=zero: zero)
        else:
            blocks += 1
            height = rows // steps
            spec = pl.BlockSpec((height, columns), lambda i: (i, 0))
            grad_spec = pl.BlockSpec(
                (height, columns), lambda i, start=low // height: (start + i, 0)
            )
        in_specs += [spec] * 3 + [grad_spec]
        out_specs += [spec] * 3
        shapes += [jax.ShapeDtypeStruct(weight.shape, jnp.float32)] * 3
        given += [weight, first, second, gradient]
    out_specs += [pl.BlockSpec(memory_space=pltpu.SMEM)] * 6
    shapes += [jax.ShapeDtypeStruct((1,), jnp.float32)] * 6
    return pl.pallas_call(
        functools.partial(adam_kernel, blocks, tuple(group[5] for group in groups)),
        grid=(steps,),
        out_shape=shapes,
        in_specs=in_specs,
        out_specs=out_specs,
        compiler_params=pltpu.CompilerParams(
            dimension_semantics=("arbitrary",), vmem_limit_bytes=VMEM_ASK
        ),
    )(*given)


class Network:
    def __init__(self, mesh):
        self.shape = (mesh.shape["dp"], mesh.shape["fsdp"])
        self.devices = self.shape[0] * self.shape[1]
        self.kernels = self.shape[1] == 8
        self.calls = 0

    def identity(self):
        self.calls += 1
        return self.calls

    def start(self, shards, own_word, own_place, batch):
        if self.kernels:
            return run_start(shards, own_word, own_place, batch, self.shape, self.identity())
        token_ids, labels, slot_rows, lengths, sop_labels = batch

        def fill(count, value):
            return jnp.full((count,), value, jnp.int32)

        rest = fill(128 - labels.shape[0], -1)
        own_facts = [token_ids, labels, rest, slot_rows, rest, lengths, sop_labels]
        own_facts = jnp.concatenate([*own_facts, fill(3 * 128 + 124, 0)]).reshape(8, 128)
        weights = [lax.all_gather(to_half(w), AXES, axis=0, tiled=True) for w in shards]
        facts = lax.all_gather(own_facts, AXES)
        place = lax.all_gather(to_half(own_place), AXES)
        words = own_word.shape[0]
        ids = facts[:, : ROWS // 128].reshape(-1) - lax.axis_index(AXES) * words
        column = jnp.arange(words, dtype=jnp.int32)
        select = to_half(ids[:, None] == column[None, :])
        terms = product(select, to_half(own_word))
        found = lax.psum_scatter(terms, AXES, scatter_dimension=0, tiled=True)
        return weights, facts, place, found

    def head(self, lengths, sop_labels, final, head, word, decoder, facts, vec):
        decoder = decoder[None]
        given = (lengths, sop_labels, final, head, word, decoder, facts, vec)
        if self.kernels:
            return run_head(*given, self.shape, self.identity())
        return self.plain_head(*given)

    def plain_head(self, lengths, sop_labels, final, head, word, decoder, facts, vec):
        short, cls = vec[SHORT_AT:], vec[CLS_AT:FF_AT].reshape(2, D)
        pool_b = vec[POOL_B * D // 128 : CLS_AT].reshape(D)
        labels = facts[:, 2, :WIRE].reshape(1, -1)
        mlm_count = jnp.sum((labels >= 0).astype(jnp.float32))
        sop_count = self.devices + jnp.sum((facts[:, 4, 1] > 0).astype(jnp.float32))
        single = jnp.float32
        offset = lax.axis_index(AXES) * word.shape[0]
        word_half, final_half = to_half(word), to_half(final)
        rows = facts[lax.axis_index(AXES), 3, :WIRE]
        pick = (rows[:, None] == jnp.arange(ROWS, dtype=jnp.int32)[None]).astype(single)
        picked = to_half(product(to_half(pick), final_half))
        dense = times_transpose(picked, head[:E]) + short[MLM_B]
        bend = jnp.tanh(GELU_A * dense * (1.0 + GELU_B * dense * dense))
        hat, inverse = norm_forward(0.5 * dense * (1.0 + bend))
        slope = 0.5 * (1.0 + bend) + (0.5 * GELU_A) * dense * (1.0 - bend * bend) * (
            1.0 + 3.0 * GELU_B * dense * dense
        )
        rows_half = to_half(hat * short[MLM_G] + short[MLM_LB])
        all_rows = lax.all_gather(rows_half, AXES, axis=0, tiled=True)
        logits = times_transpose(word_half, all_rows) + to_half(decoder).astype(single).T
        mark = jnp.arange(word.shape[0], dtype=jnp.int32)[:, None] + offset == labels
        own_top = jnp.max(logits, 0)
        own_total = jnp.sum(jnp.exp(logits - own_top), 0)
        used = (labels[0] >= 0).astype(single)
        target = jnp.sum(jnp.sum(jnp.where(mark, logits, 0.0), 0) * used)
        top = lax.pmax(own_top, AXES)
        total = lax.psum(own_total * jnp.exp(own_top - top), AXES)
        log_sum = jnp.sum((jnp.log(total) + top) * used)
        weight = used / mlm_count
        half = to_half((jnp.exp(logits - top) / total - mark.astype(single)) * weight)
        back_rows = lax.psum_scatter(
            transpose_times(half, word_half), AXES, scatter_dimension=0, tiled=True
        )
        dense_half = to_half(norm_backward(back_rows, short[MLM_G], hat, inverse) * slope)
        back_final = lax.dot_general(
            pick, product(dense_half, head[:E]), (((0,), (0,)), ((), ())), precision=PRECISE
        )
        firsts = jnp.stack([final_half[0], final_half[BUCKET]])
        pooled = jnp.tanh(times_transpose(firsts, head[E : E + D]) + pool_b)
        classes = jnp.sum(pooled[:, None] * cls[None], -1)
        powers = jnp.exp(classes - jnp.max(classes, -1, keepdims=True))
        totals = jnp.sum(powers, -1, keepdims=True)
        onehot = jnp.stack([1 - sop_labels, sop_labels], 1).astype(single)
        present = jnp.stack([jnp.float32(1.0), (lengths[1] > 0).astype(single)])
        losses = jnp.log(totals[:, 0]) + jnp.max(classes, -1) - jnp.sum(classes * onehot, -1)
        back_classes = (powers / totals - onehot) * (present / sop_count)[:, None]
        back_pooled = jnp.sum(back_classes[:, :, None] * cls[None], 1)
        pre_half = to_half(back_pooled * (1.0 - pooled * pooled))
        back_firsts = product(pre_half, head[E : E + D])
        back_final = back_final.at[0].add(back_firsts[0]).at[BUCKET].add(back_firsts[1])
        back_cls = jnp.sum(back_classes[:, :, None] * pooled[:, None], 0)
        small_sums = [column_sum(dense_half), jnp.sum(back_rows * hat, 0), jnp.sum(back_rows, 0)]
        back_head = [transpose_times(dense_half, picked), transpose_times(pre_half, firsts)]
        ends = jnp.stack([log_sum, target, jnp.sum(losses * present), mlm_count, sop_count])
        return (
            back_final,
            product(half, all_rows),
            column_sum(half.T)[None],
            to_half(jnp.pad(jnp.concatenate(back_head, 0), ((0, E), (0, 0)))),
            jnp.concatenate([column_sum(pre_half)[None], back_cls], 0),
            jnp.stack(small_sums),
            jnp.pad(ends, (0, 123))[None],
        )

    def adam(self, ends, groups):
        if self.kernels:
            updates = run_adam(ends, groups, ADAM_STEPS)
            scalars = [x.reshape(()) for x in updates[-6:]]
            return [updates[i : i + 3] for i in range(0, 3 * len(groups), 3)], scalars
        updates = []
        for weight, first, second, gradient, low, rate in groups:
            rows = weight.shape[0]
            if low is not None:
                gradient = gradient[low : low + rows]
            gradient = gradient.reshape(-1, weight.shape[1])[:rows]
            updates.append(adam_update(weight, ends[1, 0] * gradient, first, second, rate))
        return updates, [ends[i, 0] for i in range(6)]

    def finish(
        self,
        left_wide,
        left_tall,
        rights,
        outer,
        head_grad,
        own_rows,
        vector,
        facts,
        base_word,
        back_decoder,
        totals,
        places_count,
    ):
        devices = self.devices
        if self.kernels:
            out, heights, word_grad, place_grad, last, ends = run_finish(
                left_wide,
                left_tall,
                rights,
                outer,
                head_grad,
                own_rows,
                vector,
                facts,
                base_word,
                back_decoder,
                totals,
                places_count,
                self.shape,
                self.identity(),
            )
            return out, heights, word_grad, place_grad, last, ends
        back_wide = jnp.concatenate(
            [
                product(left_wide[: 3 * D], rights[0]),
                product(left_wide[3 * D : 4 * D], rights[1]),
                product(left_wide[4 * D :], rights[2]),
            ],
            0,
        )
        sums = [
            lax.psum_scatter(p.astype(jnp.float32), AXES, scatter_dimension=0, tiled=True)
            for p in (back_wide, product(left_tall, outer), head_grad)
        ]
        all_rows = lax.all_gather(own_rows, AXES, axis=0, tiled=True)
        own, words = lax.axis_index(AXES), base_word.shape[0]
        ids = facts[:, : ROWS // 128].reshape(-1) - own * words
        select = to_half(ids[:, None] == jnp.arange(words, dtype=jnp.int32)[None, :])
        word_grad = base_word + transpose_times(select, all_rows)
        by_device = all_rows.reshape(devices, ROWS, E).astype(jnp.float32)
        two = (facts[:, 4, 1] > 0)[:, None, None]
        lower, upper = by_device[:, :BUCKET], by_device[:, BUCKET:]
        lower = jnp.sum(lower + jnp.where(two, upper, 0.0), 0)
        upper = jnp.sum(jnp.where(two, 0.0, upper), 0)
        every = jnp.concatenate([lower, upper], 0)
        every = jnp.pad(every, ((0, places_count * devices - ROWS), (0, 0)))
        place_grad = lax.dynamic_slice(every, (own * places_count, 0), (places_count, E))
        squares = sum(jnp.sum(g * g) for g in (*sums, word_grad, place_grad, back_decoder))
        reduced, tails, squares = lax.psum((vector, totals, squares), AXES)
        norm = jnp.sqrt(squares + jnp.sum(reduced * reduced))
        factor = jnp.minimum(1.0, CLIP_NORM / (norm + NORM_EPSILON))
        ends = [norm, factor, totals[0, 0] - tails[0, 1], tails[0, 2]]
        ends = jnp.stack([*ends, totals[0, 3], totals[0, 4]])
        ends = jnp.broadcast_to(ends[:, None], (6, 128))
        heights = tuple(total.shape[0] for total in sums)
        return jnp.concatenate(sums, 0), heights, word_grad, place_grad, reduced, ends


CLS_AT, FF_AT, SHORT_AT = 10 * D // 128, 12 * D // 128, (12 * D + FF) // 128


def lanes_of(vec, first, count):
    return jnp.concatenate([vec[pl.ds(first + i, 1), :] for i in range(count)], 1)


def wide_row(vec, index):
    return lanes_of(vec, index * (D // 128), D // 128)


def short_row(vec, index):
    return vec[pl.ds(SHORT_AT + index, 1), :]


def nt(a, b):
    return lax.dot_general(a, b, (((1,), (1,)), ((), ())), preferred_element_type=jnp.float32)


def nn(a, b):
    return jnp.dot(a, b, preferred_element_type=jnp.float32)


def tn(a, b):
    return lax.dot_general(a, b, (((0,), (0,)), ((), ())), preferred_element_type=jnp.float32)


FORWARD_CHUNK, BACKWARD_CHUNK = 768, 256
PAIR = 2 * HEAD_DIM
PROJ_B, Q_B, V_B, O_B, LN1_G, LN1_B, FFO_B, LN2_G, LN2_B, POOL_B = range(10)


def allowed_block(lengths):
    shape = (ROWS, ROWS)
    key = lax.broadcasted_iota(jnp.int32, shape, 0)
    query = lax.broadcasted_iota(jnp.int32, shape, 1)
    two = lengths[1] > 0
    key_second = jnp.logical_and(key >= BUCKET, two).astype(jnp.int32)
    query_second = jnp.logical_and(query >= BUCKET, two).astype(jnp.int32)
    length = jnp.where(key_second == 1, lengths[1], lengths[0])
    live = key - BUCKET * key_second < length
    return jnp.logical_and(query_second == key_second, live)


def halves_down(x):
    row = lax.broadcasted_iota(jnp.int32, x.shape, 0)
    zero = jnp.zeros_like(x)
    return jnp.where(row < HEAD_DIM, x, zero), jnp.where(row < HEAD_DIM, zero, x)


def halves(x):
    lane = lax.broadcasted_iota(jnp.int32, x.shape, 1)
    zero = jnp.zeros_like(x)
    return jnp.where(lane < HEAD_DIM, x, zero), jnp.where(lane < HEAD_DIM, zero, x)


def kinds(lengths):
    row = lax.broadcasted_iota(jnp.int32, (ROWS, 1), 0)
    second = jnp.logical_and(row >= BUCKET, lengths[1] > 0).astype(jnp.int32)
    length = jnp.where(second == 1, lengths[1], lengths[0])
    return (row - BUCKET * second >= length // 2).astype(jnp.float32)


EMB_G, EMB_B, MLM_B, MLM_G, MLM_LB, TYPE_ZERO, TYPE_ONE = range(7)


def forward_kernel(
    lengths,
    found,
    place,
    lift,
    wide,
    tall,
    vec,
    final,
    embed_hat,
    embed_inverse,
    normed_half,
    rights,
    projected,
    weighting,
    hat_one,
    inverse_one,
    slope,
    active,
    hat_two,
    inverse_two,
    hidden,
):
    layer = pl.program_id(0)

    def row(index):
        return wide_row(vec, index)

    @pl.when(layer == 0)
    def _():
        two = (lengths[1] > 0).astype(jnp.float32)
        kind = kinds(lengths)
        upper = place[pl.ds(0, BUCKET), :].astype(jnp.float32)
        lower = jnp.where(two > 0, upper, place[pl.ds(BUCKET, BUCKET), :].astype(jnp.float32))
        embedded = found[...] + jnp.concatenate([upper, lower], 0)
        zero, one = short_row(vec, TYPE_ZERO), short_row(vec, TYPE_ONE)
        hat, inverse = norm_forward(embedded + jnp.where(kind > 0, one, zero))
        embed_hat[...] = hat
        embed_inverse[...] = inverse
        normed = to_half(hat * short_row(vec, EMB_G) + short_row(vec, EMB_B))
        normed_half[...] = normed
        hidden[...] = nn(normed, lift[...]) + row(PROJ_B)

    half = to_half(hidden[...])
    rights[0] = half
    for part, bias in ((0, Q_B), (1, None), (2, V_B)):
        for low in range(0, D, 256):
            here = part * D + low
            value = nt(half, wide[pl.ds(here, 256), :])
            if bias is not None:
                value = value + lanes_of(vec, (bias * D + low) // 128, 2)
            projected[:, pl.ds(here, 256)] = to_half(value)
    allowed = allowed_block(lengths)
    def scores_of(head):
        lanes = head // 2 * PAIR
        queries = halves(projected[:, pl.ds(lanes, PAIR)])[head % 2]
        return nt(projected[:, pl.ds(D + lanes, PAIR)], queries)

    def mix(head, weights):
        lanes = head // 2 * PAIR
        values = halves_down(projected[:, pl.ds(2 * D + lanes, PAIR)].T)[head % 2]
        part = nn(values, weights)
        if head % 2:
            rights[1, :, pl.ds(lanes, PAIR)] = to_half(mixes.pop() + part).T
        else:
            mixes.append(part)

    mixes, waiting, coming = [], None, scores_of(0)
    for head in range(HEADS):
        products = coming
        if head + 1 < HEADS:
            coming = scores_of(head + 1)
        scores = jnp.where(allowed, products * SCALE, MASKED)
        powers = jnp.exp(scores - jnp.max(scores, 0, keepdims=True))
        weights = powers * (1.0 / jnp.sum(powers, 0, keepdims=True))
        weighting[head] = weights
        if waiting is not None:
            mix(head - 1, waiting)
        waiting = to_half(weights)
    mix(HEADS - 1, waiting)
    first_sum = hidden[...] + nt(rights[1], wide[pl.ds(3 * D, D), :]) + row(O_B)
    hat, inverse = norm_forward(first_sum)
    hat_one[...] = hat
    inverse_one[...] = inverse
    middle = hat * row(LN1_G) + row(LN1_B)
    half = to_half(middle)
    rights[2] = half
    total = middle + row(FFO_B)

    def inner_of(low):
        return nt(half, wide[pl.ds(4 * D + low, FORWARD_CHUNK), :])

    coming = inner_of(0)
    for low in range(0, FF, FORWARD_CHUNK):
        inner = coming + lanes_of(vec, FF_AT + low // 128, FORWARD_CHUNK // 128)
        if low + FORWARD_CHUNK < FF:
            coming = inner_of(low + FORWARD_CHUNK)
        square = inner * inner
        bend = jnp.tanh(GELU_A * inner * (1.0 + GELU_B * square))
        act = to_half(0.5 * inner * (1.0 + bend))
        slope[:, pl.ds(low, FORWARD_CHUNK)] = 0.5 * (1.0 + bend) + (0.5 * GELU_A) * inner * (
            1.0 - bend * bend
        ) * (1.0 + 3.0 * GELU_B * square)
        active[pl.ds(low, FORWARD_CHUNK), :] = act.T
        total = total + nn(act, tall[pl.ds(low, FORWARD_CHUNK), :])
    hat, inverse = norm_forward(total)
    hat_two[...] = hat
    inverse_two[...] = inverse
    output = hat * row(LN2_G) + row(LN2_B)
    hidden[...] = output
    final[...] = output


def whole_spec():
    return pl.BlockSpec(memory_space=VMEM_SPACE, pipeline_mode=pl.Buffered(1))


def lift_spec():
    return pl.BlockSpec((E, D), lambda i: ((E + D) // E, 0), pipeline_mode=pl.Buffered(1))


def by_layer(*shape, order=lambda i: i):
    return pl.BlockSpec(
        (None, *shape), lambda i: (order(i),) + (0,) * len(shape), memory_space=VMEM_SPACE
    )


def run_forward(lengths, found, place, head, wide, tall, vec):
    def kept(*shape, dtype=jnp.bfloat16):
        return jax.ShapeDtypeStruct((LAYERS, *shape), dtype)

    single = jnp.float32
    names = (
        "final",
        "embed_hat",
        "embed_inverse",
        "normed_half",
        "rights",
        "projected",
        "weighting",
        "hat_one",
        "inverse_one",
        "slope",
        "active",
        "hat_two",
        "inverse_two",
    )
    outs = pl.pallas_call(
        forward_kernel,
        grid=(LAYERS,),
        out_shape=[
            jax.ShapeDtypeStruct((ROWS, D), single),
            jax.ShapeDtypeStruct((ROWS, E), single),
            jax.ShapeDtypeStruct((ROWS, 1), single),
            jax.ShapeDtypeStruct((ROWS, E), jnp.bfloat16),
            jax.ShapeDtypeStruct((3, LAYERS, ROWS, D), jnp.bfloat16),
            kept(ROWS, 3 * D),
            kept(HEADS, ROWS, ROWS, dtype=single),
            kept(ROWS, D, dtype=single),
            kept(ROWS, 1, dtype=single),
            kept(ROWS, FF, dtype=single),
            jax.ShapeDtypeStruct((FF, LAYERS * ROWS), jnp.bfloat16),
            kept(ROWS, D, dtype=single),
            kept(ROWS, 1, dtype=single),
        ],
        in_specs=[pl.BlockSpec(memory_space=pltpu.SMEM)]
        + [whole_spec()] * 2
        + [lift_spec()]
        + [whole_spec()] * 3,
        out_specs=[
            pl.BlockSpec((ROWS, D), lambda i: (0, 0)),
            pl.BlockSpec((ROWS, E), lambda i: (0, 0)),
            pl.BlockSpec((ROWS, 1), lambda i: (0, 0)),
            pl.BlockSpec((ROWS, E), lambda i: (0, 0)),
            pl.BlockSpec((3, None, ROWS, D), lambda i: (0, i, 0, 0)),
            by_layer(ROWS, 3 * D),
            by_layer(HEADS, ROWS, ROWS),
            by_layer(ROWS, D),
            by_layer(ROWS, 1),
            by_layer(ROWS, FF),
            pl.BlockSpec((FF, ROWS), lambda i: (0, i)),
            by_layer(ROWS, D),
            by_layer(ROWS, 1),
        ],
        scratch_shapes=[VMEM_SPACE((ROWS, D), single)],
        compiler_params=pltpu.CompilerParams(
            dimension_semantics=("arbitrary",), vmem_limit_bytes=VMEM_ASK
        ),
    )(lengths, found, place, head, wide, tall, vec)
    return dict(zip(names, outs))


def backward_kernel(
    lengths,
    start,
    wide_sums,
    small_sums,
    embed_hat,
    embed_inverse,
    normed_half,
    lift,
    head_in,
    wide,
    tall,
    vec,
    projected,
    weighting,
    hat_one,
    inverse_one,
    slope,
    hat_two,
    inverse_two,
    rows_out,
    back_lift,
    turned,
    outer,
    vector,
    sums,
    ff_sum,
    upstream,
    back_mixed,
    joint,
):
    step = pl.program_id(0)

    @pl.when(step == 0)
    def _():
        upstream[...] = start[...]
        sums[...] = jnp.zeros_like(sums)
        ff_sum[...] = jnp.zeros_like(ff_sum)

    def row(index):
        return wide_row(vec, index)

    def add_sum(index, value):
        here = pl.ds(index - Q_B, 1)
        sums[here, :] = sums[here, :] + jnp.sum(value, 0, keepdims=True)

    up = upstream[...]
    hat = hat_two[...]
    add_sum(LN2_G, up * hat)
    add_sum(LN2_B, up)
    back_second = norm_backward(up, row(LN2_G), hat, inverse_two[...])
    half = to_half(back_second)
    outer[...] = half
    add_sum(FFO_B, half.astype(jnp.float32))
    total = back_second

    def back_active(low):
        return nt(half, tall[pl.ds(low, BACKWARD_CHUNK), :])

    coming = back_active(0)
    for low in range(0, FF, BACKWARD_CHUNK):
        lanes = pl.ds(low, BACKWARD_CHUNK)
        product = coming
        if low + BACKWARD_CHUNK < FF:
            coming = back_active(low + BACKWARD_CHUNK)
        inner = to_half(product * slope[:, lanes])
        ff_sum[:, lanes] = ff_sum[:, lanes] + jnp.sum(
            inner.astype(jnp.float32), 0, keepdims=True
        )
        turned[pl.ds(4 * D + low, BACKWARD_CHUNK), :] = inner.T
        total = total + nn(inner, wide[pl.ds(4 * D + low, BACKWARD_CHUNK), :])
    hat = hat_one[...]
    add_sum(LN1_G, total * hat)
    add_sum(LN1_B, total)
    back_first = norm_backward(total, row(LN1_G), hat, inverse_one[...])
    upstream[...] = back_first
    half = to_half(back_first)
    add_sum(O_B, half.astype(jnp.float32))
    turned[pl.ds(3 * D, D), :] = half.T
    back_mixed[...] = to_half(nn(half, wide[pl.ds(3 * D, D), :]))

    def soft_of(head):
        lanes = head // 2 * PAIR
        grads = halves(back_mixed[:, pl.ds(lanes, PAIR)])[head % 2]
        return nt(projected[:, pl.ds(2 * D + lanes, PAIR)], grads)

    def spread(head, scores, weights):
        lanes, side = head // 2 * PAIR, head % 2
        queries = halves(projected[:, pl.ds(lanes, PAIR)])[side]
        keys = halves_down(projected[:, pl.ds(D + lanes, PAIR)].T)[side]
        grads = halves(back_mixed[:, pl.ds(lanes, PAIR)])[side]
        parts = nn(keys, scores), nn(scores, queries), nn(weights, grads)
        if side == 0:
            sides.extend(parts)
            return
        value_half = to_half(sides.pop() + parts[2])
        key_half = to_half((sides.pop() + parts[1]) * SCALE)
        query_half = to_half((sides.pop() + parts[0]) * SCALE)
        joint[:, pl.ds(lanes, PAIR)] = query_half.T
        joint[:, pl.ds(D + lanes, PAIR)] = key_half
        joint[:, pl.ds(2 * D + lanes, PAIR)] = value_half
        turned[pl.ds(lanes, PAIR), :] = query_half
        turned[pl.ds(D + lanes, PAIR), :] = key_half.T
        turned[pl.ds(2 * D + lanes, PAIR), :] = value_half.T

    sides, waiting, coming = [], None, soft_of(0)
    for head in range(HEADS):
        soft = coming
        if head + 1 < HEADS:
            coming = soft_of(head + 1)
        weights = weighting[head]
        scores = to_half(weights * (soft - jnp.sum(weights * soft, 0, keepdims=True)))
        if waiting is not None:
            spread(head - 1, *waiting)
        waiting = (scores, to_half(weights))
    spread(HEADS - 1, *waiting)
    total = upstream[...]
    for part, bias in ((0, Q_B), (1, None), (2, V_B)):
        here = pl.ds(part * D, D)
        value = joint[:, here]
        if bias is not None:
            add_sum(bias, value.astype(jnp.float32))
        total = total + nn(value, wide[here, :])
    upstream[...] = total

    @pl.when(step == LAYERS - 1)
    def _():
        half = to_half(upstream[...])
        back_lift[...] = to_half(tn(normed_half[...], half))
        back_normed = nt(half, lift[...])
        hat = embed_hat[...]
        back = norm_backward(back_normed, short_row(vec, EMB_G), hat, embed_inverse[...])
        rows_out[...] = to_half(back)
        kind = kinds(lengths)
        ones = jnp.sum(back * kind, 0, keepdims=True)
        zeros = jnp.sum(back * (1.0 - kind), 0, keepdims=True)
        vector[...] = jnp.zeros_like(vector)
        parts = [jnp.sum(half.astype(jnp.float32), 0, keepdims=True)]
        parts += [sums[pl.ds(i, 1), :] for i in range(8)]
        parts += [wide_sums[pl.ds(i, 1), :] for i in range(3)]
        parts += [ff_sum[...]]
        parts += [
            jnp.sum(back_normed * hat, 0, keepdims=True),
            jnp.sum(back_normed, 0, keepdims=True),
        ]
        parts += [small_sums[pl.ds(i, 1), :] for i in range(3)]
        parts += [zeros, ones]
        at = 0
        for part in parts:
            for low in range(0, part.shape[1], 128):
                vector[pl.ds(at, 1), :] = part[:, low : low + 128]
                at += 1


def run_backward(lengths, start, wide_sums, small_sums, head, back_head, wide, tall, vec, kept, lines):
    single, half = jnp.float32, jnp.bfloat16
    last = LAYERS - 1

    def order(i):
        return last - i

    return pl.pallas_call(
        backward_kernel,
        grid=(LAYERS,),
        out_shape=[
            jax.ShapeDtypeStruct((ROWS, E), half),
            jax.ShapeDtypeStruct(back_head.shape, half),
            jax.ShapeDtypeStruct((4 * D + FF, LAYERS * ROWS), half),
            jax.ShapeDtypeStruct((LAYERS, ROWS, D), half),
            jax.ShapeDtypeStruct((lines, 128), single),
        ],
        in_specs=[pl.BlockSpec(memory_space=pltpu.SMEM)]
        + [whole_spec()] * 6
        + [lift_spec(), pl.BlockSpec(memory_space=pl.ANY)]
        + [whole_spec()] * 3
        + [
            by_layer(ROWS, 3 * D, order=order),
            by_layer(HEADS, ROWS, ROWS, order=order),
            by_layer(ROWS, D, order=order),
            by_layer(ROWS, 1, order=order),
            by_layer(ROWS, FF, order=order),
            by_layer(ROWS, D, order=order),
            by_layer(ROWS, 1, order=order),
        ],
        out_specs=[
            pl.BlockSpec((ROWS, E), lambda i: (0, 0)),
            pl.BlockSpec((E, D), lambda i: ((E + D) // E, 0)),
            pl.BlockSpec((4 * D + FF, ROWS), lambda i: (0, order(i))),
            by_layer(ROWS, D, order=order),
            pl.BlockSpec((lines, 128), lambda i: (0, 0)),
        ],
        input_output_aliases={8: 1},
        scratch_shapes=[
            VMEM_SPACE((8, D), single),
            VMEM_SPACE((1, FF), single),
            VMEM_SPACE((ROWS, D), single),
            VMEM_SPACE((ROWS, D), half),
            VMEM_SPACE((ROWS, 3 * D), half),
        ],
        compiler_params=pltpu.CompilerParams(
            dimension_semantics=("arbitrary",), vmem_limit_bytes=VMEM_ASK
        ),
    )(
        lengths,
        start,
        wide_sums,
        small_sums,
        kept["embed_hat"],
        kept["embed_inverse"],
        kept["normed_half"],
        head,
        back_head,
        wide,
        tall,
        vec,
        kept["projected"],
        kept["weighting"],
        kept["hat_one"],
        kept["inverse_one"],
        kept["slope"],
        kept["hat_two"],
        kept["inverse_two"],
    )


def local(
    mesh,
    word_table,
    position_table,
    head_weights,
    decoder_bias,
    layer_wide,
    layer_tall,
    vectors,
    word_first,
    word_second,
    position_first,
    position_second,
    head_first,
    head_second,
    decoder_first,
    decoder_second,
    wide_first,
    wide_second,
    tall_first,
    tall_second,
    vector_first,
    vector_second,
    token_ids,
    seq_lengths,
    mlm_rows,
    mlm_labels,
    sop_labels,
):
    network = Network(mesh)

    (wide, tall, head), all_facts, place, found = network.start(
        (layer_wide.T, layer_tall, head_weights.T),
        word_table,
        position_table,
        (token_ids, mlm_labels, mlm_rows, seq_lengths, sop_labels),
    )
    devices = all_facts.shape[0]
    place = place.reshape(-1, E)
    vec = vectors.reshape(-1, 128)
    kept = run_forward(seq_lengths, found, place, head, wide, tall, vec)
    (back_final, back_word_head, back_decoder, back_head, wide_sums, small_sums, totals) = (
        network.head(
            seq_lengths,
            sop_labels,
            kept["final"],
            head,
            word_table,
            decoder_bias,
            all_facts,
            vec,
        )
    )
    total = vectors.shape[0]
    share = -(-total // (devices * 1024)) * 1024
    back_rows, back_head, turned, outer, vector_grad = run_backward(
        seq_lengths,
        back_final,
        wide_sums,
        small_sums,
        head,
        back_head,
        wide,
        tall,
        vec,
        kept,
        devices * share // 128,
    )
    sums, heights, back_word, back_place, last, ends = network.finish(
        turned,
        kept["active"],
        kept["rights"].reshape(3, -1, D),
        outer.reshape(-1, D),
        back_head,
        back_rows,
        vector_grad.reshape(devices, -1, 128),
        all_facts,
        back_word_head,
        back_decoder,
        totals,
        position_table.shape[0],
    )
    wide_at, tall_at, head_at = 0, heights[0], heights[0] + heights[1]

    def turned_group(weight, first, second, low):
        return (weight.T, first.T, second.T, sums, low, LEARN_RATE)

    def flat(x):
        return x[None]

    def lines(x):
        return x.reshape(-1, 128)

    groups = (
        (word_table, word_first, word_second, back_word, 0, LEARN_RATE),
        turned_group(layer_wide, wide_first, wide_second, wide_at),
        (layer_tall, tall_first, tall_second, sums, tall_at, LEARN_RATE),
        turned_group(head_weights, head_first, head_second, head_at),
        (position_table, position_first, position_second, back_place, None, LEARN_RATE),
        (flat(decoder_bias), flat(decoder_first), flat(decoder_second), back_decoder, None)
        + (LEARN_RATE,),
        (lines(vectors), lines(vector_first), lines(vector_second), last, None, SMALL_RATE),
    )
    arrays, scalars = network.adam(ends, groups)
    word, wide, tall, head, position, decoder, vector = arrays
    grad_norm, unused, mlm_sum, sop_total, mlm_count, sop_count = scalars

    def turn(arrays):
        return [x.T for x in arrays]

    def plain(arrays):
        return [x.reshape(-1) for x in arrays]

    updates = (*word, *position, *turn(head), *plain(decoder), *turn(wide), *tall, *plain(vector))
    return (*updates, mlm_sum, mlm_count, sop_total, sop_count, grad_norm)


def solution(mesh):
    rows = P(AXES, None)
    columns = P(None, AXES)
    flat = P(AXES)
    whole = P()
    return jax.shard_map(
        functools.partial(local, mesh),
        mesh=mesh,
        in_specs=(rows, rows, columns, flat, columns, rows, whole)
        + (rows, rows) * 2
        + (columns, columns, flat, flat, columns, columns, rows, rows, whole, whole)
        + (flat,) * 5,
        out_specs=(rows,) * 6
        + (columns,) * 3
        + (flat,) * 3
        + (columns,) * 3
        + (rows,) * 3
        + (whole,) * 8,
        check_vma=False,
    )
```

```python
import functools

import jax
import jax.numpy as jnp
from jax import lax
from jax.experimental import pallas as pl
from jax.experimental.pallas import tpu as pltpu
from jax.sharding import PartitionSpec as P

D = 768
HEADS = 12
HEAD_DIM = 64
FF = 3072
E = 128
LAYERS = 4
STEP = 10
BUCKET = 128
ROWS = 2 * BUCKET

PRECISE = lax.Precision.HIGHEST
EPSILON = 1e-06
LEARN_RATE = 0.1
SMALL_RATE = 0.5
BETA_ONE = 0.9
BETA_TWO = 0.999
ADAM_EPSILON = 1e-08
WEIGHT_DECAY = 0.01
CLIP_NORM = 0.005
NORM_EPSILON = 1e-06
MASKED = -1e30
SCALE = HEAD_DIM ** (-0.5)
AXES = ("dp", "fsdp")


def to_half(x):
    return x.astype(jnp.bfloat16)


def product(a, b):
    return jnp.dot(a, b, preferred_element_type=jnp.float32)


def times_transpose(a, b):
    return lax.dot_general(a, b, (((1,), (1,)), ((), ())), preferred_element_type=jnp.float32)


def transpose_times(a, b):
    return lax.dot_general(a, b, (((0,), (0,)), ((), ())), preferred_element_type=jnp.float32)


def column_sum(x):
    return jnp.sum(x.astype(jnp.float32), 0)


def norm_forward(x):
    centre = x - jnp.mean(x, -1, keepdims=True)
    inverse = lax.rsqrt(jnp.mean(centre * centre, -1, keepdims=True) + EPSILON)
    return centre * inverse, inverse


def norm_backward(upstream, factor, hat, inverse):
    scaled = upstream * factor
    return inverse * (
        scaled
        - jnp.mean(scaled, -1, keepdims=True)
        - hat * jnp.mean(scaled * hat, -1, keepdims=True)
    )


GELU_A = 0.7978845608028654
GELU_B = 0.044715


MESH_ID = pl.DeviceIdType.MESH
VMEM_SPACE = pltpu.VMEM
VMEM_ASK = 60 * 1024 * 1024


def greet(peers):
    barrier = pltpu.get_barrier_semaphore()
    count = 0
    for present, who in peers:
        if present is None:
            pl.semaphore_signal(barrier, inc=1, device_id=who, device_id_type=MESH_ID)
            count = count + 1
        else:

            @pl.when(present)
            def _(who=who):
                pl.semaphore_signal(barrier, inc=1, device_id=who, device_id_type=MESH_ID)

            count = count + present.astype(jnp.int32)
    pl.semaphore_wait(barrier, count)


def maybe(condition, action):
    if condition is None:
        action()
    else:
        pl.when(condition)(action)


def remote(source, target, send, receive, who):
    return pltpu.make_async_remote_copy(
        src_ref=source,
        dst_ref=target,
        send_sem=send,
        recv_sem=receive,
        device_id=who,
        device_id_type=MESH_ID,
    )


OWN, ACROSS_X, ACROSS_Y, DIAGONAL = 0, 1, 2, 3


def cuts_of(rows, share):
    tail = max(32, round(rows * share / 32) * 32)
    head = rows - tail
    return ((0, head), (head, rows))


GATHER_TAIL, FINISH_TAIL = 0.3, 0.2


def half_of(span, which):
    low, high = span
    middle = (low + high) // 2
    return (low, middle) if which == 0 else (middle, high)


def places():
    z, f = lax.axis_index("dp"), lax.axis_index("fsdp")
    q, c = f // 2, lax.rem(f, 2)
    qx = q + 1 - 2 * lax.rem(q, 2)
    qy = lax.rem(q + 2, 4)
    qd = qx + qy - q
    return z, c, (q, qx, qy, qd)


def gather_stages(planes, rows, members, x, outs, buf, sems, where, opening):
    out_sem, send, recv, side_send, side_recv = sems
    z, c, cols = where
    cuts = cuts_of(rows, GATHER_TAIL)
    at_x, at_y, mate = (z, cols[1] * 2 + c), (z, cols[2] * 2 + c), (z, cols[0] * 2 + 1 - c)
    above, below = z < planes - 1, z > 0
    up, down = (z + 1, cols[0] * 2 + c), (z - 1, cols[0] * 2 + c)
    sent = []

    def block(zs, col, core, span):
        return buf.at[zs, cols[col], core, pl.ds(span[0], span[1] - span[0])]

    def push(condition, zs, col, span, who, slot, receive, mine=False):
        def make():
            here = block(zs, col, c, span)
            source = x.at[pl.ds(span[0], span[1] - span[0])] if mine else here
            return remote(source, here, send.at[slot[0], zs, slot[1]], receive, who)

        maybe(condition, lambda: make().start())
        sent.append((condition, make))

    def await_block(zs, col, span, receive, core=None):
        here = block(zs, col, c if core is None else core, span)
        remote(here, here, send.at[0, 0, 0], receive, mate).wait_recv()

    def deliver(zs, col, core, span):
        for index, (out, (low, high)) in enumerate(zip(outs, members)):
            first, last = max(low, span[0]), min(high, span[1])
            if first < last:
                pltpu.make_async_copy(
                    buf.at[zs, cols[col], core, pl.ds(first, last - first)],
                    out.at[zs, cols[col], core, pl.ds(first - low, last - first)],
                    out_sem.at[index],
                ).start()

    def share(condition, part, zs, col, span, kind, mine=False):
        def make():
            here = block(zs, col, c, span)
            source = x.at[pl.ds(span[0], span[1] - span[0])] if mine else here
            return remote(
                source, here, side_send.at[part, zs, kind], side_recv.at[part, zs, kind], mate
            )

        def action():
            make().start()
            if not mine:
                deliver(zs, col, c, span)

        maybe(condition, action)
        sent.append((condition, make))
        shared.append((condition, part, zs, col, span, kind))

    shared = []
    whole = [cuts[0], cuts[1]]
    for part in (0, 1):
        push(above, z, OWN, whole[part], up, (part, 2), recv.at[part, z, OWN], True)
        push(below, z, OWN, whole[part], down, (part, 3), recv.at[part, z, OWN], True)
    for part in (1, 0):
        if part == 0:
            opening()
        push(None, z, OWN, whole[part], at_x, (part, 0), recv.at[part, z, ACROSS_X], True)
        push(None, z, OWN, whole[part], at_y, (part, 1), recv.at[part, z, ACROSS_Y], True)
    for part in (0, 1):
        share(None, part, z, OWN, whole[part], 0, True)
    own_copy = pltpu.make_async_copy(x, buf.at[z, cols[0], c], out_sem.at[len(members)])
    own_copy.start()

    def turn(condition, part, zs):
        span = whole[part]
        for col, which, who, slot in ((ACROSS_X, 1, at_y, 4), (ACROSS_Y, 0, at_x, 5)):
            maybe(
                condition,
                lambda col=col: await_block(zs, col, span, recv.at[part, zs, col]),
            )
            push(condition, zs, col, half_of(span, which), who, (part, slot), recv.at[part, zs, 4 + which])
            if part == 1:
                push(above, zs, col, span, up, (1, 4 + 2 * col), recv.at[1, zs, col])
                push(below, zs, col, span, down, (1, 5 + 2 * col), recv.at[1, zs, col])
            share(condition, part, zs, col, span, col)

    yield
    turn(None, 1, z)
    yield
    for which in (0, 1):
        await_block(z, DIAGONAL, half_of(whole[1], which), recv.at[1, z, 4 + which])
    push(above, z, DIAGONAL, whole[1], up, (1, 10), recv.at[1, z, DIAGONAL])
    push(below, z, DIAGONAL, whole[1], down, (1, 11), recv.at[1, z, DIAGONAL])
    share(None, 1, z, DIAGONAL, whole[1], 3)
    yield
    turn(None, 0, z)

    def settle(upto):
        while len(shared) > upto:
            condition, part, zs, col, span, kind = shared.pop(0)

            def action():
                await_block(zs, col, span, side_recv.at[part, zs, kind], 1 - c)
                deliver(zs, col, 1 - c, span)

            maybe(condition, action)

    for step in range(1, planes):
        yield
        ways = ((z - step >= 0, z - step, above, up), (z + step < planes, z + step, below, down))
        for valid, zs, further, onward in ways:
            go = jnp.logical_and(valid, further)
            pl.when(valid)(
                lambda zs=zs: await_block(zs, OWN, whole[0], recv.at[0, zs, OWN])
            )
            push(go, zs, OWN, whole[0], onward, (0, 2), recv.at[0, zs, OWN])
            push(valid, zs, OWN, whole[0], at_x, (0, 0), recv.at[0, zs, ACROSS_X])
            push(valid, zs, OWN, whole[0], at_y, (0, 1), recv.at[0, zs, ACROSS_Y])
            share(valid, 0, zs, OWN, whole[0], 0)
        yield
        for valid, zs, further, onward in ways:
            go = jnp.logical_and(valid, further)
            for col in (OWN, ACROSS_X, ACROSS_Y, DIAGONAL):
                pl.when(valid)(
                    lambda zs=zs, col=col: await_block(zs, col, whole[1], recv.at[1, zs, col])
                )
                push(go, zs, col, whole[1], onward, (1, col), recv.at[1, zs, col])
                share(valid, 1, zs, col, whole[1], col)
        yield
        for valid, zs, further, onward in ways:
            turn(valid, 0, zs)
        settle(8)
    yield
    own_copy.wait()
    deliver(z, OWN, c, (0, rows))
    everywhere = [(None, z)] + [
        (valid, zs)
        for step in range(1, planes)
        for valid, zs in ((z - step >= 0, z - step), (z + step < planes, z + step))
    ]
    for condition, zs in everywhere:
        for which in (0, 1):
            span = half_of(whole[0], which)
            maybe(
                condition,
                lambda zs=zs, which=which, span=span: await_block(
                    zs, DIAGONAL, span, recv.at[0, zs, 4 + which]
                ),
            )
            share(condition, 0, zs, DIAGONAL, span, 3 + which)
    settle(0)
    for condition, make in sent:
        maybe(condition, lambda make=make: make().wait_send())
    for index, (out, (low, high)) in enumerate(zip(outs, members)):
        pltpu.make_async_copy(
            buf.at[:, :, :, pl.ds(low, high - low)], out, out_sem.at[index]
        ).wait()


def select_stages(planes, facts, own_word, found, refs, where, offset):
    part, side, plane_in, middle, line_in, turned, sems_send, sems_recv = refs
    z, c, cols = where
    q = cols[0]
    f = q * 2 + c
    mate = (z, q * 2 + 1 - c)
    words = own_word.shape[0]
    line = [(lax.rem(z + d, planes), f) for d in range(1, planes)]
    turned[...] = to_half(own_word[...].T)
    yield

    def mate_message(col):
        return remote(
            part.at[:, col, 1 - c], side.at[:, col], sems_send.at[0, col], sems_recv.at[0, col], mate
        )

    def plane_message(col):
        return remote(
            part.at[:, col, c],
            plane_in.at[col],
            sems_send.at[1, col],
            sems_recv.at[1, col],
            (z, cols[col] * 2 + c),
        )

    def line_message(d, who):
        return remote(
            middle.at[who[0]], line_in.at[d], sems_send.at[2, d], sems_recv.at[2, d], who
        )

    def merge(col):
        mate_message(col).wait_recv()
        for zt in range(planes):
            part[zt, col, c] = part[zt, col, c] + side[zt, col]
        if col != OWN:
            plane_message(col).start()

    order = (DIAGONAL, ACROSS_X, ACROSS_Y, OWN)
    for place, col in enumerate(order):

        def body(n, unused, col=col):
            zt, core = n // 2, lax.rem(n, 2)
            ids = facts[zt, cols[col] * 2 + core]
            row = lax.broadcasted_iota(jnp.int32, (words, BUCKET), 0) + offset
            picks = jnp.concatenate(
                [to_half((row == ids[i : i + 1, :]).astype(jnp.float32)) for i in (0, 1)], 1
            )
            part[zt, col, core] = to_half(nn(turned[...], picks))
            return unused

        lax.fori_loop(0, 2 * planes, body, 0)
        mate_message(col).start()
        if place > 0:
            merge(order[place - 1])
        yield
    merge(OWN)
    total = part[:, OWN, c]
    yield
    for col in order[:3]:
        plane_message(col).wait_recv()
        total = total + plane_in[col]
    middle[...] = total
    for d, who in enumerate(line):
        line_message(d, who).start()
    yield
    total = middle[z]
    for d, who in enumerate(line):
        line_message(d, who).wait_recv()
        total = total + line_in[d]
    found[...] = total.astype(jnp.float32).T
    for col in order:
        mate_message(col).wait_send()
    for col in order[:3]:
        plane_message(col).wait_send()
    for d, who in enumerate(line):
        line_message(d, who).wait_send()


PLAN = (1, 2, 1, 1, 0, 1, 0, 0, 0, 0, 1)


def start_kernel(
    planes,
    rows,
    members,
    own_wide,
    own_tall,
    own_head,
    own_word,
    own_place,
    ids,
    labels,
    slot_rows,
    lengths,
    sop_labels,
    *refs,
):
    width = 8
    count = len(members)
    outs, (facts, place, found) = refs[:count], refs[count : count + 3]
    x, buf = refs[count + 3 : count + 5]
    gather_sems = refs[count + 5 : count + 10]
    select_refs = refs[count + 10 : count + 18]
    line_send, line_recv, plane_send, plane_recv = refs[count + 18 :]
    where = places()
    z, c, cols = where
    f = cols[0] * 2 + c
    line = [(lax.rem(z + d, planes), f) for d in range(1, planes)]
    plane = [(z, lax.rem(f + d, width)) for d in range(1, width)]
    lane = lax.broadcasted_iota(jnp.int32, (1, 128), 1)
    rest = jnp.full((1, 128 - labels.shape[1]), -1, jnp.int32)
    note = jnp.zeros((1, 128), jnp.int32)
    for at, value in enumerate((lengths[0], lengths[1], sop_labels[0], sop_labels[1])):
        note = note + jnp.where(lane == at, value, 0)
    facts[z, f] = jnp.concatenate(
        [
            ids[:, :128],
            ids[:, 128:],
            jnp.concatenate([labels[...], rest], 1),
            jnp.concatenate([slot_rows[...], rest], 1),
            note,
            jnp.zeros((3, 128), jnp.int32),
        ],
        0,
    )
    place[z, f] = to_half(own_place[...])
    greet([(None, who) for who in line + plane])
    pairs = (facts, place)

    def along(i, d, who):
        here = pairs[i].at[z, f]
        return remote(here, here, line_send.at[i, d], line_recv.at[i, d], who)

    def around(i, d, who, source):
        here = pairs[i].at[:, source]
        return remote(here, here, plane_send.at[i, d], plane_recv.at[i, d], who)

    for d, who in enumerate(line):
        for i in (0, 1):
            along(i, d, who).start()
    for (low, high), piece in zip(members, (own_wide[...], own_tall[...], own_head[...])):
        x[low:high] = to_half(piece)

    def opening():
        for d, who in enumerate(line):
            for i in (0, 1):
                source = pairs[i].at[lax.rem(z - d - 1 + planes, planes), f]
                remote(source, source, line_send.at[i, d], line_recv.at[i, d], who).wait_recv()
        for d, who in enumerate(plane):
            for i in (0, 1):
                around(i, d, who, f).start()

    gather = gather_stages(planes, rows, members, x, outs, buf, gather_sems, where, opening)
    offset = (z * width + f) * own_word.shape[0]
    select = select_stages(planes, facts, own_word, found, select_refs, where, offset)
    done = object()
    next(gather)
    next(select)
    for d in range(1, width):
        source = lax.rem(f - d + width, width)
        for i in (0, 1):
            around(i, d - 1, mate_of(where), source).wait_recv()
    for number in range(64):
        for unused in range(PLAN[number] if number < len(PLAN) else 1):
            next(select, done)
        if next(gather, done) is done:
            break
    for unused in select:
        pass
    for d, who in enumerate(line):
        for i in (0, 1):
            along(i, d, who).wait_send()
    for d, who in enumerate(plane):
        for i in (0, 1):
            around(i, d, who, f).wait_send()


def mate_of(where):
    z, c, cols = where
    return (z, cols[0] * 2 + 1 - c)


def run_start(shards, own_word, own_place, batch, mesh_shape, identity):
    planes, width = mesh_shape
    heights = tuple(shard.shape[0] for shard in shards)
    rows, columns = sum(heights), shards[1].shape[1]
    members, low = [], 0
    for height in heights:
        members.append((low, low + height))
        low += height
    half, single = jnp.bfloat16, jnp.float32
    vmem = pl.BlockSpec(memory_space=VMEM_SPACE)
    dma = pltpu.SemaphoreType.DMA
    words, features = own_word.shape
    block = (features, ROWS)
    *outs, facts, place, found = pl.pallas_call(
        functools.partial(start_kernel, planes, rows, tuple(members)),
        out_shape=[
            jax.ShapeDtypeStruct((planes, width // 2, 2, height, columns), half)
            for height in heights
        ]
        + [
            jax.ShapeDtypeStruct((planes, width, 8, 128), jnp.int32),
            jax.ShapeDtypeStruct((planes, width, *own_place.shape), half),
            jax.ShapeDtypeStruct((ROWS, features), single),
        ],
        in_specs=[vmem] * 8 + [pl.BlockSpec(memory_space=pltpu.SMEM)] * 2,
        out_specs=[pl.BlockSpec(memory_space=pl.ANY)] * len(heights) + [vmem] * 3,
        scratch_shapes=[
            VMEM_SPACE((rows, columns), half),
            VMEM_SPACE((planes, width // 2, 2, rows, columns), half),
            dma((len(heights) + 1,)),
            dma((2, planes, 12)),
            dma((2, planes, 6)),
            dma((2, planes, 5)),
            dma((2, planes, 5)),
            VMEM_SPACE((planes, 4, 2, *block), half),
            VMEM_SPACE((planes, 4, *block), half),
            VMEM_SPACE((4, planes, *block), half),
            VMEM_SPACE((planes, *block), half),
            VMEM_SPACE((planes - 1, *block), half),
            VMEM_SPACE((features, words), half),
            dma((3, 4)),
            dma((3, 4)),
            dma((2, planes)),
            dma((2, planes)),
            dma((2, width)),
            dma((2, width)),
        ],
        compiler_params=pltpu.CompilerParams(
            collective_id=identity, has_side_effects=True, vmem_limit_bytes=VMEM_ASK
        ),
    )(*shards, own_word, own_place, *[x[None] for x in batch[:3]], *batch[3:])
    weights = [out.reshape(-1, columns) for out in outs]
    devices = planes * width
    return (
        weights,
        facts.reshape(devices, 8, 128),
        place.reshape(devices, *own_place.shape),
        found,
    )


def accumulate(target, sources, height):
    step = 32

    def body(i, unused):
        rows = pl.ds(pl.multiple_of(i * step, step), step)
        total = sources[0][rows].astype(jnp.float32)
        for source in sources[1:]:
            total = total + source[rows].astype(jnp.float32)
        target[rows] = total.astype(target.dtype)
        return unused

    lax.fori_loop(0, height // step, body, 0)


ROWS_AT = 1
TURN_AT = 5
MATE_AT = 9


def far_first(i, z, planes):
    low = (2 * z < planes).astype(jnp.int32)
    falling = planes - 1 - i - (i >= planes - 1 - z).astype(jnp.int32)
    rising = i + (i >= z).astype(jnp.int32)
    last = (jnp.int32(i) == planes - 1).astype(jnp.int32)
    return last * z + (1 - last) * (low * falling + (1 - low) * rising)


def finish_kernel(
    planes,
    heights,
    split,
    left_wide,
    left_tall,
    rights_from,
    outer_from,
    head_grad,
    own_rows,
    vector_terms,
    facts,
    base_word,
    back_decoder,
    totals,
    out,
    word_grad,
    place_grad,
    last,
    ends,
    all_rows,
    both,
    side,
    half_in,
    full_in,
    line_in,
    tail_line,
    tail_half,
    tail_full,
    wide_buf,
    tall_buf,
    vector_in,
    vector_mid,
    vector_last,
    fetch,
    head_load,
    side_send,
    side_recv,
    send,
    recv,
    tail_send,
    tail_recv,
    row_send,
    row_recv,
    vec_send,
    vec_recv,
    end_send,
    end_recv,
    rights,
    outer,
    right_load,
):
    width = 8
    right_copies = [
        pltpu.make_async_copy(rights_from.at[i], rights.at[i], right_load.at[i]) for i in range(3)
    ]
    right_copies.append(pltpu.make_async_copy(outer_from, outer, right_load.at[3]))
    for copy in right_copies:
        copy.start()
    wide_height, tall_height, head_height = heights
    rows = wide_height + tall_height + head_height
    z, c, cols = places()
    q = cols[0]
    f = q * 2 + c
    x, y = lax.rem(q, 2), q // 2
    cuts = cuts_of(rows, FINISH_TAIL)
    head, tail = cuts
    head_rows, tail_rows = head[1] - head[0], tail[1] - tail[0]
    at_x, at_y, mate = (z, cols[1] * 2 + c), (z, cols[2] * 2 + c), (z, q * 2 + 1 - c)
    above, below = z < planes - 1, z > 0
    up, down = (z + 1, f), (z - 1, f)
    line = [(lax.rem(z + d, planes), f) for d in range(1, planes)]
    plane = [(z, lax.rem(f + d, width)) for d in range(1, width)]
    greet([(None, who) for who in line + plane])
    order = (DIAGONAL, ACROSS_X, ACROSS_Y, OWN)
    sent = []

    def push(condition, make):
        maybe(condition, lambda: make().start())
        sent.append((condition, make))

    def piece(ref, span):
        return ref.at[pl.ds(span[0], span[1] - span[0])]

    def plane_at(i):
        return far_first(i, z, planes)

    def turn_of(n):
        m = n - 1 - 3 * (n == 0).astype(jnp.int32) + (n > 4 * planes - 4).astype(jnp.int32)
        group, j = (m + 4) // 4 - 1, lax.rem(m + 4, 4)
        ahead = (j == 0).astype(jnp.int32)
        return group + ahead, DIAGONAL * ahead + j * (j < 3).astype(jnp.int32)

    def chip_of(n):
        i, col = turn_of(n)
        flip_x, flip_y = lax.rem(col, 2), col // 2
        return plane_at(i) * 4 + 2 * lax.rem(y + flip_y, 2) + lax.rem(x + flip_x, 2)

    def fetches(n):
        k, slot = chip_of(n), lax.rem(n, 2)
        wide_rows = pl.ds(pl.multiple_of(k * 2 * wide_height, 16), 2 * wide_height)
        tall_rows = pl.ds(pl.multiple_of(k * 2 * tall_height, 16), 2 * tall_height)
        return (
            pltpu.make_async_copy(
                left_wide.at[wide_rows], wide_buf.at[slot], fetch.at[0, slot]
            ),
            pltpu.make_async_copy(
                left_tall.at[tall_rows], tall_buf.at[slot], fetch.at[1, slot]
            ),
        )

    for copy in fetches(jnp.int32(0)):
        copy.start()

    def vector_first(d, who):
        return remote(
            vector_terms.at[:, who[1]], vector_in.at[d], vec_send.at[0, d], vec_recv.at[0, d], who
        )

    def vector_second(d, who):
        return remote(
            vector_mid.at[who[0]], vector_last.at[d], vec_send.at[1, d], vec_recv.at[1, d], who
        )

    def row_line(d, who):
        return remote(
            own_rows, all_rows.at[z, q, c], row_send.at[0, d], row_recv.at[0, d], who
        )

    def row_plane(col):
        return remote(
            all_rows.at[:, q, c],
            all_rows.at[:, q, c],
            row_send.at[1, col],
            row_recv.at[1, col],
            (z, cols[col] * 2 + c),
        )

    def row_turn(which):
        col, who = ((ACROSS_Y, at_x), (ACROSS_X, at_y))[which]
        here = all_rows.at[:, cols[col], c, pl.ds(which * BUCKET, BUCKET)]
        return remote(here, here, row_send.at[2, 1 + which], row_recv.at[2, 1 + which], who)

    def row_mate():
        return remote(
            all_rows.at[:, :, c], all_rows.at[:, :, c], row_send.at[2, 0], row_recv.at[2, 0], mate
        )

    for d, who in enumerate(line):
        push(None, functools.partial(row_line, d, who))
    for d, who in enumerate(plane):
        push(None, functools.partial(vector_first, d, who))
    all_rows[z, q, c] = own_rows[...]
    head_copies = []
    for col in order:
        copy = pltpu.make_async_copy(
            head_grad.at[:, cols[col]],
            both.at[:, col, :, pl.ds(wide_height + tall_height, head_height)],
            head_load.at[col],
        )
        copy.start()
        head_copies.append(copy)

    def side_message(zt, col):
        return remote(
            both.at[zt, col, 1 - c],
            side.at[zt, col],
            side_send.at[col, zt],
            side_recv.at[col, zt],
            mate,
        )

    def half_message(zt, which):
        return remote(
            piece(both.at[zt, DIAGONAL, c], half_of(head, which)),
            half_in.at[which, zt],
            send.at[0, which, zt],
            recv.at[0, which, zt],
            (at_x, at_y)[which],
        )

    def full_message(zt, which):
        return remote(
            piece(both.at[zt, (ACROSS_X, ACROSS_Y)[which], c], head),
            full_in.at[which, zt],
            send.at[1, which, zt],
            recv.at[1, which, zt],
            (at_x, at_y)[which],
        )

    def line_message(zt, way):
        return remote(
            piece(both.at[zt, OWN, c], head),
            line_in.at[way, zt],
            send.at[2, way, zt],
            recv.at[2, way, zt],
            (up, down)[way],
        )

    def tail_message(zt, way):
        return remote(
            both.at[zt, :, c, pl.ds(tail[0], tail_rows)],
            tail_line.at[way, zt],
            tail_send.at[way, zt],
            tail_recv.at[way, zt],
            (up, down)[way],
        )

    def merged(zt, col):
        side_message(zt, col).wait_recv()
        mine = both.at[zt, col, c]
        accumulate(mine, [mine, side.at[zt, col]], rows)

    def second(zt):
        for which, col in ((0, ACROSS_X), (1, ACROSS_Y)):
            half_message(zt, 1 - which).wait_recv()
            target = piece(both.at[zt, col, c], half_of(head, 1 - which))
            accumulate(target, [target, half_in.at[1 - which, zt]], head_rows // 2)
            full_message(zt, which).start()

    def tail_add(zt, way):
        tail_message(zt, way).wait_recv()
        for col in range(4):
            target = piece(both.at[zt, col, c], tail)
            accumulate(target, [target, tail_line.at[way, zt, col]], tail_rows)

    def ways(zt):
        return ((0, zt > z, below), (1, zt < z, above))

    def tail_open(zt):
        for way, valid, behind in ways(zt):
            go = jnp.logical_and(valid, jnp.logical_not(behind))
            pl.when(go)(lambda way=way: tail_message(zt, way).start())

    def tail_pass(zt):
        for way, valid, behind in ways(zt):

            def action(way=way):
                tail_add(zt, way)
                tail_message(zt, way).start()

            pl.when(jnp.logical_and(valid, behind))(action)

    def line_add(zt, way):
        line_message(zt, way).wait_recv()
        mine = piece(both.at[zt, OWN, c], head)
        accumulate(mine, [mine, line_in.at[way, zt]], head_rows)

    def third(zt):
        for which in (0, 1):
            full_message(zt, which).wait_recv()
        base = [piece(both.at[zt, OWN, c], head), full_in.at[0, zt], full_in.at[1, zt]]
        accumulate(base[0], base, head_rows)
        for way, valid, behind in ways(zt):
            go = jnp.logical_and(valid, jnp.logical_not(behind))
            pl.when(go)(lambda way=way: line_message(zt, way).start())

    def line_pass(zt):
        for way, valid, behind in ways(zt):

            def action(way=way):
                line_add(zt, way)
                line_message(zt, way).start()

            pl.when(jnp.logical_and(valid, behind))(action)

    def after(n):
        i, col = turn_of(n)
        zt = plane_at(i)
        merged(zt, col)

        @pl.when(col == DIAGONAL)
        def _():
            half_message(zt, 0).start()
            half_message(zt, 1).start()

        @pl.when(col == OWN)
        def _():
            second(zt)
            pl.when(i < planes - 1)(lambda: tail_open(zt))
            pl.when(i > 0)(lambda: tail_pass(plane_at(i - 1)))
            pl.when(i > 0)(lambda: third(plane_at(i - 1)))
            pl.when(i > 1)(lambda: line_pass(plane_at(i - 2)))

    for copy in head_copies + right_copies:
        copy.wait()

    def turn_rows():
        for step in (ACROSS_X, ACROSS_Y):
            here = all_rows.at[:, cols[step], c]
            remote(here, here, row_send.at[1, step], row_recv.at[1, step], mate).wait_recv()
        for which in (0, 1):
            row_turn(which).start()

    def share_rows():
        for which in (0, 1):
            here = all_rows.at[:, cols[DIAGONAL], c, pl.ds(which * BUCKET, BUCKET)]
            remote(
                here, here, row_send.at[2, 1 + which], row_recv.at[2, 1 + which], mate
            ).wait_recv()
        row_mate().start()

    def sum_vector():
        total = vector_mid[z]
        for d, who in enumerate(line):
            vector_second(d, who).wait_recv()
            total = total + vector_last[d]
        last[z, f, 0:8] = total

    def body(n, unused):
        for copy in fetches(n):
            copy.wait()

        @pl.when(n + 1 < 4 * planes)
        def _():
            for copy in fetches(n + 1):
                copy.start()

        (i, col), k, slot = turn_of(n), chip_of(n), lax.rem(n, 2)
        zt = plane_at(i)
        region = (k >= split[0]).astype(jnp.int32) + (k >= split[1]).astype(jnp.int32)
        product_wide = to_half(nn(wide_buf[slot], rights[region]))
        both[zt, col, 0, :wide_height] = product_wide[:wide_height]
        both[zt, col, 1, :wide_height] = product_wide[wide_height:]
        product_tall = to_half(nn(tall_buf[slot], outer[...]))
        here = slice(wide_height, wide_height + tall_height)
        both[zt, col, 0, here] = product_tall[:tall_height]
        both[zt, col, 1, here] = product_tall[tall_height:]
        side_message(zt, col).start()
        pl.when(n > 0)(lambda: after(n - 1))

        @pl.when(n == ROWS_AT)
        def _():
            for d, who in enumerate(line):
                row_line(d, who).wait_recv()
            for step in (ACROSS_X, ACROSS_Y):
                row_plane(step).start()
            total = vector_terms[:, f]
            for d, who in enumerate(plane):
                vector_first(d, who).wait_recv()
                total = total + vector_in[d]
            vector_mid[...] = total
            for d, who in enumerate(line):
                vector_second(d, who).start()

        pl.when(n == TURN_AT)(turn_rows)
        pl.when(n == MATE_AT)(share_rows)

        return unused

    lax.fori_loop(0, 4 * planes, body, 0)
    after(jnp.int32(4 * planes - 1))
    targets = [plane_at(i) for i in range(planes)]
    sum_vector()
    here = all_rows.at[:, :, 1 - c]
    remote(here, here, row_send.at[2, 0], row_recv.at[2, 0], mate).wait_recv()
    words = word_grad.shape[0]
    offset = (z * width + f) * words

    def look_back(first, after):
        def body(n, unused):
            zt, chip = n // 4, lax.rem(n, 4)
            row = lax.broadcasted_iota(jnp.int32, (words, BUCKET), 0) + offset
            total = word_grad[...]
            for core in (0, 1):
                ids = facts[zt, chip * 2 + core]
                picks = jnp.concatenate(
                    [to_half((row == ids[i : i + 1, :]).astype(jnp.float32)) for i in (0, 1)], 1
                )
                total = total + nn(picks, all_rows[zt, chip, core])
            word_grad[...] = total
            return unused

        lax.fori_loop(first, after, body, 0)

    word_grad[...] = base_word[...]

    def tail_half_message(which):
        return remote(
            piece(both.at[z, DIAGONAL, c], half_of(tail, which)),
            tail_half.at[which],
            tail_send.at[2, which],
            tail_recv.at[2, which],
            (at_x, at_y)[which],
        )

    def tail_full_message(which):
        return remote(
            piece(both.at[z, (ACROSS_X, ACROSS_Y)[which], c], tail),
            tail_full.at[which],
            tail_send.at[3, which],
            tail_recv.at[3, which],
            (at_x, at_y)[which],
        )

    pl.when(below)(lambda: tail_add(z, 0))
    pl.when(above)(lambda: tail_add(z, 1))
    for which in (0, 1):
        push(None, functools.partial(tail_half_message, which))
    line_pass(targets[planes - 2])
    look_back(0, 4 * planes)
    for which, col in ((1, ACROSS_X), (0, ACROSS_Y)):
        tail_half_message(which).wait_recv()
        target = piece(both.at[z, col, c], half_of(tail, which))
        accumulate(target, [target, tail_half.at[which]], tail_rows // 2)
    for which in (0, 1):
        push(None, functools.partial(tail_full_message, which))
    for which in (0, 1):
        full_message(z, which).wait_recv()
    goal = piece(out, head)
    accumulate(
        goal, [piece(both.at[z, OWN, c], head), full_in.at[0, z], full_in.at[1, z]], head_rows
    )
    for present, way in ((below, 0), (above, 1)):

        def add(way=way):
            line_message(z, way).wait_recv()
            accumulate(goal, [goal, line_in.at[way, z]], head_rows)

        pl.when(present)(add)
    for which in (0, 1):
        tail_full_message(which).wait_recv()
    accumulate(
        piece(out, tail),
        [piece(both.at[z, OWN, c], tail), tail_full.at[0], tail_full.at[1]],
        tail_rows,
    )
    height = place_grad.shape[0]
    own = z * width + f
    low_half = (own * height < BUCKET).astype(jnp.float32)
    high_half = (own * height < 2 * BUCKET).astype(jnp.float32) - low_half
    slot = pl.multiple_of(lax.rem(own * height, BUCKET), height)
    lane = lax.broadcasted_iota(jnp.int32, (1, 128), 1)
    grad = jnp.zeros((height, 128), jnp.float32)
    for zt in range(planes):
        for chip in range(4):
            for core in (0, 1):
                note = facts[zt, chip * 2 + core, 4:5, :]
                two = jnp.sum(
                    jnp.where(lane == 1, (note > 0).astype(jnp.float32), 0.0), 1, keepdims=True
                )
                lower = all_rows[zt, chip, core, pl.ds(slot, height)].astype(jnp.float32)
                upper = all_rows[zt, chip, core, pl.ds(BUCKET + slot, height)].astype(jnp.float32)
                grad = grad + low_half * (lower + two * upper) + high_half * (1.0 - two) * upper
    place_grad[...] = grad
    squares = jnp.sum(grad * grad) + jnp.sum(back_decoder[...] * back_decoder[...])
    squares = squares + jnp.sum(word_grad[...] * word_grad[...])
    squares = squares + jnp.sum(out[...] * out[...])
    last[z, f, 8:16] = jnp.concatenate(
        [totals[...], jnp.where(lane == 0, squares, 0.0), jnp.zeros((6, 128), jnp.float32)], 0
    )
    first_copies, second_copies = [], []
    for d, who in enumerate(line):
        here = last.at[z, f]
        first_copies.append(remote(here, here, end_send.at[0, d], end_recv.at[0, d], who))
        first_copies[-1].start()
    for d, who in enumerate(line):
        here = last.at[lax.rem(z - d - 1 + planes, planes), f]
        remote(here, here, end_send.at[0, d], end_recv.at[0, d], who).wait_recv()
    for d, who in enumerate(plane):
        here = last.at[:, f]
        second_copies.append(remote(here, here, end_send.at[1, d], end_recv.at[1, d], who))
        second_copies[-1].start()
    for d, who in enumerate(plane):
        here = last.at[:, lax.rem(f - d - 1 + width, width)]
        remote(here, here, end_send.at[1, d], end_recv.at[1, d], who).wait_recv()
    summed = last[...]
    tails = jnp.sum(jnp.sum(summed[:, :, 8:16], 0), 0)
    squares = jnp.sum(summed[:, :, 0:8] * summed[:, :, 0:8]) + jnp.sum(tails[1:2, :])
    norm = jnp.sqrt(jnp.broadcast_to(squares, (1, 128)))
    factor = jnp.minimum(1.0, CLIP_NORM / (norm + NORM_EPSILON))
    mlm = totals[0:1, :] - jnp.sum(jnp.where(lane == 1, tails[0:1, :], 0.0))
    def count(at):
        own = jnp.where(lane == at, totals[0:1, :], 0.0)
        return jnp.broadcast_to(jnp.sum(own, 1, keepdims=True), (1, 128))

    sop = jnp.zeros((1, 128), jnp.float32) + jnp.sum(jnp.where(lane == 2, tails[0:1, :], 0.0))
    ends[...] = jnp.concatenate(
        [norm, factor, mlm, sop, count(3), count(4), jnp.zeros((2, 128), jnp.float32)], 0
    )
    for copy in first_copies + second_copies:
        copy.wait_send()
    row_mate().wait_send()
    for condition, make in sent:
        maybe(condition, lambda make=make: make().wait_send())
    for zt in targets:
        for col in order:
            side_message(zt, col).wait_send()
        for which in (0, 1):
            half_message(zt, which).wait_send()
            full_message(zt, which).wait_send()
        for way, valid in ((0, zt > z), (1, zt < z)):

            def done(zt=zt, way=way):
                tail_message(zt, way).wait_send()
                line_message(zt, way).wait_send()

            pl.when(valid)(done)
    for step in (ACROSS_X, ACROSS_Y):
        row_plane(step).wait_send()
    for which in (0, 1):
        row_turn(which).wait_send()
    for d, who in enumerate(line):
        vector_second(d, who).wait_send()


def run_finish(
    left_wide,
    left_tall,
    rights,
    outer,
    head_grad,
    own_rows,
    vector_terms,
    facts,
    base_word,
    back_decoder,
    totals,
    places_count,
    mesh_shape,
    identity,
):
    planes, width = mesh_shape
    devices = planes * width
    columns = outer.shape[1]
    heights = (
        left_wide.shape[0] // devices,
        left_tall.shape[0] // devices,
        head_grad.shape[0] // devices,
    )
    rows = sum(heights)
    long = left_wide.shape[1]
    split = (3 * D // (2 * heights[0]), 4 * D // (2 * heights[0]))
    head, tail = (high - low for low, high in cuts_of(rows, FINISH_TAIL))
    half, single = jnp.bfloat16, jnp.float32
    block = vector_terms.shape[1:]
    vmem = pl.BlockSpec(memory_space=VMEM_SPACE)
    any_space = pl.BlockSpec(memory_space=pl.ANY)
    dma = pltpu.SemaphoreType.DMA
    out, word_grad, place_grad, last, ends = pl.pallas_call(
        functools.partial(finish_kernel, planes, heights, split),
        out_shape=[
            jax.ShapeDtypeStruct((rows, columns), single),
            jax.ShapeDtypeStruct(base_word.shape, single),
            jax.ShapeDtypeStruct((places_count, 128), single),
            jax.ShapeDtypeStruct((planes, width, 16, 128), single),
            jax.ShapeDtypeStruct((8, 128), single),
        ],
        in_specs=[any_space] * 5 + [vmem] * 6,
        out_specs=[vmem] * 5,
        scratch_shapes=[
            VMEM_SPACE((planes, width // 2, 2, *own_rows.shape), half),
            VMEM_SPACE((planes, 4, 2, rows, columns), half),
            VMEM_SPACE((planes, 4, rows, columns), half),
            VMEM_SPACE((2, planes, head // 2, columns), half),
            VMEM_SPACE((2, planes, head, columns), half),
            VMEM_SPACE((2, planes, head, columns), half),
            VMEM_SPACE((2, planes, 4, tail, columns), half),
            VMEM_SPACE((2, tail // 2, columns), half),
            VMEM_SPACE((2, tail, columns), half),
            VMEM_SPACE((2, 2 * heights[0], long), half),
            VMEM_SPACE((2, 2 * heights[1], long), half),
            VMEM_SPACE((width - 1, planes, *block), single),
            VMEM_SPACE((planes, *block), single),
            VMEM_SPACE((planes - 1, *block), single),
            dma((2, 2)),
            dma((4,)),
            dma((4, planes)),
            dma((4, planes)),
            dma((3, 2, planes)),
            dma((3, 2, planes)),
            dma((4, planes)),
            dma((4, planes)),
            dma((3, 4)),
            dma((3, 4)),
            dma((2, width)),
            dma((2, width)),
            dma((2, width)),
            dma((2, width)),
            VMEM_SPACE(rights.shape, half),
            VMEM_SPACE(outer.shape, half),
            dma((4,)),
        ],
        compiler_params=pltpu.CompilerParams(
            collective_id=identity, has_side_effects=True, vmem_limit_bytes=VMEM_ASK
        ),
    )(
        left_wide,
        left_tall,
        rights,
        outer,
        head_grad.reshape(planes, width // 2, 2, heights[2], columns),
        own_rows,
        vector_terms.reshape(planes, width, *block),
        facts.reshape(planes, width, *facts.shape[1:]),
        base_word,
        back_decoder,
        totals,
    )
    return out, heights, word_grad, place_grad, last, ends


LIFT = 128
WIRE = 48


def exact_rows(pick, values):
    first = to_half(values)
    rest = values - first.astype(jnp.float32)
    second = to_half(rest)
    third = to_half(rest - second.astype(jnp.float32))
    return nn(pick, first) + nn(pick, second) + nn(pick, third)


def lanes_to_rows(x):
    return jnp.concatenate([x[:, i : i + 128] for i in range(0, x.shape[1], 128)], 0)


def rows_to_lanes(x):
    return jnp.concatenate([x[i : i + 1] for i in range(x.shape[0])], 1)


def head_kernel(
    planes,
    lengths,
    sop_labels,
    final_from,
    head_from,
    word_from,
    decoder,
    facts,
    vec,
    back_final,
    back_word,
    back_decoder,
    back_head,
    wide_sums,
    small_sums,
    totals,
    all_t,
    stats,
    powers,
    back_t,
    plane_in,
    middle,
    line_in,
    word_half,
    sends,
    recvs,
    final,
    head,
    word,
    loads,
):
    width = 8
    inputs = [
        pltpu.make_async_copy(source, target, loads.at[number])
        for number, (source, target) in enumerate(
            ((final_from, final), (head_from, head), (word_from, word))
        )
    ]
    for copy in inputs:
        copy.start()
    z, c, cols = places()
    f = cols[0] * 2 + c
    line = [(lax.rem(z + d, planes), f) for d in range(1, planes)]
    plane = [(z, lax.rem(f + d, width)) for d in range(1, width)]
    greet([(None, who) for who in line + plane])
    offset = (z * width + f) * word.shape[0]
    words, slots = word.shape[0], planes * width * WIRE
    single = jnp.float32

    def gather_line(ref, kind):
        here = ref.at[z, f]
        return [
            remote(here, here, sends.at[kind, d], recvs.at[kind, d], who)
            for d, who in enumerate(line)
        ]

    def gather_plane(ref, kind):
        here = ref.at[:, f]
        return [
            remote(here, here, sends.at[kind, d], recvs.at[kind, d], who)
            for d, who in enumerate(plane)
        ]

    def await_line(ref, kind):
        for d in range(planes - 1):
            here = ref.at[lax.rem(z - d - 1 + planes, planes), f]
            remote(here, here, sends.at[kind, d], recvs.at[kind, d], line[d]).wait_recv()

    def await_plane(ref, kind):
        for d in range(width - 1):
            here = ref.at[:, lax.rem(f - d - 1 + width, width)]
            remote(here, here, sends.at[kind, d], recvs.at[kind, d], plane[d]).wait_recv()

    started = []
    lane = lax.broadcasted_iota(jnp.int32, (1, 128), 1)
    notes = facts[...]
    labels = jnp.concatenate([notes[i, 2:3, :WIRE] for i in range(planes * width)], 1)
    used = (lanes_to_rows(labels) >= 0).astype(single)
    mlm_count = jnp.sum(used)
    seconds = jnp.where(lane == 1, (notes[:, 4, :] > 0).astype(single), 0.0)
    sop_count = planes * width + jnp.sum(seconds)
    mlm_scale = 1.0 / jnp.broadcast_to(mlm_count, (1, 1))
    sop_scale = 1.0 / jnp.broadcast_to(sop_count, (1, 1))

    def start(copies):
        for copy in copies:
            copy.start()
        started.extend(copies)

    for copy in inputs:
        copy.wait()
    final_half = to_half(final[...])
    place = lax.broadcasted_iota(jnp.int32, (ROWS, LIFT), 0)
    scatter = to_half((place == facts[z * width + f, 3:4, :]).astype(single))
    pick = scatter.T
    picked = to_half(nn(pick, final_half))
    dense = nt(picked, head[:E, :]) + short_row(vec, MLM_B)
    bend = jnp.tanh(GELU_A * dense * (1.0 + GELU_B * dense * dense))
    hat, inverse = norm_forward(0.5 * dense * (1.0 + bend))
    slope = 0.5 * (1.0 + bend) + (0.5 * GELU_A) * dense * (1.0 - bend * bend) * (
        1.0 + 3.0 * GELU_B * dense * dense
    )
    rows_half = to_half(hat * short_row(vec, MLM_G) + short_row(vec, MLM_LB))
    all_t[z, f] = rows_half[:WIRE]
    start(gather_line(all_t, 0))

    word_half[...] = to_half(word[...])
    row16 = lax.broadcasted_iota(jnp.int32, (16, ROWS), 0)
    col16 = lax.broadcasted_iota(jnp.int32, (16, ROWS), 1)
    leads = to_half(
        (jnp.logical_and(row16 < 2, col16 == row16 * BUCKET)).astype(single)
    )
    firsts = to_half(nn(leads, final_half))
    pooled = jnp.tanh(nt(firsts, head[E : E + D, :]) + wide_row(vec, POOL_B))
    await_line(all_t, 0)
    start(gather_plane(all_t, 1))
    zero_class, one_class = lanes_of(vec, CLS_AT, D // 128), lanes_of(vec, CLS_AT + D // 128, D // 128)
    c0 = jnp.sum(pooled * zero_class, -1, keepdims=True)
    c1 = jnp.sum(pooled * one_class, -1, keepdims=True)
    class_top = jnp.maximum(c0, c1)
    e0, e1 = jnp.exp(c0 - class_top), jnp.exp(c1 - class_top)
    class_total = e0 + e1
    which = lax.broadcasted_iota(jnp.int32, (16, 1), 0)
    label = jnp.where(which == 0, sop_labels[0], sop_labels[1])
    hit = (label == 1).astype(single)
    two = (lengths[1] > 0).astype(single)
    present = jnp.where(which == 0, 1.0, jnp.where(which == 1, two, 0.0))
    losses = (jnp.log(class_total) + class_top - (c0 + hit * (c1 - c0))) * present
    weight = present * sop_scale
    back_c0 = (e0 / class_total - (1.0 - hit)) * weight
    back_c1 = (e1 / class_total - hit) * weight
    wide_sums[1:2, :] = jnp.sum(back_c0 * pooled, 0, keepdims=True)
    wide_sums[2:3, :] = jnp.sum(back_c1 * pooled, 0, keepdims=True)
    pre_half = to_half((back_c0 * zero_class + back_c1 * one_class) * (1.0 - pooled * pooled))
    wide_sums[0:1, :] = jnp.sum(pre_half.astype(single), 0, keepdims=True)
    back_head[E : E + D, :] = to_half(tn(pre_half, firsts))
    back_firsts = nn(pre_half, head[E : E + D, :])
    await_plane(all_t, 1)

    row = lax.broadcasted_iota(jnp.int32, (words, 128), 0) + offset
    bias = jnp.broadcast_to(to_half(decoder[...]).astype(single), (8, words)).T[:, 0:1]
    tops, sums, targets = [], [], []
    chunk = width * WIRE
    flat_t = all_t[...].reshape(slots, E)

    def logits_of(low):
        return nt(word_half[...], flat_t[low : low + chunk])

    coming = logits_of(0)
    for low in range(0, slots, chunk):
        logits = coming + bias
        if low + chunk < slots:
            coming = logits_of(low + chunk)
        top = jnp.max(logits, 0, keepdims=True)
        power = jnp.exp(logits - top)
        powers[:, pl.ds(low, chunk)] = power
        tops.append(top)
        sums.append(jnp.sum(power, 0, keepdims=True))
        for at in range(0, chunk, 128):
            mark = row == labels[:, low + at : low + at + 128]
            targets.append(
                jnp.sum(jnp.where(mark, logits[:, at : at + 128], 0.0), 0, keepdims=True)
            )
    own_top = lanes_to_rows(jnp.concatenate(tops, 1))
    groups = slots // 128
    stats[z, f, 0:groups] = own_top
    stats[z, f, groups : 2 * groups] = lanes_to_rows(jnp.concatenate(sums, 1))
    start(gather_line(stats, 2))
    target = jnp.sum(jnp.concatenate(targets, 0) * used)
    await_line(stats, 2)
    start(gather_plane(stats, 3))
    await_plane(stats, 3)
    every = stats[...].reshape(planes * width, 2 * groups, 128)
    top = jnp.max(every[:, :groups], 0)
    total = jnp.sum(every[:, groups:] * jnp.exp(every[:, :groups] - top[None]), 0)
    log_sum = jnp.sum((jnp.log(total) + top) * used)
    weight = used * mlm_scale
    factor = rows_to_lanes(weight * jnp.exp(own_top - top) / total)
    weight = rows_to_lanes(weight)

    def slot_terms(zz, d, who):
        return remote(
            back_t.at[zz, who[1]],
            plane_in.at[d, zz],
            sends.at[4 + zz, d],
            recvs.at[4 + zz, d],
            who,
        )

    def spread(word_sums, words_total, low, half):
        zz = low // chunk
        back_t[zz] = tn(half, word_half[...]).reshape(width, WIRE, E)
        start([slot_terms(zz, d, who) for d, who in enumerate(plane)])
        return word_sums + nt(ones, half), words_total + nn(half, flat_t[low : low + chunk])

    ready = []
    words_total = jnp.zeros((words, E), single)
    word_sums = jnp.zeros((8, words), single)
    ones = jnp.ones((8, width * WIRE), jnp.bfloat16)
    for low in range(0, slots, chunk):
        parts = []
        for at in range(low, low + chunk, 128):
            mark = row == labels[:, at : at + 128]
            part = powers[:, pl.ds(at, 128)] * factor[:, at : at + 128] - jnp.where(
                mark, weight[:, at : at + 128], 0.0
            )
            parts.append(to_half(part))
        if ready:
            word_sums, words_total = spread(word_sums, words_total, *ready.pop())
        ready.append((low, jnp.concatenate(parts, 1)))
    word_sums, words_total = spread(word_sums, words_total, *ready.pop())
    back_word[...] = words_total
    back_decoder[...] = word_sums[0:1]

    for zz in range(planes):
        total = back_t[zz, f]
        for d in range(width - 1):
            slot_terms(zz, d, plane[d]).wait_recv()
            total = total + plane_in[d, zz]
        middle[zz] = total
    start(
        [
            remote(middle.at[who[0]], line_in.at[d], sends.at[4 + planes, d], recvs.at[4 + planes, d], who)
            for d, who in enumerate(line)
        ]
    )
    total = middle[z]
    for d in range(planes - 1):
        remote(
            line_in.at[d], line_in.at[d], sends.at[4 + planes, d], recvs.at[4 + planes, d], line[d]
        ).wait_recv()
        total = total + line_in[d]
    back_rows = jnp.concatenate([total, jnp.zeros((LIFT - WIRE, E), single)], 0)
    small_sums[1:2, :] = jnp.sum(back_rows * hat, 0, keepdims=True)
    small_sums[2:3, :] = jnp.sum(back_rows, 0, keepdims=True)
    dense_half = to_half(norm_backward(back_rows, short_row(vec, MLM_G), hat, inverse) * slope)
    small_sums[0:1, :] = jnp.sum(dense_half.astype(single), 0, keepdims=True)
    back_head[:E, :] = to_half(tn(dense_half, picked))
    back_final[...] = exact_rows(scatter, nn(dense_half, head[:E, :]))
    back_final[0:1, :] = back_final[0:1, :] + back_firsts[0:1]
    back_final[BUCKET : BUCKET + 1, :] = back_final[BUCKET : BUCKET + 1, :] + back_firsts[1:2]
    sop_sum = jnp.sum(losses)
    ends = jnp.zeros((1, 128), single)
    for at, value in enumerate((log_sum, target, sop_sum, mlm_count, sop_count)):
        ends = ends + jnp.where(lane == at, value, 0.0)
    totals[...] = ends
    for copy in started:
        copy.wait_send()


def run_head(
    lengths, sop_labels, final, head, word, decoder, facts, vec, mesh_shape, identity
):
    planes, width = mesh_shape
    words = word.shape[0]
    slots = planes * width * WIRE
    groups = slots // 128
    single, half = jnp.float32, jnp.bfloat16
    vmem = pl.BlockSpec(memory_space=VMEM_SPACE)
    smem = pl.BlockSpec(memory_space=pltpu.SMEM)
    dma = pltpu.SemaphoreType.DMA
    return pl.pallas_call(
        functools.partial(head_kernel, planes),
        out_shape=[
            jax.ShapeDtypeStruct((ROWS, D), single),
            jax.ShapeDtypeStruct((words, E), single),
            jax.ShapeDtypeStruct((1, words), single),
            jax.ShapeDtypeStruct(head.shape, half),
            jax.ShapeDtypeStruct((3, D), single),
            jax.ShapeDtypeStruct((3, E), single),
            jax.ShapeDtypeStruct((1, 128), single),
        ],
        in_specs=[smem] * 2 + [pl.BlockSpec(memory_space=pl.ANY)] * 3 + [vmem] * 3,
        out_specs=[vmem] * 7,
        scratch_shapes=[
            VMEM_SPACE((planes, width, WIRE, E), half),
            VMEM_SPACE((planes, width, 2 * groups, 128), single),
            VMEM_SPACE((words, slots), single),
            VMEM_SPACE((planes, width, WIRE, E), single),
            VMEM_SPACE((width - 1, planes, WIRE, E), single),
            VMEM_SPACE((planes, WIRE, E), single),
            VMEM_SPACE((planes - 1, WIRE, E), single),
            VMEM_SPACE((words, E), half),
            dma((5 + planes, width)),
            dma((5 + planes, width)),
            VMEM_SPACE(final.shape, single),
            VMEM_SPACE(head.shape, half),
            VMEM_SPACE(word.shape, single),
            dma((3,)),
        ],
        compiler_params=pltpu.CompilerParams(
            collective_id=identity, has_side_effects=True, vmem_limit_bytes=VMEM_ASK
        ),
    )(lengths, sop_labels, final, head, word, decoder, facts, vec)


def adam_update(weight, gradient, first, second, rate):
    first = BETA_ONE * first + (1 - BETA_ONE) * gradient
    second = BETA_TWO * second + (1 - BETA_TWO) * gradient * gradient
    first_hat = first / (1 - BETA_ONE**STEP)
    second_hat = second / (1 - BETA_TWO**STEP)
    updated = weight - rate * (
        first_hat / (jnp.sqrt(second_hat) + ADAM_EPSILON) + WEIGHT_DECAY * weight
    )
    return (updated, first, second)


def adam_kernel(blocks, rates, *refs):
    count = len(rates)
    ends, refs = refs[0], refs[1:]
    ins, outs, scalars = refs[: 4 * count], refs[4 * count : 7 * count], refs[7 * count :]
    factor = ends[1:2, 0:1]

    def update(number):
        weight, first, second, gradient = ins[4 * number : 4 * number + 4]
        grad = gradient[...]
        if grad.ndim > 2:
            grad = grad[:, :, :8].reshape(-1, 128)[: weight.shape[0]]
        results = adam_update(
            weight[...], factor * grad, first[...], second[...], rates[number]
        )
        for out, result in zip(outs[3 * number : 3 * number + 3], results):
            out[...] = result

    for number in range(blocks):
        update(number)

    @pl.when(pl.program_id(0) == 0)
    def _():
        for number in range(blocks, count):
            update(number)
        lane = lax.broadcasted_iota(jnp.int32, (1, 128), 1)
        for at, scalar in enumerate(scalars):
            scalar[0] = jnp.sum(jnp.where(lane == 0, ends[at : at + 1, :], 0.0))


ADAM_STEPS = 2


def run_adam(ends, groups, steps):
    in_specs = [pl.BlockSpec(ends.shape, lambda i: (0, 0))]
    out_specs, shapes, given = [], [], [ends]
    blocks = 0
    for weight, first, second, gradient, low, rate in groups:
        rows, columns = weight.shape
        if low is None:
            spec = pl.BlockSpec(weight.shape, lambda i: (0, 0))
            zero = (0,) * gradient.ndim
            grad_spec = pl.BlockSpec(gradient.shape, lambda i, zero=zero: zero)
        else:
            blocks += 1
            height = rows // steps
            spec = pl.BlockSpec((height, columns), lambda i: (i, 0))
            grad_spec = pl.BlockSpec(
                (height, columns), lambda i, start=low // height: (start + i, 0)
            )
        in_specs += [spec] * 3 + [grad_spec]
        out_specs += [spec] * 3
        shapes += [jax.ShapeDtypeStruct(weight.shape, jnp.float32)] * 3
        given += [weight, first, second, gradient]
    out_specs += [pl.BlockSpec(memory_space=pltpu.SMEM)] * 6
    shapes += [jax.ShapeDtypeStruct((1,), jnp.float32)] * 6
    return pl.pallas_call(
        functools.partial(adam_kernel, blocks, tuple(group[5] for group in groups)),
        grid=(steps,),
        out_shape=shapes,
        in_specs=in_specs,
        out_specs=out_specs,
        compiler_params=pltpu.CompilerParams(
            dimension_semantics=("arbitrary",), vmem_limit_bytes=VMEM_ASK
        ),
    )(*given)


class Network:
    def __init__(self, mesh):
        self.shape = (mesh.shape["dp"], mesh.shape["fsdp"])
        self.devices = self.shape[0] * self.shape[1]
        self.kernels = self.shape[1] == 8
        self.calls = 0

    def identity(self):
        self.calls += 1
        return self.calls

    def start(self, shards, own_word, own_place, batch):
        if self.kernels:
            return run_start(shards, own_word, own_place, batch, self.shape, self.identity())
        token_ids, labels, slot_rows, lengths, sop_labels = batch

        def fill(count, value):
            return jnp.full((count,), value, jnp.int32)

        rest = fill(128 - labels.shape[0], -1)
        own_facts = [token_ids, labels, rest, slot_rows, rest, lengths, sop_labels]
        own_facts = jnp.concatenate([*own_facts, fill(3 * 128 + 124, 0)]).reshape(8, 128)
        weights = [lax.all_gather(to_half(w), AXES, axis=0, tiled=True) for w in shards]
        facts = lax.all_gather(own_facts, AXES)
        place = lax.all_gather(to_half(own_place), AXES)
        words = own_word.shape[0]
        ids = facts[:, : ROWS // 128].reshape(-1) - lax.axis_index(AXES) * words
        column = jnp.arange(words, dtype=jnp.int32)
        select = to_half(ids[:, None] == column[None, :])
        terms = product(select, to_half(own_word))
        found = lax.psum_scatter(terms, AXES, scatter_dimension=0, tiled=True)
        return weights, facts, place, found

    def head(self, lengths, sop_labels, final, head, word, decoder, facts, vec):
        decoder = decoder[None]
        given = (lengths, sop_labels, final, head, word, decoder, facts, vec)
        if self.kernels:
            return run_head(*given, self.shape, self.identity())
        return self.plain_head(*given)

    def plain_head(self, lengths, sop_labels, final, head, word, decoder, facts, vec):
        short, cls = vec[SHORT_AT:], vec[CLS_AT:FF_AT].reshape(2, D)
        pool_b = vec[POOL_B * D // 128 : CLS_AT].reshape(D)
        labels = facts[:, 2, :WIRE].reshape(1, -1)
        mlm_count = jnp.sum((labels >= 0).astype(jnp.float32))
        sop_count = self.devices + jnp.sum((facts[:, 4, 1] > 0).astype(jnp.float32))
        single = jnp.float32
        offset = lax.axis_index(AXES) * word.shape[0]
        word_half, final_half = to_half(word), to_half(final)
        rows = facts[lax.axis_index(AXES), 3, :WIRE]
        pick = (rows[:, None] == jnp.arange(ROWS, dtype=jnp.int32)[None]).astype(single)
        picked = to_half(product(to_half(pick), final_half))
        dense = times_transpose(picked, head[:E]) + short[MLM_B]
        bend = jnp.tanh(GELU_A * dense * (1.0 + GELU_B * dense * dense))
        hat, inverse = norm_forward(0.5 * dense * (1.0 + bend))
        slope = 0.5 * (1.0 + bend) + (0.5 * GELU_A) * dense * (1.0 - bend * bend) * (
            1.0 + 3.0 * GELU_B * dense * dense
        )
        rows_half = to_half(hat * short[MLM_G] + short[MLM_LB])
        all_rows = lax.all_gather(rows_half, AXES, axis=0, tiled=True)
        logits = times_transpose(word_half, all_rows) + to_half(decoder).astype(single).T
        mark = jnp.arange(word.shape[0], dtype=jnp.int32)[:, None] + offset == labels
        own_top = jnp.max(logits, 0)
        own_total = jnp.sum(jnp.exp(logits - own_top), 0)
        used = (labels[0] >= 0).astype(single)
        target = jnp.sum(jnp.sum(jnp.where(mark, logits, 0.0), 0) * used)
        top = lax.pmax(own_top, AXES)
        total = lax.psum(own_total * jnp.exp(own_top - top), AXES)
        log_sum = jnp.sum((jnp.log(total) + top) * used)
        weight = used / mlm_count
        half = to_half((jnp.exp(logits - top) / total - mark.astype(single)) * weight)
        back_rows = lax.psum_scatter(
            transpose_times(half, word_half), AXES, scatter_dimension=0, tiled=True
        )
        dense_half = to_half(norm_backward(back_rows, short[MLM_G], hat, inverse) * slope)
        back_final = lax.dot_general(
            pick, product(dense_half, head[:E]), (((0,), (0,)), ((), ())), precision=PRECISE
        )
        firsts = jnp.stack([final_half[0], final_half[BUCKET]])
        pooled = jnp.tanh(times_transpose(firsts, head[E : E + D]) + pool_b)
        classes = jnp.sum(pooled[:, None] * cls[None], -1)
        powers = jnp.exp(classes - jnp.max(classes, -1, keepdims=True))
        totals = jnp.sum(powers, -1, keepdims=True)
        onehot = jnp.stack([1 - sop_labels, sop_labels], 1).astype(single)
        present = jnp.stack([jnp.float32(1.0), (lengths[1] > 0).astype(single)])
        losses = jnp.log(totals[:, 0]) + jnp.max(classes, -1) - jnp.sum(classes * onehot, -1)
        back_classes = (powers / totals - onehot) * (present / sop_count)[:, None]
        back_pooled = jnp.sum(back_classes[:, :, None] * cls[None], 1)
        pre_half = to_half(back_pooled * (1.0 - pooled * pooled))
        back_firsts = product(pre_half, head[E : E + D])
        back_final = back_final.at[0].add(back_firsts[0]).at[BUCKET].add(back_firsts[1])
        back_cls = jnp.sum(back_classes[:, :, None] * pooled[:, None], 0)
        small_sums = [column_sum(dense_half), jnp.sum(back_rows * hat, 0), jnp.sum(back_rows, 0)]
        back_head = [transpose_times(dense_half, picked), transpose_times(pre_half, firsts)]
        ends = jnp.stack([log_sum, target, jnp.sum(losses * present), mlm_count, sop_count])
        return (
            back_final,
            product(half, all_rows),
            column_sum(half.T)[None],
            to_half(jnp.pad(jnp.concatenate(back_head, 0), ((0, E), (0, 0)))),
            jnp.concatenate([column_sum(pre_half)[None], back_cls], 0),
            jnp.stack(small_sums),
            jnp.pad(ends, (0, 123))[None],
        )

    def adam(self, ends, groups):
        if self.kernels:
            updates = run_adam(ends, groups, ADAM_STEPS)
            scalars = [x.reshape(()) for x in updates[-6:]]
            return [updates[i : i + 3] for i in range(0, 3 * len(groups), 3)], scalars
        updates = []
        for weight, first, second, gradient, low, rate in groups:
            rows = weight.shape[0]
            if low is not None:
                gradient = gradient[low : low + rows]
            gradient = gradient.reshape(-1, weight.shape[1])[:rows]
            updates.append(adam_update(weight, ends[1, 0] * gradient, first, second, rate))
        return updates, [ends[i, 0] for i in range(6)]

    def finish(
        self,
        left_wide,
        left_tall,
        rights,
        outer,
        head_grad,
        own_rows,
        vector,
        facts,
        base_word,
        back_decoder,
        totals,
        places_count,
    ):
        devices = self.devices
        if self.kernels:
            out, heights, word_grad, place_grad, last, ends = run_finish(
                left_wide,
                left_tall,
                rights,
                outer,
                head_grad,
                own_rows,
                vector,
                facts,
                base_word,
                back_decoder,
                totals,
                places_count,
                self.shape,
                self.identity(),
            )
            return out, heights, word_grad, place_grad, last, ends
        back_wide = jnp.concatenate(
            [
                product(left_wide[: 3 * D], rights[0]),
                product(left_wide[3 * D : 4 * D], rights[1]),
                product(left_wide[4 * D :], rights[2]),
            ],
            0,
        )
        sums = [
            lax.psum_scatter(p.astype(jnp.float32), AXES, scatter_dimension=0, tiled=True)
            for p in (back_wide, product(left_tall, outer), head_grad)
        ]
        all_rows = lax.all_gather(own_rows, AXES, axis=0, tiled=True)
        own, words = lax.axis_index(AXES), base_word.shape[0]
        ids = facts[:, : ROWS // 128].reshape(-1) - own * words
        select = to_half(ids[:, None] == jnp.arange(words, dtype=jnp.int32)[None, :])
        word_grad = base_word + transpose_times(select, all_rows)
        by_device = all_rows.reshape(devices, ROWS, E).astype(jnp.float32)
        two = (facts[:, 4, 1] > 0)[:, None, None]
        lower, upper = by_device[:, :BUCKET], by_device[:, BUCKET:]
        lower = jnp.sum(lower + jnp.where(two, upper, 0.0), 0)
        upper = jnp.sum(jnp.where(two, 0.0, upper), 0)
        every = jnp.concatenate([lower, upper], 0)
        every = jnp.pad(every, ((0, places_count * devices - ROWS), (0, 0)))
        place_grad = lax.dynamic_slice(every, (own * places_count, 0), (places_count, E))
        squares = sum(jnp.sum(g * g) for g in (*sums, word_grad, place_grad, back_decoder))
        reduced, tails, squares = lax.psum((vector, totals, squares), AXES)
        norm = jnp.sqrt(squares + jnp.sum(reduced * reduced))
        factor = jnp.minimum(1.0, CLIP_NORM / (norm + NORM_EPSILON))
        ends = [norm, factor, totals[0, 0] - tails[0, 1], tails[0, 2]]
        ends = jnp.stack([*ends, totals[0, 3], totals[0, 4]])
        ends = jnp.broadcast_to(ends[:, None], (6, 128))
        heights = tuple(total.shape[0] for total in sums)
        return jnp.concatenate(sums, 0), heights, word_grad, place_grad, reduced, ends


CLS_AT, FF_AT, SHORT_AT = 10 * D // 128, 12 * D // 128, (12 * D + FF) // 128


def lanes_of(vec, first, count):
    return jnp.concatenate([vec[pl.ds(first + i, 1), :] for i in range(count)], 1)


def wide_row(vec, index):
    return lanes_of(vec, index * (D // 128), D // 128)


def short_row(vec, index):
    return vec[pl.ds(SHORT_AT + index, 1), :]


def nt(a, b):
    return lax.dot_general(a, b, (((1,), (1,)), ((), ())), preferred_element_type=jnp.float32)


def nn(a, b):
    return jnp.dot(a, b, preferred_element_type=jnp.float32)


def tn(a, b):
    return lax.dot_general(a, b, (((0,), (0,)), ((), ())), preferred_element_type=jnp.float32)


FORWARD_CHUNK, BACKWARD_CHUNK = 768, 256
PAIR = 2 * HEAD_DIM
PROJ_B, Q_B, V_B, O_B, LN1_G, LN1_B, FFO_B, LN2_G, LN2_B, POOL_B = range(10)


def allowed_block(lengths):
    shape = (ROWS, ROWS)
    key = lax.broadcasted_iota(jnp.int32, shape, 0)
    query = lax.broadcasted_iota(jnp.int32, shape, 1)
    two = lengths[1] > 0
    key_second = jnp.logical_and(key >= BUCKET, two).astype(jnp.int32)
    query_second = jnp.logical_and(query >= BUCKET, two).astype(jnp.int32)
    length = jnp.where(key_second == 1, lengths[1], lengths[0])
    live = key - BUCKET * key_second < length
    return jnp.logical_and(query_second == key_second, live)


def halves_down(x):
    row = lax.broadcasted_iota(jnp.int32, x.shape, 0)
    zero = jnp.zeros_like(x)
    return jnp.where(row < HEAD_DIM, x, zero), jnp.where(row < HEAD_DIM, zero, x)


def halves(x):
    lane = lax.broadcasted_iota(jnp.int32, x.shape, 1)
    zero = jnp.zeros_like(x)
    return jnp.where(lane < HEAD_DIM, x, zero), jnp.where(lane < HEAD_DIM, zero, x)


def kinds(lengths):
    row = lax.broadcasted_iota(jnp.int32, (ROWS, 1), 0)
    second = jnp.logical_and(row >= BUCKET, lengths[1] > 0).astype(jnp.int32)
    length = jnp.where(second == 1, lengths[1], lengths[0])
    return (row - BUCKET * second >= length // 2).astype(jnp.float32)


EMB_G, EMB_B, MLM_B, MLM_G, MLM_LB, TYPE_ZERO, TYPE_ONE = range(7)


def forward_kernel(
    lengths,
    found,
    place,
    lift,
    wide,
    tall,
    vec,
    final,
    embed_hat,
    embed_inverse,
    normed_half,
    rights,
    projected,
    weighting,
    hat_one,
    inverse_one,
    slope,
    active,
    hat_two,
    inverse_two,
    hidden,
):
    layer = pl.program_id(0)

    def row(index):
        return wide_row(vec, index)

    @pl.when(layer == 0)
    def _():
        two = (lengths[1] > 0).astype(jnp.float32)
        kind = kinds(lengths)
        upper = place[pl.ds(0, BUCKET), :].astype(jnp.float32)
        lower = jnp.where(two > 0, upper, place[pl.ds(BUCKET, BUCKET), :].astype(jnp.float32))
        embedded = found[...] + jnp.concatenate([upper, lower], 0)
        zero, one = short_row(vec, TYPE_ZERO), short_row(vec, TYPE_ONE)
        hat, inverse = norm_forward(embedded + jnp.where(kind > 0, one, zero))
        embed_hat[...] = hat
        embed_inverse[...] = inverse
        normed = to_half(hat * short_row(vec, EMB_G) + short_row(vec, EMB_B))
        normed_half[...] = normed
        hidden[...] = nn(normed, lift[...]) + row(PROJ_B)

    half = to_half(hidden[...])
    rights[0] = half
    for part, bias in ((0, Q_B), (1, None), (2, V_B)):
        for low in range(0, D, 256):
            here = part * D + low
            value = nt(half, wide[pl.ds(here, 256), :])
            if bias is not None:
                value = value + lanes_of(vec, (bias * D + low) // 128, 2)
            projected[:, pl.ds(here, 256)] = to_half(value)
    allowed = allowed_block(lengths)
    def scores_of(head):
        lanes = head // 2 * PAIR
        queries = halves(projected[:, pl.ds(lanes, PAIR)])[head % 2]
        return nt(projected[:, pl.ds(D + lanes, PAIR)], queries)

    def mix(head, weights):
        lanes = head // 2 * PAIR
        values = halves_down(projected[:, pl.ds(2 * D + lanes, PAIR)].T)[head % 2]
        part = nn(values, weights)
        if head % 2:
            rights[1, :, pl.ds(lanes, PAIR)] = to_half(mixes.pop() + part).T
        else:
            mixes.append(part)

    mixes, waiting, coming = [], None, scores_of(0)
    for head in range(HEADS):
        products = coming
        if head + 1 < HEADS:
            coming = scores_of(head + 1)
        scores = jnp.where(allowed, products * SCALE, MASKED)
        powers = jnp.exp(scores - jnp.max(scores, 0, keepdims=True))
        weights = powers * (1.0 / jnp.sum(powers, 0, keepdims=True))
        weighting[head] = weights
        if waiting is not None:
            mix(head - 1, waiting)
        waiting = to_half(weights)
    mix(HEADS - 1, waiting)
    first_sum = hidden[...] + nt(rights[1], wide[pl.ds(3 * D, D), :]) + row(O_B)
    hat, inverse = norm_forward(first_sum)
    hat_one[...] = hat
    inverse_one[...] = inverse
    middle = hat * row(LN1_G) + row(LN1_B)
    half = to_half(middle)
    rights[2] = half
    total = middle + row(FFO_B)

    def inner_of(low):
        return nt(half, wide[pl.ds(4 * D + low, FORWARD_CHUNK), :])

    coming = inner_of(0)
    for low in range(0, FF, FORWARD_CHUNK):
        inner = coming + lanes_of(vec, FF_AT + low // 128, FORWARD_CHUNK // 128)
        if low + FORWARD_CHUNK < FF:
            coming = inner_of(low + FORWARD_CHUNK)
        square = inner * inner
        bend = jnp.tanh(GELU_A * inner * (1.0 + GELU_B * square))
        act = to_half(0.5 * inner * (1.0 + bend))
        slope[:, pl.ds(low, FORWARD_CHUNK)] = 0.5 * (1.0 + bend) + (0.5 * GELU_A) * inner * (
            1.0 - bend * bend
        ) * (1.0 + 3.0 * GELU_B * square)
        active[pl.ds(low, FORWARD_CHUNK), :] = act.T
        total = total + nn(act, tall[pl.ds(low, FORWARD_CHUNK), :])
    hat, inverse = norm_forward(total)
    hat_two[...] = hat
    inverse_two[...] = inverse
    output = hat * row(LN2_G) + row(LN2_B)
    hidden[...] = output
    final[...] = output


PIECE = 1024
WIDE_PIECES = [(low, low + D) for low in range(0, 4 * D, D)]
WIDE_PIECES += [(4 * D + low, 4 * D + low + PIECE) for low in range(0, FF, PIECE)]
OUT_PIECE, IN_PIECE, TALL_PIECE = 3, 4, len(WIDE_PIECES)
PIECES = TALL_PIECE + FF // PIECE


def weight_copy(number, wide, tall, wide_buf, tall_buf, sems):
    if number < TALL_PIECE:
        low, high = WIDE_PIECES[number]
        source, target = wide, wide_buf
    else:
        low = (number - TALL_PIECE) * PIECE
        high = low + PIECE
        source, target = tall, tall_buf
    rows = pl.ds(low, high - low)
    return pltpu.make_async_copy(source.at[rows], target.at[rows], sems.at[number])


def whole_spec():
    return pl.BlockSpec(memory_space=VMEM_SPACE, pipeline_mode=pl.Buffered(1))


def lift_spec():
    return pl.BlockSpec((E, D), lambda i: ((E + D) // E, 0), pipeline_mode=pl.Buffered(1))


def by_layer(*shape, order=lambda i: i):
    return pl.BlockSpec(
        (None, *shape), lambda i: (order(i),) + (0,) * len(shape), memory_space=VMEM_SPACE
    )


def run_forward(lengths, found, place, head, wide, tall, vec):
    def kept(*shape, dtype=jnp.bfloat16):
        return jax.ShapeDtypeStruct((LAYERS, *shape), dtype)

    single = jnp.float32
    names = (
        "final",
        "embed_hat",
        "embed_inverse",
        "normed_half",
        "rights",
        "projected",
        "weighting",
        "hat_one",
        "inverse_one",
        "slope",
        "active",
        "hat_two",
        "inverse_two",
    )
    outs = pl.pallas_call(
        forward_kernel,
        grid=(LAYERS,),
        out_shape=[
            jax.ShapeDtypeStruct((ROWS, D), single),
            jax.ShapeDtypeStruct((ROWS, E), single),
            jax.ShapeDtypeStruct((ROWS, 1), single),
            jax.ShapeDtypeStruct((ROWS, E), jnp.bfloat16),
            jax.ShapeDtypeStruct((3, LAYERS, ROWS, D), jnp.bfloat16),
            kept(ROWS, 3 * D),
            kept(HEADS, ROWS, ROWS, dtype=single),
            kept(ROWS, D, dtype=single),
            kept(ROWS, 1, dtype=single),
            kept(ROWS, FF, dtype=single),
            jax.ShapeDtypeStruct((FF, LAYERS * ROWS), jnp.bfloat16),
            kept(ROWS, D, dtype=single),
            kept(ROWS, 1, dtype=single),
        ],
        in_specs=[pl.BlockSpec(memory_space=pltpu.SMEM)]
        + [whole_spec()] * 2
        + [lift_spec()]
        + [whole_spec()] * 3,
        out_specs=[
            pl.BlockSpec((ROWS, D), lambda i: (0, 0)),
            pl.BlockSpec((ROWS, E), lambda i: (0, 0)),
            pl.BlockSpec((ROWS, 1), lambda i: (0, 0)),
            pl.BlockSpec((ROWS, E), lambda i: (0, 0)),
            pl.BlockSpec((3, None, ROWS, D), lambda i: (0, i, 0, 0)),
            by_layer(ROWS, 3 * D),
            by_layer(HEADS, ROWS, ROWS),
            by_layer(ROWS, D),
            by_layer(ROWS, 1),
            by_layer(ROWS, FF),
            pl.BlockSpec((FF, ROWS), lambda i: (0, i)),
            by_layer(ROWS, D),
            by_layer(ROWS, 1),
        ],
        scratch_shapes=[VMEM_SPACE((ROWS, D), single)],
        compiler_params=pltpu.CompilerParams(
            dimension_semantics=("arbitrary",), vmem_limit_bytes=VMEM_ASK
        ),
    )(lengths, found, place, head, wide, tall, vec)
    return dict(zip(names, outs))


def backward_kernel(
    lengths,
    start,
    wide_sums,
    small_sums,
    embed_hat,
    embed_inverse,
    normed_half,
    lift,
    head_in,
    wide_from,
    tall_from,
    vec,
    projected,
    weighting,
    hat_one,
    inverse_one,
    slope,
    hat_two,
    inverse_two,
    rows_out,
    back_lift,
    turned,
    outer,
    vector,
    sums,
    ff_sum,
    upstream,
    back_mixed,
    joint,
    wide,
    tall,
    sems,
):
    step = pl.program_id(0)

    def bring(number):
        return weight_copy(number, wide_from, tall_from, wide, tall, sems)

    @pl.when(step == 0)
    def _():
        for number in range(FF // PIECE):
            bring(TALL_PIECE + number).start()
            bring(IN_PIECE + number).start()
        for number in (OUT_PIECE, 0, 1, 2):
            bring(number).start()

    @pl.when(step == 0)
    def _():
        upstream[...] = start[...]
        sums[...] = jnp.zeros_like(sums)
        ff_sum[...] = jnp.zeros_like(ff_sum)

    def row(index):
        return wide_row(vec, index)

    def add_sum(index, value):
        here = pl.ds(index - Q_B, 1)
        sums[here, :] = sums[here, :] + jnp.sum(value, 0, keepdims=True)

    def work(first):
        def need(*numbers):
            if first:
                for number in numbers:
                    bring(number).wait()

        up = upstream[...]
        hat = hat_two[...]
        add_sum(LN2_G, up * hat)
        add_sum(LN2_B, up)
        back_second = norm_backward(up, row(LN2_G), hat, inverse_two[...])
        half = to_half(back_second)
        outer[...] = half
        add_sum(FFO_B, half.astype(jnp.float32))
        total = back_second

        def back_active(low):
            if low % PIECE == 0:
                need(TALL_PIECE + low // PIECE, IN_PIECE + low // PIECE)
            return nt(half, tall[pl.ds(low, BACKWARD_CHUNK), :])

        coming = back_active(0)
        for low in range(0, FF, BACKWARD_CHUNK):
            lanes = pl.ds(low, BACKWARD_CHUNK)
            product = coming
            if low + BACKWARD_CHUNK < FF:
                coming = back_active(low + BACKWARD_CHUNK)
            inner = to_half(product * slope[:, lanes])
            ff_sum[:, lanes] = ff_sum[:, lanes] + jnp.sum(
                inner.astype(jnp.float32), 0, keepdims=True
            )
            turned[pl.ds(4 * D + low, BACKWARD_CHUNK), :] = inner.T
            total = total + nn(inner, wide[pl.ds(4 * D + low, BACKWARD_CHUNK), :])
        hat = hat_one[...]
        add_sum(LN1_G, total * hat)
        add_sum(LN1_B, total)
        back_first = norm_backward(total, row(LN1_G), hat, inverse_one[...])
        upstream[...] = back_first
        half = to_half(back_first)
        add_sum(O_B, half.astype(jnp.float32))
        turned[pl.ds(3 * D, D), :] = half.T
        need(OUT_PIECE)
        back_mixed[...] = to_half(nn(half, wide[pl.ds(3 * D, D), :]))

        def soft_of(head):
            lanes = head // 2 * PAIR
            grads = halves(back_mixed[:, pl.ds(lanes, PAIR)])[head % 2]
            return nt(projected[:, pl.ds(2 * D + lanes, PAIR)], grads)

        def spread(head, scores, weights):
            lanes, side = head // 2 * PAIR, head % 2
            queries = halves(projected[:, pl.ds(lanes, PAIR)])[side]
            keys = halves_down(projected[:, pl.ds(D + lanes, PAIR)].T)[side]
            grads = halves(back_mixed[:, pl.ds(lanes, PAIR)])[side]
            parts = nn(keys, scores), nn(scores, queries), nn(weights, grads)
            if side == 0:
                sides.extend(parts)
                return
            value_half = to_half(sides.pop() + parts[2])
            key_half = to_half((sides.pop() + parts[1]) * SCALE)
            query_half = to_half((sides.pop() + parts[0]) * SCALE)
            joint[:, pl.ds(lanes, PAIR)] = query_half.T
            joint[:, pl.ds(D + lanes, PAIR)] = key_half
            joint[:, pl.ds(2 * D + lanes, PAIR)] = value_half
            turned[pl.ds(lanes, PAIR), :] = query_half
            turned[pl.ds(D + lanes, PAIR), :] = key_half.T
            turned[pl.ds(2 * D + lanes, PAIR), :] = value_half.T

        sides, waiting, coming = [], None, soft_of(0)
        for head in range(HEADS):
            soft = coming
            if head + 1 < HEADS:
                coming = soft_of(head + 1)
            weights = weighting[head]
            scores = to_half(weights * (soft - jnp.sum(weights * soft, 0, keepdims=True)))
            if waiting is not None:
                spread(head - 1, *waiting)
            waiting = (scores, to_half(weights))
        spread(HEADS - 1, *waiting)
        total = upstream[...]
        for part, bias in ((0, Q_B), (1, None), (2, V_B)):
            need(part)
            here = pl.ds(part * D, D)
            value = joint[:, here]
            if bias is not None:
                add_sum(bias, value.astype(jnp.float32))
            total = total + nn(value, wide[here, :])
        upstream[...] = total

    pl.when(step == 0)(lambda: work(True))
    pl.when(step > 0)(lambda: work(False))

    @pl.when(step == LAYERS - 1)
    def _():
        half = to_half(upstream[...])
        back_lift[...] = to_half(tn(normed_half[...], half))
        back_normed = nt(half, lift[...])
        hat = embed_hat[...]
        back = norm_backward(back_normed, short_row(vec, EMB_G), hat, embed_inverse[...])
        rows_out[...] = to_half(back)
        kind = kinds(lengths)
        ones = jnp.sum(back * kind, 0, keepdims=True)
        zeros = jnp.sum(back * (1.0 - kind), 0, keepdims=True)
        vector[...] = jnp.zeros_like(vector)
        parts = [jnp.sum(half.astype(jnp.float32), 0, keepdims=True)]
        parts += [sums[pl.ds(i, 1), :] for i in range(8)]
        parts += [wide_sums[pl.ds(i, 1), :] for i in range(3)]
        parts += [ff_sum[...]]
        parts += [
            jnp.sum(back_normed * hat, 0, keepdims=True),
            jnp.sum(back_normed, 0, keepdims=True),
        ]
        parts += [small_sums[pl.ds(i, 1), :] for i in range(3)]
        parts += [zeros, ones]
        at = 0
        for part in parts:
            for low in range(0, part.shape[1], 128):
                vector[pl.ds(at, 1), :] = part[:, low : low + 128]
                at += 1


def run_backward(lengths, start, wide_sums, small_sums, head, back_head, wide, tall, vec, kept, lines):
    single, half = jnp.float32, jnp.bfloat16
    last = LAYERS - 1

    def order(i):
        return last - i

    return pl.pallas_call(
        backward_kernel,
        grid=(LAYERS,),
        out_shape=[
            jax.ShapeDtypeStruct((ROWS, E), half),
            jax.ShapeDtypeStruct(back_head.shape, half),
            jax.ShapeDtypeStruct((4 * D + FF, LAYERS * ROWS), half),
            jax.ShapeDtypeStruct((LAYERS, ROWS, D), half),
            jax.ShapeDtypeStruct((lines, 128), single),
        ],
        in_specs=[pl.BlockSpec(memory_space=pltpu.SMEM)]
        + [whole_spec()] * 6
        + [lift_spec()]
        + [pl.BlockSpec(memory_space=pl.ANY)] * 3
        + [whole_spec()]
        + [
            by_layer(ROWS, 3 * D, order=order),
            by_layer(HEADS, ROWS, ROWS, order=order),
            by_layer(ROWS, D, order=order),
            by_layer(ROWS, 1, order=order),
            by_layer(ROWS, FF, order=order),
            by_layer(ROWS, D, order=order),
            by_layer(ROWS, 1, order=order),
        ],
        out_specs=[
            pl.BlockSpec((ROWS, E), lambda i: (0, 0)),
            pl.BlockSpec((E, D), lambda i: ((E + D) // E, 0)),
            pl.BlockSpec((4 * D + FF, ROWS), lambda i: (0, order(i))),
            by_layer(ROWS, D, order=order),
            pl.BlockSpec((lines, 128), lambda i: (0, 0)),
        ],
        input_output_aliases={8: 1},
        scratch_shapes=[
            VMEM_SPACE((8, D), single),
            VMEM_SPACE((1, FF), single),
            VMEM_SPACE((ROWS, D), single),
            VMEM_SPACE((ROWS, D), half),
            VMEM_SPACE((ROWS, 3 * D), half),
            VMEM_SPACE(wide.shape, half),
            VMEM_SPACE(tall.shape, half),
            pltpu.SemaphoreType.DMA((PIECES,)),
        ],
        compiler_params=pltpu.CompilerParams(
            dimension_semantics=("arbitrary",), vmem_limit_bytes=VMEM_ASK
        ),
    )(
        lengths,
        start,
        wide_sums,
        small_sums,
        kept["embed_hat"],
        kept["embed_inverse"],
        kept["normed_half"],
        head,
        back_head,
        wide,
        tall,
        vec,
        kept["projected"],
        kept["weighting"],
        kept["hat_one"],
        kept["inverse_one"],
        kept["slope"],
        kept["hat_two"],
        kept["inverse_two"],
    )


def local(
    mesh,
    word_table,
    position_table,
    head_weights,
    decoder_bias,
    layer_wide,
    layer_tall,
    vectors,
    word_first,
    word_second,
    position_first,
    position_second,
    head_first,
    head_second,
    decoder_first,
    decoder_second,
    wide_first,
    wide_second,
    tall_first,
    tall_second,
    vector_first,
    vector_second,
    token_ids,
    seq_lengths,
    mlm_rows,
    mlm_labels,
    sop_labels,
):
    network = Network(mesh)

    (wide, tall, head), all_facts, place, found = network.start(
        (layer_wide.T, layer_tall, head_weights.T),
        word_table,
        position_table,
        (token_ids, mlm_labels, mlm_rows, seq_lengths, sop_labels),
    )
    devices = all_facts.shape[0]
    place = place.reshape(-1, E)
    vec = vectors.reshape(-1, 128)
    kept = run_forward(seq_lengths, found, place, head, wide, tall, vec)
    (back_final, back_word_head, back_decoder, back_head, wide_sums, small_sums, totals) = (
        network.head(
            seq_lengths,
            sop_labels,
            kept["final"],
            head,
            word_table,
            decoder_bias,
            all_facts,
            vec,
        )
    )
    total = vectors.shape[0]
    share = -(-total // (devices * 1024)) * 1024
    back_rows, back_head, turned, outer, vector_grad = run_backward(
        seq_lengths,
        back_final,
        wide_sums,
        small_sums,
        head,
        back_head,
        wide,
        tall,
        vec,
        kept,
        devices * share // 128,
    )
    sums, heights, back_word, back_place, last, ends = network.finish(
        turned,
        kept["active"],
        kept["rights"].reshape(3, -1, D),
        outer.reshape(-1, D),
        back_head,
        back_rows,
        vector_grad.reshape(devices, -1, 128),
        all_facts,
        back_word_head,
        back_decoder,
        totals,
        position_table.shape[0],
    )
    wide_at, tall_at, head_at = 0, heights[0], heights[0] + heights[1]

    def turned_group(weight, first, second, low):
        return (weight.T, first.T, second.T, sums, low, LEARN_RATE)

    def flat(x):
        return x[None]

    def lines(x):
        return x.reshape(-1, 128)

    groups = (
        (word_table, word_first, word_second, back_word, 0, LEARN_RATE),
        turned_group(layer_wide, wide_first, wide_second, wide_at),
        (layer_tall, tall_first, tall_second, sums, tall_at, LEARN_RATE),
        turned_group(head_weights, head_first, head_second, head_at),
        (position_table, position_first, position_second, back_place, None, LEARN_RATE),
        (flat(decoder_bias), flat(decoder_first), flat(decoder_second), back_decoder, None)
        + (LEARN_RATE,),
        (lines(vectors), lines(vector_first), lines(vector_second), last, None, SMALL_RATE),
    )
    arrays, scalars = network.adam(ends, groups)
    word, wide, tall, head, position, decoder, vector = arrays
    grad_norm, unused, mlm_sum, sop_total, mlm_count, sop_count = scalars

    def turn(arrays):
        return [x.T for x in arrays]

    def plain(arrays):
        return [x.reshape(-1) for x in arrays]

    updates = (*word, *position, *turn(head), *plain(decoder), *turn(wide), *tall, *plain(vector))
    return (*updates, mlm_sum, mlm_count, sop_total, sop_count, grad_norm)


def solution(mesh):
    rows = P(AXES, None)
    columns = P(None, AXES)
    flat = P(AXES)
    whole = P()
    return jax.shard_map(
        functools.partial(local, mesh),
        mesh=mesh,
        in_specs=(rows, rows, columns, flat, columns, rows, whole)
        + (rows, rows) * 2
        + (columns, columns, flat, flat, columns, columns, rows, rows, whole, whole)
        + (flat,) * 5,
        out_specs=(rows,) * 6
        + (columns,) * 3
        + (flat,) * 3
        + (columns,) * 3
        + (rows,) * 3
        + (whole,) * 8,
        check_vma=False,
    )
```
